32 devices in a mesh: band: 4 (over y, core), tg: 8 (over z, x).
Axes of the slice: x: 2, y: 2, z: 4, core: 2. Of those that a mesh axis runs over, the one named last changes fastest.
Arguments:
- coefficients: float32 [4, 1536, 2, 128], P('band', 'tg'), may hold values from -6 to 6
- stick_col: int32 [1536], replicated, may hold values from 0 to 191, as said below
- stick_row: int32 [1536], replicated, may hold values from 0 to 191, as said below
- stick_length: int32 [1536], replicated, may hold values from 1 to 97, as said below
- plane_of_slot: int32 [192], replicated, may hold values from 0 to 191, each once
- potential: float32 [192, 192, 192], P('tg'), may hold values from -8 to 8
Outputs:
- applied: float32 [4, 1536, 2, 128], P('band', 'tg')
- subspace: float32 [2, 4, 4], P(None, 'band')
The draws below stay inside these ranges and needn't reach their ends.
Inputs may be any that keep to these rules, and one draw needn't show every extreme that they name: With signed values g(v) = v if v <= 48 else v - 192, every stick has g(stick_col)^2 + g(stick_row)^2 <= 48^2; no two sticks share a column and a row; stick 0 lies at column 0, row 0. stick_row is the grid row of each stick; the conditions stated for stick_col hold for the pairs (stick_col, stick_row). stick_length is odd; with h = (stick_length - 1) / 2: h^2 + g(stick_col)^2 + g(stick_row)^2 <= 48^2. `plane_of_slot`: each plane once.
All inputs are finite; a program needn't handle non-finite values.
Results may differ from the reference program's by a relative error of at most 0.00005.
Values sent between devices are 32-bit elements; how exact they have to be, the bound alone decides.
No kernel may reach another device: no remote copies, remote signals or barrier semaphores. Data moves between devices by JAX's collectives and lax.ppermute only.
A program may use at most 128 MiB of HBM per device.

```python
import math
import jax
import jax.numpy as jnp
import numpy as np
from jax import lax

GRID = 192
RADIUS = 48
SLEN = 128
NST = 1536
NB = 4


def stick_table():
    spread = np.arange(-RADIUS, RADIUS + 1)
    columns_all, rows_all = np.meshgrid(spread, spread, indexing='ij')
    columns_all = columns_all.ravel()
    rows_all = rows_all.ravel()
    squares = columns_all * columns_all + rows_all * rows_all
    inside = (squares <= RADIUS * RADIUS) & (squares > 0)
    columns_all = columns_all[inside]
    rows_all = rows_all[inside]
    halves = np.array([math.isqrt(int(RADIUS * RADIUS - value)) for value in squares[inside]])
    return (columns_all, rows_all, halves)


def chosen_sticks(key):
    columns_all, rows_all, halves = stick_table()
    order = jax.random.permutation(key, columns_all.shape[0])[:NST - 1]
    first = jnp.zeros((1,), jnp.int32)
    picked_col = jnp.concatenate([first, jnp.asarray(columns_all, jnp.int32)[order]])
    picked_row = jnp.concatenate([first, jnp.asarray(rows_all, jnp.int32)[order]])
    picked_half = jnp.concatenate([first + RADIUS, jnp.asarray(halves, jnp.int32)[order]])
    return (picked_col % GRID, picked_row % GRID, 2 * picked_half + 1)


def draw_stick_col(key, part):
    return chosen_sticks(key)[0]


def draw_stick_row(key, part):
    return chosen_sticks(key)[1]


def draw_stick_length(key, part):
    return chosen_sticks(key)[2]


def draw_coefficients(key, part):
    key = jax.random.fold_in(key, 7)
    shared_key, own_key = jax.random.split(key)
    shared = jax.random.normal(shared_key, (1, NST, 2, SLEN), jnp.float32)
    own = jax.random.normal(own_key, (NB, NST, 2, SLEN), jnp.float32)
    return jnp.clip(0.8 * shared + 0.6 * own, -6.0, 6.0)


def block_levels(key, extent, shards, smallest, high):
    gain = 1.0
    for axis_at, blocks in shards:
        draws = jax.random.uniform(jax.random.fold_in(jax.random.fold_in(key, 6), axis_at), (blocks,), jnp.float32, smallest / len(shards), high / len(shards))
        gain = gain * jnp.repeat(jnp.exp(draws), extent[axis_at] // blocks).reshape((-1,) + (1,) * (len(extent) - 1 - axis_at))
    return gain


def centred(key, dims, scale, bound, pieces=(), kind=jnp.bfloat16):
    drawn = scale * jax.random.normal(key, dims, jnp.float32)
    if pieces:
        drawn = drawn * block_levels(key, dims, pieces, -0.22, 0.18)
    return jnp.clip(drawn, -bound, bound).astype(kind)


def setup_inputs(seed: int = 0) -> dict:
    keys = jax.random.split(jax.random.key(seed), 7)
    coefficients = draw_coefficients(jax.random.fold_in(keys[6], 71), 0)
    stick_col = draw_stick_col(jax.random.fold_in(keys[6], 71), 0)
    stick_row = draw_stick_row(jax.random.fold_in(keys[6], 71), 0)
    stick_length = draw_stick_length(jax.random.fold_in(keys[6], 71), 0)
    plane_of_slot = jax.random.permutation(keys[4], GRID).astype(jnp.int32)
    potential = centred(keys[5], (GRID, GRID, GRID), 2.0, 8.0, ((0, 8),), jnp.float32)
    return {"coefficients": coefficients, "stick_col": stick_col, "stick_row": stick_row, "stick_length": stick_length, "plane_of_slot": plane_of_slot, "potential": potential}


def reference(coefficients, stick_col, stick_row, stick_length, plane_of_slot, potential):
    middle = (stick_length - 1) // 2
    positions = jnp.arange(SLEN, dtype=jnp.int32)
    kept_mask = (positions[None, :] < stick_length[:, None]).astype(jnp.float32)
    masked = coefficients * kept_mask[None, :, None, :]
    plane_index = (positions[None, :] - middle[:, None]) % GRID
    row_index = jnp.broadcast_to(stick_row[:, None], plane_index.shape)
    col_index = jnp.broadcast_to(stick_col[:, None], plane_index.shape)
    grid_potential = jnp.zeros((GRID, GRID, GRID), jnp.float32).at[plane_of_slot].set(potential)

    def one_band(wave):
        values = lax.complex(wave[:, 0, :], wave[:, 1, :])
        spectrum = jnp.zeros_like(values, shape=(GRID, GRID, GRID)).at[plane_index, row_index, col_index].add(values)
        field = jnp.fft.ifftn(spectrum) * (GRID ** 3)
        result = jnp.fft.fftn(grid_potential * field) / (GRID ** 3)
        picked = result[plane_index, row_index, col_index]
        return jnp.stack([jnp.real(picked), jnp.imag(picked)], axis=1)

    local = lax.map(one_band, masked)
    signed_col = jnp.where(stick_col <= RADIUS, stick_col, stick_col - GRID)
    signed_row = jnp.where(stick_row <= RADIUS, stick_row, stick_row - GRID)
    offsets = positions[None, :] - middle[:, None]
    squares = (signed_col * signed_col + signed_row * signed_row)[:, None] + offsets * offsets
    kinetic = squares.astype(jnp.float32) / (RADIUS * RADIUS)
    applied = kept_mask[None, :, None, :] * (kinetic[None, :, None, :] * masked + local)
    hi = lax.Precision.HIGHEST
    wave_real = masked[:, :, 0, :]
    wave_imag = masked[:, :, 1, :]
    out_real = applied[:, :, 0, :]
    out_imag = applied[:, :, 1, :]
    real_sum = jnp.einsum("isk,jsk->ij", wave_real, out_real, precision=hi) + jnp.einsum("isk,jsk->ij", wave_imag, out_imag, precision=hi)
    imag_sum = jnp.einsum("isk,jsk->ij", wave_real, out_imag, precision=hi) - jnp.einsum("isk,jsk->ij", wave_imag, out_real, precision=hi)
    subspace = jnp.stack([real_sum, imag_sum], axis=0) / (NST * SLEN)
    return applied, subspace
```

```python
import functools
import math

import jax
import jax.numpy as jnp
import ml_dtypes
import numpy as np
from jax import lax
from jax.experimental import pallas as pl
from jax.experimental.pallas import tpu as pltpu
from jax.sharding import PartitionSpec as P

RADIUS = 48
LANES = 128
F32 = jnp.float32
BF16 = jnp.bfloat16
VMEM_LIMIT = 56 * 1024 * 1024


def up8(n):
    return -(-n // 8) * 8


def split(x):
    hi = x.astype(BF16)
    return hi, (x - hi.astype(F32)).astype(BF16)


def dot3(a, b, dims=((1,), (0,))):
    def dot(x, y):
        return lax.dot_general(x, y, (dims, ((), ())), preferred_element_type=F32)

    return dot(a[0], b[0]) + (dot(a[0], b[1]) + dot(a[1], b[0]))


def trig(product, extent):
    n = product - extent * jnp.floor(product * (1.0 / extent) + 0.5)
    quarter = extent / 4.0
    unit = 2.0 * math.pi / extent

    def sine(m):
        u = m * unit
        v = u * u
        s = 1.0 / 6227020800.0
        for term in (-39916800.0, 362880.0, -5040.0, 120.0, -6.0, 1.0):
            s = s * v + 1.0 / term
        return u * s

    folded = jnp.where(
        jnp.abs(n) > quarter, jnp.where(n > 0, 2.0 * quarter, -2.0 * quarter) - n, n
    )
    return sine(quarter - jnp.abs(n)), sine(folded)


def pair(table):
    hi = table.astype(np.float32).astype(ml_dtypes.bfloat16)
    lo = (table - hi.astype(np.float64)).astype(ml_dtypes.bfloat16)
    return hi, lo


@functools.cache
def tables(extent):
    kept = 2 * RADIUS + 1
    rows = up8(kept)
    grid = np.arange(extent)
    freq = np.arange(kept) - RADIUS
    angle = 2.0 * np.pi * ((freq[:, None] * grid[None, :]) % extent) / extent
    cos, sin = np.cos(angle), np.sin(angle)
    pad_q = np.zeros((LANES - kept, extent))
    cq, sq = np.concatenate([cos, pad_q]), np.concatenate([sin, pad_q])
    pad_r = np.zeros((rows - kept, extent))
    cr, sr = np.concatenate([cos, pad_r]), np.concatenate([sin, pad_r])
    x_re = np.concatenate([cq, -sq], axis=0)
    x_im = np.concatenate([sq, cq], axis=0)
    y_fw = np.concatenate(
        [np.concatenate([cr.T, -sr.T], axis=1), np.concatenate([sr.T, cr.T], axis=1)], axis=0
    )
    y_bw = y_fw.T.copy()
    xb_re = x_re.T.copy()
    xb_im = x_im.T.copy()
    out = []
    for table in (x_re, x_im, y_fw, y_bw, xb_re, xb_im):
        out.extend(pair(table))
    return tuple(out)


def params():
    return pltpu.CompilerParams(vmem_limit_bytes=VMEM_LIMIT)


def wave_kernel(extent, planes, aux_ref, plane_ref, coef_ref, out_ref, kc_ref, whi_ref, wlo_ref, sc_ref, ss_ref):
    devices = out_ref.shape[0]
    sticks, _, padded = coef_ref.shape
    padded_planes = plane_ref.shape[1] // devices
    aux = aux_ref[...]
    aux_col = jnp.transpose(jnp.concatenate([aux] * (LANES // 8), axis=0))
    length = aux_col[:sticks, 0:1]
    square = aux_col[:sticks, 1:2]
    middle = (length - 1.0) * 0.5
    position = lax.broadcasted_iota(jnp.int32, (sticks, padded), 1).astype(F32)
    kept = (position < length).astype(F32)
    kinetic = (square + (position - middle) * (position - middle)) * (1.0 / (RADIUS * RADIUS))
    wave = jnp.concatenate([coef_ref[:, 0, :] * kept, coef_ref[:, 1, :] * kept], axis=1)
    kc_ref[...] = wave * jnp.concatenate([kinetic, kinetic], axis=1)

    total = plane_ref.shape[1]
    plane_row = jnp.broadcast_to(plane_ref[...], (LANES, total))
    plane_col = jnp.transpose(plane_row)[:, 0:1]
    slot = lax.broadcasted_iota(jnp.int32, (total, 1), 0)
    real = (plane_col >= 0.0).astype(F32)
    harmonic = lax.broadcasted_iota(jnp.int32, (total, padded), 1).astype(F32)
    cos, sin = trig(jnp.maximum(plane_col, 0.0) * harmonic, extent)
    cos, sin = cos * real, sin * real
    parts = []
    for d in range(devices):
        c = cos[d * padded_planes:(d + 1) * padded_planes]
        s = sin[d * padded_planes:(d + 1) * padded_planes]
        parts.append(jnp.concatenate([c, -s], axis=1))
        parts.append(jnp.concatenate([s, c], axis=1))
    table = split(jnp.concatenate(parts, axis=0))
    whi_ref[...] = table[0]
    wlo_ref[...] = table[1]
    middle_row = (aux[0:1, :sticks] - 1.0) * 0.5
    shift_cos, shift_sin = trig(jnp.maximum(plane_col, 0.0) * middle_row, extent)
    sc_ref[...] = shift_cos
    ss_ref[...] = shift_sin
    raw = dot3(table, split(wave), ((1,), (1,)))
    for d in range(devices):
        at = 2 * d * padded_planes
        re, im = raw[at:at + padded_planes], raw[at + padded_planes:at + 2 * padded_planes]
        c = shift_cos[d * padded_planes:(d + 1) * padded_planes]
        s = shift_sin[d * padded_planes:(d + 1) * padded_planes]
        along_re = re * c + im * s
        along_im = im * c - re * s
        out_ref[d, 0:padded_planes, :] = along_re[:, :LANES]
        out_ref[d, padded_planes:2 * padded_planes, :] = along_im[:, :LANES]
        out_ref[d, 2 * padded_planes:3 * padded_planes, :] = jnp.concatenate(
            [along_re[:, LANES:], along_im[:, LANES:]], axis=1
        )


def map_kernel(row_ref, col_ref, map_ref):
    rows = map_ref.shape[0]
    total = row_ref.shape[1]
    r = lax.broadcasted_iota(jnp.int32, (rows, total), 0)
    q = lax.broadcasted_iota(jnp.int32, (LANES, total), 0)
    place = lax.broadcasted_iota(jnp.int32, (LANES, total), 1) + 1
    in_row = (r == row_ref[...]).astype(F32).astype(BF16)
    in_col = q == col_ref[...]
    upper = jnp.where(in_col, place >> 6, 0).astype(F32).astype(BF16)
    lower = jnp.where(in_col, place & 63, 0).astype(F32).astype(BF16)

    def dot(x, y):
        return lax.dot_general(x, y, (((1,), (1,)), ((), ())), preferred_element_type=F32)

    found = dot(in_row, upper) * 64.0 + dot(in_row, lower)
    map_ref[...] = found.astype(jnp.int32) - 1


def lane_take(x, index):
    return jnp.take_along_axis(x, index, axis=1, mode="promise_in_bounds")


def plane_kernel(
    planes, map_ref, row_ref, col_ref, recv_ref,
    xr_hi, xr_lo, xi_hi, xi_lo, y_hi, y_lo, yb_hi, yb_lo, br_hi, br_lo, bi_hi, bi_lo,
    pot_hbm, out_ref, x_ref, gr_ref, gi_ref, pot_ref, sem,
):
    devices = recv_ref.shape[0]
    padded_planes = recv_ref.shape[1] // 3
    windows = x_ref.shape[0]
    rows = map_ref.shape[0]
    extent = pot_ref.shape[1]
    half = LANES // 2
    fetch = pltpu.make_async_copy(pot_hbm, pot_ref, sem)
    fetch.start()

    low = lax.broadcasted_iota(jnp.int32, (padded_planes, LANES), 1) < half
    for d in range(devices):
        x_ref[d] = recv_ref[d, 0:2 * padded_planes, :]
    for e in range(devices // 2):
        first = recv_ref[2 * e, 2 * padded_planes:3 * padded_planes, :]
        second = recv_ref[2 * e + 1, 2 * padded_planes:3 * padded_planes, :]
        x_ref[devices + e, 0:padded_planes, :] = jnp.where(low, first, pltpu.roll(second, half, 1))
        x_ref[devices + e, padded_planes:2 * padded_planes, :] = jnp.where(
            low, pltpu.roll(first, half, 1), second
        )

    blocks = padded_planes // 8
    grids = (gr_ref, gi_ref)

    @pl.loop(0, rows)
    def _(r):
        code = jnp.broadcast_to(map_ref[pl.ds(r, 1), :], (8, LANES))
        index = code & (LANES - 1)
        window = code >> 7
        for j in range(2 * blocks):
            value = jnp.zeros((8, LANES), F32)
            for w in range(windows):
                value = jnp.where(window == w, lane_take(x_ref[w, 8 * j:8 * j + 8, :], index), value)
            part, at = j // blocks, 8 * (j % blocks)
            grids[part][pl.ds(r + at * rows, 8, stride=rows), :] = value

    fetch.wait()
    table_xr = (xr_hi[...], xr_lo[...])
    table_xi = (xi_hi[...], xi_lo[...])
    table_y = (y_hi[...], y_lo[...])
    table_yb = (yb_hi[...], yb_lo[...])
    table_br = (br_hi[...], br_lo[...])
    table_bi = (bi_hi[...], bi_lo[...])

    @pl.loop(0, planes // 2)
    def _(step):
        base = pl.multiple_of(step * 2 * rows, 8)
        pick = pl.ds(base, 2 * rows)
        spectrum = split(jnp.concatenate([gr_ref[pick, :], gi_ref[pick, :]], axis=1))
        a_re = dot3(spectrum, table_xr)
        a_im = dot3(spectrum, table_xi)
        back_re, back_im = [], []
        for t in range(2):
            mid = jnp.concatenate(
                [a_re[t * rows:(t + 1) * rows], a_im[t * rows:(t + 1) * rows]], axis=0
            )
            field = dot3(table_y, split(mid))
            v = pot_ref[2 * step + t]
            weighted = jnp.concatenate([field[:extent] * v, field[extent:] * v], axis=0)
            back = dot3(table_yb, split(weighted))
            back_re.append(back[:rows])
            back_im.append(back[rows:])
        b_re = split(jnp.concatenate(back_re, axis=0))
        b_im = split(jnp.concatenate(back_im, axis=0))
        back = dot3(b_re, table_br) + dot3(b_im, table_bi)
        gr_ref[pick, :] = back[:, :LANES]
        gi_ref[pick, :] = back[:, LANES:]

    for w in range(windows):
        index = jnp.broadcast_to(col_ref[w:w + 1, :], (8, LANES))
        which = jnp.broadcast_to(row_ref[w:w + 1, :], (8, LANES))

        def body(r, acc):
            hit = which == r
            new = []
            for j in range(2 * blocks):
                part, at = j // blocks, 8 * (j % blocks)
                value = grids[part][pl.ds(r + at * rows, 8, stride=rows), :]
                new.append(jnp.where(hit, lane_take(value, index), acc[j]))
            return tuple(new)

        acc = lax.fori_loop(
            0, 2 * RADIUS + 1, body, tuple(jnp.zeros((8, LANES), F32) for _ in range(2 * blocks))
        )
        full = jnp.concatenate(acc, axis=0)
        if w < devices:
            out_ref[w, 0:2 * padded_planes, :] = full
        else:
            e = w - devices
            re, im = full[:padded_planes], full[padded_planes:]
            out_ref[2 * e, 2 * padded_planes:3 * padded_planes, :] = jnp.where(
                low, re, pltpu.roll(im, half, 1)
            )
            out_ref[2 * e + 1, 2 * padded_planes:3 * padded_planes, :] = jnp.where(
                low, pltpu.roll(re, half, 1), im
            )
    for d in range(devices):
        out_ref[d, 3 * padded_planes:, :] = jnp.zeros((8, LANES), F32)


def inner_kernel(bands, volume, norm, band_ref, *refs):
    kc_ref = refs[0]
    coefs = refs[1:1 + bands]
    fields = refs[1 + bands:1 + 2 * bands]
    in_ref = refs[1 + 2 * bands]
    out_ref = refs[2 + 2 * bands]
    devices = in_ref.shape[0]
    padded_planes = (in_ref.shape[1] - 8) // 3
    half = LANES // 2
    padded = coefs[0].shape[2]
    me = band_ref[0]
    low = lax.broadcasted_iota(jnp.int32, (padded_planes, LANES), 1) < half

    def fold(x):
        rows = x.shape[0]
        total = x[0:8]
        for at in range(8, rows, 8):
            total = total + x[at:at + 8]
        return total

    kc = kc_ref[...]
    kc_re, kc_im = kc[:, :padded], kc[:, padded:]
    sums = []
    for m in range(bands):
        c_re, c_im = coefs[m][:, 0, :], coefs[m][:, 1, :]
        sums.append([fold(c_re * kc_re + c_im * kc_im), fold(c_re * kc_im - c_im * kc_re)])
    local = [[jnp.zeros((8, LANES), F32), jnp.zeros((8, LANES), F32)] for _ in range(bands)]
    for d in range(devices):
        value = in_ref[d, 0:3 * padded_planes, :]
        re, im, rest = value[:padded_planes], value[padded_planes:2 * padded_planes], value[2 * padded_planes:]
        turned = pltpu.roll(rest, half, 1)
        other = jnp.concatenate([im, -re, jnp.where(low, turned, -turned)], axis=0)
        for m in range(bands):
            col = fields[m][d, 0:3 * padded_planes, :]
            local[m][0] = local[m][0] + fold(col * value)
            local[m][1] = local[m][1] + fold(col * other)
    lane = lax.broadcasted_iota(jnp.int32, (8, LANES), 1)
    row = lax.broadcasted_iota(jnp.int32, (8, LANES), 0)
    tile = jnp.zeros((8, LANES), F32)
    for m in range(bands):
        at = lax.rem(me + m, bands)
        for part, sign in ((0, 1.0), (1, -1.0)):
            partial = sums[m][part] + volume * local[m][part]
            scalar = jnp.sum(jnp.sum(partial, axis=1, keepdims=True), axis=0, keepdims=True)
            tile = jnp.where((lane == at) & (row == part), sign * norm * scalar, tile)
    for d in range(devices):
        out_ref[d, 0:3 * padded_planes, :] = in_ref[d, 0:3 * padded_planes, :]
        out_ref[d, 3 * padded_planes:, :] = tile


def final_kernel(volume, aux_ref, ret_ref, kc_ref, whi_ref, wlo_ref, sc_ref, ss_ref, out_ref, sub_ref):
    devices = ret_ref.shape[0]
    padded_planes = (ret_ref.shape[1] - 8) // 3
    sticks, _, padded = out_ref.shape
    half = LANES // 2
    bands = sub_ref.shape[2]
    total = jnp.zeros((8, LANES), F32)
    parts = []
    for d in range(devices):
        value = ret_ref[d]
        total = total + value[3 * padded_planes:]
        rest = value[2 * padded_planes:3 * padded_planes]
        re = jnp.concatenate([value[:padded_planes], rest[:, :half]], axis=1)
        im = jnp.concatenate([value[padded_planes:2 * padded_planes], rest[:, half:]], axis=1)
        c = sc_ref[d * padded_planes:(d + 1) * padded_planes, :]
        s = ss_ref[d * padded_planes:(d + 1) * padded_planes, :]
        parts.append(re * c - im * s)
        parts.append(re * s + im * c)
    stacked = jnp.concatenate(parts, axis=0)
    spare = jnp.zeros((stacked.shape[0], 2 * LANES - sticks), F32)
    turned = jnp.transpose(jnp.concatenate([stacked, spare], axis=1))[:sticks]
    local = dot3(split(turned), (whi_ref[...], wlo_ref[...])) * volume
    aux_col = jnp.transpose(jnp.concatenate([aux_ref[...]] * (LANES // 8), axis=0))
    length = aux_col[:sticks, 0:1]
    position = lax.broadcasted_iota(jnp.int32, (sticks, padded), 1).astype(F32)
    kept = position < length
    kc = kc_ref[...]
    out_ref[:, 0, :] = jnp.where(kept, kc[:, :padded] + local[:, :padded], 0.0)
    out_ref[:, 1, :] = jnp.where(kept, kc[:, padded:] + local[:, padded:], 0.0)
    sub_ref[:, 0, :] = total[0:2, :bands]


def window_order(values, devices):
    blocks = values.reshape(devices, -1)
    return jnp.concatenate(
        [blocks[:, :LANES].reshape(-1, LANES), blocks[:, LANES:].reshape(-1, LANES)], axis=0
    )


def shards(bands, devices, coefficients, stick_col, stick_row, stick_length, plane_of_slot, potential):
    extent = plane_of_slot.shape[0]
    sticks = coefficients.shape[1]
    padded = coefficients.shape[3]
    total_sticks = stick_col.shape[0]
    planes = potential.shape[0]
    padded_planes = up8(planes)
    if sticks != LANES + LANES // 2 or devices % 2 or planes % 2:
        raise ValueError("sizes")
    kept = 2 * RADIUS + 1
    rows = up8(kept)
    volume = 1.0 / (extent * extent * extent)
    me = lax.axis_index("tg")
    coef = coefficients.reshape(sticks, 2, padded)

    signed_col = jnp.where(stick_col <= RADIUS, stick_col, stick_col - extent)
    signed_row = jnp.where(stick_row <= RADIUS, stick_row, stick_row - extent)
    info = jnp.stack([stick_length, signed_col * signed_col + signed_row * signed_row])
    info = lax.dynamic_slice_in_dim(info, me * sticks, sticks, axis=1).astype(F32)
    aux = jnp.pad(info, ((0, 6), (0, 2 * LANES - sticks)), constant_values=1.0)
    slots = jnp.pad(
        plane_of_slot.astype(F32).reshape(devices, planes),
        ((0, 0), (0, padded_planes - planes)),
        constant_values=-1.0,
    ).reshape(1, devices * padded_planes)

    block = 3 * padded_planes
    total_planes = devices * padded_planes
    sent, kc, whi, wlo, shift_cos, shift_sin = pl.pallas_call(
        functools.partial(wave_kernel, extent, planes),
        out_shape=(
            jax.ShapeDtypeStruct((devices, block, LANES), F32),
            jax.ShapeDtypeStruct((sticks, 2 * padded), F32),
            jax.ShapeDtypeStruct((2 * total_planes, 2 * padded), BF16),
            jax.ShapeDtypeStruct((2 * total_planes, 2 * padded), BF16),
            jax.ShapeDtypeStruct((total_planes, sticks), F32),
            jax.ShapeDtypeStruct((total_planes, sticks), F32),
        ),
        compiler_params=params(),
        name="wave_to_planes",
    )(aux, slots, coef)

    received = lax.all_to_all(sent, "tg", split_axis=0, concat_axis=0, tiled=True)

    row_w = window_order(signed_row + RADIUS, devices)
    col_w = window_order(signed_col + RADIUS, devices)
    windows = row_w.shape[0]
    stick_map = pl.pallas_call(
        map_kernel,
        out_shape=jax.ShapeDtypeStruct((rows, LANES), jnp.int32),
        compiler_params=params(),
        name="stick_map",
    )(row_w.reshape(1, -1), col_w.reshape(1, -1))

    vmem = pl.BlockSpec(memory_space=pltpu.VMEM)
    weighted = pl.pallas_call(
        functools.partial(plane_kernel, planes),
        out_shape=jax.ShapeDtypeStruct((devices, block + 8, LANES), F32),
        in_specs=[vmem] * 16 + [pl.BlockSpec(memory_space=pl.ANY)],
        out_specs=vmem,
        scratch_shapes=[
            pltpu.VMEM((windows, 2 * padded_planes, LANES), F32),
            pltpu.VMEM((padded_planes * rows, LANES), F32),
            pltpu.VMEM((padded_planes * rows, LANES), F32),
            pltpu.VMEM(potential.shape, F32),
            pltpu.SemaphoreType.DMA,
        ],
        compiler_params=params(),
        name="planes",
    )(stick_map, row_w, col_w, received, *[jnp.asarray(t) for t in tables(extent)], potential)

    coefs, fields = [coef], [received]
    for shift in range(1, bands):
        ring = [((b + shift) % bands, b) for b in range(bands)]
        coefs.append(lax.ppermute(coef, "band", ring))
        fields.append(lax.ppermute(received, "band", ring))
    band = lax.axis_index("band").astype(jnp.int32).reshape(1)
    norm = 1.0 / (total_sticks * padded)
    outgoing = pl.pallas_call(
        functools.partial(inner_kernel, bands, volume, norm),
        out_shape=jax.ShapeDtypeStruct((devices, block + 8, LANES), F32),
        in_specs=[pl.BlockSpec(memory_space=pltpu.SMEM)] + [vmem] * (2 + 2 * bands),
        out_specs=vmem,
        compiler_params=params(),
        name="inner",
    )(band, kc, *coefs, *fields, weighted)

    returned = lax.all_to_all(outgoing, "tg", split_axis=0, concat_axis=0, tiled=True)
    applied, subspace = pl.pallas_call(
        functools.partial(final_kernel, volume),
        out_shape=(
            jax.ShapeDtypeStruct((sticks, 2, padded), F32),
            jax.ShapeDtypeStruct((2, 1, bands), F32),
        ),
        compiler_params=params(),
        name="planes_to_wave",
    )(aux, returned, kc, whi, wlo, shift_cos, shift_sin)
    return applied.reshape(1, sticks, 2, padded), subspace


def solution(mesh):
    in_specs = (P("band", "tg", None, None), P(), P(), P(), P(), P("tg", None, None))
    out_specs = (P("band", "tg", None, None), P(None, "band", None))
    body = functools.partial(shards, mesh.shape["band"], mesh.shape["tg"])
    return jax.shard_map(body, mesh=mesh, in_specs=in_specs, out_specs=out_specs, check_vma=False)
```

```python
import functools
import math

import jax
import jax.numpy as jnp
import ml_dtypes
import numpy as np
from jax import lax
from jax.experimental import pallas as pl
from jax.experimental.pallas import tpu as pltpu
from jax.sharding import PartitionSpec as P

RADIUS = 48
LANES = 128
F32 = jnp.float32
BF16 = jnp.bfloat16
VMEM_LIMIT = 56 * 1024 * 1024


def up8(n):
    return -(-n // 8) * 8


def split(x):
    hi = x.astype(BF16)
    return hi, (x - hi.astype(F32)).astype(BF16)


def dot3(a, b, dims=((1,), (0,))):
    def dot(x, y):
        return lax.dot_general(x, y, (dims, ((), ())), preferred_element_type=F32)

    return dot(a[0], b[0]) + (dot(a[0], b[1]) + dot(a[1], b[0]))


def trig(product, extent):
    n = product - extent * jnp.floor(product * (1.0 / extent) + 0.5)
    quarter = extent / 4.0
    unit = 2.0 * math.pi / extent

    def sine(m):
        u = m * unit
        v = u * u
        s = 1.0 / 6227020800.0
        for term in (-39916800.0, 362880.0, -5040.0, 120.0, -6.0, 1.0):
            s = s * v + 1.0 / term
        return u * s

    folded = jnp.where(
        jnp.abs(n) > quarter, jnp.where(n > 0, 2.0 * quarter, -2.0 * quarter) - n, n
    )
    return sine(quarter - jnp.abs(n)), sine(folded)


def pair(table):
    hi = table.astype(np.float32).astype(ml_dtypes.bfloat16)
    lo = (table - hi.astype(np.float64)).astype(ml_dtypes.bfloat16)
    return hi, lo


@functools.cache
def tables(extent):
    kept = 2 * RADIUS + 1
    rows = up8(kept)
    grid = np.arange(extent)
    freq = np.arange(kept) - RADIUS
    angle = 2.0 * np.pi * ((freq[:, None] * grid[None, :]) % extent) / extent
    cos, sin = np.cos(angle), np.sin(angle)
    pad_q = np.zeros((LANES - kept, extent))
    cq, sq = np.concatenate([cos, pad_q]), np.concatenate([sin, pad_q])
    pad_r = np.zeros((rows - kept, extent))
    cr, sr = np.concatenate([cos, pad_r]), np.concatenate([sin, pad_r])
    x_re = np.concatenate([cq, -sq], axis=0)
    x_im = np.concatenate([sq, cq], axis=0)
    y_fw = np.concatenate(
        [np.concatenate([cr.T, -sr.T], axis=1), np.concatenate([sr.T, cr.T], axis=1)], axis=0
    )
    y_bw = y_fw.T.copy()
    xb_re = x_re.T.copy()
    xb_im = x_im.T.copy()
    out = []
    for table in (x_re, x_im, y_fw, y_bw, xb_re, xb_im):
        out.extend(pair(table))
    return tuple(out)


def params():
    return pltpu.CompilerParams(vmem_limit_bytes=VMEM_LIMIT)


def wave_kernel(extent, planes, aux_ref, plane_ref, coef_ref, out_ref, kc_ref, whi_ref, wlo_ref, sc_ref, ss_ref):
    devices = out_ref.shape[0]
    sticks, _, padded = coef_ref.shape
    padded_planes = plane_ref.shape[1] // devices
    aux = aux_ref[...]
    aux_col = jnp.transpose(jnp.concatenate([aux] * (LANES // 8), axis=0))
    length = aux_col[:sticks, 0:1]
    square = aux_col[:sticks, 1:2]
    middle = (length - 1.0) * 0.5
    position = lax.broadcasted_iota(jnp.int32, (sticks, padded), 1).astype(F32)
    kept = (position < length).astype(F32)
    kinetic = (square + (position - middle) * (position - middle)) * (1.0 / (RADIUS * RADIUS))
    wave = jnp.concatenate([coef_ref[:, 0, :] * kept, coef_ref[:, 1, :] * kept], axis=1)
    kc_ref[...] = wave * jnp.concatenate([kinetic, kinetic], axis=1)

    total = plane_ref.shape[1]
    plane_row = jnp.broadcast_to(plane_ref[...], (LANES, total))
    plane_col = jnp.transpose(plane_row)[:, 0:1]
    slot = lax.broadcasted_iota(jnp.int32, (total, 1), 0)
    real = (plane_col >= 0.0).astype(F32)
    harmonic = lax.broadcasted_iota(jnp.int32, (total, padded), 1).astype(F32)
    cos, sin = trig(jnp.maximum(plane_col, 0.0) * harmonic, extent)
    cos, sin = cos * real, sin * real
    parts = []
    for d in range(devices):
        c = cos[d * padded_planes:(d + 1) * padded_planes]
        s = sin[d * padded_planes:(d + 1) * padded_planes]
        parts.append(jnp.concatenate([c, -s], axis=1))
        parts.append(jnp.concatenate([s, c], axis=1))
    table = split(jnp.concatenate(parts, axis=0))
    whi_ref[...] = table[0]
    wlo_ref[...] = table[1]
    middle_row = (aux[0:1, :sticks] - 1.0) * 0.5
    shift_cos, shift_sin = trig(jnp.maximum(plane_col, 0.0) * middle_row, extent)
    sc_ref[...] = shift_cos
    ss_ref[...] = shift_sin
    raw = dot3(table, split(wave), ((1,), (1,)))
    for d in range(devices):
        at = 2 * d * padded_planes
        re, im = raw[at:at + padded_planes], raw[at + padded_planes:at + 2 * padded_planes]
        c = shift_cos[d * padded_planes:(d + 1) * padded_planes]
        s = shift_sin[d * padded_planes:(d + 1) * padded_planes]
        along_re = re * c + im * s
        along_im = im * c - re * s
        out_ref[d, 0:padded_planes, :] = along_re[:, :LANES]
        out_ref[d, padded_planes:2 * padded_planes, :] = along_im[:, :LANES]
        out_ref[d, 2 * padded_planes:3 * padded_planes, :] = jnp.concatenate(
            [along_re[:, LANES:], along_im[:, LANES:]], axis=1
        )


def map_kernel(row_ref, col_ref, map_ref):
    rows = map_ref.shape[0]
    total = row_ref.shape[1]
    r = lax.broadcasted_iota(jnp.int32, (rows, total), 0)
    q = lax.broadcasted_iota(jnp.int32, (LANES, total), 0)
    place = lax.broadcasted_iota(jnp.int32, (LANES, total), 1) + 1
    in_row = (r == row_ref[...]).astype(F32).astype(BF16)
    in_col = q == col_ref[...]
    upper = jnp.where(in_col, place >> 6, 0).astype(F32).astype(BF16)
    lower = jnp.where(in_col, place & 63, 0).astype(F32).astype(BF16)

    def dot(x, y):
        return lax.dot_general(x, y, (((1,), (1,)), ((), ())), preferred_element_type=F32)

    found = dot(in_row, upper) * 64.0 + dot(in_row, lower)
    map_ref[...] = found.astype(jnp.int32) - 1


def lane_take(x, index):
    return jnp.take_along_axis(x, index, axis=1, mode="promise_in_bounds")


def plane_kernel(
    planes, map_ref, row_ref, col_ref, recv_ref,
    xr_hi, xr_lo, xi_hi, xi_lo, y_hi, y_lo, yb_hi, yb_lo, br_hi, br_lo, bi_hi, bi_lo,
    pot_hbm, out_ref, x_ref, gr_ref, gi_ref, pot_ref, sem,
):
    devices = recv_ref.shape[0]
    padded_planes = recv_ref.shape[1] // 3
    windows = x_ref.shape[0]
    rows = map_ref.shape[0]
    extent = pot_ref.shape[1]
    half = LANES // 2
    fetch = pltpu.make_async_copy(pot_hbm, pot_ref, sem)
    fetch.start()

    low = lax.broadcasted_iota(jnp.int32, (padded_planes, LANES), 1) < half
    for d in range(devices):
        x_ref[d] = recv_ref[d, 0:2 * padded_planes, :]
    for e in range(devices // 2):
        first = recv_ref[2 * e, 2 * padded_planes:3 * padded_planes, :]
        second = recv_ref[2 * e + 1, 2 * padded_planes:3 * padded_planes, :]
        x_ref[devices + e, 0:padded_planes, :] = jnp.where(low, first, pltpu.roll(second, half, 1))
        x_ref[devices + e, padded_planes:2 * padded_planes, :] = jnp.where(
            low, pltpu.roll(first, half, 1), second
        )

    blocks = padded_planes // 8
    grids = (gr_ref, gi_ref)

    @pl.loop(0, rows, unroll=4)
    def _(r):
        code = jnp.broadcast_to(map_ref[pl.ds(r, 1), :], (8, LANES))
        index = code & (LANES - 1)
        window = code >> 7
        for j in range(2 * blocks):
            value = jnp.zeros((8, LANES), F32)
            for w in range(windows):
                value = jnp.where(window == w, lane_take(x_ref[w, 8 * j:8 * j + 8, :], index), value)
            part, at = j // blocks, 8 * (j % blocks)
            grids[part][pl.ds(r + at * rows, 8, stride=rows), :] = value

    fetch.wait()
    table_xr = (xr_hi[...], xr_lo[...])
    table_xi = (xi_hi[...], xi_lo[...])
    table_y = (y_hi[...], y_lo[...])
    table_yb = (yb_hi[...], yb_lo[...])
    table_br = (br_hi[...], br_lo[...])
    table_bi = (bi_hi[...], bi_lo[...])

    @pl.loop(0, planes // 2)
    def _(step):
        base = pl.multiple_of(step * 2 * rows, 8)
        pick = pl.ds(base, 2 * rows)
        spectrum = split(jnp.concatenate([gr_ref[pick, :], gi_ref[pick, :]], axis=1))
        a_re = dot3(spectrum, table_xr)
        a_im = dot3(spectrum, table_xi)
        back_re, back_im = [], []
        for t in range(2):
            mid = jnp.concatenate(
                [a_re[t * rows:(t + 1) * rows], a_im[t * rows:(t + 1) * rows]], axis=0
            )
            field = dot3(table_y, split(mid))
            v = pot_ref[2 * step + t]
            weighted = jnp.concatenate([field[:extent] * v, field[extent:] * v], axis=0)
            back = dot3(table_yb, split(weighted))
            back_re.append(back[:rows])
            back_im.append(back[rows:])
        b_re = split(jnp.concatenate(back_re, axis=0))
        b_im = split(jnp.concatenate(back_im, axis=0))
        back = dot3(b_re, table_br) + dot3(b_im, table_bi)
        gr_ref[pick, :] = back[:, :LANES]
        gi_ref[pick, :] = back[:, LANES:]

    for w in range(windows):
        index = jnp.broadcast_to(col_ref[w:w + 1, :], (8, LANES))
        which = jnp.broadcast_to(row_ref[w:w + 1, :], (8, LANES))

        def body(r, acc):
            hit = which == r
            new = []
            for j in range(2 * blocks):
                part, at = j // blocks, 8 * (j % blocks)
                value = grids[part][pl.ds(r + at * rows, 8, stride=rows), :]
                new.append(jnp.where(hit, lane_take(value, index), acc[j]))
            return tuple(new)

        acc = lax.fori_loop(
            0, rows, body, tuple(jnp.zeros((8, LANES), F32) for _ in range(2 * blocks)), unroll=8
        )
        full = jnp.concatenate(acc, axis=0)
        if w < devices:
            out_ref[w, 0:2 * padded_planes, :] = full
        else:
            e = w - devices
            re, im = full[:padded_planes], full[padded_planes:]
            out_ref[2 * e, 2 * padded_planes:3 * padded_planes, :] = jnp.where(
                low, re, pltpu.roll(im, half, 1)
            )
            out_ref[2 * e + 1, 2 * padded_planes:3 * padded_planes, :] = jnp.where(
                low, pltpu.roll(re, half, 1), im
            )
    for d in range(devices):
        out_ref[d, 3 * padded_planes:, :] = jnp.zeros((8, LANES), F32)


def inner_kernel(bands, volume, norm, band_ref, *refs):
    kc_ref = refs[0]
    coefs = refs[1:1 + bands]
    fields = refs[1 + bands:1 + 2 * bands]
    in_ref = refs[1 + 2 * bands]
    out_ref = refs[2 + 2 * bands]
    devices = in_ref.shape[0]
    padded_planes = (in_ref.shape[1] - 8) // 3
    half = LANES // 2
    padded = coefs[0].shape[2]
    me = band_ref[0]
    low = lax.broadcasted_iota(jnp.int32, (padded_planes, LANES), 1) < half

    def fold(x):
        rows = x.shape[0]
        total = x[0:8]
        for at in range(8, rows, 8):
            total = total + x[at:at + 8]
        return total

    kc = kc_ref[...]
    kc_re, kc_im = kc[:, :padded], kc[:, padded:]
    sums = []
    for m in range(bands):
        c_re, c_im = coefs[m][:, 0, :], coefs[m][:, 1, :]
        sums.append([fold(c_re * kc_re + c_im * kc_im), fold(c_re * kc_im - c_im * kc_re)])
    local = [[jnp.zeros((8, LANES), F32), jnp.zeros((8, LANES), F32)] for _ in range(bands)]
    for d in range(devices):
        value = in_ref[d, 0:3 * padded_planes, :]
        re, im, rest = value[:padded_planes], value[padded_planes:2 * padded_planes], value[2 * padded_planes:]
        turned = pltpu.roll(rest, half, 1)
        other = jnp.concatenate([im, -re, jnp.where(low, turned, -turned)], axis=0)
        for m in range(bands):
            col = fields[m][d, 0:3 * padded_planes, :]
            local[m][0] = local[m][0] + fold(col * value)
            local[m][1] = local[m][1] + fold(col * other)
    lane = lax.broadcasted_iota(jnp.int32, (8, LANES), 1)
    row = lax.broadcasted_iota(jnp.int32, (8, LANES), 0)
    tile = jnp.zeros((8, LANES), F32)
    for m in range(bands):
        at = lax.rem(me + m, bands)
        for part, sign in ((0, 1.0), (1, -1.0)):
            partial = sums[m][part] + volume * local[m][part]
            scalar = jnp.sum(jnp.sum(partial, axis=1, keepdims=True), axis=0, keepdims=True)
            tile = jnp.where((lane == at) & (row == part), sign * norm * scalar, tile)
    for d in range(devices):
        out_ref[d, 0:3 * padded_planes, :] = in_ref[d, 0:3 * padded_planes, :]
        out_ref[d, 3 * padded_planes:, :] = tile


def final_kernel(volume, aux_ref, ret_ref, kc_ref, whi_ref, wlo_ref, sc_ref, ss_ref, out_ref, sub_ref):
    devices = ret_ref.shape[0]
    padded_planes = (ret_ref.shape[1] - 8) // 3
    sticks, _, padded = out_ref.shape
    half = LANES // 2
    bands = sub_ref.shape[2]
    total = jnp.zeros((8, LANES), F32)
    parts = []
    for d in range(devices):
        value = ret_ref[d]
        total = total + value[3 * padded_planes:]
        rest = value[2 * padded_planes:3 * padded_planes]
        re = jnp.concatenate([value[:padded_planes], rest[:, :half]], axis=1)
        im = jnp.concatenate([value[padded_planes:2 * padded_planes], rest[:, half:]], axis=1)
        c = sc_ref[d * padded_planes:(d + 1) * padded_planes, :]
        s = ss_ref[d * padded_planes:(d + 1) * padded_planes, :]
        parts.append(re * c - im * s)
        parts.append(re * s + im * c)
    stacked = jnp.concatenate(parts, axis=0)
    spare = jnp.zeros((stacked.shape[0], 2 * LANES - sticks), F32)
    turned = jnp.transpose(jnp.concatenate([stacked, spare], axis=1))[:sticks]
    local = dot3(split(turned), (whi_ref[...], wlo_ref[...])) * volume
    aux_col = jnp.transpose(jnp.concatenate([aux_ref[...]] * (LANES // 8), axis=0))
    length = aux_col[:sticks, 0:1]
    position = lax.broadcasted_iota(jnp.int32, (sticks, padded), 1).astype(F32)
    kept = position < length
    kc = kc_ref[...]
    out_ref[:, 0, :] = jnp.where(kept, kc[:, :padded] + local[:, :padded], 0.0)
    out_ref[:, 1, :] = jnp.where(kept, kc[:, padded:] + local[:, padded:], 0.0)
    sub_ref[:, 0, :] = total[0:2, :bands]


def window_order(values, devices):
    blocks = values.reshape(devices, -1)
    return jnp.concatenate(
        [blocks[:, :LANES].reshape(-1, LANES), blocks[:, LANES:].reshape(-1, LANES)], axis=0
    )


def shards(bands, devices, coefficients, stick_col, stick_row, stick_length, plane_of_slot, potential):
    extent = plane_of_slot.shape[0]
    sticks = coefficients.shape[1]
    padded = coefficients.shape[3]
    total_sticks = stick_col.shape[0]
    planes = potential.shape[0]
    padded_planes = up8(planes)
    if sticks != LANES + LANES // 2 or devices % 2 or planes % 2:
        raise ValueError("sizes")
    kept = 2 * RADIUS + 1
    rows = up8(kept)
    volume = 1.0 / (extent * extent * extent)
    me = lax.axis_index("tg")
    coef = coefficients.reshape(sticks, 2, padded)

    signed_col = jnp.where(stick_col <= RADIUS, stick_col, stick_col - extent)
    signed_row = jnp.where(stick_row <= RADIUS, stick_row, stick_row - extent)
    info = jnp.stack([stick_length, signed_col * signed_col + signed_row * signed_row])
    info = lax.dynamic_slice_in_dim(info, me * sticks, sticks, axis=1).astype(F32)
    aux = jnp.pad(info, ((0, 6), (0, 2 * LANES - sticks)), constant_values=1.0)
    slots = jnp.pad(
        plane_of_slot.astype(F32).reshape(devices, planes),
        ((0, 0), (0, padded_planes - planes)),
        constant_values=-1.0,
    ).reshape(1, devices * padded_planes)

    block = 3 * padded_planes
    total_planes = devices * padded_planes
    sent, kc, whi, wlo, shift_cos, shift_sin = pl.pallas_call(
        functools.partial(wave_kernel, extent, planes),
        out_shape=(
            jax.ShapeDtypeStruct((devices, block, LANES), F32),
            jax.ShapeDtypeStruct((sticks, 2 * padded), F32),
            jax.ShapeDtypeStruct((2 * total_planes, 2 * padded), BF16),
            jax.ShapeDtypeStruct((2 * total_planes, 2 * padded), BF16),
            jax.ShapeDtypeStruct((total_planes, sticks), F32),
            jax.ShapeDtypeStruct((total_planes, sticks), F32),
        ),
        compiler_params=params(),
        name="wave_to_planes",
    )(aux, slots, coef)

    received = lax.all_to_all(sent, "tg", split_axis=0, concat_axis=0, tiled=True)

    row_w = window_order(signed_row + RADIUS, devices)
    col_w = window_order(signed_col + RADIUS, devices)
    windows = row_w.shape[0]
    stick_map = pl.pallas_call(
        map_kernel,
        out_shape=jax.ShapeDtypeStruct((rows, LANES), jnp.int32),
        compiler_params=params(),
        name="stick_map",
    )(row_w.reshape(1, -1), col_w.reshape(1, -1))

    vmem = pl.BlockSpec(memory_space=pltpu.VMEM)
    weighted = pl.pallas_call(
        functools.partial(plane_kernel, planes),
        out_shape=jax.ShapeDtypeStruct((devices, block + 8, LANES), F32),
        in_specs=[vmem] * 16 + [pl.BlockSpec(memory_space=pl.ANY)],
        out_specs=vmem,
        scratch_shapes=[
            pltpu.VMEM((windows, 2 * padded_planes, LANES), F32),
            pltpu.VMEM((padded_planes * rows, LANES), F32),
            pltpu.VMEM((padded_planes * rows, LANES), F32),
            pltpu.VMEM(potential.shape, F32),
            pltpu.SemaphoreType.DMA,
        ],
        compiler_params=params(),
        name="planes",
    )(stick_map, row_w, col_w, received, *[jnp.asarray(t) for t in tables(extent)], potential)

    coefs, fields = [coef], [received]
    for shift in range(1, bands):
        ring = [((b + shift) % bands, b) for b in range(bands)]
        coefs.append(lax.ppermute(coef, "band", ring))
        fields.append(lax.ppermute(received, "band", ring))
    band = lax.axis_index("band").astype(jnp.int32).reshape(1)
    norm = 1.0 / (total_sticks * padded)
    outgoing = pl.pallas_call(
        functools.partial(inner_kernel, bands, volume, norm),
        out_shape=jax.ShapeDtypeStruct((devices, block + 8, LANES), F32),
        in_specs=[pl.BlockSpec(memory_space=pltpu.SMEM)] + [vmem] * (2 + 2 * bands),
        out_specs=vmem,
        compiler_params=params(),
        name="inner",
    )(band, kc, *coefs, *fields, weighted)

    returned = lax.all_to_all(outgoing, "tg", split_axis=0, concat_axis=0, tiled=True)
    applied, subspace = pl.pallas_call(
        functools.partial(final_kernel, volume),
        out_shape=(
            jax.ShapeDtypeStruct((sticks, 2, padded), F32),
            jax.ShapeDtypeStruct((2, 1, bands), F32),
        ),
        compiler_params=params(),
        name="planes_to_wave",
    )(aux, returned, kc, whi, wlo, shift_cos, shift_sin)
    return applied.reshape(1, sticks, 2, padded), subspace


def solution(mesh):
    in_specs = (P("band", "tg", None, None), P(), P(), P(), P(), P("tg", None, None))
    out_specs = (P("band", "tg", None, None), P(None, "band", None))
    body = functools.partial(shards, mesh.shape["band"], mesh.shape["tg"])
    return jax.shard_map(body, mesh=mesh, in_specs=in_specs, out_specs=out_specs, check_vma=False)
```

```python
import functools
import math

import jax
import jax.numpy as jnp
import ml_dtypes
import numpy as np
from jax import lax
from jax.experimental import pallas as pl
from jax.experimental.pallas import tpu as pltpu
from jax.sharding import PartitionSpec as P

RADIUS = 48
LANES = 128
F32 = jnp.float32
BF16 = jnp.bfloat16
VMEM_LIMIT = 56 * 1024 * 1024


def up8(n):
    return -(-n // 8) * 8


def split(x):
    hi = x.astype(BF16)
    return hi, (x - hi.astype(F32)).astype(BF16)


def dot3(a, b, dims=((1,), (0,))):
    def dot(x, y):
        return lax.dot_general(x, y, (dims, ((), ())), preferred_element_type=F32)

    return dot(a[0], b[0]) + (dot(a[0], b[1]) + dot(a[1], b[0]))


def trig(product, extent):
    n = product - extent * jnp.floor(product * (1.0 / extent) + 0.5)
    quarter = extent / 4.0
    unit = 2.0 * math.pi / extent

    def sine(m):
        u = m * unit
        v = u * u
        s = 1.0 / 6227020800.0
        for term in (-39916800.0, 362880.0, -5040.0, 120.0, -6.0, 1.0):
            s = s * v + 1.0 / term
        return u * s

    folded = jnp.where(
        jnp.abs(n) > quarter, jnp.where(n > 0, 2.0 * quarter, -2.0 * quarter) - n, n
    )
    return sine(quarter - jnp.abs(n)), sine(folded)


def pair(table):
    hi = table.astype(np.float32).astype(ml_dtypes.bfloat16)
    lo = (table - hi.astype(np.float64)).astype(ml_dtypes.bfloat16)
    return hi, lo


@functools.cache
def tables(extent):
    kept = 2 * RADIUS + 1
    rows = up8(kept)
    grid = np.arange(extent)
    freq = np.arange(kept) - RADIUS
    angle = 2.0 * np.pi * ((freq[:, None] * grid[None, :]) % extent) / extent
    cos, sin = np.cos(angle), np.sin(angle)
    pad_q = np.zeros((LANES - kept, extent))
    cq, sq = np.concatenate([cos, pad_q]), np.concatenate([sin, pad_q])
    pad_r = np.zeros((rows - kept, extent))
    cr, sr = np.concatenate([cos, pad_r]), np.concatenate([sin, pad_r])
    x_re = np.concatenate([cq, -sq], axis=0)
    x_im = np.concatenate([sq, cq], axis=0)
    y_fw = np.concatenate(
        [np.concatenate([cr.T, -sr.T], axis=1), np.concatenate([sr.T, cr.T], axis=1)], axis=0
    )
    y_bw = y_fw.T.copy()
    xb_re = x_re.T.copy()
    xb_im = x_im.T.copy()
    out = []
    for table in (x_re, x_im, y_fw, y_bw, xb_re, xb_im):
        out.extend(pair(table))
    return tuple(out)


def params():
    return pltpu.CompilerParams(vmem_limit_bytes=VMEM_LIMIT)


def wave_kernel(extent, planes, aux_ref, plane_ref, coef_ref, out_ref, kc_ref, whi_ref, wlo_ref, sc_ref, ss_ref):
    devices = out_ref.shape[0]
    sticks, _, padded = coef_ref.shape
    padded_planes = plane_ref.shape[1] // devices
    aux = aux_ref[...]
    aux_col = jnp.transpose(jnp.concatenate([aux] * (LANES // 8), axis=0))
    length = aux_col[:sticks, 0:1]
    square = aux_col[:sticks, 1:2]
    middle = (length - 1.0) * 0.5
    position = lax.broadcasted_iota(jnp.int32, (sticks, padded), 1).astype(F32)
    kept = (position < length).astype(F32)
    kinetic = (square + (position - middle) * (position - middle)) * (1.0 / (RADIUS * RADIUS))
    wave = jnp.concatenate([coef_ref[:, 0, :] * kept, coef_ref[:, 1, :] * kept], axis=1)
    kc_ref[...] = wave * jnp.concatenate([kinetic, kinetic], axis=1)

    total = plane_ref.shape[1]
    plane_row = jnp.broadcast_to(plane_ref[...], (LANES, total))
    plane_col = jnp.transpose(plane_row)[:, 0:1]
    slot = lax.broadcasted_iota(jnp.int32, (total, 1), 0)
    real = (plane_col >= 0.0).astype(F32)
    harmonic = lax.broadcasted_iota(jnp.int32, (total, padded), 1).astype(F32)
    cos, sin = trig(jnp.maximum(plane_col, 0.0) * harmonic, extent)
    cos, sin = cos * real, sin * real
    parts = []
    for d in range(devices):
        c = cos[d * padded_planes:(d + 1) * padded_planes]
        s = sin[d * padded_planes:(d + 1) * padded_planes]
        parts.append(jnp.concatenate([c, -s], axis=1))
        parts.append(jnp.concatenate([s, c], axis=1))
    table = split(jnp.concatenate(parts, axis=0))
    whi_ref[...] = table[0]
    wlo_ref[...] = table[1]
    middle_row = (aux[0:1, :sticks] - 1.0) * 0.5
    shift_cos, shift_sin = trig(jnp.maximum(plane_col, 0.0) * middle_row, extent)
    sc_ref[...] = shift_cos
    ss_ref[...] = shift_sin
    raw = dot3(table, split(wave), ((1,), (1,)))
    for d in range(devices):
        at = 2 * d * padded_planes
        re, im = raw[at:at + padded_planes], raw[at + padded_planes:at + 2 * padded_planes]
        c = shift_cos[d * padded_planes:(d + 1) * padded_planes]
        s = shift_sin[d * padded_planes:(d + 1) * padded_planes]
        along_re = re * c + im * s
        along_im = im * c - re * s
        out_ref[d, 0:padded_planes, :] = along_re[:, :LANES]
        out_ref[d, padded_planes:2 * padded_planes, :] = along_im[:, :LANES]
        out_ref[d, 2 * padded_planes:3 * padded_planes, :] = jnp.concatenate(
            [along_re[:, LANES:], along_im[:, LANES:]], axis=1
        )


def map_kernel(row_ref, col_ref, map_ref):
    rows = map_ref.shape[0]
    total = row_ref.shape[1]
    r = lax.broadcasted_iota(jnp.int32, (rows, total), 0)
    q = lax.broadcasted_iota(jnp.int32, (LANES, total), 0)
    place = lax.broadcasted_iota(jnp.int32, (LANES, total), 1) + 1
    in_row = (r == row_ref[...]).astype(F32).astype(BF16)
    in_col = q == col_ref[...]
    upper = jnp.where(in_col, place >> 6, 0).astype(F32).astype(BF16)
    lower = jnp.where(in_col, place & 63, 0).astype(F32).astype(BF16)

    def dot(x, y):
        return lax.dot_general(x, y, (((1,), (1,)), ((), ())), preferred_element_type=F32)

    found = dot(in_row, upper) * 64.0 + dot(in_row, lower)
    map_ref[...] = found.astype(jnp.int32) - 1


def lane_take(x, index):
    return jnp.take_along_axis(x, index, axis=1, mode="promise_in_bounds")


def plane_kernel(
    planes, map_ref, row_ref, col_ref, recv_ref,
    xr_hi, xr_lo, xi_hi, xi_lo, y_hi, y_lo, yb_hi, yb_lo, br_hi, br_lo, bi_hi, bi_lo,
    pot_hbm, out_ref, x_ref, gr_ref, gi_ref, pot_ref, sem,
):
    devices = recv_ref.shape[0]
    padded_planes = recv_ref.shape[1] // 3
    windows = x_ref.shape[0]
    rows = map_ref.shape[0]
    extent = pot_ref.shape[1]
    half = LANES // 2
    fetch = pltpu.make_async_copy(pot_hbm, pot_ref, sem)
    fetch.start()

    low = lax.broadcasted_iota(jnp.int32, (padded_planes, LANES), 1) < half
    for d in range(devices):
        x_ref[d] = recv_ref[d, 0:2 * padded_planes, :]
    for e in range(devices // 2):
        first = recv_ref[2 * e, 2 * padded_planes:3 * padded_planes, :]
        second = recv_ref[2 * e + 1, 2 * padded_planes:3 * padded_planes, :]
        x_ref[devices + e, 0:padded_planes, :] = jnp.where(low, first, pltpu.roll(second, half, 1))
        x_ref[devices + e, padded_planes:2 * padded_planes, :] = jnp.where(
            low, pltpu.roll(first, half, 1), second
        )

    blocks = padded_planes // 8
    grids = (gr_ref, gi_ref)

    @pl.loop(0, rows, unroll=8)
    def _(r):
        code = jnp.broadcast_to(map_ref[pl.ds(r, 1), :], (8, LANES))
        index = code & (LANES - 1)
        window = code >> 7
        for j in range(2 * blocks):
            value = jnp.zeros((8, LANES), F32)
            for w in range(windows):
                value = jnp.where(window == w, lane_take(x_ref[w, 8 * j:8 * j + 8, :], index), value)
            part, at = j // blocks, 8 * (j % blocks)
            grids[part][pl.ds(r + at * rows, 8, stride=rows), :] = value

    fetch.wait()
    table_xr = (xr_hi[...], xr_lo[...])
    table_xi = (xi_hi[...], xi_lo[...])
    table_y = (y_hi[...], y_lo[...])
    table_yb = (yb_hi[...], yb_lo[...])
    table_br = (br_hi[...], br_lo[...])
    table_bi = (bi_hi[...], bi_lo[...])

    @pl.loop(0, planes // 2, unroll=3)
    def _(step):
        base = pl.multiple_of(step * 2 * rows, 8)
        pick = pl.ds(base, 2 * rows)
        spectrum = split(jnp.concatenate([gr_ref[pick, :], gi_ref[pick, :]], axis=1))
        a_re = dot3(spectrum, table_xr)
        a_im = dot3(spectrum, table_xi)
        back_re, back_im = [], []
        for t in range(2):
            mid = jnp.concatenate(
                [a_re[t * rows:(t + 1) * rows], a_im[t * rows:(t + 1) * rows]], axis=0
            )
            field = dot3(table_y, split(mid))
            v = pot_ref[2 * step + t]
            weighted = jnp.concatenate([field[:extent] * v, field[extent:] * v], axis=0)
            back = dot3(table_yb, split(weighted))
            back_re.append(back[:rows])
            back_im.append(back[rows:])
        b_re = split(jnp.concatenate(back_re, axis=0))
        b_im = split(jnp.concatenate(back_im, axis=0))
        back = dot3(b_re, table_br) + dot3(b_im, table_bi)
        gr_ref[pick, :] = back[:, :LANES]
        gi_ref[pick, :] = back[:, LANES:]

    for w in range(windows):
        index = jnp.broadcast_to(col_ref[w:w + 1, :], (8, LANES))
        which = jnp.broadcast_to(row_ref[w:w + 1, :], (8, LANES))

        def body(r, acc):
            hit = which == r
            new = []
            for j in range(2 * blocks):
                part, at = j // blocks, 8 * (j % blocks)
                value = grids[part][pl.ds(r + at * rows, 8, stride=rows), :]
                new.append(jnp.where(hit, lane_take(value, index), acc[j]))
            return tuple(new)

        acc = lax.fori_loop(
            0, rows, body, tuple(jnp.zeros((8, LANES), F32) for _ in range(2 * blocks)), unroll=26
        )
        full = jnp.concatenate(acc, axis=0)
        if w < devices:
            out_ref[w, 0:2 * padded_planes, :] = full
        else:
            e = w - devices
            re, im = full[:padded_planes], full[padded_planes:]
            out_ref[2 * e, 2 * padded_planes:3 * padded_planes, :] = jnp.where(
                low, re, pltpu.roll(im, half, 1)
            )
            out_ref[2 * e + 1, 2 * padded_planes:3 * padded_planes, :] = jnp.where(
                low, pltpu.roll(re, half, 1), im
            )
    for d in range(devices):
        out_ref[d, 3 * padded_planes:, :] = jnp.zeros((8, LANES), F32)


def inner_kernel(bands, volume, norm, band_ref, *refs):
    kc_ref = refs[0]
    coefs = refs[1:1 + bands]
    fields = refs[1 + bands:1 + 2 * bands]
    in_ref = refs[1 + 2 * bands]
    out_ref = refs[2 + 2 * bands]
    devices = in_ref.shape[0]
    padded_planes = (in_ref.shape[1] - 8) // 3
    half = LANES // 2
    padded = coefs[0].shape[2]
    me = band_ref[0]
    low = lax.broadcasted_iota(jnp.int32, (padded_planes, LANES), 1) < half

    def fold(x):
        rows = x.shape[0]
        total = x[0:8]
        for at in range(8, rows, 8):
            total = total + x[at:at + 8]
        return total

    kc = kc_ref[...]
    kc_re, kc_im = kc[:, :padded], kc[:, padded:]
    sums = []
    for m in range(bands):
        c_re, c_im = coefs[m][:, 0, :], coefs[m][:, 1, :]
        sums.append([fold(c_re * kc_re + c_im * kc_im), fold(c_re * kc_im - c_im * kc_re)])
    local = [[jnp.zeros((8, LANES), F32), jnp.zeros((8, LANES), F32)] for _ in range(bands)]
    for d in range(devices):
        value = in_ref[d, 0:3 * padded_planes, :]
        re, im, rest = value[:padded_planes], value[padded_planes:2 * padded_planes], value[2 * padded_planes:]
        turned = pltpu.roll(rest, half, 1)
        other = jnp.concatenate([im, -re, jnp.where(low, turned, -turned)], axis=0)
        for m in range(bands):
            col = fields[m][d, 0:3 * padded_planes, :]
            local[m][0] = local[m][0] + fold(col * value)
            local[m][1] = local[m][1] + fold(col * other)
    lane = lax.broadcasted_iota(jnp.int32, (8, LANES), 1)
    row = lax.broadcasted_iota(jnp.int32, (8, LANES), 0)
    tile = jnp.zeros((8, LANES), F32)
    for m in range(bands):
        at = lax.rem(me + m, bands)
        for part, sign in ((0, 1.0), (1, -1.0)):
            partial = sums[m][part] + volume * local[m][part]
            scalar = jnp.sum(jnp.sum(partial, axis=1, keepdims=True), axis=0, keepdims=True)
            tile = jnp.where((lane == at) & (row == part), sign * norm * scalar, tile)
    for d in range(devices):
        out_ref[d, 0:3 * padded_planes, :] = in_ref[d, 0:3 * padded_planes, :]
        out_ref[d, 3 * padded_planes:, :] = tile


def final_kernel(volume, aux_ref, ret_ref, kc_ref, whi_ref, wlo_ref, sc_ref, ss_ref, out_ref, sub_ref):
    devices = ret_ref.shape[0]
    padded_planes = (ret_ref.shape[1] - 8) // 3
    sticks, _, padded = out_ref.shape
    half = LANES // 2
    bands = sub_ref.shape[2]
    total = jnp.zeros((8, LANES), F32)
    parts = []
    for d in range(devices):
        value = ret_ref[d]
        total = total + value[3 * padded_planes:]
        rest = value[2 * padded_planes:3 * padded_planes]
        re = jnp.concatenate([value[:padded_planes], rest[:, :half]], axis=1)
        im = jnp.concatenate([value[padded_planes:2 * padded_planes], rest[:, half:]], axis=1)
        c = sc_ref[d * padded_planes:(d + 1) * padded_planes, :]
        s = ss_ref[d * padded_planes:(d + 1) * padded_planes, :]
        parts.append(re * c - im * s)
        parts.append(re * s + im * c)
    stacked = jnp.concatenate(parts, axis=0)
    spare = jnp.zeros((stacked.shape[0], 2 * LANES - sticks), F32)
    turned = jnp.transpose(jnp.concatenate([stacked, spare], axis=1))[:sticks]
    local = dot3(split(turned), (whi_ref[...], wlo_ref[...])) * volume
    aux_col = jnp.transpose(jnp.concatenate([aux_ref[...]] * (LANES // 8), axis=0))
    length = aux_col[:sticks, 0:1]
    position = lax.broadcasted_iota(jnp.int32, (sticks, padded), 1).astype(F32)
    kept = position < length
    kc = kc_ref[...]
    out_ref[:, 0, :] = jnp.where(kept, kc[:, :padded] + local[:, :padded], 0.0)
    out_ref[:, 1, :] = jnp.where(kept, kc[:, padded:] + local[:, padded:], 0.0)
    sub_ref[:, 0, :] = total[0:2, :bands]


def window_order(values, devices):
    blocks = values.reshape(devices, -1)
    return jnp.concatenate(
        [blocks[:, :LANES].reshape(-1, LANES), blocks[:, LANES:].reshape(-1, LANES)], axis=0
    )


def shards(bands, devices, coefficients, stick_col, stick_row, stick_length, plane_of_slot, potential):
    extent = plane_of_slot.shape[0]
    sticks = coefficients.shape[1]
    padded = coefficients.shape[3]
    total_sticks = stick_col.shape[0]
    planes = potential.shape[0]
    padded_planes = up8(planes)
    if sticks != LANES + LANES // 2 or devices % 2 or planes % 2:
        raise ValueError("sizes")
    kept = 2 * RADIUS + 1
    rows = up8(kept)
    volume = 1.0 / (extent * extent * extent)
    me = lax.axis_index("tg")
    coef = coefficients.reshape(sticks, 2, padded)

    signed_col = jnp.where(stick_col <= RADIUS, stick_col, stick_col - extent)
    signed_row = jnp.where(stick_row <= RADIUS, stick_row, stick_row - extent)
    info = jnp.stack([stick_length, signed_col * signed_col + signed_row * signed_row])
    info = lax.dynamic_slice_in_dim(info, me * sticks, sticks, axis=1).astype(F32)
    aux = jnp.pad(info, ((0, 6), (0, 2 * LANES - sticks)), constant_values=1.0)
    slots = jnp.pad(
        plane_of_slot.astype(F32).reshape(devices, planes),
        ((0, 0), (0, padded_planes - planes)),
        constant_values=-1.0,
    ).reshape(1, devices * padded_planes)

    block = 3 * padded_planes
    total_planes = devices * padded_planes
    sent, kc, whi, wlo, shift_cos, shift_sin = pl.pallas_call(
        functools.partial(wave_kernel, extent, planes),
        out_shape=(
            jax.ShapeDtypeStruct((devices, block, LANES), F32),
            jax.ShapeDtypeStruct((sticks, 2 * padded), F32),
            jax.ShapeDtypeStruct((2 * total_planes, 2 * padded), BF16),
            jax.ShapeDtypeStruct((2 * total_planes, 2 * padded), BF16),
            jax.ShapeDtypeStruct((total_planes, sticks), F32),
            jax.ShapeDtypeStruct((total_planes, sticks), F32),
        ),
        compiler_params=params(),
        name="wave_to_planes",
    )(aux, slots, coef)

    received = lax.all_to_all(sent, "tg", split_axis=0, concat_axis=0, tiled=True)

    row_w = window_order(signed_row + RADIUS, devices)
    col_w = window_order(signed_col + RADIUS, devices)
    windows = row_w.shape[0]
    stick_map = pl.pallas_call(
        map_kernel,
        out_shape=jax.ShapeDtypeStruct((rows, LANES), jnp.int32),
        compiler_params=params(),
        name="stick_map",
    )(row_w.reshape(1, -1), col_w.reshape(1, -1))

    vmem = pl.BlockSpec(memory_space=pltpu.VMEM)
    weighted = pl.pallas_call(
        functools.partial(plane_kernel, planes),
        out_shape=jax.ShapeDtypeStruct((devices, block + 8, LANES), F32),
        in_specs=[vmem] * 16 + [pl.BlockSpec(memory_space=pl.ANY)],
        out_specs=vmem,
        scratch_shapes=[
            pltpu.VMEM((windows, 2 * padded_planes, LANES), F32),
            pltpu.VMEM((padded_planes * rows, LANES), F32),
            pltpu.VMEM((padded_planes * rows, LANES), F32),
            pltpu.VMEM(potential.shape, F32),
            pltpu.SemaphoreType.DMA,
        ],
        compiler_params=params(),
        name="planes",
    )(stick_map, row_w, col_w, received, *[jnp.asarray(t) for t in tables(extent)], potential)

    coefs, fields = [coef], [received]
    for shift in range(1, bands):
        ring = [((b + shift) % bands, b) for b in range(bands)]
        coefs.append(lax.ppermute(coef, "band", ring))
        fields.append(lax.ppermute(received, "band", ring))
    band = lax.axis_index("band").astype(jnp.int32).reshape(1)
    norm = 1.0 / (total_sticks * padded)
    outgoing = pl.pallas_call(
        functools.partial(inner_kernel, bands, volume, norm),
        out_shape=jax.ShapeDtypeStruct((devices, block + 8, LANES), F32),
        in_specs=[pl.BlockSpec(memory_space=pltpu.SMEM)] + [vmem] * (2 + 2 * bands),
        out_specs=vmem,
        compiler_params=params(),
        name="inner",
    )(band, kc, *coefs, *fields, weighted)

    returned = lax.all_to_all(outgoing, "tg", split_axis=0, concat_axis=0, tiled=True)
    applied, subspace = pl.pallas_call(
        functools.partial(final_kernel, volume),
        out_shape=(
            jax.ShapeDtypeStruct((sticks, 2, padded), F32),
            jax.ShapeDtypeStruct((2, 1, bands), F32),
        ),
        compiler_params=params(),
        name="planes_to_wave",
    )(aux, returned, kc, whi, wlo, shift_cos, shift_sin)
    return applied.reshape(1, sticks, 2, padded), subspace


def solution(mesh):
    in_specs = (P("band", "tg", None, None), P(), P(), P(), P(), P("tg", None, None))
    out_specs = (P("band", "tg", None, None), P(None, "band", None))
    body = functools.partial(shards, mesh.shape["band"], mesh.shape["tg"])
    return jax.shard_map(body, mesh=mesh, in_specs=in_specs, out_specs=out_specs, check_vma=False)
```

```python
import functools
import math

import jax
import jax.numpy as jnp
import ml_dtypes
import numpy as np
from jax import lax
from jax.experimental import pallas as pl
from jax.experimental.pallas import tpu as pltpu
from jax.sharding import PartitionSpec as P

RADIUS = 48
LANES = 128
F32 = jnp.float32
BF16 = jnp.bfloat16
VMEM_LIMIT = 56 * 1024 * 1024


def up8(n):
    return -(-n // 8) * 8


def split(x):
    hi = x.astype(BF16)
    return hi, (x - hi.astype(F32)).astype(BF16)


def dot3(a, b, dims=((1,), (0,))):
    def dot(x, y):
        return lax.dot_general(x, y, (dims, ((), ())), preferred_element_type=F32)

    return dot(a[0], b[0]) + (dot(a[0], b[1]) + dot(a[1], b[0]))


def trig(product, extent):
    n = product - extent * jnp.floor(product * (1.0 / extent) + 0.5)
    quarter = extent / 4.0
    unit = 2.0 * math.pi / extent

    def sine(m):
        u = m * unit
        v = u * u
        s = 1.0 / 6227020800.0
        for term in (-39916800.0, 362880.0, -5040.0, 120.0, -6.0, 1.0):
            s = s * v + 1.0 / term
        return u * s

    folded = jnp.where(
        jnp.abs(n) > quarter, jnp.where(n > 0, 2.0 * quarter, -2.0 * quarter) - n, n
    )
    return sine(quarter - jnp.abs(n)), sine(folded)


def pair(table):
    hi = table.astype(np.float32).astype(ml_dtypes.bfloat16)
    lo = (table - hi.astype(np.float64)).astype(ml_dtypes.bfloat16)
    return hi, lo


@functools.cache
def tables(extent):
    kept = 2 * RADIUS + 1
    rows = up8(kept)
    grid = np.arange(extent)
    freq = np.arange(kept) - RADIUS
    angle = 2.0 * np.pi * ((freq[:, None] * grid[None, :]) % extent) / extent
    cos, sin = np.cos(angle), np.sin(angle)
    pad_q = np.zeros((LANES - kept, extent))
    cq, sq = np.concatenate([cos, pad_q]), np.concatenate([sin, pad_q])
    pad_r = np.zeros((rows - kept, extent))
    cr, sr = np.concatenate([cos, pad_r]), np.concatenate([sin, pad_r])
    x_re = np.concatenate([cq, -sq], axis=0)
    x_im = np.concatenate([sq, cq], axis=0)
    y_fw = np.concatenate(
        [np.concatenate([cr.T, -sr.T], axis=1), np.concatenate([sr.T, cr.T], axis=1)], axis=0
    )
    y_bw = y_fw.T.copy()
    xb_re = x_re.T.copy()
    xb_im = x_im.T.copy()
    out = []
    for table in (x_re, x_im, y_fw, y_bw, xb_re, xb_im):
        out.extend(pair(table))
    return tuple(out)


def params():
    return pltpu.CompilerParams(vmem_limit_bytes=VMEM_LIMIT)


def wave_kernel(extent, me_ref, info_ref, plane_ref, coef_ref, out_ref, kc_ref, len_ref, whi_ref, wlo_ref, sc_ref, ss_ref):
    devices = out_ref.shape[0]
    sticks, _, padded = coef_ref.shape
    padded_planes = plane_ref.shape[1] // devices
    me = me_ref[0]
    length_row = info_ref[0, pl.ds(me, 1), :].astype(F32)
    at_row = info_ref[1, pl.ds(me, 1), :]
    at_col = info_ref[2, pl.ds(me, 1), :]
    at_row = jnp.where(at_row <= RADIUS, at_row, at_row - extent).astype(F32)
    at_col = jnp.where(at_col <= RADIUS, at_col, at_col - extent).astype(F32)
    square_row = at_row * at_row + at_col * at_col
    spare = jnp.ones((1, 2 * LANES - sticks), F32)
    aux = jnp.concatenate(
        [
            jnp.broadcast_to(jnp.concatenate([length_row, spare], axis=1), (LANES // 2, 2 * LANES)),
            jnp.broadcast_to(jnp.concatenate([square_row, spare], axis=1), (LANES // 2, 2 * LANES)),
        ],
        axis=0,
    )
    aux_col = jnp.transpose(aux)[:sticks]
    len_ref[...] = aux_col
    length = aux_col[:, 0:1]
    square = aux_col[:, LANES // 2:LANES // 2 + 1]
    middle = (length - 1.0) * 0.5
    position = lax.broadcasted_iota(jnp.int32, (sticks, padded), 1).astype(F32)
    kept = (position < length).astype(F32)
    kinetic = (square + (position - middle) * (position - middle)) * (1.0 / (RADIUS * RADIUS))
    wave = jnp.concatenate([coef_ref[:, 0, :] * kept, coef_ref[:, 1, :] * kept], axis=1)
    kc_ref[...] = wave * jnp.concatenate([kinetic, kinetic], axis=1)

    total = plane_ref.shape[1]
    plane_row = jnp.broadcast_to(plane_ref[...].astype(F32), (LANES, total))
    plane_col = jnp.transpose(plane_row)[:, 0:1]
    real = (plane_col >= 0.0).astype(F32)
    plane_col = jnp.maximum(plane_col, 0.0)
    harmonic = lax.broadcasted_iota(jnp.int32, (total, padded), 1).astype(F32)
    cos, sin = trig(plane_col * harmonic, extent)
    cos, sin = cos * real, sin * real
    parts = []
    for d in range(devices):
        c = cos[d * padded_planes:(d + 1) * padded_planes]
        s = sin[d * padded_planes:(d + 1) * padded_planes]
        parts.append(jnp.concatenate([c, -s], axis=1))
        parts.append(jnp.concatenate([s, c], axis=1))
    table = split(jnp.concatenate(parts, axis=0))
    whi_ref[...] = table[0]
    wlo_ref[...] = table[1]
    shift_cos, shift_sin = trig(plane_col * ((length_row - 1.0) * 0.5), extent)
    sc_ref[...] = shift_cos
    ss_ref[...] = shift_sin
    raw = dot3(table, split(wave), ((1,), (1,)))
    for d in range(devices):
        at = 2 * d * padded_planes
        re, im = raw[at:at + padded_planes], raw[at + padded_planes:at + 2 * padded_planes]
        c = shift_cos[d * padded_planes:(d + 1) * padded_planes]
        s = shift_sin[d * padded_planes:(d + 1) * padded_planes]
        along_re = re * c + im * s
        along_im = im * c - re * s
        out_ref[d, 0:padded_planes, :] = along_re[:, :LANES]
        out_ref[d, padded_planes:2 * padded_planes, :] = along_im[:, :LANES]
        out_ref[d, 2 * padded_planes:3 * padded_planes, :] = jnp.concatenate(
            [along_re[:, LANES:], along_im[:, LANES:]], axis=1
        )


def window_row(values):
    devices = values.shape[0]
    parts = [values[d:d + 1, :LANES] for d in range(devices)]
    parts += [values[d:d + 1, LANES:] for d in range(devices)]
    return jnp.concatenate(parts, axis=1)


def map_kernel(extent, info_ref, map_ref, first_ref, src_ref, dst_ref, row_ref, col_ref):
    windows = src_ref.shape[0]
    total = windows * LANES

    def signed(part):
        value = info_ref[part]
        return window_row(jnp.where(value <= RADIUS, value, value - extent) + RADIUS)

    def dot(x, y, dims=((1,), (0,))):
        return lax.dot_general(x, y, (dims, ((), ())), preferred_element_type=F32)

    def bits(condition):
        return condition.astype(F32).astype(BF16)

    nt = ((1,), (1,))
    own_row, own_col = signed(1), signed(2)
    tall = lax.broadcasted_iota(jnp.int32, (LANES, total), 0)
    place = lax.broadcasted_iota(jnp.int32, (LANES, total), 1)
    in_col = tall == own_col
    row_hot, col_hot = bits(tall == own_row), bits(in_col)
    down = lax.broadcasted_iota(jnp.int32, (LANES, LANES), 0)
    across = lax.broadcasted_iota(jnp.int32, (LANES, LANES), 1)
    before = bits(down < across)
    after = bits(down > across)
    upto = bits(down >= across)
    ones = jnp.ones((LANES, LANES), BF16)
    taken = dot(row_hot, col_hot, nt)
    taken_t = dot(col_hot, row_hot, nt)
    taken_b, taken_tb = taken.astype(BF16), taken_t.astype(BF16)
    start = dot(dot(after, taken_b).astype(BF16), ones)
    end = start + dot(taken_b, ones)
    start_t = dot(ones, dot(taken_tb, before).astype(BF16))
    limit = windows - 1.0
    first = jnp.minimum(jnp.floor(start * (1.0 / LANES)), limit)
    code = jnp.where(taken > 0.5, dot(taken_b, before) + start - LANES * first, -1.0)
    map_ref[...] = code.astype(jnp.int32)
    first_ref[...] = jnp.minimum(jnp.floor(start_t[0:8] * (1.0 / LANES)), limit).astype(jnp.int32)

    spot = place.astype(F32)
    in_range = (spot >= start[:, 0:1]) & (spot < end[:, 0:1])
    sorted_hot = bits(in_range)
    sorted_row = jnp.sum(jnp.where(in_range, tall, 0).astype(F32), axis=0, keepdims=True)
    sorted_rank = spot[0:1] - jnp.sum(jnp.where(in_range, start[:, 0:1], 0.0), axis=0, keepdims=True)
    counts = dot(dot(upto, taken_tb).astype(BF16), sorted_hot)
    sorted_col = jnp.sum((counts <= sorted_rank).astype(F32), axis=0, keepdims=True)
    names = place + 1
    name_hi = dot(jnp.where(in_col, names >> 6, 0).astype(F32).astype(BF16), row_hot, nt)
    name_lo = dot(jnp.where(in_col, names & 63, 0).astype(F32).astype(BF16), row_hot, nt)
    named = dot(name_hi.astype(BF16), sorted_hot) * 64.0 + dot(name_lo.astype(BF16), sorted_hot)
    source = jnp.sum(jnp.where(tall.astype(F32) == sorted_col, named, 0.0), axis=0, keepdims=True) - 1.0
    place_t = dot(after, taken_tb) + start_t
    place_hi = jnp.floor(place_t * (1.0 / 64.0))
    place_lo = place_t - 64.0 * place_hi
    placed = dot(place_hi.astype(BF16), row_hot) * 64.0 + dot(place_lo.astype(BF16), row_hot)
    target = jnp.sum(jnp.where(in_col, placed, 0.0), axis=0, keepdims=True)
    for values, ref in ((source, src_ref), (target, dst_ref), (sorted_row, row_ref), (sorted_col, col_ref)):
        values = values.astype(jnp.int32)
        for w in range(windows):
            ref[w:w + 1, :] = values[:, w * LANES:(w + 1) * LANES]
    row_ref[windows:windows + 1, :] = jnp.full((1, LANES), -1, jnp.int32)
    col_ref[windows:windows + 1, :] = jnp.zeros((1, LANES), jnp.int32)


def lane_take(x, index):
    return jnp.take_along_axis(x, index, axis=1, mode="promise_in_bounds")


def plane_kernel(
    planes, first_ref, map_ref, src_ref, dst_ref, row_ref, col_ref, recv_ref,
    xr_hi, xr_lo, xi_hi, xi_lo, y_hi, y_lo, yb_hi, yb_lo, br_hi, br_lo, bi_hi, bi_lo,
    pot_hbm, out_ref, x_ref, s_ref, gr_ref, gi_ref, pot_ref, sem,
):
    devices = recv_ref.shape[0]
    padded_planes = recv_ref.shape[1] // 3
    windows = x_ref.shape[0]
    rows = gr_ref.shape[0] // padded_planes
    extent = pot_ref.shape[1]
    half = LANES // 2
    fetch = pltpu.make_async_copy(pot_hbm, pot_ref, sem)
    fetch.start()

    low = lax.broadcasted_iota(jnp.int32, (padded_planes, LANES), 1) < half
    for d in range(devices):
        x_ref[d] = recv_ref[d, 0:2 * padded_planes, :]
    for e in range(devices // 2):
        first = recv_ref[2 * e, 2 * padded_planes:3 * padded_planes, :]
        second = recv_ref[2 * e + 1, 2 * padded_planes:3 * padded_planes, :]
        x_ref[devices + e, 0:padded_planes, :] = jnp.where(low, first, pltpu.roll(second, half, 1))
        x_ref[devices + e, padded_planes:2 * padded_planes, :] = jnp.where(
            low, pltpu.roll(first, half, 1), second
        )

    blocks = padded_planes // 8
    grids = (gr_ref, gi_ref)

    def reorder(order_ref, from_ref, to_ref):
        @pl.loop(0, windows, unroll=4)
        def _(v):
            order = jnp.broadcast_to(order_ref[pl.ds(v, 1), :], (8, LANES))
            index = order & (LANES - 1)
            window = order >> 7
            for j in range(2 * blocks):
                value = jnp.zeros((8, LANES), F32)
                for w in range(windows):
                    value = jnp.where(window == w, lane_take(from_ref[w, 8 * j:8 * j + 8, :], index), value)
                to_ref[v, 8 * j:8 * j + 8, :] = value

    reorder(src_ref, x_ref, s_ref)

    @pl.loop(0, rows, unroll=8)
    def _(r):
        first = first_ref[0, r]
        code = jnp.broadcast_to(map_ref[pl.ds(r, 1), :], (8, LANES))
        index = code & (LANES - 1)
        window = code >> 7
        for j in range(2 * blocks):
            lead = lane_take(s_ref[first, 8 * j:8 * j + 8, :], index)
            trail = lane_take(s_ref[first + 1, 8 * j:8 * j + 8, :], index)
            value = jnp.where(window == 0, lead, jnp.where(window == 1, trail, 0.0))
            part, at = j // blocks, 8 * (j % blocks)
            grids[part][pl.ds(r + at * rows, 8, stride=rows), :] = value

    fetch.wait()
    table_xr = (xr_hi[...], xr_lo[...])
    table_xi = (xi_hi[...], xi_lo[...])
    table_y = (y_hi[...], y_lo[...])
    table_yb = (yb_hi[...], yb_lo[...])
    table_br = (br_hi[...], br_lo[...])
    table_bi = (bi_hi[...], bi_lo[...])

    @pl.loop(0, planes // 2, unroll=3)
    def _(step):
        base = pl.multiple_of(step * 2 * rows, 8)
        pick = pl.ds(base, 2 * rows)
        spectrum = split(jnp.concatenate([gr_ref[pick, :], gi_ref[pick, :]], axis=1))
        a_re = dot3(spectrum, table_xr)
        a_im = dot3(spectrum, table_xi)
        back_re, back_im = [], []
        for t in range(2):
            mid = jnp.concatenate(
                [a_re[t * rows:(t + 1) * rows], a_im[t * rows:(t + 1) * rows]], axis=0
            )
            field = dot3(table_y, split(mid))
            v = pot_ref[2 * step + t]
            weighted = jnp.concatenate([field[:extent] * v, field[extent:] * v], axis=0)
            back = dot3(table_yb, split(weighted))
            back_re.append(back[:rows])
            back_im.append(back[rows:])
        b_re = split(jnp.concatenate(back_re, axis=0))
        b_im = split(jnp.concatenate(back_im, axis=0))
        back = dot3(b_re, table_br) + dot3(b_im, table_bi)
        gr_ref[pick, :] = back[:, :LANES]
        gi_ref[pick, :] = back[:, LANES:]

    @pl.loop(0, rows, unroll=8)
    def _(r):
        first = first_ref[0, r]
        values = []
        for j in range(2 * blocks):
            part, at = j // blocks, 8 * (j % blocks)
            values.append(grids[part][pl.ds(r + at * rows, 8, stride=rows), :])
        for t in range(2):
            index = jnp.broadcast_to(col_ref[pl.ds(first + t, 1), :], (8, LANES))
            hit = jnp.broadcast_to(row_ref[pl.ds(first + t, 1), :], (8, LANES)) == r
            for j in range(2 * blocks):
                pltpu.store(
                    s_ref.at[first + t, 8 * j:8 * j + 8, :], lane_take(values[j], index), mask=hit
                )

    reorder(dst_ref, s_ref, x_ref)
    for w in range(devices):
        out_ref[w, 0:2 * padded_planes, :] = x_ref[w]
    for e in range(devices // 2):
        re = x_ref[devices + e, 0:padded_planes, :]
        im = x_ref[devices + e, padded_planes:2 * padded_planes, :]
        out_ref[2 * e, 2 * padded_planes:3 * padded_planes, :] = jnp.where(
            low, re, pltpu.roll(im, half, 1)
        )
        out_ref[2 * e + 1, 2 * padded_planes:3 * padded_planes, :] = jnp.where(
            low, pltpu.roll(re, half, 1), im
        )
    for d in range(devices):
        out_ref[d, 3 * padded_planes:, :] = jnp.zeros((8, LANES), F32)


def inner_kernel(bands, volume, norm, band_ref, *refs):
    kc_ref = refs[0]
    coefs = refs[1:1 + bands]
    fields = refs[1 + bands:1 + 2 * bands]
    in_ref = refs[1 + 2 * bands]
    out_ref = refs[2 + 2 * bands]
    devices = in_ref.shape[0]
    padded_planes = (in_ref.shape[1] - 8) // 3
    half = LANES // 2
    padded = coefs[0].shape[2]
    me = band_ref[0]
    low = lax.broadcasted_iota(jnp.int32, (padded_planes, LANES), 1) < half

    def fold(x):
        rows = x.shape[0]
        total = x[0:8]
        for at in range(8, rows, 8):
            total = total + x[at:at + 8]
        return total

    kc = kc_ref[...]
    kc_re, kc_im = kc[:, :padded], kc[:, padded:]
    sums = []
    for m in range(bands):
        c_re, c_im = coefs[m][:, 0, :], coefs[m][:, 1, :]
        sums.append([fold(c_re * kc_re + c_im * kc_im), fold(c_re * kc_im - c_im * kc_re)])
    local = [[jnp.zeros((8, LANES), F32), jnp.zeros((8, LANES), F32)] for _ in range(bands)]
    for d in range(devices):
        value = in_ref[d, 0:3 * padded_planes, :]
        re, im, rest = value[:padded_planes], value[padded_planes:2 * padded_planes], value[2 * padded_planes:]
        turned = pltpu.roll(rest, half, 1)
        other = jnp.concatenate([im, -re, jnp.where(low, turned, -turned)], axis=0)
        for m in range(bands):
            col = fields[m][d, 0:3 * padded_planes, :]
            local[m][0] = local[m][0] + fold(col * value)
            local[m][1] = local[m][1] + fold(col * other)
    lane = lax.broadcasted_iota(jnp.int32, (8, LANES), 1)
    row = lax.broadcasted_iota(jnp.int32, (8, LANES), 0)
    tile = jnp.zeros((8, LANES), F32)
    for m in range(bands):
        at = lax.rem(me + m, bands)
        for part, sign in ((0, 1.0), (1, -1.0)):
            partial = sums[m][part] + volume * local[m][part]
            scalar = jnp.sum(jnp.sum(partial, axis=1, keepdims=True), axis=0, keepdims=True)
            tile = jnp.where((lane == at) & (row == part), sign * norm * scalar, tile)
    for d in range(devices):
        out_ref[d, 0:3 * padded_planes, :] = in_ref[d, 0:3 * padded_planes, :]
        out_ref[d, 3 * padded_planes:, :] = tile


def final_kernel(volume, len_ref, ret_ref, kc_ref, whi_ref, wlo_ref, sc_ref, ss_ref, out_ref, sub_ref):
    devices = ret_ref.shape[0]
    padded_planes = (ret_ref.shape[1] - 8) // 3
    sticks, _, padded = out_ref.shape
    half = LANES // 2
    bands = sub_ref.shape[2]
    total = jnp.zeros((8, LANES), F32)
    parts = []
    for d in range(devices):
        value = ret_ref[d]
        total = total + value[3 * padded_planes:]
        rest = value[2 * padded_planes:3 * padded_planes]
        re = jnp.concatenate([value[:padded_planes], rest[:, :half]], axis=1)
        im = jnp.concatenate([value[padded_planes:2 * padded_planes], rest[:, half:]], axis=1)
        c = sc_ref[d * padded_planes:(d + 1) * padded_planes, :]
        s = ss_ref[d * padded_planes:(d + 1) * padded_planes, :]
        parts.append(re * c - im * s)
        parts.append(re * s + im * c)
    stacked = jnp.concatenate(parts, axis=0)
    spare = jnp.zeros((stacked.shape[0], 2 * LANES - sticks), F32)
    turned = jnp.transpose(jnp.concatenate([stacked, spare], axis=1))[:sticks]
    local = dot3(split(turned), (whi_ref[...], wlo_ref[...])) * volume
    position = lax.broadcasted_iota(jnp.int32, (sticks, padded), 1).astype(F32)
    kept = position < len_ref[:, 0:1]
    kc = kc_ref[...]
    out_ref[:, 0, :] = jnp.where(kept, kc[:, :padded] + local[:, :padded], 0.0)
    out_ref[:, 1, :] = jnp.where(kept, kc[:, padded:] + local[:, padded:], 0.0)
    sub_ref[:, 0, :] = total[0:2, :bands]


def shards(bands, devices, coefficients, stick_col, stick_row, stick_length, plane_of_slot, potential):
    extent = plane_of_slot.shape[0]
    sticks = coefficients.shape[1]
    padded = coefficients.shape[3]
    total_sticks = stick_col.shape[0]
    planes = potential.shape[0]
    padded_planes = up8(planes)
    if sticks != LANES + LANES // 2 or devices % 2 or planes % 2:
        raise ValueError("sizes")
    kept = 2 * RADIUS + 1
    rows = up8(kept)
    volume = 1.0 / (extent * extent * extent)
    me = lax.axis_index("tg").astype(jnp.int32)
    coef = coefficients.reshape(sticks, 2, padded)

    info = jnp.stack([stick_length, stick_row, stick_col]).reshape(3, devices, sticks)
    slots = plane_of_slot.reshape(devices, planes)
    if padded_planes > planes:
        slots = jnp.pad(slots, ((0, 0), (0, padded_planes - planes)), constant_values=-1)
    slots = slots.reshape(1, devices * padded_planes)
    windows = total_sticks // LANES
    smem = pl.BlockSpec(memory_space=pltpu.SMEM)
    vmem = pl.BlockSpec(memory_space=pltpu.VMEM)

    block = 3 * padded_planes
    total_planes = devices * padded_planes
    sent, kc, lengths, whi, wlo, shift_cos, shift_sin = pl.pallas_call(
        functools.partial(wave_kernel, extent),
        out_shape=(
            jax.ShapeDtypeStruct((devices, block, LANES), F32),
            jax.ShapeDtypeStruct((sticks, 2 * padded), F32),
            jax.ShapeDtypeStruct((sticks, LANES), F32),
            jax.ShapeDtypeStruct((2 * total_planes, 2 * padded), BF16),
            jax.ShapeDtypeStruct((2 * total_planes, 2 * padded), BF16),
            jax.ShapeDtypeStruct((total_planes, sticks), F32),
            jax.ShapeDtypeStruct((total_planes, sticks), F32),
        ),
        in_specs=[smem] + [vmem] * 3,
        compiler_params=params(),
        name="wave_to_planes",
    )(me.reshape(1), info, slots, coef)

    received = lax.all_to_all(sent, "tg", split_axis=0, concat_axis=0, tiled=True)

    window_list = jax.ShapeDtypeStruct((windows, LANES), jnp.int32)
    longer_list = jax.ShapeDtypeStruct((windows + 1, LANES), jnp.int32)
    stick_map, first, source, target, row_w, col_w = pl.pallas_call(
        functools.partial(map_kernel, extent),
        out_shape=(
            jax.ShapeDtypeStruct((LANES, LANES), jnp.int32),
            jax.ShapeDtypeStruct((8, LANES), jnp.int32),
            window_list,
            window_list,
            longer_list,
            longer_list,
        ),
        compiler_params=params(),
        name="stick_map",
    )(info)

    weighted = pl.pallas_call(
        functools.partial(plane_kernel, planes),
        out_shape=jax.ShapeDtypeStruct((devices, block + 8, LANES), F32),
        in_specs=[smem] + [vmem] * 18 + [pl.BlockSpec(memory_space=pl.ANY)],
        out_specs=vmem,
        scratch_shapes=[
            pltpu.VMEM((windows, 2 * padded_planes, LANES), F32),
            pltpu.VMEM((windows + 1, 2 * padded_planes, LANES), F32),
            pltpu.VMEM((padded_planes * rows, LANES), F32),
            pltpu.VMEM((padded_planes * rows, LANES), F32),
            pltpu.VMEM(potential.shape, F32),
            pltpu.SemaphoreType.DMA,
        ],
        compiler_params=params(),
        name="planes",
    )(first, stick_map, source, target, row_w, col_w, received, *[jnp.asarray(t) for t in tables(extent)], potential)

    coefs, fields = [coef], [received]
    for shift in range(1, bands):
        ring = [((b + shift) % bands, b) for b in range(bands)]
        coefs.append(lax.ppermute(coef, "band", ring))
        fields.append(lax.ppermute(received, "band", ring))
    band = lax.axis_index("band").astype(jnp.int32).reshape(1)
    norm = 1.0 / (total_sticks * padded)
    outgoing = pl.pallas_call(
        functools.partial(inner_kernel, bands, volume, norm),
        out_shape=jax.ShapeDtypeStruct((devices, block + 8, LANES), F32),
        in_specs=[pl.BlockSpec(memory_space=pltpu.SMEM)] + [vmem] * (2 + 2 * bands),
        out_specs=vmem,
        compiler_params=params(),
        name="inner",
    )(band, kc, *coefs, *fields, weighted)

    returned = lax.all_to_all(outgoing, "tg", split_axis=0, concat_axis=0, tiled=True)
    applied, subspace = pl.pallas_call(
        functools.partial(final_kernel, volume),
        out_shape=(
            jax.ShapeDtypeStruct((sticks, 2, padded), F32),
            jax.ShapeDtypeStruct((2, 1, bands), F32),
        ),
        compiler_params=params(),
        name="planes_to_wave",
    )(lengths, returned, kc, whi, wlo, shift_cos, shift_sin)
    return applied.reshape(1, sticks, 2, padded), subspace


def solution(mesh):
    in_specs = (P("band", "tg", None, None), P(), P(), P(), P(), P("tg", None, None))
    out_specs = (P("band", "tg", None, None), P(None, "band", None))
    body = functools.partial(shards, mesh.shape["band"], mesh.shape["tg"])
    return jax.shard_map(body, mesh=mesh, in_specs=in_specs, out_specs=out_specs, check_vma=False)
```

```python
import functools
import math

import jax
import jax.numpy as jnp
import ml_dtypes
import numpy as np
from jax import lax
from jax.experimental import pallas as pl
from jax.experimental.pallas import tpu as pltpu
from jax.sharding import PartitionSpec as P

RADIUS = 48
LANES = 128
F32 = jnp.float32
BF16 = jnp.bfloat16
VMEM_LIMIT = 56 * 1024 * 1024


def up8(n):
    return -(-n // 8) * 8


def split(x):
    hi = x.astype(BF16)
    return hi, (x - hi.astype(F32)).astype(BF16)


def dot3(a, b, dims=((1,), (0,))):
    def dot(x, y):
        return lax.dot_general(x, y, (dims, ((), ())), preferred_element_type=F32)

    return dot(a[0], b[0]) + (dot(a[0], b[1]) + dot(a[1], b[0]))


def trig(product, extent):
    n = product - extent * jnp.floor(product * (1.0 / extent) + 0.5)
    quarter = extent / 4.0
    unit = 2.0 * math.pi / extent

    def sine(m):
        u = m * unit
        v = u * u
        s = 1.0 / 6227020800.0
        for term in (-39916800.0, 362880.0, -5040.0, 120.0, -6.0, 1.0):
            s = s * v + 1.0 / term
        return u * s

    folded = jnp.where(
        jnp.abs(n) > quarter, jnp.where(n > 0, 2.0 * quarter, -2.0 * quarter) - n, n
    )
    return sine(quarter - jnp.abs(n)), sine(folded)


def pair(table):
    hi = table.astype(np.float32).astype(ml_dtypes.bfloat16)
    lo = (table - hi.astype(np.float64)).astype(ml_dtypes.bfloat16)
    return hi, lo


def row_blocks():
    even = -(-(RADIUS + 1) // 16) * 16
    odd = -(-RADIUS // 16) * 16
    return even, odd


@functools.cache
def tables(extent):
    kept = 2 * RADIUS + 1
    half = extent // 2
    grid = np.arange(extent)
    freq = np.arange(kept) - RADIUS

    def angles(f, g):
        a = 2.0 * np.pi * ((f[:, None] * g[None, :]) % extent) / extent
        return np.cos(a), np.sin(a)

    cos, sin = angles(freq, grid)
    wide = 2 * LANES
    x_table = np.zeros((wide, 2 * wide))
    x_table[:kept, :extent] = cos
    x_table[LANES:LANES + kept, :extent] = -sin
    x_table[:kept, wide:wide + extent] = sin
    x_table[LANES:LANES + kept, wide:wide + extent] = cos
    forward, back = [], []
    for offset, rows in zip((0, 1), row_blocks()):
        cos, sin = angles(freq[offset::2], grid[:half])
        count = cos.shape[0]
        table = np.zeros((2 * half, rows))
        table[:half, :count] = cos.T
        table[half:, :count] = sin.T
        hi, lo = pair(table)
        forward.append(np.concatenate([hi, hi, lo], axis=1))
        table = np.zeros((2 * rows, half))
        table[:count] = cos
        table[rows:rows + count] = sin
        hi, lo = pair(table)
        back.append(np.concatenate([hi, hi, lo], axis=1))
    hi, lo = pair(x_table)
    x_forward = np.concatenate([hi, hi, lo], axis=0)
    hi, lo = pair(x_table.T.copy())
    x_back = np.concatenate([hi, hi, lo], axis=0)
    return (*forward, x_forward, x_back, *back)


def params():
    return pltpu.CompilerParams(vmem_limit_bytes=VMEM_LIMIT)


def cost(flops, nbytes):
    return pl.CostEstimate(flops=int(flops), bytes_accessed=int(nbytes), transcendentals=0)


def wave_kernel(extent, me_ref, info_ref, plane_ref, coef_ref, out_ref, kc_ref, len_ref, whi_ref, wlo_ref, sc_ref, ss_ref):
    devices = out_ref.shape[0]
    sticks, _, padded = coef_ref.shape
    padded_planes = plane_ref.shape[1] // devices
    me = me_ref[0]
    length_row = info_ref[0, pl.ds(me, 1), :].astype(F32)
    at_row = info_ref[1, pl.ds(me, 1), :]
    at_col = info_ref[2, pl.ds(me, 1), :]
    at_row = jnp.where(at_row <= RADIUS, at_row, at_row - extent).astype(F32)
    at_col = jnp.where(at_col <= RADIUS, at_col, at_col - extent).astype(F32)
    square_row = at_row * at_row + at_col * at_col
    spare = jnp.ones((1, 2 * LANES - sticks), F32)
    aux = jnp.concatenate(
        [
            jnp.broadcast_to(jnp.concatenate([length_row, spare], axis=1), (LANES // 2, 2 * LANES)),
            jnp.broadcast_to(jnp.concatenate([square_row, spare], axis=1), (LANES // 2, 2 * LANES)),
        ],
        axis=0,
    )
    aux_col = jnp.transpose(aux)[:sticks]
    len_ref[...] = aux_col
    length = aux_col[:, 0:1]
    square = aux_col[:, LANES // 2:LANES // 2 + 1]
    middle = (length - 1.0) * 0.5
    position = lax.broadcasted_iota(jnp.int32, (sticks, padded), 1).astype(F32)
    kept = (position < length).astype(F32)
    kinetic = (square + (position - middle) * (position - middle)) * (1.0 / (RADIUS * RADIUS))
    wave = jnp.concatenate([coef_ref[:, 0, :] * kept, coef_ref[:, 1, :] * kept], axis=1)
    kc_ref[...] = wave * jnp.concatenate([kinetic, kinetic], axis=1)

    total = plane_ref.shape[1]
    plane_row = jnp.broadcast_to(plane_ref[...].astype(F32), (LANES, total))
    plane_col = jnp.transpose(plane_row)[:, 0:1]
    real = (plane_col >= 0.0).astype(F32)
    plane_col = jnp.maximum(plane_col, 0.0)
    harmonic = lax.broadcasted_iota(jnp.int32, (total, padded), 1).astype(F32)
    cos, sin = trig(plane_col * harmonic, extent)
    cos, sin = cos * real, sin * real
    parts = []
    for d in range(devices):
        c = cos[d * padded_planes:(d + 1) * padded_planes]
        s = sin[d * padded_planes:(d + 1) * padded_planes]
        parts.append(jnp.concatenate([c, -s], axis=1))
        parts.append(jnp.concatenate([s, c], axis=1))
    table = split(jnp.concatenate(parts, axis=0))
    whi_ref[...] = table[0]
    wlo_ref[...] = table[1]
    shift_cos, shift_sin = trig(plane_col * ((length_row - 1.0) * 0.5), extent)
    sc_ref[...] = shift_cos
    ss_ref[...] = shift_sin
    raw = dot3(table, split(wave), ((1,), (1,)))
    for d in range(devices):
        at = 2 * d * padded_planes
        re, im = raw[at:at + padded_planes], raw[at + padded_planes:at + 2 * padded_planes]
        c = shift_cos[d * padded_planes:(d + 1) * padded_planes]
        s = shift_sin[d * padded_planes:(d + 1) * padded_planes]
        along_re = re * c + im * s
        along_im = im * c - re * s
        out_ref[d, 0:padded_planes, :] = along_re[:, :LANES]
        out_ref[d, padded_planes:2 * padded_planes, :] = along_im[:, :LANES]
        out_ref[d, 2 * padded_planes:3 * padded_planes, :] = jnp.concatenate(
            [along_re[:, LANES:], along_im[:, LANES:]], axis=1
        )


def window_row(values):
    devices = values.shape[0]
    parts = [values[d:d + 1, :LANES] for d in range(devices)]
    parts += [values[d:d + 1, LANES:] for d in range(devices)]
    return jnp.concatenate(parts, axis=1)


def map_kernel(extent, info_ref, map_ref, first_ref, src_ref, dst_ref, row_ref, col_ref):
    windows = src_ref.shape[0]
    total = windows * LANES

    def signed(part):
        value = info_ref[part]
        return window_row(jnp.where(value <= RADIUS, value, value - extent) + RADIUS)

    def dot(x, y, dims=((1,), (0,))):
        return lax.dot_general(x, y, (dims, ((), ())), preferred_element_type=F32)

    def bits(condition):
        return condition.astype(F32).astype(BF16)

    nt = ((1,), (1,))
    own_row, own_col = signed(1), signed(2)
    own_row = (own_row & 1) * row_blocks()[0] + (own_row >> 1)
    tall = lax.broadcasted_iota(jnp.int32, (LANES, total), 0)
    place = lax.broadcasted_iota(jnp.int32, (LANES, total), 1)
    in_col = tall == own_col
    row_hot, col_hot = bits(tall == own_row), bits(in_col)
    down = lax.broadcasted_iota(jnp.int32, (LANES, LANES), 0)
    across = lax.broadcasted_iota(jnp.int32, (LANES, LANES), 1)
    before = bits(down < across)
    after = bits(down > across)
    upto = bits(down >= across)
    ones = jnp.ones((LANES, LANES), BF16)
    taken = dot(row_hot, col_hot, nt)
    taken_t = dot(col_hot, row_hot, nt)
    taken_b, taken_tb = taken.astype(BF16), taken_t.astype(BF16)
    start = dot(dot(after, taken_b).astype(BF16), ones)
    end = start + dot(taken_b, ones)
    start_t = dot(ones, dot(taken_tb, before).astype(BF16))
    limit = windows - 1.0
    first = jnp.minimum(jnp.floor(start * (1.0 / LANES)), limit)
    code = jnp.where(taken > 0.5, dot(taken_b, before) + start - LANES * first, -1.0)
    map_ref[...] = code.astype(jnp.int32)
    first_ref[...] = jnp.minimum(jnp.floor(start_t[0:8] * (1.0 / LANES)), limit).astype(jnp.int32)

    spot = place.astype(F32)
    in_range = (spot >= start[:, 0:1]) & (spot < end[:, 0:1])
    sorted_hot = bits(in_range)
    sorted_row = jnp.sum(jnp.where(in_range, tall, 0).astype(F32), axis=0, keepdims=True)
    sorted_rank = spot[0:1] - jnp.sum(jnp.where(in_range, start[:, 0:1], 0.0), axis=0, keepdims=True)
    counts = dot(dot(upto, taken_tb).astype(BF16), sorted_hot)
    sorted_col = jnp.sum((counts <= sorted_rank).astype(F32), axis=0, keepdims=True)
    names = place + 1
    name_hi = dot(jnp.where(in_col, names >> 6, 0).astype(F32).astype(BF16), row_hot, nt)
    name_lo = dot(jnp.where(in_col, names & 63, 0).astype(F32).astype(BF16), row_hot, nt)
    named = dot(name_hi.astype(BF16), sorted_hot) * 64.0 + dot(name_lo.astype(BF16), sorted_hot)
    source = jnp.sum(jnp.where(tall.astype(F32) == sorted_col, named, 0.0), axis=0, keepdims=True) - 1.0
    place_t = dot(after, taken_tb) + start_t
    place_hi = jnp.floor(place_t * (1.0 / 64.0))
    place_lo = place_t - 64.0 * place_hi
    placed = dot(place_hi.astype(BF16), row_hot) * 64.0 + dot(place_lo.astype(BF16), row_hot)
    target = jnp.sum(jnp.where(in_col, placed, 0.0), axis=0, keepdims=True)
    for values, ref in ((source, src_ref), (target, dst_ref), (sorted_row, row_ref), (sorted_col, col_ref)):
        values = values.astype(jnp.int32)
        for w in range(windows):
            ref[w:w + 1, :] = values[:, w * LANES:(w + 1) * LANES]
    row_ref[windows:windows + 1, :] = jnp.full((1, LANES), -1, jnp.int32)
    col_ref[windows:windows + 1, :] = jnp.zeros((1, LANES), jnp.int32)


def lane_take(x, index):
    return jnp.take_along_axis(x, index, axis=1, mode="promise_in_bounds")


def plane_kernel(
    planes, first_ref, map_ref, src_ref, dst_ref, row_ref, col_ref, recv_ref,
    y_even, y_odd, x_forward, x_back, back_even, back_odd,
    pot_hbm, out_ref, x_ref, s_ref, gr_ref, gi_ref, pot_ref, sem,
):
    devices = recv_ref.shape[0]
    padded_planes = recv_ref.shape[1] // 3
    windows = x_ref.shape[0]
    rows = gr_ref.shape[0] // padded_planes
    extent = pot_ref.shape[1]
    half = LANES // 2
    fetch = pltpu.make_async_copy(pot_hbm, pot_ref, sem)
    fetch.start()

    low = lax.broadcasted_iota(jnp.int32, (padded_planes, LANES), 1) < half
    for d in range(devices):
        x_ref[d] = recv_ref[d, 0:2 * padded_planes, :]
    for e in range(devices // 2):
        first = recv_ref[2 * e, 2 * padded_planes:3 * padded_planes, :]
        second = recv_ref[2 * e + 1, 2 * padded_planes:3 * padded_planes, :]
        x_ref[devices + e, 0:padded_planes, :] = jnp.where(low, first, pltpu.roll(second, half, 1))
        x_ref[devices + e, padded_planes:2 * padded_planes, :] = jnp.where(
            low, pltpu.roll(first, half, 1), second
        )

    blocks = padded_planes // 8
    grids = (gr_ref, gi_ref)

    def reorder(order_ref, from_ref, to_ref):
        @pl.loop(0, windows, unroll=4)
        def _(v):
            order = jnp.broadcast_to(order_ref[pl.ds(v, 1), :], (8, LANES))
            index = order & (LANES - 1)
            window = order >> 7
            for j in range(2 * blocks):
                value = jnp.zeros((8, LANES), F32)
                for w in range(windows):
                    value = jnp.where(window == w, lane_take(from_ref[w, 8 * j:8 * j + 8, :], index), value)
                to_ref[v, 8 * j:8 * j + 8, :] = value

    reorder(src_ref, x_ref, s_ref)

    @pl.loop(0, rows, unroll=8)
    def _(r):
        first = first_ref[0, r]
        code = jnp.broadcast_to(map_ref[pl.ds(r, 1), :], (8, LANES))
        index = code & (LANES - 1)
        window = code >> 7
        for j in range(2 * blocks):
            lead = lane_take(s_ref[first, 8 * j:8 * j + 8, :], index)
            trail = lane_take(s_ref[first + 1, 8 * j:8 * j + 8, :], index)
            value = jnp.where(window == 0, lead, jnp.where(window == 1, trail, 0.0))
            part, at = j // blocks, 8 * (j % blocks)
            grids[part][pl.ds(r + at * rows, 8, stride=rows), :] = value

    fetch.wait()
    even_rows, odd_rows = row_blocks()
    folded = extent // 2
    group = 4 if planes % 4 == 0 else 2

    def dot(x, y):
        return jnp.dot(x, y, preferred_element_type=F32)

    def stack(x, axis):
        hi, lo = split(x)
        return jnp.concatenate([hi, lo, hi], axis=axis)

    def times_wave(both, cut, sign):
        cos, sin = both[:cut], both[cut:]
        re = cos[:, :LANES] - sign * sin[:, LANES:]
        im = cos[:, LANES:] + sign * sin[:, :LANES]
        return re, im

    @pl.loop(0, planes // group)
    def _(step):
        lines = []
        for t in range(group):
            base = pl.multiple_of((step * group + t) * rows, 16)
            even, odd = pl.ds(base, even_rows), pl.ds(base + even_rows, odd_rows)
            parts = []
            for pick, table, size in ((even, y_even, even_rows), (odd, y_odd, odd_rows)):
                spectrum = jnp.concatenate([gr_ref[pick, :], gi_ref[pick, :]], axis=1)
                parts.append(times_wave(dot(table[...], stack(spectrum, 0)), folded, 1.0))
            (e_re, e_im), (o_re, o_im) = parts
            lines.append(jnp.concatenate([e_re + o_re, e_im + o_im], axis=1))
            lines.append(jnp.concatenate([e_re - o_re, e_im - o_im], axis=1))
        field = dot(stack(jnp.concatenate(lines, axis=0), 1), x_forward[...])
        wide = field.shape[1] // 2
        spare = jnp.zeros((extent, wide - extent), F32)
        weighted = []
        for t in range(group):
            v = jnp.concatenate([pot_ref[step * group + t], spare], axis=1)
            mine = field[t * extent:(t + 1) * extent]
            weighted.append(jnp.concatenate([mine[:, :wide] * v, mine[:, wide:] * v], axis=1))
        back = dot(stack(jnp.concatenate(weighted, axis=0), 1), x_back[...])
        for t in range(group):
            base = pl.multiple_of((step * group + t) * rows, 16)
            even, odd = pl.ds(base, even_rows), pl.ds(base + even_rows, odd_rows)
            upper = back[t * extent:t * extent + folded]
            lower = back[t * extent + folded:(t + 1) * extent]
            for pick, table, size, value in (
                (even, back_even, even_rows, upper + lower), (odd, back_odd, odd_rows, upper - lower)
            ):
                re, im = times_wave(dot(table[...], stack(value, 0)), size, -1.0)
                gr_ref[pick, :] = re
                gi_ref[pick, :] = im

    @pl.loop(0, rows, unroll=8)
    def _(r):
        first = first_ref[0, r]
        values = []
        for j in range(2 * blocks):
            part, at = j // blocks, 8 * (j % blocks)
            values.append(grids[part][pl.ds(r + at * rows, 8, stride=rows), :])
        for t in range(2):
            index = jnp.broadcast_to(col_ref[pl.ds(first + t, 1), :], (8, LANES))
            hit = jnp.broadcast_to(row_ref[pl.ds(first + t, 1), :], (8, LANES)) == r
            for j in range(2 * blocks):
                pltpu.store(
                    s_ref.at[first + t, 8 * j:8 * j + 8, :], lane_take(values[j], index), mask=hit
                )

    reorder(dst_ref, s_ref, x_ref)
    for w in range(devices):
        out_ref[w, 0:2 * padded_planes, :] = x_ref[w]
    for e in range(devices // 2):
        re = x_ref[devices + e, 0:padded_planes, :]
        im = x_ref[devices + e, padded_planes:2 * padded_planes, :]
        out_ref[2 * e, 2 * padded_planes:3 * padded_planes, :] = jnp.where(
            low, re, pltpu.roll(im, half, 1)
        )
        out_ref[2 * e + 1, 2 * padded_planes:3 * padded_planes, :] = jnp.where(
            low, pltpu.roll(re, half, 1), im
        )
    for d in range(devices):
        out_ref[d, 3 * padded_planes:, :] = jnp.zeros((8, LANES), F32)


def inner_kernel(bands, volume, norm, band_ref, *refs):
    kc_ref = refs[0]
    coefs = refs[1:1 + bands]
    fields = refs[1 + bands:1 + 2 * bands]
    in_ref = refs[1 + 2 * bands]
    out_ref = refs[2 + 2 * bands]
    devices = in_ref.shape[0]
    padded_planes = (in_ref.shape[1] - 8) // 3
    half = LANES // 2
    padded = coefs[0].shape[2]
    me = band_ref[0]
    low = lax.broadcasted_iota(jnp.int32, (padded_planes, LANES), 1) < half

    def fold(x):
        rows = x.shape[0]
        total = x[0:8]
        for at in range(8, rows, 8):
            total = total + x[at:at + 8]
        return total

    kc = kc_ref[...]
    kc_re, kc_im = kc[:, :padded], kc[:, padded:]
    sums = []
    for m in range(bands):
        c_re, c_im = coefs[m][:, 0, :], coefs[m][:, 1, :]
        sums.append([fold(c_re * kc_re + c_im * kc_im), fold(c_re * kc_im - c_im * kc_re)])
    local = [[jnp.zeros((8, LANES), F32), jnp.zeros((8, LANES), F32)] for _ in range(bands)]
    for d in range(devices):
        value = in_ref[d, 0:3 * padded_planes, :]
        re, im, rest = value[:padded_planes], value[padded_planes:2 * padded_planes], value[2 * padded_planes:]
        turned = pltpu.roll(rest, half, 1)
        other = jnp.concatenate([im, -re, jnp.where(low, turned, -turned)], axis=0)
        for m in range(bands):
            col = fields[m][d, 0:3 * padded_planes, :]
            local[m][0] = local[m][0] + fold(col * value)
            local[m][1] = local[m][1] + fold(col * other)
    lane = lax.broadcasted_iota(jnp.int32, (8, LANES), 1)
    row = lax.broadcasted_iota(jnp.int32, (8, LANES), 0)
    tile = jnp.zeros((8, LANES), F32)
    for m in range(bands):
        at = lax.rem(me + m, bands)
        for part, sign in ((0, 1.0), (1, -1.0)):
            partial = sums[m][part] + volume * local[m][part]
            scalar = jnp.sum(jnp.sum(partial, axis=1, keepdims=True), axis=0, keepdims=True)
            tile = jnp.where((lane == at) & (row == part), sign * norm * scalar, tile)
    for d in range(devices):
        out_ref[d, 0:3 * padded_planes, :] = in_ref[d, 0:3 * padded_planes, :]
        out_ref[d, 3 * padded_planes:, :] = tile


def final_kernel(volume, len_ref, ret_ref, kc_ref, whi_ref, wlo_ref, sc_ref, ss_ref, out_ref, sub_ref):
    devices = ret_ref.shape[0]
    padded_planes = (ret_ref.shape[1] - 8) // 3
    sticks, _, padded = out_ref.shape
    half = LANES // 2
    bands = sub_ref.shape[2]
    total = jnp.zeros((8, LANES), F32)
    parts = []
    for d in range(devices):
        value = ret_ref[d]
        total = total + value[3 * padded_planes:]
        rest = value[2 * padded_planes:3 * padded_planes]
        re = jnp.concatenate([value[:padded_planes], rest[:, :half]], axis=1)
        im = jnp.concatenate([value[padded_planes:2 * padded_planes], rest[:, half:]], axis=1)
        c = sc_ref[d * padded_planes:(d + 1) * padded_planes, :]
        s = ss_ref[d * padded_planes:(d + 1) * padded_planes, :]
        parts.append(re * c - im * s)
        parts.append(re * s + im * c)
    stacked = jnp.concatenate(parts, axis=0)
    spare = jnp.zeros((stacked.shape[0], 2 * LANES - sticks), F32)
    turned = jnp.transpose(jnp.concatenate([stacked, spare], axis=1))[:sticks]
    local = dot3(split(turned), (whi_ref[...], wlo_ref[...])) * volume
    position = lax.broadcasted_iota(jnp.int32, (sticks, padded), 1).astype(F32)
    kept = position < len_ref[:, 0:1]
    kc = kc_ref[...]
    out_ref[:, 0, :] = jnp.where(kept, kc[:, :padded] + local[:, :padded], 0.0)
    out_ref[:, 1, :] = jnp.where(kept, kc[:, padded:] + local[:, padded:], 0.0)
    sub_ref[:, 0, :] = total[0:2, :bands]


def shards(bands, devices, coefficients, stick_col, stick_row, stick_length, plane_of_slot, potential):
    extent = plane_of_slot.shape[0]
    sticks = coefficients.shape[1]
    padded = coefficients.shape[3]
    total_sticks = stick_col.shape[0]
    planes = potential.shape[0]
    padded_planes = up8(planes)
    if sticks != LANES + LANES // 2 or devices % 2 or planes % 2:
        raise ValueError("sizes")
    rows = sum(row_blocks())
    volume = 1.0 / (extent * extent * extent)
    me = lax.axis_index("tg").astype(jnp.int32)
    coef = coefficients.reshape(sticks, 2, padded)

    info = jnp.stack([stick_length, stick_row, stick_col]).reshape(3, devices, sticks)
    slots = plane_of_slot.reshape(devices, planes)
    if padded_planes > planes:
        slots = jnp.pad(slots, ((0, 0), (0, padded_planes - planes)), constant_values=-1)
    slots = slots.reshape(1, devices * padded_planes)
    windows = total_sticks // LANES
    smem = pl.BlockSpec(memory_space=pltpu.SMEM)
    vmem = pl.BlockSpec(memory_space=pltpu.VMEM)

    block = 3 * padded_planes
    total_planes = devices * padded_planes
    sent, kc, lengths, whi, wlo, shift_cos, shift_sin = pl.pallas_call(
        functools.partial(wave_kernel, extent),
        out_shape=(
            jax.ShapeDtypeStruct((devices, block, LANES), F32),
            jax.ShapeDtypeStruct((sticks, 2 * padded), F32),
            jax.ShapeDtypeStruct((sticks, LANES), F32),
            jax.ShapeDtypeStruct((2 * total_planes, 2 * padded), BF16),
            jax.ShapeDtypeStruct((2 * total_planes, 2 * padded), BF16),
            jax.ShapeDtypeStruct((total_planes, sticks), F32),
            jax.ShapeDtypeStruct((total_planes, sticks), F32),
        ),
        in_specs=[smem] + [vmem] * 3,
        compiler_params=params(),
        name="wave_to_planes",
    )(me.reshape(1), info, slots, coef)

    received = lax.all_to_all(sent, "tg", split_axis=0, concat_axis=0, tiled=True)

    window_list = jax.ShapeDtypeStruct((windows, LANES), jnp.int32)
    longer_list = jax.ShapeDtypeStruct((windows + 1, LANES), jnp.int32)
    stick_map, first, source, target, row_w, col_w = pl.pallas_call(
        functools.partial(map_kernel, extent),
        out_shape=(
            jax.ShapeDtypeStruct((LANES, LANES), jnp.int32),
            jax.ShapeDtypeStruct((8, LANES), jnp.int32),
            window_list,
            window_list,
            longer_list,
            longer_list,
        ),
        compiler_params=params(),
        cost_estimate=cost(4e9, 1e5),
        name="stick_map",
    )(info)

    weighted = pl.pallas_call(
        functools.partial(plane_kernel, planes),
        out_shape=jax.ShapeDtypeStruct((devices, block + 8, LANES), F32),
        in_specs=[smem] + [vmem] * 12 + [pl.BlockSpec(memory_space=pl.ANY)],
        out_specs=vmem,
        scratch_shapes=[
            pltpu.VMEM((windows, 2 * padded_planes, LANES), F32),
            pltpu.VMEM((windows + 1, 2 * padded_planes, LANES), F32),
            pltpu.VMEM((padded_planes * rows, LANES), F32),
            pltpu.VMEM((padded_planes * rows, LANES), F32),
            pltpu.VMEM(potential.shape, F32),
            pltpu.SemaphoreType.DMA,
        ],
        compiler_params=params(),
        cost_estimate=cost(2e10, 1e7),
        name="planes",
    )(first, stick_map, source, target, row_w, col_w, received, *[jnp.asarray(t) for t in tables(extent)], potential)

    coefs, fields = [coef], [received]
    for shift in range(1, bands):
        ring = [((b + shift) % bands, b) for b in range(bands)]
        coefs.append(lax.ppermute(coef, "band", ring))
        fields.append(lax.ppermute(received, "band", ring))
    band = lax.axis_index("band").astype(jnp.int32).reshape(1)
    norm = 1.0 / (total_sticks * padded)
    outgoing = pl.pallas_call(
        functools.partial(inner_kernel, bands, volume, norm),
        out_shape=jax.ShapeDtypeStruct((devices, block + 8, LANES), F32),
        in_specs=[pl.BlockSpec(memory_space=pltpu.SMEM)] + [vmem] * (2 + 2 * bands),
        out_specs=vmem,
        compiler_params=params(),
        name="inner",
    )(band, kc, *coefs, *fields, weighted)

    returned = lax.all_to_all(outgoing, "tg", split_axis=0, concat_axis=0, tiled=True)
    applied, subspace = pl.pallas_call(
        functools.partial(final_kernel, volume),
        out_shape=(
            jax.ShapeDtypeStruct((sticks, 2, padded), F32),
            jax.ShapeDtypeStruct((2, 1, bands), F32),
        ),
        compiler_params=params(),
        name="planes_to_wave",
    )(lengths, returned, kc, whi, wlo, shift_cos, shift_sin)
    return applied.reshape(1, sticks, 2, padded), subspace


def solution(mesh):
    in_specs = (P("band", "tg", None, None), P(), P(), P(), P(), P("tg", None, None))
    out_specs = (P("band", "tg", None, None), P(None, "band", None))
    body = functools.partial(shards, mesh.shape["band"], mesh.shape["tg"])
    return jax.shard_map(body, mesh=mesh, in_specs=in_specs, out_specs=out_specs, check_vma=False)
```

```python
import functools
import math

import jax
import jax.numpy as jnp
import ml_dtypes
import numpy as np
from jax import lax
from jax.experimental import pallas as pl
from jax.experimental.pallas import tpu as pltpu
from jax.sharding import PartitionSpec as P

RADIUS = 48
LANES = 128
F32 = jnp.float32
BF16 = jnp.bfloat16
VMEM_LIMIT = 56 * 1024 * 1024


def up8(n):
    return -(-n // 8) * 8


def split(x):
    hi = x.astype(BF16)
    return hi, (x - hi.astype(F32)).astype(BF16)


def dot3(a, b, dims=((1,), (0,))):
    def dot(x, y):
        return lax.dot_general(x, y, (dims, ((), ())), preferred_element_type=F32)

    return dot(a[0], b[0]) + (dot(a[0], b[1]) + dot(a[1], b[0]))


def trig(product, extent):
    n = product - extent * jnp.floor(product * (1.0 / extent) + 0.5)
    quarter = extent / 4.0
    unit = 2.0 * math.pi / extent

    def sine(m):
        u = m * unit
        v = u * u
        s = 1.0 / 6227020800.0
        for term in (-39916800.0, 362880.0, -5040.0, 120.0, -6.0, 1.0):
            s = s * v + 1.0 / term
        return u * s

    folded = jnp.where(
        jnp.abs(n) > quarter, jnp.where(n > 0, 2.0 * quarter, -2.0 * quarter) - n, n
    )
    return sine(quarter - jnp.abs(n)), sine(folded)


def pair(table):
    hi = table.astype(np.float32).astype(ml_dtypes.bfloat16)
    lo = (table - hi.astype(np.float64)).astype(ml_dtypes.bfloat16)
    return hi, lo


def row_blocks():
    even = -(-(RADIUS + 1) // 16) * 16
    odd = -(-RADIUS // 16) * 16
    return even, odd


@functools.cache
def tables(extent):
    kept = 2 * RADIUS + 1
    half = extent // 2
    grid = np.arange(extent)
    freq = np.arange(kept) - RADIUS

    def angles(f, g):
        a = 2.0 * np.pi * ((f[:, None] * g[None, :]) % extent) / extent
        return np.cos(a), np.sin(a)

    cos, sin = angles(freq, grid)
    wide = 2 * LANES
    x_table = np.zeros((wide, 2 * wide))
    x_table[:kept, :extent] = cos
    x_table[LANES:LANES + kept, :extent] = -sin
    x_table[:kept, wide:wide + extent] = sin
    x_table[LANES:LANES + kept, wide:wide + extent] = cos
    forward, back = [], []
    for offset, rows in zip((0, 1), row_blocks()):
        cos, sin = angles(freq[offset::2], grid[:half])
        count = cos.shape[0]
        table = np.zeros((2 * half, rows))
        table[:half, :count] = cos.T
        table[half:, :count] = sin.T
        hi, lo = pair(table)
        forward.append(np.concatenate([hi, hi, lo], axis=1))
        table = np.zeros((2 * rows, half))
        table[:count] = cos
        table[rows:rows + count] = sin
        hi, lo = pair(table)
        back.append(np.concatenate([hi, hi, lo], axis=1))
    hi, lo = pair(x_table)
    x_forward = np.concatenate([hi, hi, lo], axis=0)
    hi, lo = pair(x_table.T.copy())
    x_back = np.concatenate([hi, hi, lo], axis=0)
    return (*forward, x_forward, x_back, *back)


def params():
    return pltpu.CompilerParams(vmem_limit_bytes=VMEM_LIMIT)


def cost(flops, nbytes):
    return pl.CostEstimate(flops=int(flops), bytes_accessed=int(nbytes), transcendentals=0)


def wave_kernel(extent, me_ref, length_ref, row_ref, col_ref, plane_ref, coef_ref, out_ref, kc_ref, len_ref, whi_ref, wlo_ref, sc_ref, ss_ref):
    devices = out_ref.shape[0]
    sticks, _, padded = coef_ref.shape
    padded_planes = plane_ref.shape[1] // devices
    me = me_ref[0]
    half = LANES // 2
    lead = (me * sticks) // LANES
    odd = (me * sticks) % LANES != 0

    def own(ref):
        first, second = ref[pl.ds(lead, 1), :], ref[pl.ds(lead + 1, 1), :]
        both = jnp.concatenate([first, second], axis=1)
        return jnp.where(odd, both[:, half:], both[:, :sticks])

    length_row = own(length_ref).astype(F32)
    at_row = own(row_ref)
    at_col = own(col_ref)
    at_row = jnp.where(at_row <= RADIUS, at_row, at_row - extent).astype(F32)
    at_col = jnp.where(at_col <= RADIUS, at_col, at_col - extent).astype(F32)
    square_row = at_row * at_row + at_col * at_col
    spare = jnp.ones((1, 2 * LANES - sticks), F32)
    aux = jnp.concatenate(
        [
            jnp.broadcast_to(jnp.concatenate([length_row, spare], axis=1), (LANES // 2, 2 * LANES)),
            jnp.broadcast_to(jnp.concatenate([square_row, spare], axis=1), (LANES // 2, 2 * LANES)),
        ],
        axis=0,
    )
    aux_col = jnp.transpose(aux)[:sticks]
    len_ref[...] = aux_col
    length = aux_col[:, 0:1]
    square = aux_col[:, LANES // 2:LANES // 2 + 1]
    middle = (length - 1.0) * 0.5
    position = lax.broadcasted_iota(jnp.int32, (sticks, padded), 1).astype(F32)
    kept = (position < length).astype(F32)
    kinetic = (square + (position - middle) * (position - middle)) * (1.0 / (RADIUS * RADIUS))
    wave = jnp.concatenate([coef_ref[:, 0, :] * kept, coef_ref[:, 1, :] * kept], axis=1)
    kc_ref[...] = wave * jnp.concatenate([kinetic, kinetic], axis=1)

    total = plane_ref.shape[1]
    plane_row = jnp.broadcast_to(plane_ref[...].astype(F32), (LANES, total))
    plane_col = jnp.transpose(plane_row)[:, 0:1]
    real = (plane_col >= 0.0).astype(F32)
    plane_col = jnp.maximum(plane_col, 0.0)
    harmonic = lax.broadcasted_iota(jnp.int32, (total, padded), 1).astype(F32)
    cos, sin = trig(plane_col * harmonic, extent)
    cos, sin = cos * real, sin * real
    parts = []
    for d in range(devices):
        c = cos[d * padded_planes:(d + 1) * padded_planes]
        s = sin[d * padded_planes:(d + 1) * padded_planes]
        parts.append(jnp.concatenate([c, -s], axis=1))
        parts.append(jnp.concatenate([s, c], axis=1))
    table = split(jnp.concatenate(parts, axis=0))
    whi_ref[...] = table[0]
    wlo_ref[...] = table[1]
    shift_cos, shift_sin = trig(plane_col * ((length_row - 1.0) * 0.5), extent)
    sc_ref[...] = shift_cos
    ss_ref[...] = shift_sin
    raw = dot3(table, split(wave), ((1,), (1,)))
    for d in range(devices):
        at = 2 * d * padded_planes
        re, im = raw[at:at + padded_planes], raw[at + padded_planes:at + 2 * padded_planes]
        c = shift_cos[d * padded_planes:(d + 1) * padded_planes]
        s = shift_sin[d * padded_planes:(d + 1) * padded_planes]
        along_re = re * c + im * s
        along_im = im * c - re * s
        out_ref[d, 0:padded_planes, :] = along_re[:, :LANES]
        out_ref[d, padded_planes:2 * padded_planes, :] = along_im[:, :LANES]
        out_ref[d, 2 * padded_planes:3 * padded_planes, :] = jnp.concatenate(
            [along_re[:, LANES:], along_im[:, LANES:]], axis=1
        )


def window_row(values, sticks):
    line = jnp.concatenate([values[i:i + 1] for i in range(values.shape[0])], axis=1)
    starts = range(0, line.shape[1], sticks)
    parts = [line[:, at:at + LANES] for at in starts]
    parts += [line[:, at + LANES:at + sticks] for at in starts]
    return jnp.concatenate(parts, axis=1)


def map_kernel(extent, sticks, in_row_ref, in_col_ref, map_ref, first_ref, src_ref, dst_ref, row_ref, col_ref):
    windows = src_ref.shape[0]
    total = windows * LANES

    def signed(ref):
        value = ref[...]
        return window_row(jnp.where(value <= RADIUS, value, value - extent) + RADIUS, sticks)

    def dot(x, y, dims=((1,), (0,))):
        return lax.dot_general(x, y, (dims, ((), ())), preferred_element_type=F32)

    def bits(condition):
        return condition.astype(F32).astype(BF16)

    nt = ((1,), (1,))
    own_row, own_col = signed(in_row_ref), signed(in_col_ref)
    own_row = (own_row & 1) * row_blocks()[0] + (own_row >> 1)
    tall = lax.broadcasted_iota(jnp.int32, (LANES, total), 0)
    place = lax.broadcasted_iota(jnp.int32, (LANES, total), 1)
    in_col = tall == own_col
    row_hot, col_hot = bits(tall == own_row), bits(in_col)
    down = lax.broadcasted_iota(jnp.int32, (LANES, LANES), 0)
    across = lax.broadcasted_iota(jnp.int32, (LANES, LANES), 1)
    before = bits(down < across)
    after = bits(down > across)
    upto = bits(down >= across)
    ones = jnp.ones((LANES, LANES), BF16)
    taken = dot(row_hot, col_hot, nt)
    taken_t = dot(col_hot, row_hot, nt)
    taken_b, taken_tb = taken.astype(BF16), taken_t.astype(BF16)
    start = dot(dot(after, taken_b).astype(BF16), ones)
    end = start + dot(taken_b, ones)
    start_t = dot(ones, dot(taken_tb, before).astype(BF16))
    limit = windows - 1.0
    first = jnp.minimum(jnp.floor(start * (1.0 / LANES)), limit)
    code = jnp.where(taken > 0.5, dot(taken_b, before) + start - LANES * first, -1.0)
    map_ref[...] = code.astype(jnp.int32)
    first_ref[...] = jnp.minimum(jnp.floor(start_t[0:8] * (1.0 / LANES)), limit).astype(jnp.int32)

    spot = place.astype(F32)
    in_range = (spot >= start[:, 0:1]) & (spot < end[:, 0:1])
    sorted_hot = bits(in_range)
    sorted_row = jnp.sum(jnp.where(in_range, tall, 0).astype(F32), axis=0, keepdims=True)
    sorted_rank = spot[0:1] - jnp.sum(jnp.where(in_range, start[:, 0:1], 0.0), axis=0, keepdims=True)
    counts = dot(dot(upto, taken_tb).astype(BF16), sorted_hot)
    sorted_col = jnp.sum((counts <= sorted_rank).astype(F32), axis=0, keepdims=True)
    names = place + 1
    name_hi = dot(jnp.where(in_col, names >> 6, 0).astype(F32).astype(BF16), row_hot, nt)
    name_lo = dot(jnp.where(in_col, names & 63, 0).astype(F32).astype(BF16), row_hot, nt)
    named = dot(name_hi.astype(BF16), sorted_hot) * 64.0 + dot(name_lo.astype(BF16), sorted_hot)
    source = jnp.sum(jnp.where(tall.astype(F32) == sorted_col, named, 0.0), axis=0, keepdims=True) - 1.0
    place_t = dot(after, taken_tb) + start_t
    place_hi = jnp.floor(place_t * (1.0 / 64.0))
    place_lo = place_t - 64.0 * place_hi
    placed = dot(place_hi.astype(BF16), row_hot) * 64.0 + dot(place_lo.astype(BF16), row_hot)
    target = jnp.sum(jnp.where(in_col, placed, 0.0), axis=0, keepdims=True)
    for values, ref in ((source, src_ref), (target, dst_ref), (sorted_row, row_ref), (sorted_col, col_ref)):
        values = values.astype(jnp.int32)
        for w in range(windows):
            ref[w:w + 1, :] = values[:, w * LANES:(w + 1) * LANES]
    row_ref[windows:windows + 1, :] = jnp.full((1, LANES), -1, jnp.int32)
    col_ref[windows:windows + 1, :] = jnp.zeros((1, LANES), jnp.int32)


def lane_take(x, index):
    return jnp.take_along_axis(x, index, axis=1, mode="promise_in_bounds")


def plane_kernel(
    planes, first_ref, map_ref, src_ref, dst_ref, row_ref, col_ref, recv_ref,
    y_even, y_odd, x_forward, x_back, back_even, back_odd,
    pot_hbm, out_ref, x_ref, s_ref, gr_ref, gi_ref, pot_ref, sem,
):
    devices = recv_ref.shape[0]
    padded_planes = recv_ref.shape[1] // 3
    windows = x_ref.shape[0]
    rows = gr_ref.shape[0] // padded_planes
    extent = pot_ref.shape[1]
    half = LANES // 2
    fetch = pltpu.make_async_copy(pot_hbm, pot_ref, sem)
    fetch.start()

    low = lax.broadcasted_iota(jnp.int32, (padded_planes, LANES), 1) < half
    for d in range(devices):
        x_ref[d] = recv_ref[d, 0:2 * padded_planes, :]
    for e in range(devices // 2):
        first = recv_ref[2 * e, 2 * padded_planes:3 * padded_planes, :]
        second = recv_ref[2 * e + 1, 2 * padded_planes:3 * padded_planes, :]
        x_ref[devices + e, 0:padded_planes, :] = jnp.where(low, first, pltpu.roll(second, half, 1))
        x_ref[devices + e, padded_planes:2 * padded_planes, :] = jnp.where(
            low, pltpu.roll(first, half, 1), second
        )

    blocks = padded_planes // 8
    grids = (gr_ref, gi_ref)

    def reorder(order_ref, from_ref, to_ref):
        @pl.loop(0, windows, unroll=4)
        def _(v):
            order = jnp.broadcast_to(order_ref[pl.ds(v, 1), :], (8, LANES))
            index = order & (LANES - 1)
            window = order >> 7
            for j in range(2 * blocks):
                value = jnp.zeros((8, LANES), F32)
                for w in range(windows):
                    value = jnp.where(window == w, lane_take(from_ref[w, 8 * j:8 * j + 8, :], index), value)
                to_ref[v, 8 * j:8 * j + 8, :] = value

    reorder(src_ref, x_ref, s_ref)

    @pl.loop(0, rows, unroll=8)
    def _(r):
        first = first_ref[0, r]
        code = jnp.broadcast_to(map_ref[pl.ds(r, 1), :], (8, LANES))
        index = code & (LANES - 1)
        window = code >> 7
        for j in range(2 * blocks):
            lead = lane_take(s_ref[first, 8 * j:8 * j + 8, :], index)
            trail = lane_take(s_ref[first + 1, 8 * j:8 * j + 8, :], index)
            value = jnp.where(window == 0, lead, jnp.where(window == 1, trail, 0.0))
            part, at = j // blocks, 8 * (j % blocks)
            grids[part][pl.ds(r + at * rows, 8, stride=rows), :] = value

    fetch.wait()
    even_rows, odd_rows = row_blocks()
    folded = extent // 2
    group = 2

    def dot(x, y):
        return jnp.dot(x, y, preferred_element_type=F32)

    def stack(x, axis):
        hi, lo = split(x)
        return jnp.concatenate([hi, lo, hi], axis=axis)

    def times_wave(both, cut, sign):
        cos, sin = both[:cut], both[cut:]
        re = cos[:, :LANES] - sign * sin[:, LANES:]
        im = cos[:, LANES:] + sign * sin[:, :LANES]
        return re, im

    @pl.loop(0, planes // group, unroll=3)
    def _(step):
        lines = []
        for t in range(group):
            base = pl.multiple_of((step * group + t) * rows, 16)
            even, odd = pl.ds(base, even_rows), pl.ds(base + even_rows, odd_rows)
            parts = []
            for pick, table, size in ((even, y_even, even_rows), (odd, y_odd, odd_rows)):
                spectrum = jnp.concatenate([gr_ref[pick, :], gi_ref[pick, :]], axis=1)
                parts.append(times_wave(dot(table[...], stack(spectrum, 0)), folded, 1.0))
            (e_re, e_im), (o_re, o_im) = parts
            lines.append(jnp.concatenate([e_re + o_re, e_im + o_im], axis=1))
            lines.append(jnp.concatenate([e_re - o_re, e_im - o_im], axis=1))
        field = dot(stack(jnp.concatenate(lines, axis=0), 1), x_forward[...])
        wide = field.shape[1] // 2
        spare = jnp.zeros((extent, wide - extent), F32)
        weighted = []
        for t in range(group):
            v = jnp.concatenate([pot_ref[step * group + t], spare], axis=1)
            mine = field[t * extent:(t + 1) * extent]
            weighted.append(jnp.concatenate([mine[:, :wide] * v, mine[:, wide:] * v], axis=1))
        back = dot(stack(jnp.concatenate(weighted, axis=0), 1), x_back[...])
        for t in range(group):
            base = pl.multiple_of((step * group + t) * rows, 16)
            even, odd = pl.ds(base, even_rows), pl.ds(base + even_rows, odd_rows)
            upper = back[t * extent:t * extent + folded]
            lower = back[t * extent + folded:(t + 1) * extent]
            for pick, table, size, value in (
                (even, back_even, even_rows, upper + lower), (odd, back_odd, odd_rows, upper - lower)
            ):
                re, im = times_wave(dot(table[...], stack(value, 0)), size, -1.0)
                gr_ref[pick, :] = re
                gi_ref[pick, :] = im

    @pl.loop(0, rows, unroll=8)
    def _(r):
        first = first_ref[0, r]
        values = []
        for j in range(2 * blocks):
            part, at = j // blocks, 8 * (j % blocks)
            values.append(grids[part][pl.ds(r + at * rows, 8, stride=rows), :])
        for t in range(2):
            index = jnp.broadcast_to(col_ref[pl.ds(first + t, 1), :], (8, LANES))
            hit = jnp.broadcast_to(row_ref[pl.ds(first + t, 1), :], (8, LANES)) == r
            for j in range(2 * blocks):
                pltpu.store(
                    s_ref.at[first + t, 8 * j:8 * j + 8, :], lane_take(values[j], index), mask=hit
                )

    reorder(dst_ref, s_ref, x_ref)
    for w in range(devices):
        out_ref[w, 0:2 * padded_planes, :] = x_ref[w]
    for e in range(devices // 2):
        re = x_ref[devices + e, 0:padded_planes, :]
        im = x_ref[devices + e, padded_planes:2 * padded_planes, :]
        out_ref[2 * e, 2 * padded_planes:3 * padded_planes, :] = jnp.where(
            low, re, pltpu.roll(im, half, 1)
        )
        out_ref[2 * e + 1, 2 * padded_planes:3 * padded_planes, :] = jnp.where(
            low, pltpu.roll(re, half, 1), im
        )
    for d in range(devices):
        out_ref[d, 3 * padded_planes:, :] = jnp.zeros((8, LANES), F32)


def inner_kernel(bands, volume, norm, band_ref, *refs):
    kc_ref = refs[0]
    coefs = refs[1:1 + bands]
    fields = refs[1 + bands:1 + 2 * bands]
    in_ref = refs[1 + 2 * bands]
    out_ref = refs[2 + 2 * bands]
    devices = in_ref.shape[0]
    padded_planes = (in_ref.shape[1] - 8) // 3
    half = LANES // 2
    padded = coefs[0].shape[2]
    me = band_ref[0]
    low = lax.broadcasted_iota(jnp.int32, (padded_planes, LANES), 1) < half

    def fold(x):
        rows = x.shape[0]
        total = x[0:8]
        for at in range(8, rows, 8):
            total = total + x[at:at + 8]
        return total

    kc = kc_ref[...]
    kc_re, kc_im = kc[:, :padded], kc[:, padded:]
    sums = []
    for m in range(bands):
        c_re, c_im = coefs[m][:, 0, :], coefs[m][:, 1, :]
        sums.append([fold(c_re * kc_re + c_im * kc_im), fold(c_re * kc_im - c_im * kc_re)])
    local = [[jnp.zeros((8, LANES), F32), jnp.zeros((8, LANES), F32)] for _ in range(bands)]
    for d in range(devices):
        value = in_ref[d, 0:3 * padded_planes, :]
        re, im, rest = value[:padded_planes], value[padded_planes:2 * padded_planes], value[2 * padded_planes:]
        turned = pltpu.roll(rest, half, 1)
        other = jnp.concatenate([im, -re, jnp.where(low, turned, -turned)], axis=0)
        for m in range(bands):
            col = fields[m][d, 0:3 * padded_planes, :]
            local[m][0] = local[m][0] + fold(col * value)
            local[m][1] = local[m][1] + fold(col * other)
    lane = lax.broadcasted_iota(jnp.int32, (8, LANES), 1)
    row = lax.broadcasted_iota(jnp.int32, (8, LANES), 0)
    tile = jnp.zeros((8, LANES), F32)
    for m in range(bands):
        at = lax.rem(me + m, bands)
        for part, sign in ((0, 1.0), (1, -1.0)):
            partial = sums[m][part] + volume * local[m][part]
            scalar = jnp.sum(jnp.sum(partial, axis=1, keepdims=True), axis=0, keepdims=True)
            tile = jnp.where((lane == at) & (row == part), sign * norm * scalar, tile)
    for d in range(devices):
        out_ref[d, 0:3 * padded_planes, :] = in_ref[d, 0:3 * padded_planes, :]
        out_ref[d, 3 * padded_planes:, :] = tile


def final_kernel(volume, len_ref, ret_ref, kc_ref, whi_ref, wlo_ref, sc_ref, ss_ref, out_ref, sub_ref):
    devices = ret_ref.shape[0]
    padded_planes = (ret_ref.shape[1] - 8) // 3
    sticks, _, padded = out_ref.shape
    half = LANES // 2
    bands = sub_ref.shape[2]
    total = jnp.zeros((8, LANES), F32)
    parts = []
    for d in range(devices):
        value = ret_ref[d]
        total = total + value[3 * padded_planes:]
        rest = value[2 * padded_planes:3 * padded_planes]
        re = jnp.concatenate([value[:padded_planes], rest[:, :half]], axis=1)
        im = jnp.concatenate([value[padded_planes:2 * padded_planes], rest[:, half:]], axis=1)
        c = sc_ref[d * padded_planes:(d + 1) * padded_planes, :]
        s = ss_ref[d * padded_planes:(d + 1) * padded_planes, :]
        parts.append(re * c - im * s)
        parts.append(re * s + im * c)
    stacked = jnp.concatenate(parts, axis=0)
    spare = jnp.zeros((stacked.shape[0], 2 * LANES - sticks), F32)
    turned = jnp.transpose(jnp.concatenate([stacked, spare], axis=1))[:sticks]
    local = dot3(split(turned), (whi_ref[...], wlo_ref[...])) * volume
    position = lax.broadcasted_iota(jnp.int32, (sticks, padded), 1).astype(F32)
    kept = position < len_ref[:, 0:1]
    kc = kc_ref[...]
    out_ref[:, 0, :] = jnp.where(kept, kc[:, :padded] + local[:, :padded], 0.0)
    out_ref[:, 1, :] = jnp.where(kept, kc[:, padded:] + local[:, padded:], 0.0)
    sub_ref[:, 0, :] = total[0:2, :bands]


def shards(bands, devices, coefficients, stick_col, stick_row, stick_length, plane_of_slot, potential):
    extent = plane_of_slot.shape[0]
    sticks = coefficients.shape[1]
    padded = coefficients.shape[3]
    total_sticks = stick_col.shape[0]
    planes = potential.shape[0]
    padded_planes = up8(planes)
    if sticks != LANES + LANES // 2 or devices % 2 or planes % 2:
        raise ValueError("sizes")
    rows = sum(row_blocks())
    volume = 1.0 / (extent * extent * extent)
    me = lax.axis_index("tg").astype(jnp.int32)
    coef = coefficients.reshape(sticks, 2, padded)

    length, row, col = (v.reshape(-1, LANES) for v in (stick_length, stick_row, stick_col))
    slots = plane_of_slot.reshape(devices, planes)
    if padded_planes > planes:
        slots = jnp.pad(slots, ((0, 0), (0, padded_planes - planes)), constant_values=-1)
    slots = slots.reshape(1, devices * padded_planes)
    windows = total_sticks // LANES
    smem = pl.BlockSpec(memory_space=pltpu.SMEM)
    vmem = pl.BlockSpec(memory_space=pltpu.VMEM)

    block = 3 * padded_planes
    total_planes = devices * padded_planes
    sent, kc, lengths, whi, wlo, shift_cos, shift_sin = pl.pallas_call(
        functools.partial(wave_kernel, extent),
        out_shape=(
            jax.ShapeDtypeStruct((devices, block, LANES), F32),
            jax.ShapeDtypeStruct((sticks, 2 * padded), F32),
            jax.ShapeDtypeStruct((sticks, LANES), F32),
            jax.ShapeDtypeStruct((2 * total_planes, 2 * padded), BF16),
            jax.ShapeDtypeStruct((2 * total_planes, 2 * padded), BF16),
            jax.ShapeDtypeStruct((total_planes, sticks), F32),
            jax.ShapeDtypeStruct((total_planes, sticks), F32),
        ),
        in_specs=[smem] + [vmem] * 5,
        compiler_params=params(),
        name="wave_to_planes",
    )(me.reshape(1), length, row, col, slots, coef)

    received = lax.all_to_all(sent, "tg", split_axis=0, concat_axis=0, tiled=True)

    window_list = jax.ShapeDtypeStruct((windows, LANES), jnp.int32)
    longer_list = jax.ShapeDtypeStruct((windows + 1, LANES), jnp.int32)
    stick_map, first, source, target, row_w, col_w = pl.pallas_call(
        functools.partial(map_kernel, extent, sticks),
        out_shape=(
            jax.ShapeDtypeStruct((LANES, LANES), jnp.int32),
            jax.ShapeDtypeStruct((8, LANES), jnp.int32),
            window_list,
            window_list,
            longer_list,
            longer_list,
        ),
        compiler_params=params(),
        cost_estimate=cost(4e9, 1e5),
        name="stick_map",
    )(row, col)

    weighted = pl.pallas_call(
        functools.partial(plane_kernel, planes),
        out_shape=jax.ShapeDtypeStruct((devices, block + 8, LANES), F32),
        in_specs=[smem] + [vmem] * 12 + [pl.BlockSpec(memory_space=pl.ANY)],
        out_specs=vmem,
        scratch_shapes=[
            pltpu.VMEM((windows, 2 * padded_planes, LANES), F32),
            pltpu.VMEM((windows + 1, 2 * padded_planes, LANES), F32),
            pltpu.VMEM((padded_planes * rows, LANES), F32),
            pltpu.VMEM((padded_planes * rows, LANES), F32),
            pltpu.VMEM(potential.shape, F32),
            pltpu.SemaphoreType.DMA,
        ],
        compiler_params=params(),
        cost_estimate=cost(2e10, 1e7),
        name="planes",
    )(first, stick_map, source, target, row_w, col_w, received, *[jnp.asarray(t) for t in tables(extent)], potential)

    coefs, fields = [coef], [received]
    for shift in range(1, bands):
        ring = [((b + shift) % bands, b) for b in range(bands)]
        coefs.append(lax.ppermute(coef, "band", ring))
        fields.append(lax.ppermute(received, "band", ring))
    band = lax.axis_index("band").astype(jnp.int32).reshape(1)
    norm = 1.0 / (total_sticks * padded)
    outgoing = pl.pallas_call(
        functools.partial(inner_kernel, bands, volume, norm),
        out_shape=jax.ShapeDtypeStruct((devices, block + 8, LANES), F32),
        in_specs=[pl.BlockSpec(memory_space=pltpu.SMEM)] + [vmem] * (2 + 2 * bands),
        out_specs=vmem,
        compiler_params=params(),
        name="inner",
    )(band, kc, *coefs, *fields, weighted)

    returned = lax.all_to_all(outgoing, "tg", split_axis=0, concat_axis=0, tiled=True)
    applied, subspace = pl.pallas_call(
        functools.partial(final_kernel, volume),
        out_shape=(
            jax.ShapeDtypeStruct((sticks, 2, padded), F32),
            jax.ShapeDtypeStruct((2, 1, bands), F32),
        ),
        compiler_params=params(),
        name="planes_to_wave",
    )(lengths, returned, kc, whi, wlo, shift_cos, shift_sin)
    return applied.reshape(1, sticks, 2, padded), subspace


def solution(mesh):
    in_specs = (P("band", "tg", None, None), P(), P(), P(), P(), P("tg", None, None))
    out_specs = (P("band", "tg", None, None), P(None, "band", None))
    body = functools.partial(shards, mesh.shape["band"], mesh.shape["tg"])
    return jax.shard_map(body, mesh=mesh, in_specs=in_specs, out_specs=out_specs, check_vma=False)
```

```python
import functools
import math

import jax
import jax.numpy as jnp
import ml_dtypes
import numpy as np
from jax import lax
from jax.experimental import pallas as pl
from jax.experimental.pallas import tpu as pltpu
from jax.sharding import PartitionSpec as P

RADIUS = 48
LANES = 128
F32 = jnp.float32
BF16 = jnp.bfloat16
VMEM_LIMIT = 56 * 1024 * 1024


def up8(n):
    return -(-n // 8) * 8


def split(x):
    hi = x.astype(BF16)
    return hi, (x - hi.astype(F32)).astype(BF16)


def dot3(a, b, dims=((1,), (0,))):
    def dot(x, y):
        return lax.dot_general(x, y, (dims, ((), ())), preferred_element_type=F32)

    return dot(a[0], b[0]) + (dot(a[0], b[1]) + dot(a[1], b[0]))


def trig(product, extent):
    n = product - extent * jnp.floor(product * (1.0 / extent) + 0.5)
    quarter = extent / 4.0
    unit = 2.0 * math.pi / extent

    def sine(m):
        u = m * unit
        v = u * u
        s = 1.0 / 6227020800.0
        for term in (-39916800.0, 362880.0, -5040.0, 120.0, -6.0, 1.0):
            s = s * v + 1.0 / term
        return u * s

    folded = jnp.where(
        jnp.abs(n) > quarter, jnp.where(n > 0, 2.0 * quarter, -2.0 * quarter) - n, n
    )
    return sine(quarter - jnp.abs(n)), sine(folded)


def pair(table):
    hi = table.astype(np.float32).astype(ml_dtypes.bfloat16)
    lo = (table - hi.astype(np.float64)).astype(ml_dtypes.bfloat16)
    return hi, lo


def row_blocks():
    even = -(-(RADIUS + 1) // 16) * 16
    odd = -(-RADIUS // 16) * 16
    return even, odd


@functools.cache
def tables(extent):
    kept = 2 * RADIUS + 1
    half = extent // 2
    grid = np.arange(extent)
    freq = np.arange(kept) - RADIUS

    def angles(f, g):
        a = 2.0 * np.pi * ((f[:, None] * g[None, :]) % extent) / extent
        return np.cos(a), np.sin(a)

    cos, sin = angles(freq, grid)
    wide = 2 * LANES
    x_table = np.zeros((wide, 2 * wide))
    x_table[:kept, :extent] = cos
    x_table[LANES:LANES + kept, :extent] = -sin
    x_table[:kept, wide:wide + extent] = sin
    x_table[LANES:LANES + kept, wide:wide + extent] = cos
    forward, back = [], []
    for offset, rows in zip((0, 1), row_blocks()):
        cos, sin = angles(freq[offset::2], grid[:half])
        count = cos.shape[0]
        table = np.zeros((2 * half, rows))
        table[:half, :count] = cos.T
        table[half:, :count] = sin.T
        hi, lo = pair(table)
        forward.append(np.concatenate([hi, hi, lo], axis=1))
        table = np.zeros((2 * rows, half))
        table[:count] = cos
        table[rows:rows + count] = sin
        hi, lo = pair(table)
        back.append(np.concatenate([hi, hi, lo], axis=1))
    hi, lo = pair(x_table)
    x_forward = np.concatenate([hi, hi, lo], axis=0)
    hi, lo = pair(x_table.T.copy())
    x_back = np.concatenate([hi, hi, lo], axis=0)
    return (*forward, x_forward, x_back, *back)


def params():
    return pltpu.CompilerParams(vmem_limit_bytes=VMEM_LIMIT)


def cost(flops, nbytes):
    return pl.CostEstimate(flops=int(flops), bytes_accessed=int(nbytes), transcendentals=0)


def wave_kernel(extent, me_ref, length_ref, row_ref, col_ref, plane_ref, coef_ref, out_ref, kc_ref, len_ref, whi_ref, wlo_ref, sc_ref, ss_ref):
    devices = out_ref.shape[0]
    sticks, _, padded = coef_ref.shape
    padded_planes = plane_ref.shape[1] // devices
    me = me_ref[0]
    half = LANES // 2
    lead = (me * sticks) // LANES
    odd = (me * sticks) % LANES != 0

    def own(ref):
        first, second = ref[pl.ds(lead, 1), :], ref[pl.ds(lead + 1, 1), :]
        both = jnp.concatenate([first, second], axis=1)
        return jnp.where(odd, both[:, half:], both[:, :sticks])

    length_row = own(length_ref).astype(F32)
    at_row = own(row_ref)
    at_col = own(col_ref)
    at_row = jnp.where(at_row <= RADIUS, at_row, at_row - extent).astype(F32)
    at_col = jnp.where(at_col <= RADIUS, at_col, at_col - extent).astype(F32)
    square_row = at_row * at_row + at_col * at_col
    spare = jnp.ones((1, 2 * LANES - sticks), F32)
    aux = jnp.concatenate(
        [
            jnp.broadcast_to(jnp.concatenate([length_row, spare], axis=1), (LANES // 2, 2 * LANES)),
            jnp.broadcast_to(jnp.concatenate([square_row, spare], axis=1), (LANES // 2, 2 * LANES)),
        ],
        axis=0,
    )
    aux_col = jnp.transpose(aux)[:sticks]
    len_ref[...] = aux_col
    length = aux_col[:, 0:1]
    square = aux_col[:, LANES // 2:LANES // 2 + 1]
    middle = (length - 1.0) * 0.5
    position = lax.broadcasted_iota(jnp.int32, (sticks, padded), 1).astype(F32)
    kept = (position < length).astype(F32)
    kinetic = (square + (position - middle) * (position - middle)) * (1.0 / (RADIUS * RADIUS))
    wave = jnp.concatenate([coef_ref[:, 0, :] * kept, coef_ref[:, 1, :] * kept], axis=1)
    kc_ref[...] = wave * jnp.concatenate([kinetic, kinetic], axis=1)

    total = plane_ref.shape[1]
    plane_row = jnp.broadcast_to(plane_ref[...].astype(F32), (LANES, total))
    plane_col = jnp.transpose(plane_row)[:, 0:1]
    real = (plane_col >= 0.0).astype(F32)
    plane_col = jnp.maximum(plane_col, 0.0)
    harmonic = lax.broadcasted_iota(jnp.int32, (total, padded), 1).astype(F32)
    cos, sin = trig(plane_col * harmonic, extent)
    cos, sin = cos * real, sin * real
    parts = []
    for d in range(devices):
        c = cos[d * padded_planes:(d + 1) * padded_planes]
        s = sin[d * padded_planes:(d + 1) * padded_planes]
        parts.append(jnp.concatenate([c, -s], axis=1))
        parts.append(jnp.concatenate([s, c], axis=1))
    table = split(jnp.concatenate(parts, axis=0))
    whi_ref[...] = table[0]
    wlo_ref[...] = table[1]
    shift_cos, shift_sin = trig(plane_col * ((length_row - 1.0) * 0.5), extent)
    sc_ref[...] = shift_cos
    ss_ref[...] = shift_sin
    raw = dot3(table, split(wave), ((1,), (1,)))
    for d in range(devices):
        at = 2 * d * padded_planes
        re, im = raw[at:at + padded_planes], raw[at + padded_planes:at + 2 * padded_planes]
        c = shift_cos[d * padded_planes:(d + 1) * padded_planes]
        s = shift_sin[d * padded_planes:(d + 1) * padded_planes]
        along_re = re * c + im * s
        along_im = im * c - re * s
        out_ref[d, 0:padded_planes, :] = along_re[:, :LANES]
        out_ref[d, padded_planes:2 * padded_planes, :] = along_im[:, :LANES]
        out_ref[d, 2 * padded_planes:3 * padded_planes, :] = jnp.concatenate(
            [along_re[:, LANES:], along_im[:, LANES:]], axis=1
        )


def window_row(values, sticks):
    line = jnp.concatenate([values[i:i + 1] for i in range(values.shape[0])], axis=1)
    starts = range(0, line.shape[1], sticks)
    parts = [line[:, at:at + LANES] for at in starts]
    parts += [line[:, at + LANES:at + sticks] for at in starts]
    return jnp.concatenate(parts, axis=1)


def map_kernel(extent, sticks, in_row_ref, in_col_ref, map_ref, first_ref, src_ref, dst_ref, row_ref, col_ref):
    windows = src_ref.shape[0]
    total = windows * LANES

    def signed(ref):
        value = ref[...]
        return window_row(jnp.where(value <= RADIUS, value, value - extent) + RADIUS, sticks)

    def dot(x, y, dims=((1,), (0,))):
        return lax.dot_general(x, y, (dims, ((), ())), preferred_element_type=F32)

    def bits(condition):
        return condition.astype(F32).astype(BF16)

    nt = ((1,), (1,))
    own_row, own_col = signed(in_row_ref), signed(in_col_ref)
    own_row = (own_row & 1) * row_blocks()[0] + (own_row >> 1)
    tall = lax.broadcasted_iota(jnp.int32, (LANES, total), 0)
    place = lax.broadcasted_iota(jnp.int32, (LANES, total), 1)
    in_col = tall == own_col
    row_hot, col_hot = bits(tall == own_row), bits(in_col)
    down = lax.broadcasted_iota(jnp.int32, (LANES, LANES), 0)
    across = lax.broadcasted_iota(jnp.int32, (LANES, LANES), 1)
    before = bits(down < across)
    after = bits(down > across)
    upto = bits(down >= across)
    ones = jnp.ones((LANES, LANES), BF16)
    taken = dot(row_hot, col_hot, nt)
    taken_t = dot(col_hot, row_hot, nt)
    taken_b, taken_tb = taken.astype(BF16), taken_t.astype(BF16)
    start = dot(dot(after, taken_b).astype(BF16), ones)
    end = start + dot(taken_b, ones)
    start_t = dot(ones, dot(taken_tb, before).astype(BF16))
    limit = windows - 1.0
    first = jnp.minimum(jnp.floor(start * (1.0 / LANES)), limit)
    code = jnp.where(taken > 0.5, dot(taken_b, before) + start - LANES * first, -1.0)
    map_ref[...] = code.astype(jnp.int32)
    first_ref[...] = jnp.minimum(jnp.floor(start_t[0:8] * (1.0 / LANES)), limit).astype(jnp.int32)

    spot = place.astype(F32)
    in_range = (spot >= start[:, 0:1]) & (spot < end[:, 0:1])
    sorted_hot = bits(in_range)
    sorted_row = jnp.sum(jnp.where(in_range, tall, 0).astype(F32), axis=0, keepdims=True)
    sorted_rank = spot[0:1] - jnp.sum(jnp.where(in_range, start[:, 0:1], 0.0), axis=0, keepdims=True)
    counts = dot(dot(upto, taken_tb).astype(BF16), sorted_hot)
    sorted_col = jnp.sum((counts <= sorted_rank).astype(F32), axis=0, keepdims=True)
    names = place + 1
    name_hi = dot(jnp.where(in_col, names >> 6, 0).astype(F32).astype(BF16), row_hot, nt)
    name_lo = dot(jnp.where(in_col, names & 63, 0).astype(F32).astype(BF16), row_hot, nt)
    named = dot(name_hi.astype(BF16), sorted_hot) * 64.0 + dot(name_lo.astype(BF16), sorted_hot)
    source = jnp.sum(jnp.where(tall.astype(F32) == sorted_col, named, 0.0), axis=0, keepdims=True) - 1.0
    place_t = dot(after, taken_tb) + start_t
    place_hi = jnp.floor(place_t * (1.0 / 64.0))
    place_lo = place_t - 64.0 * place_hi
    placed = dot(place_hi.astype(BF16), row_hot) * 64.0 + dot(place_lo.astype(BF16), row_hot)
    target = jnp.sum(jnp.where(in_col, placed, 0.0), axis=0, keepdims=True)
    for values, ref in ((source, src_ref), (target, dst_ref), (sorted_row, row_ref), (sorted_col, col_ref)):
        values = values.astype(jnp.int32)
        for w in range(windows):
            ref[w:w + 1, :] = values[:, w * LANES:(w + 1) * LANES]
    row_ref[windows:windows + 1, :] = jnp.full((1, LANES), -1, jnp.int32)
    col_ref[windows:windows + 1, :] = jnp.zeros((1, LANES), jnp.int32)


def lane_take(x, index):
    return jnp.take_along_axis(x, index, axis=1, mode="promise_in_bounds")


def plane_kernel(
    planes, first_ref, map_ref, src_ref, dst_ref, row_ref, col_ref, recv_ref,
    y_even, y_odd, x_forward, x_back, back_even, back_odd,
    pot_hbm, out_ref, x_ref, s_ref, gr_ref, gi_ref, pot_ref, sem,
):
    devices = recv_ref.shape[0]
    padded_planes = recv_ref.shape[1] // 3
    windows = x_ref.shape[0]
    rows = gr_ref.shape[0] // padded_planes
    extent = pot_ref.shape[1]
    half = LANES // 2
    fetch = pltpu.make_async_copy(pot_hbm, pot_ref, sem)
    fetch.start()

    low = lax.broadcasted_iota(jnp.int32, (padded_planes, LANES), 1) < half
    for d in range(devices):
        x_ref[d] = recv_ref[d, 0:2 * padded_planes, :]
    for e in range(devices // 2):
        first = recv_ref[2 * e, 2 * padded_planes:3 * padded_planes, :]
        second = recv_ref[2 * e + 1, 2 * padded_planes:3 * padded_planes, :]
        x_ref[devices + e, 0:padded_planes, :] = jnp.where(low, first, pltpu.roll(second, half, 1))
        x_ref[devices + e, padded_planes:2 * padded_planes, :] = jnp.where(
            low, pltpu.roll(first, half, 1), second
        )

    blocks = padded_planes // 8
    grids = (gr_ref, gi_ref)

    def reorder(order_ref, from_ref, to_ref):
        @pl.loop(0, windows, unroll=4)
        def _(v):
            order = jnp.broadcast_to(order_ref[pl.ds(v, 1), :], (8, LANES))
            index = order & (LANES - 1)
            window = order >> 7
            for j in range(2 * blocks):
                value = jnp.zeros((8, LANES), F32)
                for w in range(windows):
                    value = jnp.where(window == w, lane_take(from_ref[w, 8 * j:8 * j + 8, :], index), value)
                to_ref[v, 8 * j:8 * j + 8, :] = value

    reorder(src_ref, x_ref, s_ref)

    @pl.loop(0, rows, unroll=8)
    def _(r):
        first = first_ref[0, r]
        code = jnp.broadcast_to(map_ref[pl.ds(r, 1), :], (8, LANES))
        index = code & (LANES - 1)
        window = code >> 7
        for j in range(2 * blocks):
            lead = lane_take(s_ref[first, 8 * j:8 * j + 8, :], index)
            trail = lane_take(s_ref[first + 1, 8 * j:8 * j + 8, :], index)
            value = jnp.where(window == 0, lead, jnp.where(window == 1, trail, 0.0))
            part, at = j // blocks, 8 * (j % blocks)
            grids[part][pl.ds(r + at * rows, 8, stride=rows), :] = value

    fetch.wait()
    even_rows, odd_rows = row_blocks()
    folded = extent // 2
    group = next(g for g in (8, 4, 2) if planes % g == 0)

    def dot(x, y):
        return jnp.dot(x, y, preferred_element_type=F32)

    def stack(x, axis):
        hi, lo = split(x)
        return jnp.concatenate([hi, lo, hi], axis=axis)

    def times_wave(both, cut, sign):
        cos, sin = both[:cut], both[cut:]
        re = cos[:, :LANES] - sign * sin[:, LANES:]
        im = cos[:, LANES:] + sign * sin[:, :LANES]
        return re, im

    @pl.loop(0, planes // group)
    def _(step):
        lines = []
        for t in range(group):
            base = pl.multiple_of((step * group + t) * rows, 16)
            even, odd = pl.ds(base, even_rows), pl.ds(base + even_rows, odd_rows)
            parts = []
            for pick, table, size in ((even, y_even, even_rows), (odd, y_odd, odd_rows)):
                spectrum = jnp.concatenate([gr_ref[pick, :], gi_ref[pick, :]], axis=1)
                parts.append(times_wave(dot(table[...], stack(spectrum, 0)), folded, 1.0))
            (e_re, e_im), (o_re, o_im) = parts
            lines.append(jnp.concatenate([e_re + o_re, e_im + o_im], axis=1))
            lines.append(jnp.concatenate([e_re - o_re, e_im - o_im], axis=1))
        field = dot(stack(jnp.concatenate(lines, axis=0), 1), x_forward[...])
        wide = field.shape[1] // 2
        spare = jnp.zeros((extent, wide - extent), F32)
        weighted = []
        for t in range(group):
            v = jnp.concatenate([pot_ref[step * group + t], spare], axis=1)
            mine = field[t * extent:(t + 1) * extent]
            weighted.append(jnp.concatenate([mine[:, :wide] * v, mine[:, wide:] * v], axis=1))
        back = dot(stack(jnp.concatenate(weighted, axis=0), 1), x_back[...])
        for t in range(group):
            base = pl.multiple_of((step * group + t) * rows, 16)
            even, odd = pl.ds(base, even_rows), pl.ds(base + even_rows, odd_rows)
            upper = back[t * extent:t * extent + folded]
            lower = back[t * extent + folded:(t + 1) * extent]
            for pick, table, size, value in (
                (even, back_even, even_rows, upper + lower), (odd, back_odd, odd_rows, upper - lower)
            ):
                re, im = times_wave(dot(table[...], stack(value, 0)), size, -1.0)
                gr_ref[pick, :] = re
                gi_ref[pick, :] = im

    @pl.loop(0, rows, unroll=8)
    def _(r):
        first = first_ref[0, r]
        values = []
        for j in range(2 * blocks):
            part, at = j // blocks, 8 * (j % blocks)
            values.append(grids[part][pl.ds(r + at * rows, 8, stride=rows), :])
        for t in range(2):
            index = jnp.broadcast_to(col_ref[pl.ds(first + t, 1), :], (8, LANES))
            hit = jnp.broadcast_to(row_ref[pl.ds(first + t, 1), :], (8, LANES)) == r
            for j in range(2 * blocks):
                pltpu.store(
                    s_ref.at[first + t, 8 * j:8 * j + 8, :], lane_take(values[j], index), mask=hit
                )

    reorder(dst_ref, s_ref, x_ref)
    for w in range(devices):
        out_ref[w, 0:2 * padded_planes, :] = x_ref[w]
    for e in range(devices // 2):
        re = x_ref[devices + e, 0:padded_planes, :]
        im = x_ref[devices + e, padded_planes:2 * padded_planes, :]
        out_ref[2 * e, 2 * padded_planes:3 * padded_planes, :] = jnp.where(
            low, re, pltpu.roll(im, half, 1)
        )
        out_ref[2 * e + 1, 2 * padded_planes:3 * padded_planes, :] = jnp.where(
            low, pltpu.roll(re, half, 1), im
        )
    for d in range(devices):
        out_ref[d, 3 * padded_planes:, :] = jnp.zeros((8, LANES), F32)


def inner_kernel(bands, volume, norm, place_ref, *refs):
    kc_ref = refs[0]
    coefs = refs[1:1 + bands]
    fields = refs[1 + bands:1 + 2 * bands]
    in_ref = refs[1 + 2 * bands]
    out_refs = refs[2 + 2 * bands:]
    devices = in_ref.shape[0]
    padded_planes = (in_ref.shape[1] - 8) // 3
    half = LANES // 2
    padded = coefs[0].shape[2]
    me, mine = place_ref[0], place_ref[1]
    low = lax.broadcasted_iota(jnp.int32, (padded_planes, LANES), 1) < half

    def fold(x):
        rows = x.shape[0]
        total = x[0:8]
        for at in range(8, rows, 8):
            total = total + x[at:at + 8]
        return total

    kc = kc_ref[...]
    kc_re, kc_im = kc[:, :padded], kc[:, padded:]
    sums = []
    for m in range(bands):
        c_re, c_im = coefs[m][:, 0, :], coefs[m][:, 1, :]
        sums.append([fold(c_re * kc_re + c_im * kc_im), fold(c_re * kc_im - c_im * kc_re)])
    local = [[jnp.zeros((8, LANES), F32), jnp.zeros((8, LANES), F32)] for _ in range(bands)]
    for d in range(devices):
        value = in_ref[d, 0:3 * padded_planes, :]
        re, im, rest = value[:padded_planes], value[padded_planes:2 * padded_planes], value[2 * padded_planes:]
        turned = pltpu.roll(rest, half, 1)
        other = jnp.concatenate([im, -re, jnp.where(low, turned, -turned)], axis=0)
        for m in range(bands):
            col = fields[m][d, 0:3 * padded_planes, :]
            local[m][0] = local[m][0] + fold(col * value)
            local[m][1] = local[m][1] + fold(col * other)
    lane = lax.broadcasted_iota(jnp.int32, (8, LANES), 1)
    row = lax.broadcasted_iota(jnp.int32, (8, LANES), 0)
    tile = jnp.zeros((8, LANES), F32)
    for m in range(bands):
        at = lax.rem(me + m, bands)
        for part, sign in ((0, 1.0), (1, -1.0)):
            partial = sums[m][part] + volume * local[m][part]
            scalar = jnp.sum(jnp.sum(partial, axis=1, keepdims=True), axis=0, keepdims=True)
            tile = jnp.where((lane == at) & (row == part), sign * norm * scalar, tile)
    for k in range(devices):
        out_refs[k][0:3 * padded_planes, :] = in_ref[lax.rem(mine + k, devices), 0:3 * padded_planes, :]
        out_refs[k][3 * padded_planes:, :] = tile


def final_kernel(volume, devices, me_ref, len_ref, *refs):
    ret_refs = refs[:devices]
    kc_ref, whi_ref, wlo_ref, sc_ref, ss_ref, out_ref, sub_ref, stack_ref = refs[devices:]
    padded_planes = (ret_refs[0].shape[0] - 8) // 3
    sticks, _, padded = out_ref.shape
    half = LANES // 2
    bands = sub_ref.shape[2]
    total = jnp.zeros((8, LANES), F32)
    me = me_ref[0]
    for k in range(devices):
        value = ret_refs[k][...]
        base = pl.multiple_of(lax.rem(me + devices - k, devices) * padded_planes, 8)
        total = total + value[3 * padded_planes:]
        rest = value[2 * padded_planes:3 * padded_planes]
        re = jnp.concatenate([value[:padded_planes], rest[:, :half]], axis=1)
        im = jnp.concatenate([value[padded_planes:2 * padded_planes], rest[:, half:]], axis=1)
        c = sc_ref[pl.ds(base, padded_planes), :]
        s = ss_ref[pl.ds(base, padded_planes), :]
        stack_ref[pl.ds(2 * base, padded_planes), :sticks] = re * c - im * s
        stack_ref[pl.ds(2 * base + padded_planes, padded_planes), :sticks] = re * s + im * c
    turned = jnp.transpose(stack_ref[...])[:sticks]
    local = dot3(split(turned), (whi_ref[...], wlo_ref[...])) * volume
    position = lax.broadcasted_iota(jnp.int32, (sticks, padded), 1).astype(F32)
    kept = position < len_ref[:, 0:1]
    kc = kc_ref[...]
    out_ref[:, 0, :] = jnp.where(kept, kc[:, :padded] + local[:, :padded], 0.0)
    out_ref[:, 1, :] = jnp.where(kept, kc[:, padded:] + local[:, padded:], 0.0)
    sub_ref[:, 0, :] = total[0:2, :bands]


def shards(bands, devices, coefficients, stick_col, stick_row, stick_length, plane_of_slot, potential):
    extent = plane_of_slot.shape[0]
    sticks = coefficients.shape[1]
    padded = coefficients.shape[3]
    total_sticks = stick_col.shape[0]
    planes = potential.shape[0]
    padded_planes = up8(planes)
    if sticks != LANES + LANES // 2 or devices % 2 or planes % 2:
        raise ValueError("sizes")
    rows = sum(row_blocks())
    volume = 1.0 / (extent * extent * extent)
    me = lax.axis_index("tg").astype(jnp.int32)
    coef = coefficients.reshape(sticks, 2, padded)

    length, row, col = (v.reshape(-1, LANES) for v in (stick_length, stick_row, stick_col))
    slots = plane_of_slot.reshape(devices, planes)
    if padded_planes > planes:
        slots = jnp.pad(slots, ((0, 0), (0, padded_planes - planes)), constant_values=-1)
    slots = slots.reshape(1, devices * padded_planes)
    windows = total_sticks // LANES
    smem = pl.BlockSpec(memory_space=pltpu.SMEM)
    vmem = pl.BlockSpec(memory_space=pltpu.VMEM)

    block = 3 * padded_planes
    total_planes = devices * padded_planes
    sent, kc, lengths, whi, wlo, shift_cos, shift_sin = pl.pallas_call(
        functools.partial(wave_kernel, extent),
        out_shape=(
            jax.ShapeDtypeStruct((devices, block, LANES), F32),
            jax.ShapeDtypeStruct((sticks, 2 * padded), F32),
            jax.ShapeDtypeStruct((sticks, LANES), F32),
            jax.ShapeDtypeStruct((2 * total_planes, 2 * padded), BF16),
            jax.ShapeDtypeStruct((2 * total_planes, 2 * padded), BF16),
            jax.ShapeDtypeStruct((total_planes, sticks), F32),
            jax.ShapeDtypeStruct((total_planes, sticks), F32),
        ),
        in_specs=[smem] + [vmem] * 5,
        compiler_params=params(),
        name="wave_to_planes",
    )(me.reshape(1), length, row, col, slots, coef)

    received = lax.all_to_all(sent, "tg", split_axis=0, concat_axis=0, tiled=True)

    window_list = jax.ShapeDtypeStruct((windows, LANES), jnp.int32)
    longer_list = jax.ShapeDtypeStruct((windows + 1, LANES), jnp.int32)
    stick_map, first, source, target, row_w, col_w = pl.pallas_call(
        functools.partial(map_kernel, extent, sticks),
        out_shape=(
            jax.ShapeDtypeStruct((LANES, LANES), jnp.int32),
            jax.ShapeDtypeStruct((8, LANES), jnp.int32),
            window_list,
            window_list,
            longer_list,
            longer_list,
        ),
        compiler_params=params(),
        cost_estimate=cost(4e9, 1e5),
        name="stick_map",
    )(row, col)

    weighted = pl.pallas_call(
        functools.partial(plane_kernel, planes),
        out_shape=jax.ShapeDtypeStruct((devices, block + 8, LANES), F32),
        in_specs=[smem] + [vmem] * 12 + [pl.BlockSpec(memory_space=pl.ANY)],
        out_specs=vmem,
        scratch_shapes=[
            pltpu.VMEM((windows, 2 * padded_planes, LANES), F32),
            pltpu.VMEM((windows + 1, 2 * padded_planes, LANES), F32),
            pltpu.VMEM((padded_planes * rows, LANES), F32),
            pltpu.VMEM((padded_planes * rows, LANES), F32),
            pltpu.VMEM(potential.shape, F32),
            pltpu.SemaphoreType.DMA,
        ],
        compiler_params=params(),
        cost_estimate=cost(2e10, 1e7),
        name="planes",
    )(first, stick_map, source, target, row_w, col_w, received, *[jnp.asarray(t) for t in tables(extent)], potential)

    coefs, fields = [coef], [received]
    for shift in range(1, bands):
        ring = [((b + shift) % bands, b) for b in range(bands)]
        coefs.append(lax.ppermute(coef, "band", ring))
        fields.append(lax.ppermute(received, "band", ring))
    band = lax.axis_index("band").astype(jnp.int32)
    norm = 1.0 / (total_sticks * padded)
    places = jnp.stack([band, me])
    outgoing = pl.pallas_call(
        functools.partial(inner_kernel, bands, volume, norm),
        out_shape=(jax.ShapeDtypeStruct((block + 8, LANES), F32),) * devices,
        in_specs=[smem] + [vmem] * (2 + 2 * bands),
        compiler_params=params(),
        name="inner",
    )(places, kc, *coefs, *fields, weighted)

    returned = [outgoing[0]]
    for k in range(1, devices):
        ring = [(d, (d + k) % devices) for d in range(devices)]
        returned.append(lax.ppermute(outgoing[k], "tg", ring))
    applied, subspace = pl.pallas_call(
        functools.partial(final_kernel, volume, devices),
        out_shape=(
            jax.ShapeDtypeStruct((sticks, 2, padded), F32),
            jax.ShapeDtypeStruct((2, 1, bands), F32),
        ),
        in_specs=[smem] + [vmem] * (6 + devices),
        scratch_shapes=[pltpu.VMEM((2 * total_planes, 2 * LANES), F32)],
        compiler_params=params(),
        name="planes_to_wave",
    )(me.reshape(1), lengths, *returned, kc, whi, wlo, shift_cos, shift_sin)
    return applied.reshape(1, sticks, 2, padded), subspace


def solution(mesh):
    in_specs = (P("band", "tg", None, None), P(), P(), P(), P(), P("tg", None, None))
    out_specs = (P("band", "tg", None, None), P(None, "band", None))
    body = functools.partial(shards, mesh.shape["band"], mesh.shape["tg"])
    return jax.shard_map(body, mesh=mesh, in_specs=in_specs, out_specs=out_specs, check_vma=False)
```

```python
import functools
import math

import jax
import jax.numpy as jnp
import ml_dtypes
import numpy as np
from jax import lax
from jax.experimental import pallas as pl
from jax.experimental.pallas import tpu as pltpu
from jax.sharding import PartitionSpec as P

RADIUS = 48
LANES = 128
F32 = jnp.float32
BF16 = jnp.bfloat16


def up8(n):
    return -(-n // 8) * 8


def split(x):
    hi = x.astype(BF16)
    return hi, (x - hi.astype(F32)).astype(BF16)


def dot3(a, b, dims=((1,), (0,))):
    def dot(x, y):
        return lax.dot_general(x, y, (dims, ((), ())), preferred_element_type=F32)

    return dot(a[0], b[0]) + (dot(a[0], b[1]) + dot(a[1], b[0]))


def trig(product, extent):
    n = product - extent * jnp.floor(product * (1.0 / extent) + 0.5)
    quarter = extent / 4.0
    unit = 2.0 * math.pi / extent

    def sine(m):
        u = m * unit
        v = u * u
        s = 1.0 / 6227020800.0
        for term in (-39916800.0, 362880.0, -5040.0, 120.0, -6.0, 1.0):
            s = s * v + 1.0 / term
        return u * s

    folded = jnp.where(
        jnp.abs(n) > quarter, jnp.where(n > 0, 2.0 * quarter, -2.0 * quarter) - n, n
    )
    return sine(quarter - jnp.abs(n)), sine(folded)


def pair(table):
    hi = table.astype(np.float32).astype(ml_dtypes.bfloat16)
    lo = (table - hi.astype(np.float64)).astype(ml_dtypes.bfloat16)
    return hi, lo


def row_blocks():
    even = -(-(RADIUS + 1) // 16) * 16
    odd = -(-RADIUS // 16) * 16
    return even, odd


@functools.cache
def tables(extent):
    kept = 2 * RADIUS + 1
    half = extent // 2
    grid = np.arange(extent)
    freq = np.arange(kept) - RADIUS

    def angles(f, g):
        a = 2.0 * np.pi * ((f[:, None] * g[None, :]) % extent) / extent
        return np.cos(a), np.sin(a)

    cos, sin = angles(freq, grid)
    wide = 2 * LANES
    x_table = np.zeros((wide, 2 * wide))
    x_table[:kept, :extent] = cos
    x_table[LANES:LANES + kept, :extent] = -sin
    x_table[:kept, wide:wide + extent] = sin
    x_table[LANES:LANES + kept, wide:wide + extent] = cos
    forward, back = [], []
    for offset, rows in zip((0, 1), row_blocks()):
        cos, sin = angles(freq[offset::2], grid[:half])
        count = cos.shape[0]
        table = np.zeros((2 * half, rows))
        table[:half, :count] = cos.T
        table[half:, :count] = sin.T
        hi, lo = pair(table)
        forward.append(np.concatenate([hi, hi, lo], axis=1))
        table = np.zeros((2 * rows, half))
        table[:count] = cos
        table[rows:rows + count] = sin
        hi, lo = pair(table)
        back.append(np.concatenate([hi, hi, lo], axis=1))
    hi, lo = pair(x_table)
    x_forward = np.concatenate([hi, hi, lo], axis=0)
    hi, lo = pair(x_table.T.copy())
    x_back = np.concatenate([hi, hi, lo], axis=0)
    return (*forward, x_forward, x_back, *back)


def params(megabytes):
    return pltpu.CompilerParams(vmem_limit_bytes=int(min(megabytes, 56) * 2**20))


def cost(flops, nbytes):
    return pl.CostEstimate(flops=int(flops), bytes_accessed=int(nbytes), transcendentals=0)


def wave_kernel(extent, me_ref, length_ref, row_ref, col_ref, plane_ref, coef_ref, out_ref, kc_ref, len_ref, whi_ref, wlo_ref, sc_ref, ss_ref):
    devices = out_ref.shape[0]
    sticks, _, padded = coef_ref.shape
    padded_planes = plane_ref.shape[1] // devices
    me = me_ref[0]
    half = LANES // 2
    lead = (me * sticks) // LANES
    odd = (me * sticks) % LANES != 0

    def own(ref):
        first, second = ref[pl.ds(lead, 1), :], ref[pl.ds(lead + 1, 1), :]
        both = jnp.concatenate([first, second], axis=1)
        return jnp.where(odd, both[:, half:], both[:, :sticks])

    length_row = own(length_ref).astype(F32)
    at_row = own(row_ref)
    at_col = own(col_ref)
    at_row = jnp.where(at_row <= RADIUS, at_row, at_row - extent).astype(F32)
    at_col = jnp.where(at_col <= RADIUS, at_col, at_col - extent).astype(F32)
    square_row = at_row * at_row + at_col * at_col
    spare = jnp.ones((1, 2 * LANES - sticks), F32)
    aux = jnp.concatenate(
        [
            jnp.broadcast_to(jnp.concatenate([length_row, spare], axis=1), (LANES // 2, 2 * LANES)),
            jnp.broadcast_to(jnp.concatenate([square_row, spare], axis=1), (LANES // 2, 2 * LANES)),
        ],
        axis=0,
    )
    aux_col = jnp.transpose(aux)[:sticks]
    len_ref[...] = aux_col
    length = aux_col[:, 0:1]
    square = aux_col[:, LANES // 2:LANES // 2 + 1]
    middle = (length - 1.0) * 0.5
    position = lax.broadcasted_iota(jnp.int32, (sticks, padded), 1).astype(F32)
    kept = (position < length).astype(F32)
    kinetic = (square + (position - middle) * (position - middle)) * (1.0 / (RADIUS * RADIUS))
    wave = jnp.concatenate([coef_ref[:, 0, :] * kept, coef_ref[:, 1, :] * kept], axis=1)
    kc_ref[...] = wave * jnp.concatenate([kinetic, kinetic], axis=1)

    total = plane_ref.shape[1]
    plane_row = jnp.broadcast_to(plane_ref[...].astype(F32), (LANES, total))
    plane_col = jnp.transpose(plane_row)[:, 0:1]
    real = (plane_col >= 0.0).astype(F32)
    plane_col = jnp.maximum(plane_col, 0.0)
    harmonic = lax.broadcasted_iota(jnp.int32, (total, padded), 1).astype(F32)
    cos, sin = trig(plane_col * harmonic, extent)
    cos, sin = cos * real, sin * real
    parts = []
    for d in range(devices):
        c = cos[d * padded_planes:(d + 1) * padded_planes]
        s = sin[d * padded_planes:(d + 1) * padded_planes]
        parts.append(jnp.concatenate([c, -s], axis=1))
        parts.append(jnp.concatenate([s, c], axis=1))
    table = split(jnp.concatenate(parts, axis=0))
    whi_ref[...] = table[0]
    wlo_ref[...] = table[1]
    shift_cos, shift_sin = trig(plane_col * ((length_row - 1.0) * 0.5), extent)
    sc_ref[...] = shift_cos
    ss_ref[...] = shift_sin
    raw = dot3(table, split(wave), ((1,), (1,)))
    for d in range(devices):
        at = 2 * d * padded_planes
        re, im = raw[at:at + padded_planes], raw[at + padded_planes:at + 2 * padded_planes]
        c = shift_cos[d * padded_planes:(d + 1) * padded_planes]
        s = shift_sin[d * padded_planes:(d + 1) * padded_planes]
        along_re = re * c + im * s
        along_im = im * c - re * s
        out_ref[d, 0:padded_planes, :] = along_re[:, :LANES]
        out_ref[d, padded_planes:2 * padded_planes, :] = along_im[:, :LANES]
        out_ref[d, 2 * padded_planes:3 * padded_planes, :] = jnp.concatenate(
            [along_re[:, LANES:], along_im[:, LANES:]], axis=1
        )


def window_row(values, sticks):
    line = jnp.concatenate([values[i:i + 1] for i in range(values.shape[0])], axis=1)
    starts = range(0, line.shape[1], sticks)
    parts = [line[:, at:at + LANES] for at in starts]
    parts += [line[:, at + LANES:at + sticks] for at in starts]
    return jnp.concatenate(parts, axis=1)


def map_kernel(extent, sticks, in_row_ref, in_col_ref, map_ref, first_ref, src_ref, dst_ref, row_ref, col_ref):
    windows = src_ref.shape[0]
    total = windows * LANES

    def signed(ref):
        value = ref[...]
        return window_row(jnp.where(value <= RADIUS, value, value - extent) + RADIUS, sticks)

    def dot(x, y, dims=((1,), (0,))):
        return lax.dot_general(x, y, (dims, ((), ())), preferred_element_type=F32)

    def bits(condition):
        return condition.astype(F32).astype(BF16)

    nt = ((1,), (1,))
    own_row, own_col = signed(in_row_ref), signed(in_col_ref)
    own_row = (own_row & 1) * row_blocks()[0] + (own_row >> 1)
    tall = lax.broadcasted_iota(jnp.int32, (LANES, total), 0)
    place = lax.broadcasted_iota(jnp.int32, (LANES, total), 1)
    in_col = tall == own_col
    row_hot, col_hot = bits(tall == own_row), bits(in_col)
    down = lax.broadcasted_iota(jnp.int32, (LANES, LANES), 0)
    across = lax.broadcasted_iota(jnp.int32, (LANES, LANES), 1)
    before = bits(down < across)
    after = bits(down > across)
    upto = bits(down >= across)
    ones = jnp.ones((LANES, LANES), BF16)
    taken = dot(row_hot, col_hot, nt)
    taken_t = dot(col_hot, row_hot, nt)
    taken_b, taken_tb = taken.astype(BF16), taken_t.astype(BF16)
    start = dot(dot(after, taken_b).astype(BF16), ones)
    end = start + dot(taken_b, ones)
    start_t = dot(ones, dot(taken_tb, before).astype(BF16))
    limit = windows - 1.0
    first = jnp.minimum(jnp.floor(start * (1.0 / LANES)), limit)
    code = jnp.where(taken > 0.5, dot(taken_b, before) + start - LANES * first, -1.0)
    map_ref[...] = code.astype(jnp.int32)
    first_ref[...] = jnp.minimum(jnp.floor(start_t[0:8] * (1.0 / LANES)), limit).astype(jnp.int32)

    spot = place.astype(F32)
    in_range = (spot >= start[:, 0:1]) & (spot < end[:, 0:1])
    sorted_hot = bits(in_range)
    sorted_row = jnp.sum(jnp.where(in_range, tall, 0).astype(F32), axis=0, keepdims=True)
    sorted_rank = spot[0:1] - jnp.sum(jnp.where(in_range, start[:, 0:1], 0.0), axis=0, keepdims=True)
    counts = dot(dot(upto, taken_tb).astype(BF16), sorted_hot)
    sorted_col = jnp.sum((counts <= sorted_rank).astype(F32), axis=0, keepdims=True)
    names = place + 1
    name_hi = dot(jnp.where(in_col, names >> 6, 0).astype(F32).astype(BF16), row_hot, nt)
    name_lo = dot(jnp.where(in_col, names & 63, 0).astype(F32).astype(BF16), row_hot, nt)
    named = dot(name_hi.astype(BF16), sorted_hot) * 64.0 + dot(name_lo.astype(BF16), sorted_hot)
    source = jnp.sum(jnp.where(tall.astype(F32) == sorted_col, named, 0.0), axis=0, keepdims=True) - 1.0
    place_t = dot(after, taken_tb) + start_t
    place_hi = jnp.floor(place_t * (1.0 / 64.0))
    place_lo = place_t - 64.0 * place_hi
    placed = dot(place_hi.astype(BF16), row_hot) * 64.0 + dot(place_lo.astype(BF16), row_hot)
    target = jnp.sum(jnp.where(in_col, placed, 0.0), axis=0, keepdims=True)
    for values, ref in ((source, src_ref), (target, dst_ref), (sorted_row, row_ref), (sorted_col, col_ref)):
        values = values.astype(jnp.int32)
        for w in range(windows):
            ref[w:w + 1, :] = values[:, w * LANES:(w + 1) * LANES]
    row_ref[windows:windows + 1, :] = jnp.full((1, LANES), -1, jnp.int32)
    col_ref[windows:windows + 1, :] = jnp.zeros((1, LANES), jnp.int32)


def lane_take(x, index):
    return jnp.take_along_axis(x, index, axis=1, mode="promise_in_bounds")


def plane_kernel(
    planes, first_ref, map_ref, src_ref, dst_ref, row_ref, col_ref, recv_ref,
    y_even, y_odd, x_forward, x_back, back_even, back_odd,
    pot_hbm, out_ref, x_ref, s_ref, gr_ref, gi_ref, pot_ref, sem,
):
    devices = recv_ref.shape[0]
    padded_planes = recv_ref.shape[1] // 3
    windows = x_ref.shape[0]
    rows = gr_ref.shape[0] // padded_planes
    extent = pot_ref.shape[1]
    half = LANES // 2
    fetch = pltpu.make_async_copy(pot_hbm, pot_ref, sem)
    fetch.start()

    low = lax.broadcasted_iota(jnp.int32, (padded_planes, LANES), 1) < half
    for d in range(devices):
        x_ref[d] = recv_ref[d, 0:2 * padded_planes, :]
    for e in range(devices // 2):
        first = recv_ref[2 * e, 2 * padded_planes:3 * padded_planes, :]
        second = recv_ref[2 * e + 1, 2 * padded_planes:3 * padded_planes, :]
        x_ref[devices + e, 0:padded_planes, :] = jnp.where(low, first, pltpu.roll(second, half, 1))
        x_ref[devices + e, padded_planes:2 * padded_planes, :] = jnp.where(
            low, pltpu.roll(first, half, 1), second
        )

    blocks = padded_planes // 8
    grids = (gr_ref, gi_ref)

    def reorder(order_ref, from_ref, to_ref):
        @pl.loop(0, windows, unroll=4)
        def _(v):
            order = jnp.broadcast_to(order_ref[pl.ds(v, 1), :], (8, LANES))
            index = order & (LANES - 1)
            window = order >> 7
            for j in range(2 * blocks):
                value = jnp.zeros((8, LANES), F32)
                for w in range(windows):
                    value = jnp.where(window == w, lane_take(from_ref[w, 8 * j:8 * j + 8, :], index), value)
                to_ref[v, 8 * j:8 * j + 8, :] = value

    reorder(src_ref, x_ref, s_ref)

    @pl.loop(0, rows, unroll=8)
    def _(r):
        first = first_ref[0, r]
        code = jnp.broadcast_to(map_ref[pl.ds(r, 1), :], (8, LANES))
        index = code & (LANES - 1)
        window = code >> 7
        for j in range(2 * blocks):
            lead = lane_take(s_ref[first, 8 * j:8 * j + 8, :], index)
            trail = lane_take(s_ref[first + 1, 8 * j:8 * j + 8, :], index)
            value = jnp.where(window == 0, lead, jnp.where(window == 1, trail, 0.0))
            part, at = j // blocks, 8 * (j % blocks)
            grids[part][pl.ds(r + at * rows, 8, stride=rows), :] = value

    fetch.wait()
    even_rows, odd_rows = row_blocks()
    folded = extent // 2
    group = next(g for g in (8, 4, 2) if planes % g == 0)

    def dot(x, y):
        return jnp.dot(x, y, preferred_element_type=F32)

    def stack(x, axis):
        hi, lo = split(x)
        return jnp.concatenate([hi, lo, hi], axis=axis)

    def times_wave(both, cut, sign):
        cos, sin = both[:cut], both[cut:]
        re = cos[:, :LANES] - sign * sin[:, LANES:]
        im = cos[:, LANES:] + sign * sin[:, :LANES]
        return re, im

    @pl.loop(0, planes // group)
    def _(step):
        lines = []
        for t in range(group):
            base = pl.multiple_of((step * group + t) * rows, 16)
            even, odd = pl.ds(base, even_rows), pl.ds(base + even_rows, odd_rows)
            parts = []
            for pick, table, size in ((even, y_even, even_rows), (odd, y_odd, odd_rows)):
                spectrum = jnp.concatenate([gr_ref[pick, :], gi_ref[pick, :]], axis=1)
                parts.append(times_wave(dot(table[...], stack(spectrum, 0)), folded, 1.0))
            (e_re, e_im), (o_re, o_im) = parts
            lines.append(jnp.concatenate([e_re + o_re, e_im + o_im], axis=1))
            lines.append(jnp.concatenate([e_re - o_re, e_im - o_im], axis=1))
        field = dot(stack(jnp.concatenate(lines, axis=0), 1), x_forward[...])
        wide = field.shape[1] // 2
        spare = jnp.zeros((extent, wide - extent), F32)
        weighted = []
        for t in range(group):
            v = jnp.concatenate([pot_ref[step * group + t], spare], axis=1)
            mine = field[t * extent:(t + 1) * extent]
            weighted.append(jnp.concatenate([mine[:, :wide] * v, mine[:, wide:] * v], axis=1))
        back = dot(stack(jnp.concatenate(weighted, axis=0), 1), x_back[...])
        for t in range(group):
            base = pl.multiple_of((step * group + t) * rows, 16)
            even, odd = pl.ds(base, even_rows), pl.ds(base + even_rows, odd_rows)
            upper = back[t * extent:t * extent + folded]
            lower = back[t * extent + folded:(t + 1) * extent]
            for pick, table, size, value in (
                (even, back_even, even_rows, upper + lower), (odd, back_odd, odd_rows, upper - lower)
            ):
                re, im = times_wave(dot(table[...], stack(value, 0)), size, -1.0)
                gr_ref[pick, :] = re
                gi_ref[pick, :] = im

    @pl.loop(0, rows, unroll=8)
    def _(r):
        first = first_ref[0, r]
        values = []
        for j in range(2 * blocks):
            part, at = j // blocks, 8 * (j % blocks)
            values.append(grids[part][pl.ds(r + at * rows, 8, stride=rows), :])
        for t in range(2):
            index = jnp.broadcast_to(col_ref[pl.ds(first + t, 1), :], (8, LANES))
            hit = jnp.broadcast_to(row_ref[pl.ds(first + t, 1), :], (8, LANES)) == r
            for j in range(2 * blocks):
                pltpu.store(
                    s_ref.at[first + t, 8 * j:8 * j + 8, :], lane_take(values[j], index), mask=hit
                )

    reorder(dst_ref, s_ref, x_ref)
    for w in range(devices):
        out_ref[w, 0:2 * padded_planes, :] = x_ref[w]
    for e in range(devices // 2):
        re = x_ref[devices + e, 0:padded_planes, :]
        im = x_ref[devices + e, padded_planes:2 * padded_planes, :]
        out_ref[2 * e, 2 * padded_planes:3 * padded_planes, :] = jnp.where(
            low, re, pltpu.roll(im, half, 1)
        )
        out_ref[2 * e + 1, 2 * padded_planes:3 * padded_planes, :] = jnp.where(
            low, pltpu.roll(re, half, 1), im
        )
    for d in range(devices):
        out_ref[d, 3 * padded_planes:, :] = jnp.zeros((8, LANES), F32)


def inner_kernel(bands, volume, norm, place_ref, *refs):
    kc_ref = refs[0]
    coefs = refs[1:1 + bands]
    fields = refs[1 + bands:1 + 2 * bands]
    in_ref = refs[1 + 2 * bands]
    out_refs = refs[2 + 2 * bands:]
    devices = in_ref.shape[0]
    padded_planes = (in_ref.shape[1] - 8) // 3
    half = LANES // 2
    padded = coefs[0].shape[2]
    me, mine = place_ref[0], place_ref[1]
    low = lax.broadcasted_iota(jnp.int32, (padded_planes, LANES), 1) < half

    def fold(x):
        rows = x.shape[0]
        total = x[0:8]
        for at in range(8, rows, 8):
            total = total + x[at:at + 8]
        return total

    kc = kc_ref[...]
    kc_re, kc_im = kc[:, :padded], kc[:, padded:]
    sums = []
    for m in range(bands):
        c_re, c_im = coefs[m][:, 0, :], coefs[m][:, 1, :]
        sums.append([fold(c_re * kc_re + c_im * kc_im), fold(c_re * kc_im - c_im * kc_re)])
    local = [[jnp.zeros((8, LANES), F32), jnp.zeros((8, LANES), F32)] for _ in range(bands)]
    for d in range(devices):
        value = in_ref[d, 0:3 * padded_planes, :]
        re, im, rest = value[:padded_planes], value[padded_planes:2 * padded_planes], value[2 * padded_planes:]
        turned = pltpu.roll(rest, half, 1)
        other = jnp.concatenate([im, -re, jnp.where(low, turned, -turned)], axis=0)
        for m in range(bands):
            col = fields[m][d, 0:3 * padded_planes, :]
            local[m][0] = local[m][0] + fold(col * value)
            local[m][1] = local[m][1] + fold(col * other)
    lane = lax.broadcasted_iota(jnp.int32, (8, LANES), 1)
    row = lax.broadcasted_iota(jnp.int32, (8, LANES), 0)
    tile = jnp.zeros((8, LANES), F32)
    for m in range(bands):
        at = lax.rem(me + m, bands)
        for part, sign in ((0, 1.0), (1, -1.0)):
            partial = sums[m][part] + volume * local[m][part]
            scalar = jnp.sum(jnp.sum(partial, axis=1, keepdims=True), axis=0, keepdims=True)
            tile = jnp.where((lane == at) & (row == part), sign * norm * scalar, tile)
    for k in range(devices):
        out_refs[k][0:3 * padded_planes, :] = in_ref[lax.rem(mine + k, devices), 0:3 * padded_planes, :]
        out_refs[k][3 * padded_planes:, :] = tile


def final_kernel(volume, devices, me_ref, len_ref, *refs):
    ret_refs = refs[:devices]
    kc_ref, whi_ref, wlo_ref, sc_ref, ss_ref, out_ref, sub_ref, stack_ref = refs[devices:]
    padded_planes = (ret_refs[0].shape[0] - 8) // 3
    sticks, _, padded = out_ref.shape
    half = LANES // 2
    bands = sub_ref.shape[2]
    total = jnp.zeros((8, LANES), F32)
    me = me_ref[0]
    for k in range(devices):
        value = ret_refs[k][...]
        base = pl.multiple_of(lax.rem(me + devices - k, devices) * padded_planes, 8)
        total = total + value[3 * padded_planes:]
        rest = value[2 * padded_planes:3 * padded_planes]
        re = jnp.concatenate([value[:padded_planes], rest[:, :half]], axis=1)
        im = jnp.concatenate([value[padded_planes:2 * padded_planes], rest[:, half:]], axis=1)
        c = sc_ref[pl.ds(base, padded_planes), :]
        s = ss_ref[pl.ds(base, padded_planes), :]
        stack_ref[pl.ds(2 * base, padded_planes), :sticks] = re * c - im * s
        stack_ref[pl.ds(2 * base + padded_planes, padded_planes), :sticks] = re * s + im * c
    turned = jnp.transpose(stack_ref[...])[:sticks]
    local = dot3(split(turned), (whi_ref[...], wlo_ref[...])) * volume
    position = lax.broadcasted_iota(jnp.int32, (sticks, padded), 1).astype(F32)
    kept = position < len_ref[:, 0:1]
    kc = kc_ref[...]
    out_ref[:, 0, :] = jnp.where(kept, kc[:, :padded] + local[:, :padded], 0.0)
    out_ref[:, 1, :] = jnp.where(kept, kc[:, padded:] + local[:, padded:], 0.0)
    sub_ref[:, 0, :] = total[0:2, :bands]


def shards(bands, devices, coefficients, stick_col, stick_row, stick_length, plane_of_slot, potential):
    extent = plane_of_slot.shape[0]
    sticks = coefficients.shape[1]
    padded = coefficients.shape[3]
    total_sticks = stick_col.shape[0]
    planes = potential.shape[0]
    padded_planes = up8(planes)
    if sticks != LANES + LANES // 2 or devices % 2 or planes % 2:
        raise ValueError("sizes")
    rows = sum(row_blocks())
    volume = 1.0 / (extent * extent * extent)
    me = lax.axis_index("tg").astype(jnp.int32)
    coef = coefficients.reshape(sticks, 2, padded)

    length, row, col = (v.reshape(-1, LANES) for v in (stick_length, stick_row, stick_col))
    slots = plane_of_slot.reshape(devices, planes)
    if padded_planes > planes:
        slots = jnp.pad(slots, ((0, 0), (0, padded_planes - planes)), constant_values=-1)
    slots = slots.reshape(1, devices * padded_planes)
    windows = total_sticks // LANES
    smem = pl.BlockSpec(memory_space=pltpu.SMEM)
    vmem = pl.BlockSpec(memory_space=pltpu.VMEM)

    block = 3 * padded_planes
    total_planes = devices * padded_planes
    sent, kc, lengths, whi, wlo, shift_cos, shift_sin = pl.pallas_call(
        functools.partial(wave_kernel, extent),
        out_shape=(
            jax.ShapeDtypeStruct((devices, block, LANES), F32),
            jax.ShapeDtypeStruct((sticks, 2 * padded), F32),
            jax.ShapeDtypeStruct((sticks, LANES), F32),
            jax.ShapeDtypeStruct((2 * total_planes, 2 * padded), BF16),
            jax.ShapeDtypeStruct((2 * total_planes, 2 * padded), BF16),
            jax.ShapeDtypeStruct((total_planes, sticks), F32),
            jax.ShapeDtypeStruct((total_planes, sticks), F32),
        ),
        in_specs=[smem] + [vmem] * 5,
        compiler_params=params(8 + 8 * total_planes / 192),
        name="wave_to_planes",
    )(me.reshape(1), length, row, col, slots, coef)

    received = lax.all_to_all(sent, "tg", split_axis=0, concat_axis=0, tiled=True)

    window_list = jax.ShapeDtypeStruct((windows, LANES), jnp.int32)
    longer_list = jax.ShapeDtypeStruct((windows + 1, LANES), jnp.int32)
    stick_map, first, source, target, row_w, col_w = pl.pallas_call(
        functools.partial(map_kernel, extent, sticks),
        out_shape=(
            jax.ShapeDtypeStruct((LANES, LANES), jnp.int32),
            jax.ShapeDtypeStruct((8, LANES), jnp.int32),
            window_list,
            window_list,
            longer_list,
            longer_list,
        ),
        compiler_params=params(14 * total_sticks / 1536),
        cost_estimate=cost(4e9, 1e5),
        name="stick_map",
    )(row, col)

    weighted = pl.pallas_call(
        functools.partial(plane_kernel, planes),
        out_shape=jax.ShapeDtypeStruct((devices, block + 8, LANES), F32),
        in_specs=[smem] + [vmem] * 12 + [pl.BlockSpec(memory_space=pl.ANY)],
        out_specs=vmem,
        scratch_shapes=[
            pltpu.VMEM((windows, 2 * padded_planes, LANES), F32),
            pltpu.VMEM((windows + 1, 2 * padded_planes, LANES), F32),
            pltpu.VMEM((padded_planes * rows, LANES), F32),
            pltpu.VMEM((padded_planes * rows, LANES), F32),
            pltpu.VMEM(potential.shape, F32),
            pltpu.SemaphoreType.DMA,
        ],
        compiler_params=params(36),
        cost_estimate=cost(2e10, 1e7),
        name="planes",
    )(first, stick_map, source, target, row_w, col_w, received, *[jnp.asarray(t) for t in tables(extent)], potential)

    coefs, fields = [coef], [received]
    for shift in range(1, bands):
        ring = [((b + shift) % bands, b) for b in range(bands)]
        coefs.append(lax.ppermute(coef, "band", ring))
        fields.append(lax.ppermute(received, "band", ring))
    band = lax.axis_index("band").astype(jnp.int32)
    norm = 1.0 / (total_sticks * padded)
    places = jnp.stack([band, me])
    outgoing = pl.pallas_call(
        functools.partial(inner_kernel, bands, volume, norm),
        out_shape=(jax.ShapeDtypeStruct((block + 8, LANES), F32),) * devices,
        in_specs=[smem] + [vmem] * (2 + 2 * bands),
        compiler_params=params(6 + 1.5 * bands),
        name="inner",
    )(places, kc, *coefs, *fields, weighted)

    returned = [outgoing[0]]
    for k in range(1, devices):
        ring = [(d, (d + k) % devices) for d in range(devices)]
        returned.append(lax.ppermute(outgoing[k], "tg", ring))
    applied, subspace = pl.pallas_call(
        functools.partial(final_kernel, volume, devices),
        out_shape=(
            jax.ShapeDtypeStruct((sticks, 2, padded), F32),
            jax.ShapeDtypeStruct((2, 1, bands), F32),
        ),
        in_specs=[smem] + [vmem] * (6 + devices),
        scratch_shapes=[pltpu.VMEM((2 * total_planes, 2 * LANES), F32)],
        compiler_params=params(6 + 6 * total_planes / 192),
        name="planes_to_wave",
    )(me.reshape(1), lengths, *returned, kc, whi, wlo, shift_cos, shift_sin)
    return applied.reshape(1, sticks, 2, padded), subspace


def solution(mesh):
    in_specs = (P("band", "tg", None, None), P(), P(), P(), P(), P("tg", None, None))
    out_specs = (P("band", "tg", None, None), P(None, "band", None))
    body = functools.partial(shards, mesh.shape["band"], mesh.shape["tg"])
    return jax.shard_map(body, mesh=mesh, in_specs=in_specs, out_specs=out_specs, check_vma=False)
```

```python
import functools
import math

import jax
import jax.numpy as jnp
import ml_dtypes
import numpy as np
from jax import lax
from jax.experimental import pallas as pl
from jax.experimental.pallas import tpu as pltpu
from jax.sharding import PartitionSpec as P

RADIUS = 48
LANES = 128
F32 = jnp.float32
BF16 = jnp.bfloat16


def up8(n):
    return -(-n // 8) * 8


def split(x):
    hi = x.astype(BF16)
    return hi, (x - hi.astype(F32)).astype(BF16)


def dot3(a, b, dims=((1,), (0,))):
    def dot(x, y):
        return lax.dot_general(x, y, (dims, ((), ())), preferred_element_type=F32)

    return dot(a[0], b[0]) + (dot(a[0], b[1]) + dot(a[1], b[0]))


def trig(product, extent):
    n = product - extent * jnp.floor(product * (1.0 / extent) + 0.5)
    quarter = extent / 4.0
    unit = 2.0 * math.pi / extent

    def sine(m):
        u = m * unit
        v = u * u
        s = 1.0 / 6227020800.0
        for term in (-39916800.0, 362880.0, -5040.0, 120.0, -6.0, 1.0):
            s = s * v + 1.0 / term
        return u * s

    folded = jnp.where(
        jnp.abs(n) > quarter, jnp.where(n > 0, 2.0 * quarter, -2.0 * quarter) - n, n
    )
    return sine(quarter - jnp.abs(n)), sine(folded)


def pair(table):
    hi = table.astype(np.float32).astype(ml_dtypes.bfloat16)
    lo = (table - hi.astype(np.float64)).astype(ml_dtypes.bfloat16)
    return hi, lo


def row_blocks():
    even = -(-(RADIUS + 1) // 16) * 16
    odd = -(-RADIUS // 16) * 16
    return even, odd


@functools.cache
def tables(extent):
    kept = 2 * RADIUS + 1
    half = extent // 2
    grid = np.arange(extent)
    freq = np.arange(kept) - RADIUS

    def angles(f, g):
        a = 2.0 * np.pi * ((f[:, None] * g[None, :]) % extent) / extent
        return np.cos(a), np.sin(a)

    cos, sin = angles(freq, grid)
    wide = 2 * LANES
    x_table = np.zeros((wide, 2 * wide))
    x_table[:kept, :extent] = cos
    x_table[LANES:LANES + kept, :extent] = -sin
    x_table[:kept, wide:wide + extent] = sin
    x_table[LANES:LANES + kept, wide:wide + extent] = cos
    forward, back = [], []
    for offset, rows in zip((0, 1), row_blocks()):
        cos, sin = angles(freq[offset::2], grid[:half])
        count = cos.shape[0]
        table = np.zeros((2 * half, rows))
        table[:half, :count] = cos.T
        table[half:, :count] = sin.T
        hi, lo = pair(table)
        forward.append(np.concatenate([hi, hi, lo], axis=1))
        table = np.zeros((2 * rows, half))
        table[:count] = cos
        table[rows:rows + count] = sin
        hi, lo = pair(table)
        back.append(np.concatenate([hi, hi, lo], axis=1))
    hi, lo = pair(x_table)
    x_forward = np.concatenate([hi, hi, lo], axis=0)
    hi, lo = pair(x_table.T.copy())
    x_back = np.concatenate([hi, hi, lo], axis=0)
    depth = x_back.shape[0] // 2
    rows = [x_forward, np.concatenate([x_back[:depth], x_back[depth:]], axis=1)]
    y_rows = np.zeros((2 * half, 2 * wide), hi.dtype)
    y_rows[:, :forward[0].shape[1]] = forward[0]
    y_rows[:, wide:wide + forward[1].shape[1]] = forward[1]
    rows.append(y_rows)
    for table in back:
        rows.append(np.pad(table, ((0, 0), (0, 2 * wide - table.shape[1]))))
    return np.concatenate(rows, axis=0)


def params(megabytes):
    return pltpu.CompilerParams(vmem_limit_bytes=int(min(megabytes, 56) * 2**20))


def fetch_all(sources, targets, sems):
    copies = [
        pltpu.make_async_copy(source, target, sems.at[i])
        for i, (source, target) in enumerate(zip(sources, targets))
    ]
    for copy in copies:
        copy.start()
    return copies


def cost(flops, nbytes):
    return pl.CostEstimate(flops=int(flops), bytes_accessed=int(nbytes), transcendentals=0)


def wave_kernel(
    extent, me_ref, length_hbm, row_hbm, col_hbm, plane_hbm, coef_hbm,
    out_ref, kc_ref, len_ref, whi_ref, wlo_ref, sc_ref, ss_ref,
    length_ref, row_ref, col_ref, plane_ref, coef_ref, sems,
):
    copies = fetch_all(
        (length_hbm, row_hbm, col_hbm, plane_hbm, coef_hbm),
        (length_ref, row_ref, col_ref, plane_ref, coef_ref),
        sems,
    )
    for copy in copies:
        copy.wait()
    devices = out_ref.shape[0]
    sticks, _, padded = coef_ref.shape
    padded_planes = plane_ref.shape[1] // devices
    me = me_ref[0]
    half = LANES // 2
    lead = (me * sticks) // LANES
    odd = (me * sticks) % LANES != 0

    def own(ref):
        first, second = ref[pl.ds(lead, 1), :], ref[pl.ds(lead + 1, 1), :]
        both = jnp.concatenate([first, second], axis=1)
        return jnp.where(odd, both[:, half:], both[:, :sticks])

    length_row = own(length_ref).astype(F32)
    at_row = own(row_ref)
    at_col = own(col_ref)
    at_row = jnp.where(at_row <= RADIUS, at_row, at_row - extent).astype(F32)
    at_col = jnp.where(at_col <= RADIUS, at_col, at_col - extent).astype(F32)
    square_row = at_row * at_row + at_col * at_col
    spare = jnp.ones((1, 2 * LANES - sticks), F32)
    aux = jnp.concatenate(
        [
            jnp.broadcast_to(jnp.concatenate([length_row, spare], axis=1), (LANES // 2, 2 * LANES)),
            jnp.broadcast_to(jnp.concatenate([square_row, spare], axis=1), (LANES // 2, 2 * LANES)),
        ],
        axis=0,
    )
    aux_col = jnp.transpose(aux)[:sticks]
    len_ref[...] = aux_col
    length = aux_col[:, 0:1]
    square = aux_col[:, LANES // 2:LANES // 2 + 1]
    middle = (length - 1.0) * 0.5
    position = lax.broadcasted_iota(jnp.int32, (sticks, padded), 1).astype(F32)
    kept = (position < length).astype(F32)
    kinetic = (square + (position - middle) * (position - middle)) * (1.0 / (RADIUS * RADIUS))
    wave = jnp.concatenate([coef_ref[:, 0, :] * kept, coef_ref[:, 1, :] * kept], axis=1)
    kc_ref[...] = wave * jnp.concatenate([kinetic, kinetic], axis=1)

    total = plane_ref.shape[1]
    plane_row = jnp.broadcast_to(plane_ref[...].astype(F32), (LANES, total))
    plane_col = jnp.transpose(plane_row)[:, 0:1]
    real = (plane_col >= 0.0).astype(F32)
    plane_col = jnp.maximum(plane_col, 0.0)
    harmonic = lax.broadcasted_iota(jnp.int32, (total, padded), 1).astype(F32)
    cos, sin = trig(plane_col * harmonic, extent)
    cos, sin = cos * real, sin * real
    parts = []
    for d in range(devices):
        c = cos[d * padded_planes:(d + 1) * padded_planes]
        s = sin[d * padded_planes:(d + 1) * padded_planes]
        parts.append(jnp.concatenate([c, -s], axis=1))
        parts.append(jnp.concatenate([s, c], axis=1))
    table = split(jnp.concatenate(parts, axis=0))
    whi_ref[...] = table[0]
    wlo_ref[...] = table[1]
    shift_cos, shift_sin = trig(plane_col * ((length_row - 1.0) * 0.5), extent)
    sc_ref[...] = shift_cos
    ss_ref[...] = shift_sin
    raw = dot3(table, split(wave), ((1,), (1,)))
    for d in range(devices):
        at = 2 * d * padded_planes
        re, im = raw[at:at + padded_planes], raw[at + padded_planes:at + 2 * padded_planes]
        c = shift_cos[d * padded_planes:(d + 1) * padded_planes]
        s = shift_sin[d * padded_planes:(d + 1) * padded_planes]
        along_re = re * c + im * s
        along_im = im * c - re * s
        out_ref[d, 0:padded_planes, :] = along_re[:, :LANES]
        out_ref[d, padded_planes:2 * padded_planes, :] = along_im[:, :LANES]
        out_ref[d, 2 * padded_planes:3 * padded_planes, :] = jnp.concatenate(
            [along_re[:, LANES:], along_im[:, LANES:]], axis=1
        )


def window_row(values, sticks):
    line = jnp.concatenate([values[i:i + 1] for i in range(values.shape[0])], axis=1)
    starts = range(0, line.shape[1], sticks)
    parts = [line[:, at:at + LANES] for at in starts]
    parts += [line[:, at + LANES:at + sticks] for at in starts]
    return jnp.concatenate(parts, axis=1)


def map_kernel(
    extent, sticks, in_row_hbm, in_col_hbm, map_ref, first_ref, src_ref, dst_ref, row_ref, col_ref,
    in_row_ref, in_col_ref, sems,
):
    for copy in fetch_all((in_row_hbm, in_col_hbm), (in_row_ref, in_col_ref), sems):
        copy.wait()
    windows = src_ref.shape[0]
    total = windows * LANES

    def signed(ref):
        value = ref[...]
        return window_row(jnp.where(value <= RADIUS, value, value - extent) + RADIUS, sticks)

    def dot(x, y, dims=((1,), (0,))):
        return lax.dot_general(x, y, (dims, ((), ())), preferred_element_type=F32)

    def bits(condition):
        return condition.astype(F32).astype(BF16)

    nt = ((1,), (1,))
    own_row, own_col = signed(in_row_ref), signed(in_col_ref)
    own_row = (own_row & 1) * row_blocks()[0] + (own_row >> 1)
    tall = lax.broadcasted_iota(jnp.int32, (LANES, total), 0)
    place = lax.broadcasted_iota(jnp.int32, (LANES, total), 1)
    in_col = tall == own_col
    row_hot, col_hot = bits(tall == own_row), bits(in_col)
    down = lax.broadcasted_iota(jnp.int32, (LANES, LANES), 0)
    across = lax.broadcasted_iota(jnp.int32, (LANES, LANES), 1)
    before = bits(down < across)
    after = bits(down > across)
    upto = bits(down >= across)
    ones = jnp.ones((LANES, LANES), BF16)
    taken = dot(row_hot, col_hot, nt)
    taken_t = dot(col_hot, row_hot, nt)
    taken_b, taken_tb = taken.astype(BF16), taken_t.astype(BF16)
    start = dot(dot(after, taken_b).astype(BF16), ones)
    end = start + dot(taken_b, ones)
    start_t = dot(ones, dot(taken_tb, before).astype(BF16))
    limit = windows - 1.0
    first = jnp.minimum(jnp.floor(start * (1.0 / LANES)), limit)
    code = jnp.where(taken > 0.5, dot(taken_b, before) + start - LANES * first, -1.0)
    map_ref[...] = code.astype(jnp.int32)
    first_ref[...] = jnp.minimum(jnp.floor(start_t[0:8] * (1.0 / LANES)), limit).astype(jnp.int32)

    spot = place.astype(F32)
    in_range = (spot >= start[:, 0:1]) & (spot < end[:, 0:1])
    sorted_hot = bits(in_range)
    sorted_row = jnp.sum(jnp.where(in_range, tall, 0).astype(F32), axis=0, keepdims=True)
    sorted_rank = spot[0:1] - jnp.sum(jnp.where(in_range, start[:, 0:1], 0.0), axis=0, keepdims=True)
    counts = dot(dot(upto, taken_tb).astype(BF16), sorted_hot)
    sorted_col = jnp.sum((counts <= sorted_rank).astype(F32), axis=0, keepdims=True)
    names = place + 1
    name_hi = dot(jnp.where(in_col, names >> 6, 0).astype(F32).astype(BF16), row_hot, nt)
    name_lo = dot(jnp.where(in_col, names & 63, 0).astype(F32).astype(BF16), row_hot, nt)
    named = dot(name_hi.astype(BF16), sorted_hot) * 64.0 + dot(name_lo.astype(BF16), sorted_hot)
    source = jnp.sum(jnp.where(tall.astype(F32) == sorted_col, named, 0.0), axis=0, keepdims=True) - 1.0
    place_t = dot(after, taken_tb) + start_t
    place_hi = jnp.floor(place_t * (1.0 / 64.0))
    place_lo = place_t - 64.0 * place_hi
    placed = dot(place_hi.astype(BF16), row_hot) * 64.0 + dot(place_lo.astype(BF16), row_hot)
    target = jnp.sum(jnp.where(in_col, placed, 0.0), axis=0, keepdims=True)
    for values, ref in ((source, src_ref), (target, dst_ref), (sorted_row, row_ref), (sorted_col, col_ref)):
        values = values.astype(jnp.int32)
        for w in range(windows):
            ref[w:w + 1, :] = values[:, w * LANES:(w + 1) * LANES]
    row_ref[windows:windows + 1, :] = jnp.full((1, LANES), -1, jnp.int32)
    col_ref[windows:windows + 1, :] = jnp.zeros((1, LANES), jnp.int32)


def lane_take(x, index):
    return jnp.take_along_axis(x, index, axis=1, mode="promise_in_bounds")


def plane_kernel(
    planes, first_ref, map_ref, src_ref, dst_ref, row_ref, col_ref, recv_ref,
    *refs,
):
    table_hbm, pot_hbm, out_ref, x_ref, s_ref, gr_ref, gi_ref, table_ref, pot_ref, sems = refs
    devices = recv_ref.shape[0]
    padded_planes = recv_ref.shape[1] // 3
    windows = x_ref.shape[0]
    rows = gr_ref.shape[0] // padded_planes
    extent = pot_ref.shape[1]
    half = LANES // 2
    copies = fetch_all((table_hbm, pot_hbm), (table_ref, pot_ref), sems)

    low = lax.broadcasted_iota(jnp.int32, (padded_planes, LANES), 1) < half
    for d in range(devices):
        x_ref[d] = recv_ref[d, 0:2 * padded_planes, :]
    for e in range(devices // 2):
        first = recv_ref[2 * e, 2 * padded_planes:3 * padded_planes, :]
        second = recv_ref[2 * e + 1, 2 * padded_planes:3 * padded_planes, :]
        x_ref[devices + e, 0:padded_planes, :] = jnp.where(low, first, pltpu.roll(second, half, 1))
        x_ref[devices + e, padded_planes:2 * padded_planes, :] = jnp.where(
            low, pltpu.roll(first, half, 1), second
        )

    blocks = padded_planes // 8
    grids = (gr_ref, gi_ref)

    def reorder(order_ref, from_ref, to_ref):
        @pl.loop(0, windows, unroll=4)
        def _(v):
            order = jnp.broadcast_to(order_ref[pl.ds(v, 1), :], (8, LANES))
            index = order & (LANES - 1)
            window = order >> 7
            for j in range(2 * blocks):
                value = jnp.zeros((8, LANES), F32)
                for w in range(windows):
                    value = jnp.where(window == w, lane_take(from_ref[w, 8 * j:8 * j + 8, :], index), value)
                to_ref[v, 8 * j:8 * j + 8, :] = value

    reorder(src_ref, x_ref, s_ref)

    @pl.loop(0, rows, unroll=8)
    def _(r):
        first = first_ref[0, r]
        code = jnp.broadcast_to(map_ref[pl.ds(r, 1), :], (8, LANES))
        index = code & (LANES - 1)
        window = code >> 7
        for j in range(2 * blocks):
            lead = lane_take(s_ref[first, 8 * j:8 * j + 8, :], index)
            trail = lane_take(s_ref[first + 1, 8 * j:8 * j + 8, :], index)
            value = jnp.where(window == 0, lead, jnp.where(window == 1, trail, 0.0))
            part, at = j // blocks, 8 * (j % blocks)
            grids[part][pl.ds(r + at * rows, 8, stride=rows), :] = value

    for copy in copies:
        copy.wait()
    even_rows, odd_rows = row_blocks()
    folded = extent // 2
    group = next(g for g in (8, 4, 2) if planes % g == 0)

    wide = table_ref.shape[1] // 2
    deep = 6 * LANES
    at_y = deep + 3 * wide
    at_even = at_y + extent
    at_odd = at_even + 2 * even_rows
    x_forward = table_ref[0:deep, :]
    x_back = jnp.concatenate(
        [table_ref[deep:at_y, :wide], table_ref[deep:at_y, wide:]], axis=0
    )
    y_even = table_ref[at_y:at_even, :3 * even_rows]
    y_odd = table_ref[at_y:at_even, wide:wide + 3 * odd_rows]
    back_even = table_ref[at_even:at_odd, :3 * folded]
    back_odd = table_ref[at_odd:at_odd + 2 * odd_rows, :3 * folded]

    def dot(x, y):
        return jnp.dot(x, y, preferred_element_type=F32)

    def stack(x, axis):
        hi, lo = split(x)
        return jnp.concatenate([hi, lo, hi], axis=axis)

    def times_wave(both, cut, sign):
        cos, sin = both[:cut], both[cut:]
        re = cos[:, :LANES] - sign * sin[:, LANES:]
        im = cos[:, LANES:] + sign * sin[:, :LANES]
        return re, im

    @pl.loop(0, planes // group)
    def _(step):
        lines = []
        for t in range(group):
            base = pl.multiple_of((step * group + t) * rows, 16)
            even, odd = pl.ds(base, even_rows), pl.ds(base + even_rows, odd_rows)
            parts = []
            for pick, table, size in ((even, y_even, even_rows), (odd, y_odd, odd_rows)):
                spectrum = jnp.concatenate([gr_ref[pick, :], gi_ref[pick, :]], axis=1)
                parts.append(times_wave(dot(table, stack(spectrum, 0)), folded, 1.0))
            (e_re, e_im), (o_re, o_im) = parts
            lines.append(jnp.concatenate([e_re + o_re, e_im + o_im], axis=1))
            lines.append(jnp.concatenate([e_re - o_re, e_im - o_im], axis=1))
        field = dot(stack(jnp.concatenate(lines, axis=0), 1), x_forward)
        spare = jnp.zeros((extent, wide - extent), F32)
        weighted = []
        for t in range(group):
            v = jnp.concatenate([pot_ref[step * group + t], spare], axis=1)
            mine = field[t * extent:(t + 1) * extent]
            weighted.append(jnp.concatenate([mine[:, :wide] * v, mine[:, wide:] * v], axis=1))
        back = dot(stack(jnp.concatenate(weighted, axis=0), 1), x_back)
        for t in range(group):
            base = pl.multiple_of((step * group + t) * rows, 16)
            even, odd = pl.ds(base, even_rows), pl.ds(base + even_rows, odd_rows)
            upper = back[t * extent:t * extent + folded]
            lower = back[t * extent + folded:(t + 1) * extent]
            for pick, table, size, value in (
                (even, back_even, even_rows, upper + lower), (odd, back_odd, odd_rows, upper - lower)
            ):
                re, im = times_wave(dot(table, stack(value, 0)), size, -1.0)
                gr_ref[pick, :] = re
                gi_ref[pick, :] = im

    @pl.loop(0, rows, unroll=8)
    def _(r):
        first = first_ref[0, r]
        values = []
        for j in range(2 * blocks):
            part, at = j // blocks, 8 * (j % blocks)
            values.append(grids[part][pl.ds(r + at * rows, 8, stride=rows), :])
        for t in range(2):
            index = jnp.broadcast_to(col_ref[pl.ds(first + t, 1), :], (8, LANES))
            hit = jnp.broadcast_to(row_ref[pl.ds(first + t, 1), :], (8, LANES)) == r
            for j in range(2 * blocks):
                pltpu.store(
                    s_ref.at[first + t, 8 * j:8 * j + 8, :], lane_take(values[j], index), mask=hit
                )

    reorder(dst_ref, s_ref, x_ref)
    for w in range(devices):
        out_ref[w, 0:2 * padded_planes, :] = x_ref[w]
    for e in range(devices // 2):
        re = x_ref[devices + e, 0:padded_planes, :]
        im = x_ref[devices + e, padded_planes:2 * padded_planes, :]
        out_ref[2 * e, 2 * padded_planes:3 * padded_planes, :] = jnp.where(
            low, re, pltpu.roll(im, half, 1)
        )
        out_ref[2 * e + 1, 2 * padded_planes:3 * padded_planes, :] = jnp.where(
            low, pltpu.roll(re, half, 1), im
        )
    for d in range(devices):
        out_ref[d, 3 * padded_planes:, :] = jnp.zeros((8, LANES), F32)


def inner_kernel(bands, volume, norm, place_ref, *refs):
    kc_ref = refs[0]
    coefs = refs[1:1 + bands]
    fields = refs[1 + bands:1 + 2 * bands]
    in_ref = refs[1 + 2 * bands]
    out_refs = refs[2 + 2 * bands:]
    devices = in_ref.shape[0]
    padded_planes = (in_ref.shape[1] - 8) // 3
    half = LANES // 2
    padded = coefs[0].shape[2]
    me, mine = place_ref[0], place_ref[1]
    low = lax.broadcasted_iota(jnp.int32, (padded_planes, LANES), 1) < half

    def fold(x):
        rows = x.shape[0]
        total = x[0:8]
        for at in range(8, rows, 8):
            total = total + x[at:at + 8]
        return total

    kc = kc_ref[...]
    kc_re, kc_im = kc[:, :padded], kc[:, padded:]
    sums = []
    for m in range(bands):
        c_re, c_im = coefs[m][:, 0, :], coefs[m][:, 1, :]
        sums.append([fold(c_re * kc_re + c_im * kc_im), fold(c_re * kc_im - c_im * kc_re)])
    local = [[jnp.zeros((8, LANES), F32), jnp.zeros((8, LANES), F32)] for _ in range(bands)]
    for d in range(devices):
        value = in_ref[d, 0:3 * padded_planes, :]
        re, im, rest = value[:padded_planes], value[padded_planes:2 * padded_planes], value[2 * padded_planes:]
        turned = pltpu.roll(rest, half, 1)
        other = jnp.concatenate([im, -re, jnp.where(low, turned, -turned)], axis=0)
        for m in range(bands):
            col = fields[m][d, 0:3 * padded_planes, :]
            local[m][0] = local[m][0] + fold(col * value)
            local[m][1] = local[m][1] + fold(col * other)
    lane = lax.broadcasted_iota(jnp.int32, (8, LANES), 1)
    row = lax.broadcasted_iota(jnp.int32, (8, LANES), 0)
    tile = jnp.zeros((8, LANES), F32)
    for m in range(bands):
        at = lax.rem(me + m, bands)
        for part, sign in ((0, 1.0), (1, -1.0)):
            partial = sums[m][part] + volume * local[m][part]
            scalar = jnp.sum(jnp.sum(partial, axis=1, keepdims=True), axis=0, keepdims=True)
            tile = jnp.where((lane == at) & (row == part), sign * norm * scalar, tile)
    for k in range(devices):
        out_refs[k][0:3 * padded_planes, :] = in_ref[lax.rem(mine + k, devices), 0:3 * padded_planes, :]
        out_refs[k][3 * padded_planes:, :] = tile


def final_kernel(volume, devices, me_ref, len_ref, *refs):
    ret_refs = refs[:devices]
    kc_ref, whi_ref, wlo_ref, sc_ref, ss_ref, out_ref, sub_ref, stack_ref = refs[devices:]
    padded_planes = (ret_refs[0].shape[0] - 8) // 3
    sticks, _, padded = out_ref.shape
    half = LANES // 2
    bands = sub_ref.shape[2]
    total = jnp.zeros((8, LANES), F32)
    me = me_ref[0]
    for k in range(devices):
        value = ret_refs[k][...]
        base = pl.multiple_of(lax.rem(me + devices - k, devices) * padded_planes, 8)
        total = total + value[3 * padded_planes:]
        rest = value[2 * padded_planes:3 * padded_planes]
        re = jnp.concatenate([value[:padded_planes], rest[:, :half]], axis=1)
        im = jnp.concatenate([value[padded_planes:2 * padded_planes], rest[:, half:]], axis=1)
        c = sc_ref[pl.ds(base, padded_planes), :]
        s = ss_ref[pl.ds(base, padded_planes), :]
        stack_ref[pl.ds(2 * base, padded_planes), :sticks] = re * c - im * s
        stack_ref[pl.ds(2 * base + padded_planes, padded_planes), :sticks] = re * s + im * c
    turned = jnp.transpose(stack_ref[...])[:sticks]
    local = dot3(split(turned), (whi_ref[...], wlo_ref[...])) * volume
    position = lax.broadcasted_iota(jnp.int32, (sticks, padded), 1).astype(F32)
    kept = position < len_ref[:, 0:1]
    kc = kc_ref[...]
    out_ref[:, 0, :] = jnp.where(kept, kc[:, :padded] + local[:, :padded], 0.0)
    out_ref[:, 1, :] = jnp.where(kept, kc[:, padded:] + local[:, padded:], 0.0)
    sub_ref[:, 0, :] = total[0:2, :bands]


def shards(bands, devices, coefficients, stick_col, stick_row, stick_length, plane_of_slot, potential):
    extent = plane_of_slot.shape[0]
    sticks = coefficients.shape[1]
    padded = coefficients.shape[3]
    total_sticks = stick_col.shape[0]
    planes = potential.shape[0]
    padded_planes = up8(planes)
    if sticks != LANES + LANES // 2 or devices % 2 or planes % 2:
        raise ValueError("sizes")
    rows = sum(row_blocks())
    volume = 1.0 / (extent * extent * extent)
    me = lax.axis_index("tg").astype(jnp.int32)
    coef = coefficients.reshape(sticks, 2, padded)

    length, row, col = (v.reshape(-1, LANES) for v in (stick_length, stick_row, stick_col))
    slots = plane_of_slot.reshape(devices, planes)
    if padded_planes > planes:
        slots = jnp.pad(slots, ((0, 0), (0, padded_planes - planes)), constant_values=-1)
    slots = slots.reshape(1, devices * padded_planes)
    windows = total_sticks // LANES
    smem = pl.BlockSpec(memory_space=pltpu.SMEM)
    vmem = pl.BlockSpec(memory_space=pltpu.VMEM)
    hbm = pl.BlockSpec(memory_space=pltpu.HBM)

    block = 3 * padded_planes
    total_planes = devices * padded_planes
    sent, kc, lengths, whi, wlo, shift_cos, shift_sin = pl.pallas_call(
        functools.partial(wave_kernel, extent),
        out_shape=(
            jax.ShapeDtypeStruct((devices, block, LANES), F32),
            jax.ShapeDtypeStruct((sticks, 2 * padded), F32),
            jax.ShapeDtypeStruct((sticks, LANES), F32),
            jax.ShapeDtypeStruct((2 * total_planes, 2 * padded), BF16),
            jax.ShapeDtypeStruct((2 * total_planes, 2 * padded), BF16),
            jax.ShapeDtypeStruct((total_planes, sticks), F32),
            jax.ShapeDtypeStruct((total_planes, sticks), F32),
        ),
        in_specs=[smem] + [hbm] * 5,
        scratch_shapes=[
            pltpu.VMEM(length.shape, jnp.int32),
            pltpu.VMEM(row.shape, jnp.int32),
            pltpu.VMEM(col.shape, jnp.int32),
            pltpu.VMEM(slots.shape, jnp.int32),
            pltpu.VMEM(coef.shape, F32),
            pltpu.SemaphoreType.DMA((5,)),
        ],
        compiler_params=params(56),
        name="wave_to_planes",
    )(me.reshape(1), length, row, col, slots, coef)

    received = lax.all_to_all(sent, "tg", split_axis=0, concat_axis=0, tiled=True)

    window_list = jax.ShapeDtypeStruct((windows, LANES), jnp.int32)
    longer_list = jax.ShapeDtypeStruct((windows + 1, LANES), jnp.int32)
    stick_map, first, source, target, row_w, col_w = pl.pallas_call(
        functools.partial(map_kernel, extent, sticks),
        out_shape=(
            jax.ShapeDtypeStruct((LANES, LANES), jnp.int32),
            jax.ShapeDtypeStruct((8, LANES), jnp.int32),
            window_list,
            window_list,
            longer_list,
            longer_list,
        ),
        in_specs=[hbm] * 2,
        scratch_shapes=[
            pltpu.VMEM(row.shape, jnp.int32),
            pltpu.VMEM(col.shape, jnp.int32),
            pltpu.SemaphoreType.DMA((2,)),
        ],
        compiler_params=params(14 * total_sticks / 1536),
        cost_estimate=cost(4e9, 1e5),
        name="stick_map",
    )(row, col)

    constants = jnp.asarray(tables(extent))
    weighted = pl.pallas_call(
        functools.partial(plane_kernel, planes),
        out_shape=jax.ShapeDtypeStruct((devices, block + 8, LANES), F32),
        in_specs=[smem] + [vmem] * 6 + [hbm] * 2,
        out_specs=vmem,
        scratch_shapes=[
            pltpu.VMEM((windows, 2 * padded_planes, LANES), F32),
            pltpu.VMEM((windows + 1, 2 * padded_planes, LANES), F32),
            pltpu.VMEM((padded_planes * rows, LANES), F32),
            pltpu.VMEM((padded_planes * rows, LANES), F32),
            pltpu.VMEM(constants.shape, BF16),
            pltpu.VMEM(potential.shape, F32),
            pltpu.SemaphoreType.DMA((2,)),
        ],
        compiler_params=params(52),
        cost_estimate=cost(2e10, 1e7),
        name="planes",
    )(first, stick_map, source, target, row_w, col_w, received, constants, potential)

    coefs, fields = [coef], [received]
    for shift in range(1, bands):
        ring = [((b + shift) % bands, b) for b in range(bands)]
        coefs.append(lax.ppermute(coef, "band", ring))
        fields.append(lax.ppermute(received, "band", ring))
    band = lax.axis_index("band").astype(jnp.int32)
    norm = 1.0 / (total_sticks * padded)
    places = jnp.stack([band, me])
    outgoing = pl.pallas_call(
        functools.partial(inner_kernel, bands, volume, norm),
        out_shape=(jax.ShapeDtypeStruct((block + 8, LANES), F32),) * devices,
        in_specs=[smem] + [vmem] * (2 + 2 * bands),
        compiler_params=params(6 + 1.5 * bands),
        name="inner",
    )(places, kc, *coefs, *fields, weighted)

    returned = [outgoing[0]]
    for k in range(1, devices):
        ring = [(d, (d + k) % devices) for d in range(devices)]
        returned.append(lax.ppermute(outgoing[k], "tg", ring))
    applied, subspace = pl.pallas_call(
        functools.partial(final_kernel, volume, devices),
        out_shape=(
            jax.ShapeDtypeStruct((sticks, 2, padded), F32),
            jax.ShapeDtypeStruct((2, 1, bands), F32),
        ),
        in_specs=[smem] + [vmem] * (6 + devices),
        scratch_shapes=[pltpu.VMEM((2 * total_planes, 2 * LANES), F32)],
        compiler_params=params(6 + 6 * total_planes / 192),
        name="planes_to_wave",
    )(me.reshape(1), lengths, *returned, kc, whi, wlo, shift_cos, shift_sin)
    return applied.reshape(1, sticks, 2, padded), subspace


def solution(mesh):
    in_specs = (P("band", "tg", None, None), P(), P(), P(), P(), P("tg", None, None))
    out_specs = (P("band", "tg", None, None), P(None, "band", None))
    body = functools.partial(shards, mesh.shape["band"], mesh.shape["tg"])
    return jax.shard_map(body, mesh=mesh, in_specs=in_specs, out_specs=out_specs, check_vma=False)
```

```python
import functools
import math

import jax
import jax.numpy as jnp
import ml_dtypes
import numpy as np
from jax import lax
from jax.experimental import pallas as pl
from jax.experimental.pallas import tpu as pltpu
from jax.sharding import PartitionSpec as P

RADIUS = 48
LANES = 128
F32 = jnp.float32
BF16 = jnp.bfloat16


def up8(n):
    return -(-n // 8) * 8


def split(x):
    hi = x.astype(BF16)
    return hi, (x - hi.astype(F32)).astype(BF16)


def dot3(a, b, dims=((1,), (0,))):
    def dot(x, y):
        return lax.dot_general(x, y, (dims, ((), ())), preferred_element_type=F32)

    return dot(a[0], b[0]) + (dot(a[0], b[1]) + dot(a[1], b[0]))


def trig(product, extent):
    n = product - extent * jnp.floor(product * (1.0 / extent) + 0.5)
    quarter = extent / 4.0
    unit = 2.0 * math.pi / extent

    def sine(m):
        u = m * unit
        v = u * u
        s = 1.0 / 6227020800.0
        for term in (-39916800.0, 362880.0, -5040.0, 120.0, -6.0, 1.0):
            s = s * v + 1.0 / term
        return u * s

    folded = jnp.where(
        jnp.abs(n) > quarter, jnp.where(n > 0, 2.0 * quarter, -2.0 * quarter) - n, n
    )
    return sine(quarter - jnp.abs(n)), sine(folded)


def pair(table):
    hi = table.astype(np.float32).astype(ml_dtypes.bfloat16)
    lo = (table - hi.astype(np.float64)).astype(ml_dtypes.bfloat16)
    return hi, lo


def row_blocks():
    even = -(-(RADIUS + 1) // 16) * 16
    odd = -(-RADIUS // 16) * 16
    return even, odd


@functools.cache
def tables(extent):
    half = extent // 2
    grid = np.arange(extent)
    freq = np.arange(2 * RADIUS + 1) - RADIUS

    def angles(f, g):
        a = 2.0 * np.pi * ((f[:, None] * g[None, :]) % extent) / extent
        return np.cos(a), np.sin(a)

    wide = 2 * LANES
    x_forward, x_back, forward, back = [], [], [], []
    for offset, rows in zip((0, 1), row_blocks()):
        cos, sin = angles(freq[offset::2], grid[:half])
        count = cos.shape[0]
        table = np.zeros((LANES, wide))
        table[:count, :half] = cos
        table[LANES // 2:LANES // 2 + count, :half] = -sin
        table[:count, LANES:LANES + half] = sin
        table[LANES // 2:LANES // 2 + count, LANES:LANES + half] = cos
        hi, lo = pair(table)
        x_forward.append(np.concatenate([hi, hi, lo], axis=0))
        hi, lo = pair(table.T.copy())
        x_back.append(
            np.concatenate(
                [np.concatenate([hi, lo], axis=1), np.concatenate([hi, np.zeros_like(lo)], axis=1)], axis=0
            )
        )
        parts = []
        for wave in (cos, sin):
            table = np.zeros((half, rows))
            table[:, :count] = wave.T
            hi, lo = pair(table)
            parts += [hi, hi, lo]
        forward.append(np.concatenate(parts, axis=1))
        table = np.zeros((2 * rows, half))
        table[:count] = cos
        table[rows:rows + count] = sin
        hi, lo = pair(table)
        back.append(np.concatenate([hi, hi, lo], axis=1))
    rows = [np.concatenate(x_forward, axis=1), np.concatenate(x_back, axis=1)]
    for table in forward + back:
        rows.append(np.pad(table, ((0, 0), (0, 2 * wide - table.shape[1]))))
    return np.concatenate(rows, axis=0)


def params(megabytes):
    return pltpu.CompilerParams(vmem_limit_bytes=int(min(megabytes, 56) * 2**20))


def fetch_all(sources, targets, sems):
    copies = [
        pltpu.make_async_copy(source, target, sems.at[i])
        for i, (source, target) in enumerate(zip(sources, targets))
    ]
    for copy in copies:
        copy.start()
    return copies


def cost(flops, nbytes):
    return pl.CostEstimate(flops=int(flops), bytes_accessed=int(nbytes), transcendentals=0)


def wave_kernel(
    extent, me_ref, length_hbm, row_hbm, col_hbm, plane_hbm, coef_hbm,
    out_ref, kc_ref, len_ref, whi_ref, wlo_ref, sc_ref, ss_ref,
    length_ref, row_ref, col_ref, plane_ref, coef_ref, sems,
):
    copies = fetch_all(
        (length_hbm, row_hbm, col_hbm, plane_hbm, coef_hbm),
        (length_ref, row_ref, col_ref, plane_ref, coef_ref),
        sems,
    )
    for copy in copies:
        copy.wait()
    devices = out_ref.shape[0]
    sticks, _, padded = coef_ref.shape
    padded_planes = plane_ref.shape[1] // devices
    me = me_ref[0]
    half = LANES // 2
    lead = (me * sticks) // LANES
    odd = (me * sticks) % LANES != 0

    def own(ref):
        first, second = ref[pl.ds(lead, 1), :], ref[pl.ds(lead + 1, 1), :]
        both = jnp.concatenate([first, second], axis=1)
        return jnp.where(odd, both[:, half:], both[:, :sticks])

    length_row = own(length_ref).astype(F32)
    at_row = own(row_ref)
    at_col = own(col_ref)
    at_row = jnp.where(at_row <= RADIUS, at_row, at_row - extent).astype(F32)
    at_col = jnp.where(at_col <= RADIUS, at_col, at_col - extent).astype(F32)
    square_row = at_row * at_row + at_col * at_col
    spare = jnp.ones((1, 2 * LANES - sticks), F32)
    aux = jnp.concatenate(
        [
            jnp.broadcast_to(jnp.concatenate([length_row, spare], axis=1), (LANES // 2, 2 * LANES)),
            jnp.broadcast_to(jnp.concatenate([square_row, spare], axis=1), (LANES // 2, 2 * LANES)),
        ],
        axis=0,
    )
    aux_col = jnp.transpose(aux)[:sticks]
    len_ref[...] = aux_col
    length = aux_col[:, 0:1]
    square = aux_col[:, LANES // 2:LANES // 2 + 1]
    middle = (length - 1.0) * 0.5
    position = lax.broadcasted_iota(jnp.int32, (sticks, padded), 1).astype(F32)
    kept = (position < length).astype(F32)
    kinetic = (square + (position - middle) * (position - middle)) * (1.0 / (RADIUS * RADIUS))
    wave = jnp.concatenate([coef_ref[:, 0, :] * kept, coef_ref[:, 1, :] * kept], axis=1)
    kc_ref[...] = wave * jnp.concatenate([kinetic, kinetic], axis=1)

    total = plane_ref.shape[1]
    plane_row = jnp.broadcast_to(plane_ref[...].astype(F32), (LANES, total))
    plane_col = jnp.transpose(plane_row)[:, 0:1]
    real = (plane_col >= 0.0).astype(F32)
    plane_col = jnp.maximum(plane_col, 0.0)
    harmonic = lax.broadcasted_iota(jnp.int32, (total, padded), 1).astype(F32)
    cos, sin = trig(plane_col * harmonic, extent)
    cos, sin = cos * real, sin * real
    parts = []
    for d in range(devices):
        c = cos[d * padded_planes:(d + 1) * padded_planes]
        s = sin[d * padded_planes:(d + 1) * padded_planes]
        parts.append(jnp.concatenate([c, -s], axis=1))
        parts.append(jnp.concatenate([s, c], axis=1))
    table = split(jnp.concatenate(parts, axis=0))
    whi_ref[...] = table[0]
    wlo_ref[...] = table[1]
    shift_cos, shift_sin = trig(plane_col * ((length_row - 1.0) * 0.5), extent)
    sc_ref[...] = shift_cos
    ss_ref[...] = shift_sin
    raw = dot3(table, split(wave), ((1,), (1,)))
    for d in range(devices):
        at = 2 * d * padded_planes
        re, im = raw[at:at + padded_planes], raw[at + padded_planes:at + 2 * padded_planes]
        c = shift_cos[d * padded_planes:(d + 1) * padded_planes]
        s = shift_sin[d * padded_planes:(d + 1) * padded_planes]
        along_re = re * c + im * s
        along_im = im * c - re * s
        out_ref[d, 0:padded_planes, :] = along_re[:, :LANES]
        out_ref[d, padded_planes:2 * padded_planes, :] = along_im[:, :LANES]
        out_ref[d, 2 * padded_planes:3 * padded_planes, :] = jnp.concatenate(
            [along_re[:, LANES:], along_im[:, LANES:]], axis=1
        )


def window_row(values, sticks):
    line = jnp.concatenate([values[i:i + 1] for i in range(values.shape[0])], axis=1)
    starts = range(0, line.shape[1], sticks)
    parts = [line[:, at:at + LANES] for at in starts]
    parts += [line[:, at + LANES:at + sticks] for at in starts]
    return jnp.concatenate(parts, axis=1)


def map_kernel(
    extent, sticks, in_row_hbm, in_col_hbm,
    even_ref, odd_ref, first_ref, src_ref, dst_ref, row_ref, col_ref,
    in_row_ref, in_col_ref, sems,
):
    for copy in fetch_all((in_row_hbm, in_col_hbm), (in_row_ref, in_col_ref), sems):
        copy.wait()
    windows = src_ref.shape[0]
    total = windows * LANES

    def signed(ref):
        value = ref[...]
        return window_row(jnp.where(value <= RADIUS, value, value - extent) + RADIUS, sticks)

    def dot(x, y, dims=((1,), (0,))):
        return lax.dot_general(x, y, (dims, ((), ())), preferred_element_type=F32)

    def bits(condition):
        return condition.astype(F32).astype(BF16)

    nt = ((1,), (1,))
    own_row, own_col = signed(in_row_ref), signed(in_col_ref)
    half = LANES // 2
    own_row = (own_row & 1) * row_blocks()[0] + (own_row >> 1)
    own_col = (own_col & 1) * half + (own_col >> 1)
    tall = lax.broadcasted_iota(jnp.int32, (LANES, total), 0)
    place = lax.broadcasted_iota(jnp.int32, (LANES, total), 1)
    in_col = tall == own_col
    row_hot, col_hot = bits(tall == own_row), bits(in_col)
    down = lax.broadcasted_iota(jnp.int32, (LANES, LANES), 0)
    across = lax.broadcasted_iota(jnp.int32, (LANES, LANES), 1)
    before = bits(down < across)
    after = bits(down > across)
    upto = bits(down >= across)
    ones = jnp.ones((LANES, LANES), BF16)
    taken = dot(row_hot, col_hot, nt)
    taken_t = dot(col_hot, row_hot, nt)
    taken_b, taken_tb = taken.astype(BF16), taken_t.astype(BF16)
    start = dot(dot(after, taken_b).astype(BF16), ones)
    end = start + dot(taken_b, ones)
    start_t = dot(ones, dot(taken_tb, before).astype(BF16))
    left = across < half
    standing = dot(taken_b, before) + start
    low_ones = bits(down < half)
    high_start = start + dot(taken_b, low_ones)
    ones_t = bits(across < half)
    high_start_t = start_t + dot(ones_t, taken_tb)
    limit = 2.0 * windows - 1.0

    def first_window(value):
        return jnp.minimum(jnp.floor(value * (1.0 / half)), limit)

    for ref, begin in ((even_ref, start), (odd_ref, high_start)):
        code = jnp.where(taken > 0.5, standing - half * first_window(begin), -1.0)
        turned = pltpu.roll(code, half, 1)
        both = jnp.where(left, code, turned) if ref is even_ref else jnp.where(left, turned, code)
        ref[...] = both.astype(jnp.int32)
    first_ref[...] = jnp.concatenate(
        [first_window(start_t[0:8]), first_window(high_start_t[0:8])], axis=0
    ).astype(jnp.int32)

    spot = place.astype(F32)
    in_range = (spot >= start[:, 0:1]) & (spot < end[:, 0:1])
    sorted_hot = bits(in_range)
    sorted_row = jnp.sum(jnp.where(in_range, tall, 0).astype(F32), axis=0, keepdims=True)
    sorted_rank = spot[0:1] - jnp.sum(jnp.where(in_range, start[:, 0:1], 0.0), axis=0, keepdims=True)
    counts = dot(dot(upto, taken_tb).astype(BF16), sorted_hot)
    sorted_col = jnp.sum((counts <= sorted_rank).astype(F32), axis=0, keepdims=True)
    names = place + 1
    name_hi = dot(jnp.where(in_col, names >> 6, 0).astype(F32).astype(BF16), row_hot, nt)
    name_lo = dot(jnp.where(in_col, names & 63, 0).astype(F32).astype(BF16), row_hot, nt)
    named = dot(name_hi.astype(BF16), sorted_hot) * 64.0 + dot(name_lo.astype(BF16), sorted_hot)
    source = jnp.sum(jnp.where(tall.astype(F32) == sorted_col, named, 0.0), axis=0, keepdims=True) - 1.0
    place_t = dot(after, taken_tb) + start_t
    place_hi = jnp.floor(place_t * (1.0 / 64.0))
    place_lo = place_t - 64.0 * place_hi
    placed = dot(place_hi.astype(BF16), row_hot) * 64.0 + dot(place_lo.astype(BF16), row_hot)
    target = jnp.sum(jnp.where(in_col, placed, 0.0), axis=0, keepdims=True)
    for values, ref in ((source, src_ref), (target, dst_ref)):
        values = values.astype(jnp.int32)
        for w in range(windows):
            ref[w:w + 1, :] = values[:, w * LANES:(w + 1) * LANES]
    is_left = left[0:8]
    shift = jnp.where(is_left, 0, half)
    sorted_col = sorted_col.astype(jnp.int32)
    sorted_key = sorted_row.astype(jnp.int32) * 2 + (sorted_col >> 6)
    sorted_col = sorted_col & (half - 1)
    for values, ref, add in ((sorted_key, row_ref, 0), (sorted_col, col_ref, shift)):
        for w in range(windows):
            line = jnp.broadcast_to(values[:, w * LANES:(w + 1) * LANES], (8, LANES))
            turned = pltpu.roll(line, half, 1)
            ref[2 * w:2 * w + 1, :] = (jnp.where(is_left, line, turned) + add)[0:1]
            ref[2 * w + 1:2 * w + 2, :] = (jnp.where(is_left, turned, line) + add)[0:1]
    row_ref[2 * windows:2 * windows + 1, :] = jnp.full((1, LANES), -1, jnp.int32)
    col_ref[2 * windows:2 * windows + 1, :] = jnp.zeros((1, LANES), jnp.int32)


def lane_take(x, index):
    return jnp.take_along_axis(x, index, axis=1, mode="promise_in_bounds")


def plane_kernel(
    planes, first_ref, even_ref, odd_ref, src_ref, dst_ref, row_ref, col_ref, recv_ref,
    *refs,
):
    table_hbm, pot_hbm, out_ref, x_ref, s_ref, t_ref, ge_ref, go_ref, table_ref, pot_ref, sems = refs
    devices = recv_ref.shape[0]
    padded_planes = recv_ref.shape[1] // 3
    windows = x_ref.shape[0]
    rows = ge_ref.shape[0] // padded_planes
    extent = pot_ref.shape[1]
    half = LANES // 2
    copies = fetch_all((table_hbm, pot_hbm), (table_ref, pot_ref), sems)

    low = lax.broadcasted_iota(jnp.int32, (padded_planes, LANES), 1) < half
    for d in range(devices):
        x_ref[d] = recv_ref[d, 0:2 * padded_planes, :]
    for e in range(devices // 2):
        first = recv_ref[2 * e, 2 * padded_planes:3 * padded_planes, :]
        second = recv_ref[2 * e + 1, 2 * padded_planes:3 * padded_planes, :]
        x_ref[devices + e, 0:padded_planes, :] = jnp.where(low, first, pltpu.roll(second, half, 1))
        x_ref[devices + e, padded_planes:2 * padded_planes, :] = jnp.where(
            low, pltpu.roll(first, half, 1), second
        )

    blocks = padded_planes // 8

    def reorder(order_ref, from_ref, to_ref):
        @pl.loop(0, windows, unroll=4)
        def _(v):
            order = jnp.broadcast_to(order_ref[pl.ds(v, 1), :], (8, LANES))
            index = order & (LANES - 1)
            window = order >> 7
            for j in range(2 * blocks):
                value = jnp.zeros((8, LANES), F32)
                for w in range(windows):
                    value = jnp.where(window == w, lane_take(from_ref[w, 8 * j:8 * j + 8, :], index), value)
                to_ref[v, 8 * j:8 * j + 8, :] = value

    reorder(src_ref, x_ref, s_ref)
    for w in range(windows):
        re, im = s_ref[w, 0:padded_planes, :], s_ref[w, padded_planes:2 * padded_planes, :]
        t_ref[2 * w] = jnp.where(low, re, pltpu.roll(im, half, 1))
        t_ref[2 * w + 1] = jnp.where(low, pltpu.roll(re, half, 1), im)

    left = low[0:8]
    upper_lanes = jnp.where(left, 0, half)
    sides = ((0, even_ref, ge_ref), (1, odd_ref, go_ref))

    @pl.loop(0, rows, unroll=8)
    def _(r):
        for side, code_ref, grid_ref in sides:
            first = first_ref[8 * side, r]
            code = jnp.broadcast_to(code_ref[pl.ds(r, 1), :], (8, LANES))
            index = (code & (half - 1)) + upper_lanes
            window = code >> 6
            for j in range(blocks):
                lead = lane_take(t_ref[first, 8 * j:8 * j + 8, :], index)
                trail = lane_take(t_ref[first + 1, 8 * j:8 * j + 8, :], index)
                value = jnp.where(window == 0, lead, jnp.where(window == 1, trail, 0.0))
                grid_ref[pl.ds(r + 8 * j * rows, 8, stride=rows), :] = value

    for copy in copies:
        copy.wait()
    even_rows, odd_rows = row_blocks()
    folded = extent // 2
    group = next(g for g in (8, 4, 2) if planes % g == 0)
    wide = 2 * LANES
    at_back = 3 * LANES
    at_y = at_back + 2 * wide
    at_even = at_y + 2 * folded
    at_odd = at_even + 2 * even_rows
    x_forward = (table_ref[0:at_back, :wide], table_ref[0:at_back, wide:])
    x_back = (table_ref[at_back:at_y, :wide], table_ref[at_back:at_y, wide:])
    y_even = table_ref[at_y:at_y + folded, :6 * even_rows]
    y_odd = table_ref[at_y + folded:at_even, :6 * odd_rows]
    back_even = table_ref[at_even:at_odd, :3 * folded]
    back_odd = table_ref[at_odd:at_odd + 2 * odd_rows, :3 * folded]

    def dot(x, y):
        return jnp.dot(x, y, preferred_element_type=F32)

    def stack(x, axis):
        hi, lo = split(x)
        return jnp.concatenate([hi, lo, hi], axis=axis)

    def turn(x):
        lane = lax.broadcasted_iota(jnp.int32, (x.shape[0], LANES), 1) < half
        parts = []
        for at in range(0, x.shape[1], LANES):
            rolled = pltpu.roll(x[:, at:at + LANES], half, 1)
            parts.append(jnp.where(lane, -rolled, rolled))
        return jnp.concatenate(parts, axis=1)

    @pl.loop(0, planes // group)
    def _(step):
        lines = []
        for t in range(group):
            base = pl.multiple_of((step * group + t) * rows, 16)
            parts = []
            for at, size, table in ((0, even_rows, y_even), (even_rows, odd_rows, y_odd)):
                pick = pl.ds(base + at, size)
                spectrum = jnp.concatenate([ge_ref[pick, :], go_ref[pick, :]], axis=1)
                both = jnp.concatenate([stack(spectrum, 0), stack(turn(spectrum), 0)], axis=0)
                parts.append(dot(table, both))
            lines.append(parts[0] + parts[1])
            lines.append(parts[0] - parts[1])
        lines = jnp.concatenate(lines, axis=0)
        field_even = dot(stack(lines[:, :LANES], 1), x_forward[0])
        field_odd = dot(stack(lines[:, LANES:], 1), x_forward[1])
        spare = jnp.zeros((extent, LANES - folded), F32)
        sums, differences = [], []
        for t in range(group):
            v = pot_ref[step * group + t]
            v_near = jnp.concatenate([v[:, :folded], spare], axis=1)
            v_far = jnp.concatenate([v[:, folded:], spare], axis=1)
            even = field_even[t * extent:(t + 1) * extent]
            odd = field_odd[t * extent:(t + 1) * extent]
            near = (even + odd) * jnp.concatenate([v_near, v_near], axis=1)
            far = (even - odd) * jnp.concatenate([v_far, v_far], axis=1)
            sums.append(near + far)
            differences.append(near - far)
        back = []
        for weighted, table in ((sums, x_back[0]), (differences, x_back[1])):
            both = dot(jnp.concatenate(split(jnp.concatenate(weighted, axis=0)), axis=1), table)
            back.append(both[:, :LANES] + both[:, LANES:])
        back = jnp.concatenate(back, axis=1)
        for t in range(group):
            base = pl.multiple_of((step * group + t) * rows, 16)
            upper = back[t * extent:t * extent + folded]
            lower = back[t * extent + folded:(t + 1) * extent]
            for at, size, table, value in (
                (0, even_rows, back_even, upper + lower), (even_rows, odd_rows, back_odd, upper - lower)
            ):
                both = dot(table, stack(value, 0))
                value = both[:size] - turn(both[size:])
                pick = pl.ds(base + at, size)
                ge_ref[pick, :] = value[:, :LANES]
                go_ref[pick, :] = value[:, LANES:]

    @pl.loop(0, rows, unroll=8)
    def _(r):
        for side, _, grid_ref in sides:
            first = first_ref[8 * side, r]
            values = [grid_ref[pl.ds(r + 8 * j * rows, 8, stride=rows), :] for j in range(blocks)]
            for t in range(2):
                index = jnp.broadcast_to(col_ref[pl.ds(first + t, 1), :], (8, LANES))
                hit = jnp.broadcast_to(row_ref[pl.ds(first + t, 1), :], (8, LANES)) == 2 * r + side
                for j in range(blocks):
                    pltpu.store(
                        t_ref.at[first + t, 8 * j:8 * j + 8, :], lane_take(values[j], index), mask=hit
                    )

    for w in range(windows):
        first, second = t_ref[2 * w], t_ref[2 * w + 1]
        s_ref[w, 0:padded_planes, :] = jnp.where(low, first, pltpu.roll(second, half, 1))
        s_ref[w, padded_planes:2 * padded_planes, :] = jnp.where(low, pltpu.roll(first, half, 1), second)
    reorder(dst_ref, s_ref, x_ref)
    for w in range(devices):
        out_ref[w, 0:2 * padded_planes, :] = x_ref[w]
    for e in range(devices // 2):
        re = x_ref[devices + e, 0:padded_planes, :]
        im = x_ref[devices + e, padded_planes:2 * padded_planes, :]
        out_ref[2 * e, 2 * padded_planes:3 * padded_planes, :] = jnp.where(
            low, re, pltpu.roll(im, half, 1)
        )
        out_ref[2 * e + 1, 2 * padded_planes:3 * padded_planes, :] = jnp.where(
            low, pltpu.roll(re, half, 1), im
        )
    for d in range(devices):
        out_ref[d, 3 * padded_planes:, :] = jnp.zeros((8, LANES), F32)


def inner_kernel(bands, volume, norm, place_ref, *refs):
    kc_ref = refs[0]
    coefs = refs[1:1 + bands]
    fields = refs[1 + bands:1 + 2 * bands]
    in_ref = refs[1 + 2 * bands]
    out_refs = refs[2 + 2 * bands:]
    devices = in_ref.shape[0]
    padded_planes = (in_ref.shape[1] - 8) // 3
    half = LANES // 2
    padded = coefs[0].shape[2]
    me, mine = place_ref[0], place_ref[1]
    low = lax.broadcasted_iota(jnp.int32, (padded_planes, LANES), 1) < half

    def fold(x):
        rows = x.shape[0]
        total = x[0:8]
        for at in range(8, rows, 8):
            total = total + x[at:at + 8]
        return total

    kc = kc_ref[...]
    kc_re, kc_im = kc[:, :padded], kc[:, padded:]
    sums = []
    for m in range(bands):
        c_re, c_im = coefs[m][:, 0, :], coefs[m][:, 1, :]
        sums.append([fold(c_re * kc_re + c_im * kc_im), fold(c_re * kc_im - c_im * kc_re)])
    local = [[jnp.zeros((8, LANES), F32), jnp.zeros((8, LANES), F32)] for _ in range(bands)]
    for d in range(devices):
        value = in_ref[d, 0:3 * padded_planes, :]
        re, im, rest = value[:padded_planes], value[padded_planes:2 * padded_planes], value[2 * padded_planes:]
        turned = pltpu.roll(rest, half, 1)
        other = jnp.concatenate([im, -re, jnp.where(low, turned, -turned)], axis=0)
        for m in range(bands):
            col = fields[m][d, 0:3 * padded_planes, :]
            local[m][0] = local[m][0] + fold(col * value)
            local[m][1] = local[m][1] + fold(col * other)
    lane = lax.broadcasted_iota(jnp.int32, (8, LANES), 1)
    row = lax.broadcasted_iota(jnp.int32, (8, LANES), 0)
    tile = jnp.zeros((8, LANES), F32)
    for m in range(bands):
        at = lax.rem(me + m, bands)
        for part, sign in ((0, 1.0), (1, -1.0)):
            partial = sums[m][part] + volume * local[m][part]
            scalar = jnp.sum(jnp.sum(partial, axis=1, keepdims=True), axis=0, keepdims=True)
            tile = jnp.where((lane == at) & (row == part), sign * norm * scalar, tile)
    for k in range(devices):
        out_refs[k][0:3 * padded_planes, :] = in_ref[lax.rem(mine + k, devices), 0:3 * padded_planes, :]
        out_refs[k][3 * padded_planes:, :] = tile


def final_kernel(volume, devices, me_ref, len_ref, *refs):
    ret_refs = refs[:devices]
    kc_ref, whi_ref, wlo_ref, sc_ref, ss_ref, out_ref, sub_ref, stack_ref = refs[devices:]
    padded_planes = (ret_refs[0].shape[0] - 8) // 3
    sticks, _, padded = out_ref.shape
    half = LANES // 2
    bands = sub_ref.shape[2]
    total = jnp.zeros((8, LANES), F32)
    me = me_ref[0]
    for k in range(devices):
        value = ret_refs[k][...]
        base = pl.multiple_of(lax.rem(me + devices - k, devices) * padded_planes, 8)
        total = total + value[3 * padded_planes:]
        rest = value[2 * padded_planes:3 * padded_planes]
        re = jnp.concatenate([value[:padded_planes], rest[:, :half]], axis=1)
        im = jnp.concatenate([value[padded_planes:2 * padded_planes], rest[:, half:]], axis=1)
        c = sc_ref[pl.ds(base, padded_planes), :]
        s = ss_ref[pl.ds(base, padded_planes), :]
        stack_ref[pl.ds(2 * base, padded_planes), :sticks] = re * c - im * s
        stack_ref[pl.ds(2 * base + padded_planes, padded_planes), :sticks] = re * s + im * c
    turned = jnp.transpose(stack_ref[...])[:sticks]
    local = dot3(split(turned), (whi_ref[...], wlo_ref[...])) * volume
    position = lax.broadcasted_iota(jnp.int32, (sticks, padded), 1).astype(F32)
    kept = position < len_ref[:, 0:1]
    kc = kc_ref[...]
    out_ref[:, 0, :] = jnp.where(kept, kc[:, :padded] + local[:, :padded], 0.0)
    out_ref[:, 1, :] = jnp.where(kept, kc[:, padded:] + local[:, padded:], 0.0)
    sub_ref[:, 0, :] = total[0:2, :bands]


def shards(bands, devices, coefficients, stick_col, stick_row, stick_length, plane_of_slot, potential):
    extent = plane_of_slot.shape[0]
    sticks = coefficients.shape[1]
    padded = coefficients.shape[3]
    total_sticks = stick_col.shape[0]
    planes = potential.shape[0]
    padded_planes = up8(planes)
    if sticks != LANES + LANES // 2 or devices % 2 or planes % 2:
        raise ValueError("sizes")
    rows = sum(row_blocks())
    volume = 1.0 / (extent * extent * extent)
    me = lax.axis_index("tg").astype(jnp.int32)
    coef = coefficients.reshape(sticks, 2, padded)

    length, row, col = (v.reshape(-1, LANES) for v in (stick_length, stick_row, stick_col))
    slots = plane_of_slot.reshape(devices, planes)
    if padded_planes > planes:
        slots = jnp.pad(slots, ((0, 0), (0, padded_planes - planes)), constant_values=-1)
    slots = slots.reshape(1, devices * padded_planes)
    windows = total_sticks // LANES
    smem = pl.BlockSpec(memory_space=pltpu.SMEM)
    vmem = pl.BlockSpec(memory_space=pltpu.VMEM)
    hbm = pl.BlockSpec(memory_space=pltpu.HBM)

    block = 3 * padded_planes
    total_planes = devices * padded_planes
    sent, kc, lengths, whi, wlo, shift_cos, shift_sin = pl.pallas_call(
        functools.partial(wave_kernel, extent),
        out_shape=(
            jax.ShapeDtypeStruct((devices, block, LANES), F32),
            jax.ShapeDtypeStruct((sticks, 2 * padded), F32),
            jax.ShapeDtypeStruct((sticks, LANES), F32),
            jax.ShapeDtypeStruct((2 * total_planes, 2 * padded), BF16),
            jax.ShapeDtypeStruct((2 * total_planes, 2 * padded), BF16),
            jax.ShapeDtypeStruct((total_planes, sticks), F32),
            jax.ShapeDtypeStruct((total_planes, sticks), F32),
        ),
        in_specs=[smem] + [hbm] * 5,
        scratch_shapes=[
            pltpu.VMEM(length.shape, jnp.int32),
            pltpu.VMEM(row.shape, jnp.int32),
            pltpu.VMEM(col.shape, jnp.int32),
            pltpu.VMEM(slots.shape, jnp.int32),
            pltpu.VMEM(coef.shape, F32),
            pltpu.SemaphoreType.DMA((5,)),
        ],
        compiler_params=params(56),
        name="wave_to_planes",
    )(me.reshape(1), length, row, col, slots, coef)

    received = lax.all_to_all(sent, "tg", split_axis=0, concat_axis=0, tiled=True)

    window_list = jax.ShapeDtypeStruct((windows, LANES), jnp.int32)
    longer_list = jax.ShapeDtypeStruct((2 * windows + 1, LANES), jnp.int32)
    square = jax.ShapeDtypeStruct((LANES, LANES), jnp.int32)
    even_map, odd_map, first, source, target, row_w, col_w = pl.pallas_call(
        functools.partial(map_kernel, extent, sticks),
        out_shape=(
            square,
            square,
            jax.ShapeDtypeStruct((16, LANES), jnp.int32),
            window_list,
            window_list,
            longer_list,
            longer_list,
        ),
        in_specs=[hbm] * 2,
        scratch_shapes=[
            pltpu.VMEM(row.shape, jnp.int32),
            pltpu.VMEM(col.shape, jnp.int32),
            pltpu.SemaphoreType.DMA((2,)),
        ],
        compiler_params=params(14 * total_sticks / 1536),
        cost_estimate=cost(4e9, 1e5),
        name="stick_map",
    )(row, col)

    constants = jnp.asarray(tables(extent))
    weighted = pl.pallas_call(
        functools.partial(plane_kernel, planes),
        out_shape=jax.ShapeDtypeStruct((devices, block + 8, LANES), F32),
        in_specs=[smem] + [vmem] * 7 + [hbm] * 2,
        out_specs=vmem,
        scratch_shapes=[
            pltpu.VMEM((windows, 2 * padded_planes, LANES), F32),
            pltpu.VMEM((windows, 2 * padded_planes, LANES), F32),
            pltpu.VMEM((2 * windows + 1, padded_planes, LANES), F32),
            pltpu.VMEM((padded_planes * rows, LANES), F32),
            pltpu.VMEM((padded_planes * rows, LANES), F32),
            pltpu.VMEM(constants.shape, BF16),
            pltpu.VMEM(potential.shape, F32),
            pltpu.SemaphoreType.DMA((2,)),
        ],
        compiler_params=params(52),
        cost_estimate=cost(2e10, 1e7),
        name="planes",
    )(first, even_map, odd_map, source, target, row_w, col_w, received, constants, potential)

    coefs, fields = [coef], [received]
    for shift in range(1, bands):
        ring = [((b + shift) % bands, b) for b in range(bands)]
        coefs.append(lax.ppermute(coef, "band", ring))
        fields.append(lax.ppermute(received, "band", ring))
    band = lax.axis_index("band").astype(jnp.int32)
    norm = 1.0 / (total_sticks * padded)
    places = jnp.stack([band, me])
    outgoing = pl.pallas_call(
        functools.partial(inner_kernel, bands, volume, norm),
        out_shape=(jax.ShapeDtypeStruct((block + 8, LANES), F32),) * devices,
        in_specs=[smem] + [vmem] * (2 + 2 * bands),
        compiler_params=params(6 + 1.5 * bands),
        name="inner",
    )(places, kc, *coefs, *fields, weighted)

    returned = [outgoing[0]]
    for k in range(1, devices):
        ring = [(d, (d + k) % devices) for d in range(devices)]
        returned.append(lax.ppermute(outgoing[k], "tg", ring))
    applied, subspace = pl.pallas_call(
        functools.partial(final_kernel, volume, devices),
        out_shape=(
            jax.ShapeDtypeStruct((sticks, 2, padded), F32),
            jax.ShapeDtypeStruct((2, 1, bands), F32),
        ),
        in_specs=[smem] + [vmem] * (6 + devices),
        scratch_shapes=[pltpu.VMEM((2 * total_planes, 2 * LANES), F32)],
        compiler_params=params(6 + 6 * total_planes / 192),
        name="planes_to_wave",
    )(me.reshape(1), lengths, *returned, kc, whi, wlo, shift_cos, shift_sin)
    return applied.reshape(1, sticks, 2, padded), subspace


def solution(mesh):
    in_specs = (P("band", "tg", None, None), P(), P(), P(), P(), P("tg", None, None))
    out_specs = (P("band", "tg", None, None), P(None, "band", None))
    body = functools.partial(shards, mesh.shape["band"], mesh.shape["tg"])
    return jax.shard_map(body, mesh=mesh, in_specs=in_specs, out_specs=out_specs, check_vma=False)
```

```python
import functools
import math

import jax
import jax.numpy as jnp
import ml_dtypes
import numpy as np
from jax import lax
from jax.experimental import pallas as pl
from jax.experimental.pallas import tpu as pltpu
from jax.sharding import PartitionSpec as P

RADIUS = 48
LANES = 128
F32 = jnp.float32
BF16 = jnp.bfloat16


def up8(n):
    return -(-n // 8) * 8


def split(x):
    hi = x.astype(BF16)
    return hi, (x - hi.astype(F32)).astype(BF16)


def dot3(a, b, dims=((1,), (0,))):
    def dot(x, y):
        return lax.dot_general(x, y, (dims, ((), ())), preferred_element_type=F32)

    return dot(a[0], b[0]) + (dot(a[0], b[1]) + dot(a[1], b[0]))


def trig(product, extent):
    n = product - extent * jnp.floor(product * (1.0 / extent) + 0.5)
    quarter = extent / 4.0
    unit = 2.0 * math.pi / extent

    def sine(m):
        u = m * unit
        v = u * u
        s = 1.0 / 6227020800.0
        for term in (-39916800.0, 362880.0, -5040.0, 120.0, -6.0, 1.0):
            s = s * v + 1.0 / term
        return u * s

    folded = jnp.where(
        jnp.abs(n) > quarter, jnp.where(n > 0, 2.0 * quarter, -2.0 * quarter) - n, n
    )
    return sine(quarter - jnp.abs(n)), sine(folded)


def pair(table):
    hi = table.astype(np.float32).astype(ml_dtypes.bfloat16)
    lo = (table - hi.astype(np.float64)).astype(ml_dtypes.bfloat16)
    return hi, lo


def row_blocks():
    even = -(-(RADIUS + 1) // 16) * 16
    odd = -(-RADIUS // 16) * 16
    return even, odd


@functools.cache
def tables(extent):
    half = extent // 2
    grid = np.arange(extent)
    freq = np.arange(2 * RADIUS + 1) - RADIUS

    def angles(f, g):
        a = 2.0 * np.pi * ((f[:, None] * g[None, :]) % extent) / extent
        return np.cos(a), np.sin(a)

    wide = 2 * LANES
    x_forward, x_back, forward, back = [], [], [], []
    for offset, rows in zip((0, 1), row_blocks()):
        cos, sin = angles(freq[offset::2], grid[:half])
        count = cos.shape[0]
        table = np.zeros((LANES, wide))
        table[:count, :half] = cos
        table[LANES // 2:LANES // 2 + count, :half] = -sin
        table[:count, LANES:LANES + half] = sin
        table[LANES // 2:LANES // 2 + count, LANES:LANES + half] = cos
        hi, lo = pair(table)
        x_forward.append(np.concatenate([hi, hi, lo], axis=0))
        hi, lo = pair(table.T.copy())
        x_back.append(
            np.concatenate(
                [np.concatenate([hi, lo], axis=1), np.concatenate([hi, np.zeros_like(lo)], axis=1)], axis=0
            )
        )
        parts = []
        for wave in (cos, sin):
            table = np.zeros((half, rows))
            table[:, :count] = wave.T
            hi, lo = pair(table)
            parts += [hi, hi, lo]
        forward.append(np.concatenate(parts, axis=1))
        table = np.zeros((2 * rows, half))
        table[:count] = cos
        table[rows:rows + count] = sin
        hi, lo = pair(table)
        back.append(np.concatenate([hi, hi, lo], axis=1))
    rows = [np.concatenate(x_forward, axis=1), np.concatenate(x_back, axis=1)]
    for table in forward + back:
        rows.append(np.pad(table, ((0, 0), (0, 2 * wide - table.shape[1]))))
    return np.concatenate(rows, axis=0)


def params(megabytes):
    return pltpu.CompilerParams(vmem_limit_bytes=int(min(megabytes, 56) * 2**20))


def fetch_all(sources, targets, sems):
    copies = [
        pltpu.make_async_copy(source, target, sems.at[i])
        for i, (source, target) in enumerate(zip(sources, targets))
    ]
    for copy in copies:
        copy.start()
    return copies


def cost(flops, nbytes):
    return pl.CostEstimate(flops=int(flops), bytes_accessed=int(nbytes), transcendentals=0)


def wave_kernel(
    extent, me_ref, length_hbm, row_hbm, col_hbm, plane_hbm, coef_hbm,
    out_ref, kc_ref, len_ref, whi_ref, wlo_ref, sc_ref, ss_ref,
    length_ref, row_ref, col_ref, plane_ref, coef_ref, sems,
):
    copies = fetch_all(
        (length_hbm, row_hbm, col_hbm, plane_hbm, coef_hbm),
        (length_ref, row_ref, col_ref, plane_ref, coef_ref),
        sems,
    )
    for copy in copies:
        copy.wait()
    devices = out_ref.shape[0]
    sticks, _, padded = coef_ref.shape
    padded_planes = plane_ref.shape[1] // devices
    me = me_ref[0]
    half = LANES // 2
    lead = (me * sticks) // LANES
    odd = (me * sticks) % LANES != 0

    def own(ref):
        first, second = ref[pl.ds(lead, 1), :], ref[pl.ds(lead + 1, 1), :]
        both = jnp.concatenate([first, second], axis=1)
        return jnp.where(odd, both[:, half:], both[:, :sticks])

    length_row = own(length_ref).astype(F32)
    at_row = own(row_ref)
    at_col = own(col_ref)
    at_row = jnp.where(at_row <= RADIUS, at_row, at_row - extent).astype(F32)
    at_col = jnp.where(at_col <= RADIUS, at_col, at_col - extent).astype(F32)
    square_row = at_row * at_row + at_col * at_col
    spare = jnp.ones((1, 2 * LANES - sticks), F32)
    aux = jnp.concatenate(
        [
            jnp.broadcast_to(jnp.concatenate([length_row, spare], axis=1), (LANES // 2, 2 * LANES)),
            jnp.broadcast_to(jnp.concatenate([square_row, spare], axis=1), (LANES // 2, 2 * LANES)),
        ],
        axis=0,
    )
    aux_col = jnp.transpose(aux)[:sticks]
    len_ref[...] = aux_col
    length = aux_col[:, 0:1]
    square = aux_col[:, LANES // 2:LANES // 2 + 1]
    middle = (length - 1.0) * 0.5
    position = lax.broadcasted_iota(jnp.int32, (sticks, padded), 1).astype(F32)
    kept = (position < length).astype(F32)
    kinetic = (square + (position - middle) * (position - middle)) * (1.0 / (RADIUS * RADIUS))
    wave = jnp.concatenate([coef_ref[:, 0, :] * kept, coef_ref[:, 1, :] * kept], axis=1)
    kc_ref[...] = wave * jnp.concatenate([kinetic, kinetic], axis=1)

    total = plane_ref.shape[1]
    plane_row = jnp.broadcast_to(plane_ref[...].astype(F32), (LANES, total))
    plane_col = jnp.transpose(plane_row)[:, 0:1]
    real = (plane_col >= 0.0).astype(F32)
    plane_col = jnp.maximum(plane_col, 0.0)
    harmonic = lax.broadcasted_iota(jnp.int32, (total, padded), 1).astype(F32)
    cos, sin = trig(plane_col * harmonic, extent)
    cos, sin = cos * real, sin * real
    parts = []
    for d in range(devices):
        c = cos[d * padded_planes:(d + 1) * padded_planes]
        s = sin[d * padded_planes:(d + 1) * padded_planes]
        parts.append(jnp.concatenate([c, -s], axis=1))
        parts.append(jnp.concatenate([s, c], axis=1))
    table = split(jnp.concatenate(parts, axis=0))
    whi_ref[...] = table[0]
    wlo_ref[...] = table[1]
    shift_cos, shift_sin = trig(plane_col * ((length_row - 1.0) * 0.5), extent)
    sc_ref[...] = shift_cos
    ss_ref[...] = shift_sin
    raw = dot3(table, split(wave), ((1,), (1,)))
    for d in range(devices):
        at = 2 * d * padded_planes
        re, im = raw[at:at + padded_planes], raw[at + padded_planes:at + 2 * padded_planes]
        c = shift_cos[d * padded_planes:(d + 1) * padded_planes]
        s = shift_sin[d * padded_planes:(d + 1) * padded_planes]
        along_re = re * c + im * s
        along_im = im * c - re * s
        out_ref[d, 0:padded_planes, :] = along_re[:, :LANES]
        out_ref[d, padded_planes:2 * padded_planes, :] = along_im[:, :LANES]
        out_ref[d, 2 * padded_planes:3 * padded_planes, :] = jnp.concatenate(
            [along_re[:, LANES:], along_im[:, LANES:]], axis=1
        )


def window_row(values, sticks):
    line = jnp.concatenate([values[i:i + 1] for i in range(values.shape[0])], axis=1)
    starts = range(0, line.shape[1], sticks)
    parts = [line[:, at:at + LANES] for at in starts]
    parts += [line[:, at + LANES:at + sticks] for at in starts]
    return jnp.concatenate(parts, axis=1)


def map_kernel(
    extent, sticks, in_row_hbm, in_col_hbm,
    even_ref, odd_ref, first_ref, src_ref, dst_ref, row_ref, col_ref,
    in_row_ref, in_col_ref, sems,
):
    for copy in fetch_all((in_row_hbm, in_col_hbm), (in_row_ref, in_col_ref), sems):
        copy.wait()
    windows = src_ref.shape[0]
    total = windows * LANES

    def signed(ref):
        value = ref[...]
        return window_row(jnp.where(value <= RADIUS, value, value - extent) + RADIUS, sticks)

    def dot(x, y, dims=((1,), (0,))):
        return lax.dot_general(x, y, (dims, ((), ())), preferred_element_type=F32)

    def bits(condition):
        return condition.astype(F32).astype(BF16)

    nt = ((1,), (1,))
    own_row, own_col = signed(in_row_ref), signed(in_col_ref)
    half = LANES // 2
    own_row = (own_row & 1) * row_blocks()[0] + (own_row >> 1)
    own_col = (own_col & 1) * half + (own_col >> 1)
    tall = lax.broadcasted_iota(jnp.int32, (LANES, total), 0)
    place = lax.broadcasted_iota(jnp.int32, (LANES, total), 1)
    in_col = tall == own_col
    row_hot, col_hot = bits(tall == own_row), bits(in_col)
    down = lax.broadcasted_iota(jnp.int32, (LANES, LANES), 0)
    across = lax.broadcasted_iota(jnp.int32, (LANES, LANES), 1)
    before = bits(down < across)
    after = bits(down > across)
    upto = bits(down >= across)
    ones = jnp.ones((LANES, LANES), BF16)
    taken = dot(row_hot, col_hot, nt)
    taken_t = dot(col_hot, row_hot, nt)
    taken_b, taken_tb = taken.astype(BF16), taken_t.astype(BF16)
    start = dot(dot(after, taken_b).astype(BF16), ones)
    end = start + dot(taken_b, ones)
    start_t = dot(ones, dot(taken_tb, before).astype(BF16))
    left = across < half
    standing = dot(taken_b, before) + start
    low_ones = bits(down < half)
    high_start = start + dot(taken_b, low_ones)
    ones_t = bits(across < half)
    high_start_t = start_t + dot(ones_t, taken_tb)
    limit = 2.0 * windows - 1.0

    def first_window(value):
        return jnp.minimum(jnp.floor(value * (1.0 / half)), limit)

    for ref, begin in ((even_ref, start), (odd_ref, high_start)):
        code = jnp.where(taken > 0.5, standing - half * first_window(begin), -1.0)
        turned = pltpu.roll(code, half, 1)
        both = jnp.where(left, code, turned) if ref is even_ref else jnp.where(left, turned, code)
        ref[...] = both.astype(jnp.int32)
    first_ref[...] = jnp.concatenate(
        [first_window(start_t[0:8]), first_window(high_start_t[0:8])], axis=0
    ).astype(jnp.int32)

    spot = place.astype(F32)
    in_range = (spot >= start[:, 0:1]) & (spot < end[:, 0:1])
    sorted_hot = bits(in_range)
    sorted_row = jnp.sum(jnp.where(in_range, tall, 0).astype(F32), axis=0, keepdims=True)
    sorted_rank = spot[0:1] - jnp.sum(jnp.where(in_range, start[:, 0:1], 0.0), axis=0, keepdims=True)
    counts = dot(dot(upto, taken_tb).astype(BF16), sorted_hot)
    sorted_col = jnp.sum((counts <= sorted_rank).astype(F32), axis=0, keepdims=True)
    names = place + 1
    name_hi = dot(jnp.where(in_col, names >> 6, 0).astype(F32).astype(BF16), row_hot, nt)
    name_lo = dot(jnp.where(in_col, names & 63, 0).astype(F32).astype(BF16), row_hot, nt)
    named = dot(name_hi.astype(BF16), sorted_hot) * 64.0 + dot(name_lo.astype(BF16), sorted_hot)
    source = jnp.sum(jnp.where(tall.astype(F32) == sorted_col, named, 0.0), axis=0, keepdims=True) - 1.0
    place_t = dot(after, taken_tb) + start_t
    place_hi = jnp.floor(place_t * (1.0 / 64.0))
    place_lo = place_t - 64.0 * place_hi
    placed = dot(place_hi.astype(BF16), row_hot) * 64.0 + dot(place_lo.astype(BF16), row_hot)
    target = jnp.sum(jnp.where(in_col, placed, 0.0), axis=0, keepdims=True)
    for values, ref in ((source, src_ref), (target, dst_ref)):
        values = values.astype(jnp.int32)
        for w in range(windows):
            ref[w:w + 1, :] = values[:, w * LANES:(w + 1) * LANES]
    is_left = left[0:8]
    shift = jnp.where(is_left, 0, half)
    sorted_col = sorted_col.astype(jnp.int32)
    sorted_key = sorted_row.astype(jnp.int32) * 2 + (sorted_col >> 6)
    sorted_col = sorted_col & (half - 1)
    for values, ref, add in ((sorted_key, row_ref, 0), (sorted_col, col_ref, shift)):
        for w in range(windows):
            line = jnp.broadcast_to(values[:, w * LANES:(w + 1) * LANES], (8, LANES))
            turned = pltpu.roll(line, half, 1)
            ref[2 * w:2 * w + 1, :] = (jnp.where(is_left, line, turned) + add)[0:1]
            ref[2 * w + 1:2 * w + 2, :] = (jnp.where(is_left, turned, line) + add)[0:1]
    row_ref[2 * windows:2 * windows + 1, :] = jnp.full((1, LANES), -1, jnp.int32)
    col_ref[2 * windows:2 * windows + 1, :] = jnp.zeros((1, LANES), jnp.int32)


def lane_take(x, index):
    return jnp.take_along_axis(x, index, axis=1, mode="promise_in_bounds")


def plane_kernel(
    planes, first_ref, even_ref, odd_ref, src_ref, dst_ref, row_ref, col_ref, recv_ref,
    *refs,
):
    table_hbm, pot_hbm, out_ref, x_ref, s_ref, t_ref, ge_ref, go_ref, table_ref, pot_ref, sems = refs
    devices = recv_ref.shape[0]
    padded_planes = recv_ref.shape[1] // 3
    windows = x_ref.shape[0]
    rows = ge_ref.shape[0] // padded_planes
    extent = pot_ref.shape[1]
    half = LANES // 2
    copies = fetch_all((table_hbm, pot_hbm), (table_ref, pot_ref), sems)

    low = lax.broadcasted_iota(jnp.int32, (padded_planes, LANES), 1) < half
    for d in range(devices):
        x_ref[d] = recv_ref[d, 0:2 * padded_planes, :]
    for e in range(devices // 2):
        first = recv_ref[2 * e, 2 * padded_planes:3 * padded_planes, :]
        second = recv_ref[2 * e + 1, 2 * padded_planes:3 * padded_planes, :]
        x_ref[devices + e, 0:padded_planes, :] = jnp.where(low, first, pltpu.roll(second, half, 1))
        x_ref[devices + e, padded_planes:2 * padded_planes, :] = jnp.where(
            low, pltpu.roll(first, half, 1), second
        )

    blocks = padded_planes // 8

    def reorder(order_ref, from_ref, to_ref):
        @pl.loop(0, windows, unroll=4)
        def _(v):
            order = jnp.broadcast_to(order_ref[pl.ds(v, 1), :], (8, LANES))
            index = order & (LANES - 1)
            window = order >> 7
            for j in range(2 * blocks):
                value = jnp.zeros((8, LANES), F32)
                for w in range(windows):
                    value = jnp.where(window == w, lane_take(from_ref[w, 8 * j:8 * j + 8, :], index), value)
                to_ref[v, 8 * j:8 * j + 8, :] = value

    reorder(src_ref, x_ref, s_ref)
    for w in range(windows):
        re, im = s_ref[w, 0:padded_planes, :], s_ref[w, padded_planes:2 * padded_planes, :]
        t_ref[2 * w] = jnp.where(low, re, pltpu.roll(im, half, 1))
        t_ref[2 * w + 1] = jnp.where(low, pltpu.roll(re, half, 1), im)

    left = low[0:8]
    upper_lanes = jnp.where(left, 0, half)
    sides = ((0, even_ref, ge_ref), (1, odd_ref, go_ref))

    @pl.loop(0, rows, unroll=8)
    def _(r):
        for side, code_ref, grid_ref in sides:
            first = first_ref[8 * side, r]
            code = jnp.broadcast_to(code_ref[pl.ds(r, 1), :], (8, LANES))
            index = (code & (half - 1)) + upper_lanes
            window = code >> 6
            for j in range(blocks):
                lead = lane_take(t_ref[first, 8 * j:8 * j + 8, :], index)
                trail = lane_take(t_ref[first + 1, 8 * j:8 * j + 8, :], index)
                value = jnp.where(window == 0, lead, jnp.where(window == 1, trail, 0.0))
                grid_ref[pl.ds(r + 8 * j * rows, 8, stride=rows), :] = value

    for copy in copies:
        copy.wait()
    even_rows, odd_rows = row_blocks()
    folded = extent // 2
    group = next(g for g in (8, 4, 2) if planes % g == 0)
    wide = 2 * LANES
    at_back = 3 * LANES
    at_y = at_back + 2 * wide
    at_even = at_y + 2 * folded
    at_odd = at_even + 2 * even_rows
    x_forward = (table_ref[0:at_back, :wide], table_ref[0:at_back, wide:])
    x_back = (table_ref[at_back:at_y, :wide], table_ref[at_back:at_y, wide:])
    y_even = table_ref[at_y:at_y + folded, :6 * even_rows]
    y_odd = table_ref[at_y + folded:at_even, :6 * odd_rows]
    back_even = table_ref[at_even:at_odd, :3 * folded]
    back_odd = table_ref[at_odd:at_odd + 2 * odd_rows, :3 * folded]

    def dot(x, y):
        return jnp.dot(x, y, preferred_element_type=F32)

    def stack(x, axis):
        hi, lo = split(x)
        return jnp.concatenate([hi, lo, hi], axis=axis)

    def turn(x):
        lane = lax.broadcasted_iota(jnp.int32, (x.shape[0], LANES), 1) < half
        parts = []
        for at in range(0, x.shape[1], LANES):
            rolled = pltpu.roll(x[:, at:at + LANES], half, 1)
            parts.append(jnp.where(lane, -rolled, rolled))
        return jnp.concatenate(parts, axis=1)

    @pl.loop(0, planes // group)
    def _(step):
        lines = []
        for t in range(group):
            base = pl.multiple_of((step * group + t) * rows, 16)
            parts = []
            for at, size, table in ((0, even_rows, y_even), (even_rows, odd_rows, y_odd)):
                pick = pl.ds(base + at, size)
                spectrum = jnp.concatenate([ge_ref[pick, :], go_ref[pick, :]], axis=1)
                both = jnp.concatenate([stack(spectrum, 0), stack(turn(spectrum), 0)], axis=0)
                parts.append(dot(table, both))
            lines.append(parts[0] + parts[1])
            lines.append(parts[0] - parts[1])
        lines = jnp.concatenate(lines, axis=0)
        field_even = dot(stack(lines[:, :LANES], 1), x_forward[0])
        field_odd = dot(stack(lines[:, LANES:], 1), x_forward[1])
        spare = jnp.zeros((extent, LANES - folded), F32)
        sums, differences = [], []
        for t in range(group):
            v = pot_ref[step * group + t]
            v_near = jnp.concatenate([v[:, :folded], spare], axis=1)
            v_far = jnp.concatenate([v[:, folded:], spare], axis=1)
            even = field_even[t * extent:(t + 1) * extent]
            odd = field_odd[t * extent:(t + 1) * extent]
            near = (even + odd) * jnp.concatenate([v_near, v_near], axis=1)
            far = (even - odd) * jnp.concatenate([v_far, v_far], axis=1)
            sums.append(near + far)
            differences.append(near - far)
        back = []
        for weighted, table in ((sums, x_back[0]), (differences, x_back[1])):
            both = dot(jnp.concatenate(split(jnp.concatenate(weighted, axis=0)), axis=1), table)
            back.append(both[:, :LANES] + both[:, LANES:])
        back = jnp.concatenate(back, axis=1)
        for t in range(group):
            base = pl.multiple_of((step * group + t) * rows, 16)
            upper = back[t * extent:t * extent + folded]
            lower = back[t * extent + folded:(t + 1) * extent]
            for at, size, table, value in (
                (0, even_rows, back_even, upper + lower), (even_rows, odd_rows, back_odd, upper - lower)
            ):
                both = dot(table, stack(value, 0))
                value = both[:size] - turn(both[size:])
                pick = pl.ds(base + at, size)
                ge_ref[pick, :] = value[:, :LANES]
                go_ref[pick, :] = value[:, LANES:]

    @pl.loop(0, rows, unroll=8)
    def _(r):
        for side, _, grid_ref in sides:
            first = first_ref[8 * side, r]
            values = [grid_ref[pl.ds(r + 8 * j * rows, 8, stride=rows), :] for j in range(blocks)]
            for t in range(2):
                index = jnp.broadcast_to(col_ref[pl.ds(first + t, 1), :], (8, LANES))
                hit = jnp.broadcast_to(row_ref[pl.ds(first + t, 1), :], (8, LANES)) == 2 * r + side
                for j in range(blocks):
                    pltpu.store(
                        t_ref.at[first + t, 8 * j:8 * j + 8, :], lane_take(values[j], index), mask=hit
                    )

    for w in range(windows):
        first, second = t_ref[2 * w], t_ref[2 * w + 1]
        s_ref[w, 0:padded_planes, :] = jnp.where(low, first, pltpu.roll(second, half, 1))
        s_ref[w, padded_planes:2 * padded_planes, :] = jnp.where(low, pltpu.roll(first, half, 1), second)
    reorder(dst_ref, s_ref, x_ref)
    for w in range(devices):
        out_ref[w, 0:2 * padded_planes, :] = x_ref[w]
    for e in range(devices // 2):
        re = x_ref[devices + e, 0:padded_planes, :]
        im = x_ref[devices + e, padded_planes:2 * padded_planes, :]
        out_ref[2 * e, 2 * padded_planes:3 * padded_planes, :] = jnp.where(
            low, re, pltpu.roll(im, half, 1)
        )
        out_ref[2 * e + 1, 2 * padded_planes:3 * padded_planes, :] = jnp.where(
            low, pltpu.roll(re, half, 1), im
        )
    for d in range(devices):
        out_ref[d, 3 * padded_planes:, :] = jnp.zeros((8, LANES), F32)


def inner_kernel(bands, volume, norm, place_ref, *refs):
    kc_ref = refs[0]
    coefs = refs[1:1 + bands]
    fields = refs[1 + bands:1 + 2 * bands]
    in_ref = refs[1 + 2 * bands]
    out_refs = refs[2 + 2 * bands:]
    devices = in_ref.shape[0]
    padded_planes = (in_ref.shape[1] - 8) // 3
    half = LANES // 2
    padded = coefs[0].shape[2]
    me, mine = place_ref[0], place_ref[1]
    low = lax.broadcasted_iota(jnp.int32, (padded_planes, LANES), 1) < half

    def fold(x):
        rows = x.shape[0]
        total = x[0:8]
        for at in range(8, rows, 8):
            total = total + x[at:at + 8]
        return total

    kc = kc_ref[...]
    kc_re, kc_im = kc[:, :padded], kc[:, padded:]
    sums = []
    for m in range(bands):
        c_re, c_im = coefs[m][:, 0, :], coefs[m][:, 1, :]
        sums.append([fold(c_re * kc_re + c_im * kc_im), fold(c_re * kc_im - c_im * kc_re)])
    local = [[jnp.zeros((8, LANES), F32), jnp.zeros((8, LANES), F32)] for _ in range(bands)]
    for d in range(devices):
        value = in_ref[d, 0:3 * padded_planes, :]
        re, im, rest = value[:padded_planes], value[padded_planes:2 * padded_planes], value[2 * padded_planes:]
        turned = pltpu.roll(rest, half, 1)
        other = jnp.concatenate([im, -re, jnp.where(low, turned, -turned)], axis=0)
        for m in range(bands):
            col = fields[m][d, 0:3 * padded_planes, :]
            local[m][0] = local[m][0] + fold(col * value)
            local[m][1] = local[m][1] + fold(col * other)
    lane = lax.broadcasted_iota(jnp.int32, (8, LANES), 1)
    row = lax.broadcasted_iota(jnp.int32, (8, LANES), 0)
    tile = jnp.zeros((8, LANES), F32)
    for m in range(bands):
        at = me ^ m
        for part, sign in ((0, 1.0), (1, -1.0)):
            partial = sums[m][part] + volume * local[m][part]
            scalar = jnp.sum(jnp.sum(partial, axis=1, keepdims=True), axis=0, keepdims=True)
            tile = jnp.where((lane == at) & (row == part), sign * norm * scalar, tile)
    for k in range(devices):
        out_refs[k][0:3 * padded_planes, :] = in_ref[mine ^ k, 0:3 * padded_planes, :]
        out_refs[k][3 * padded_planes:, :] = tile


def final_kernel(volume, devices, me_ref, len_ref, *refs):
    ret_refs = refs[:devices]
    kc_ref, whi_ref, wlo_ref, sc_ref, ss_ref, out_ref, sub_ref, stack_ref = refs[devices:]
    padded_planes = (ret_refs[0].shape[0] - 8) // 3
    sticks, _, padded = out_ref.shape
    half = LANES // 2
    bands = sub_ref.shape[2]
    total = jnp.zeros((8, LANES), F32)
    me = me_ref[0]
    for k in range(devices):
        value = ret_refs[k][...]
        base = pl.multiple_of((me ^ k) * padded_planes, 8)
        total = total + value[3 * padded_planes:]
        rest = value[2 * padded_planes:3 * padded_planes]
        re = jnp.concatenate([value[:padded_planes], rest[:, :half]], axis=1)
        im = jnp.concatenate([value[padded_planes:2 * padded_planes], rest[:, half:]], axis=1)
        c = sc_ref[pl.ds(base, padded_planes), :]
        s = ss_ref[pl.ds(base, padded_planes), :]
        stack_ref[pl.ds(2 * base, padded_planes), :sticks] = re * c - im * s
        stack_ref[pl.ds(2 * base + padded_planes, padded_planes), :sticks] = re * s + im * c
    turned = jnp.transpose(stack_ref[...])[:sticks]
    local = dot3(split(turned), (whi_ref[...], wlo_ref[...])) * volume
    position = lax.broadcasted_iota(jnp.int32, (sticks, padded), 1).astype(F32)
    kept = position < len_ref[:, 0:1]
    kc = kc_ref[...]
    out_ref[:, 0, :] = jnp.where(kept, kc[:, :padded] + local[:, :padded], 0.0)
    out_ref[:, 1, :] = jnp.where(kept, kc[:, padded:] + local[:, padded:], 0.0)
    sub_ref[:, 0, :] = total[0:2, :bands]


def pairs(count, k):
    return [(d, d ^ k) for d in range(count)]


def shards(bands, devices, coefficients, stick_col, stick_row, stick_length, plane_of_slot, potential):
    extent = plane_of_slot.shape[0]
    sticks = coefficients.shape[1]
    padded = coefficients.shape[3]
    total_sticks = stick_col.shape[0]
    planes = potential.shape[0]
    padded_planes = up8(planes)
    powers = devices & (devices - 1) == 0 and bands & (bands - 1) == 0
    if sticks != LANES + LANES // 2 or not powers or planes % 2:
        raise ValueError("sizes")
    rows = sum(row_blocks())
    volume = 1.0 / (extent * extent * extent)
    me = lax.axis_index("tg").astype(jnp.int32)
    coef = coefficients.reshape(sticks, 2, padded)

    length, row, col = (v.reshape(-1, LANES) for v in (stick_length, stick_row, stick_col))
    slots = plane_of_slot.reshape(devices, planes)
    if padded_planes > planes:
        slots = jnp.pad(slots, ((0, 0), (0, padded_planes - planes)), constant_values=-1)
    slots = slots.reshape(1, devices * padded_planes)
    windows = total_sticks // LANES
    smem = pl.BlockSpec(memory_space=pltpu.SMEM)
    vmem = pl.BlockSpec(memory_space=pltpu.VMEM)
    hbm = pl.BlockSpec(memory_space=pltpu.HBM)

    block = 3 * padded_planes
    total_planes = devices * padded_planes
    sent, kc, lengths, whi, wlo, shift_cos, shift_sin = pl.pallas_call(
        functools.partial(wave_kernel, extent),
        out_shape=(
            jax.ShapeDtypeStruct((devices, block, LANES), F32),
            jax.ShapeDtypeStruct((sticks, 2 * padded), F32),
            jax.ShapeDtypeStruct((sticks, LANES), F32),
            jax.ShapeDtypeStruct((2 * total_planes, 2 * padded), BF16),
            jax.ShapeDtypeStruct((2 * total_planes, 2 * padded), BF16),
            jax.ShapeDtypeStruct((total_planes, sticks), F32),
            jax.ShapeDtypeStruct((total_planes, sticks), F32),
        ),
        in_specs=[smem] + [hbm] * 5,
        scratch_shapes=[
            pltpu.VMEM(length.shape, jnp.int32),
            pltpu.VMEM(row.shape, jnp.int32),
            pltpu.VMEM(col.shape, jnp.int32),
            pltpu.VMEM(slots.shape, jnp.int32),
            pltpu.VMEM(coef.shape, F32),
            pltpu.SemaphoreType.DMA((5,)),
        ],
        compiler_params=params(56),
        name="wave_to_planes",
    )(me.reshape(1), length, row, col, slots, coef)

    received = lax.all_to_all(sent, "tg", split_axis=0, concat_axis=0, tiled=True)

    window_list = jax.ShapeDtypeStruct((windows, LANES), jnp.int32)
    longer_list = jax.ShapeDtypeStruct((2 * windows + 1, LANES), jnp.int32)
    square = jax.ShapeDtypeStruct((LANES, LANES), jnp.int32)
    even_map, odd_map, first, source, target, row_w, col_w = pl.pallas_call(
        functools.partial(map_kernel, extent, sticks),
        out_shape=(
            square,
            square,
            jax.ShapeDtypeStruct((16, LANES), jnp.int32),
            window_list,
            window_list,
            longer_list,
            longer_list,
        ),
        in_specs=[hbm] * 2,
        scratch_shapes=[
            pltpu.VMEM(row.shape, jnp.int32),
            pltpu.VMEM(col.shape, jnp.int32),
            pltpu.SemaphoreType.DMA((2,)),
        ],
        compiler_params=params(14 * total_sticks / 1536),
        cost_estimate=cost(4e9, 1e5),
        name="stick_map",
    )(row, col)

    constants = jnp.asarray(tables(extent))
    weighted = pl.pallas_call(
        functools.partial(plane_kernel, planes),
        out_shape=jax.ShapeDtypeStruct((devices, block + 8, LANES), F32),
        in_specs=[smem] + [vmem] * 7 + [hbm] * 2,
        out_specs=vmem,
        scratch_shapes=[
            pltpu.VMEM((windows, 2 * padded_planes, LANES), F32),
            pltpu.VMEM((windows, 2 * padded_planes, LANES), F32),
            pltpu.VMEM((2 * windows + 1, padded_planes, LANES), F32),
            pltpu.VMEM((padded_planes * rows, LANES), F32),
            pltpu.VMEM((padded_planes * rows, LANES), F32),
            pltpu.VMEM(constants.shape, BF16),
            pltpu.VMEM(potential.shape, F32),
            pltpu.SemaphoreType.DMA((2,)),
        ],
        compiler_params=params(52),
        cost_estimate=cost(2e10, 1e7),
        name="planes",
    )(first, even_map, odd_map, source, target, row_w, col_w, received, constants, potential)

    coefs, fields = [coef], [received]
    for m in range(1, bands):
        coefs.append(lax.ppermute(coef, "band", pairs(bands, m)))
        fields.append(lax.ppermute(received, "band", pairs(bands, m)))
    band = lax.axis_index("band").astype(jnp.int32)
    norm = 1.0 / (total_sticks * padded)
    places = jnp.stack([band, me])
    outgoing = pl.pallas_call(
        functools.partial(inner_kernel, bands, volume, norm),
        out_shape=(jax.ShapeDtypeStruct((block + 8, LANES), F32),) * devices,
        in_specs=[smem] + [vmem] * (2 + 2 * bands),
        compiler_params=params(6 + 1.5 * bands),
        name="inner",
    )(places, kc, *coefs, *fields, weighted)

    returned = [outgoing[0]]
    for k in range(1, devices):
        returned.append(lax.ppermute(outgoing[k], "tg", pairs(devices, k)))
    applied, subspace = pl.pallas_call(
        functools.partial(final_kernel, volume, devices),
        out_shape=(
            jax.ShapeDtypeStruct((sticks, 2, padded), F32),
            jax.ShapeDtypeStruct((2, 1, bands), F32),
        ),
        in_specs=[smem] + [vmem] * (6 + devices),
        scratch_shapes=[pltpu.VMEM((2 * total_planes, 2 * LANES), F32)],
        compiler_params=params(6 + 6 * total_planes / 192),
        name="planes_to_wave",
    )(me.reshape(1), lengths, *returned, kc, whi, wlo, shift_cos, shift_sin)
    return applied.reshape(1, sticks, 2, padded), subspace


def solution(mesh):
    in_specs = (P("band", "tg", None, None), P(), P(), P(), P(), P("tg", None, None))
    out_specs = (P("band", "tg", None, None), P(None, "band", None))
    body = functools.partial(shards, mesh.shape["band"], mesh.shape["tg"])
    return jax.shard_map(body, mesh=mesh, in_specs=in_specs, out_specs=out_specs, check_vma=False)
```

```python
import functools
import math

import jax
import jax.numpy as jnp
import ml_dtypes
import numpy as np
from jax import lax
from jax.experimental import pallas as pl
from jax.experimental.pallas import tpu as pltpu
from jax.sharding import PartitionSpec as P

RADIUS = 48
LANES = 128
F32 = jnp.float32
BF16 = jnp.bfloat16


def up8(n):
    return -(-n // 8) * 8


def split(x):
    hi = x.astype(BF16)
    return hi, (x - hi.astype(F32)).astype(BF16)


def dot3(a, b, dims=((1,), (0,))):
    def dot(x, y):
        return lax.dot_general(x, y, (dims, ((), ())), preferred_element_type=F32)

    return dot(a[0], b[0]) + (dot(a[0], b[1]) + dot(a[1], b[0]))


def trig(product, extent):
    n = product - extent * jnp.floor(product * (1.0 / extent) + 0.5)
    quarter = extent / 4.0
    unit = 2.0 * math.pi / extent

    def sine(m):
        u = m * unit
        v = u * u
        s = 1.0 / 6227020800.0
        for term in (-39916800.0, 362880.0, -5040.0, 120.0, -6.0, 1.0):
            s = s * v + 1.0 / term
        return u * s

    folded = jnp.where(
        jnp.abs(n) > quarter, jnp.where(n > 0, 2.0 * quarter, -2.0 * quarter) - n, n
    )
    return sine(quarter - jnp.abs(n)), sine(folded)


def pair(table):
    hi = table.astype(np.float32).astype(ml_dtypes.bfloat16)
    lo = (table - hi.astype(np.float64)).astype(ml_dtypes.bfloat16)
    return hi, lo


def row_blocks():
    even = -(-(RADIUS + 1) // 16) * 16
    odd = -(-RADIUS // 16) * 16
    return even, odd


@functools.cache
def tables(extent):
    half = extent // 2
    grid = np.arange(extent)
    freq = np.arange(2 * RADIUS + 1) - RADIUS

    def angles(f, g):
        a = 2.0 * np.pi * ((f[:, None] * g[None, :]) % extent) / extent
        return np.cos(a), np.sin(a)

    wide = 2 * LANES
    x_forward, x_back, forward, back = [], [], [], []
    for offset, rows in zip((0, 1), row_blocks()):
        cos, sin = angles(freq[offset::2], grid[:half])
        count = cos.shape[0]
        table = np.zeros((LANES, wide))
        table[:count, :half] = cos
        table[LANES // 2:LANES // 2 + count, :half] = -sin
        table[:count, LANES:LANES + half] = sin
        table[LANES // 2:LANES // 2 + count, LANES:LANES + half] = cos
        hi, lo = pair(table)
        x_forward.append(np.concatenate([hi, hi, lo], axis=0))
        hi, lo = pair(table.T.copy())
        x_back.append(
            np.concatenate(
                [np.concatenate([hi, lo], axis=1), np.concatenate([hi, np.zeros_like(lo)], axis=1)], axis=0
            )
        )
        parts = []
        for wave in (cos, sin):
            table = np.zeros((half, rows))
            table[:, :count] = wave.T
            hi, lo = pair(table)
            parts += [hi, hi, lo]
        forward.append(np.concatenate(parts, axis=1))
        table = np.zeros((2 * rows, half))
        table[:count] = cos
        table[rows:rows + count] = sin
        hi, lo = pair(table)
        back.append(np.concatenate([hi, hi, lo], axis=1))
    rows = [np.concatenate(x_forward, axis=1), np.concatenate(x_back, axis=1)]
    for table in forward + back:
        rows.append(np.pad(table, ((0, 0), (0, 2 * wide - table.shape[1]))))
    return np.concatenate(rows, axis=0)


def params(megabytes):
    return pltpu.CompilerParams(vmem_limit_bytes=int(min(megabytes, 56) * 2**20))


def fetch_all(sources, targets, sems):
    copies = [
        pltpu.make_async_copy(source, target, sems.at[i])
        for i, (source, target) in enumerate(zip(sources, targets))
    ]
    for copy in copies:
        copy.start()
    return copies


def cost(flops, nbytes):
    return pl.CostEstimate(flops=int(flops), bytes_accessed=int(nbytes), transcendentals=0)


def wave_kernel(
    extent, devices, me_ref, length_hbm, row_hbm, col_hbm, plane_hbm, coef_hbm, *refs,
):
    out_refs, refs = refs[:devices], refs[devices:]
    kc_ref, len_ref, whi_ref, wlo_ref, sc_ref, ss_ref = refs[:6]
    length_ref, row_ref, col_ref, plane_ref, coef_ref, out_ref, sems = refs[6:]
    copies = fetch_all(
        (length_hbm, row_hbm, col_hbm, plane_hbm, coef_hbm),
        (length_ref, row_ref, col_ref, plane_ref, coef_ref),
        sems,
    )
    for copy in copies:
        copy.wait()
    sticks, _, padded = coef_ref.shape
    padded_planes = plane_ref.shape[1] // devices
    me = me_ref[0]
    half = LANES // 2
    lead = (me * sticks) // LANES
    odd = (me * sticks) % LANES != 0

    def own(ref):
        first, second = ref[pl.ds(lead, 1), :], ref[pl.ds(lead + 1, 1), :]
        both = jnp.concatenate([first, second], axis=1)
        return jnp.where(odd, both[:, half:], both[:, :sticks])

    length_row = own(length_ref).astype(F32)
    at_row = own(row_ref)
    at_col = own(col_ref)
    at_row = jnp.where(at_row <= RADIUS, at_row, at_row - extent).astype(F32)
    at_col = jnp.where(at_col <= RADIUS, at_col, at_col - extent).astype(F32)
    square_row = at_row * at_row + at_col * at_col
    spare = jnp.ones((1, 2 * LANES - sticks), F32)
    aux = jnp.concatenate(
        [
            jnp.broadcast_to(jnp.concatenate([length_row, spare], axis=1), (LANES // 2, 2 * LANES)),
            jnp.broadcast_to(jnp.concatenate([square_row, spare], axis=1), (LANES // 2, 2 * LANES)),
        ],
        axis=0,
    )
    aux_col = jnp.transpose(aux)[:sticks]
    len_ref[...] = aux_col
    length = aux_col[:, 0:1]
    square = aux_col[:, LANES // 2:LANES // 2 + 1]
    middle = (length - 1.0) * 0.5
    position = lax.broadcasted_iota(jnp.int32, (sticks, padded), 1).astype(F32)
    kept = (position < length).astype(F32)
    kinetic = (square + (position - middle) * (position - middle)) * (1.0 / (RADIUS * RADIUS))
    wave = jnp.concatenate([coef_ref[:, 0, :] * kept, coef_ref[:, 1, :] * kept], axis=1)
    kc_ref[...] = wave * jnp.concatenate([kinetic, kinetic], axis=1)

    total = plane_ref.shape[1]
    plane_row = jnp.broadcast_to(plane_ref[...].astype(F32), (LANES, total))
    plane_col = jnp.transpose(plane_row)[:, 0:1]
    real = (plane_col >= 0.0).astype(F32)
    plane_col = jnp.maximum(plane_col, 0.0)
    harmonic = lax.broadcasted_iota(jnp.int32, (total, padded), 1).astype(F32)
    cos, sin = trig(plane_col * harmonic, extent)
    cos, sin = cos * real, sin * real
    parts = []
    for d in range(devices):
        c = cos[d * padded_planes:(d + 1) * padded_planes]
        s = sin[d * padded_planes:(d + 1) * padded_planes]
        parts.append(jnp.concatenate([c, -s], axis=1))
        parts.append(jnp.concatenate([s, c], axis=1))
    table = split(jnp.concatenate(parts, axis=0))
    whi_ref[...] = table[0]
    wlo_ref[...] = table[1]
    shift_cos, shift_sin = trig(plane_col * ((length_row - 1.0) * 0.5), extent)
    sc_ref[...] = shift_cos
    ss_ref[...] = shift_sin
    raw = dot3(table, split(wave), ((1,), (1,)))
    for d in range(devices):
        at = 2 * d * padded_planes
        re, im = raw[at:at + padded_planes], raw[at + padded_planes:at + 2 * padded_planes]
        c = shift_cos[d * padded_planes:(d + 1) * padded_planes]
        s = shift_sin[d * padded_planes:(d + 1) * padded_planes]
        along_re = re * c + im * s
        along_im = im * c - re * s
        out_ref[d, 0:padded_planes, :] = along_re[:, :LANES]
        out_ref[d, padded_planes:2 * padded_planes, :] = along_im[:, :LANES]
        out_ref[d, 2 * padded_planes:3 * padded_planes, :] = jnp.concatenate(
            [along_re[:, LANES:], along_im[:, LANES:]], axis=1
        )
    for k in range(devices):
        out_refs[k][...] = out_ref[lax.rem(me + k, devices)]


def merge_kernel(devices, me_ref, *refs):
    me = me_ref[0]
    for k in range(devices):
        refs[devices][lax.rem(me + devices - k, devices)] = refs[k][...]


def window_row(values, sticks):
    line = jnp.concatenate([values[i:i + 1] for i in range(values.shape[0])], axis=1)
    starts = range(0, line.shape[1], sticks)
    parts = [line[:, at:at + LANES] for at in starts]
    parts += [line[:, at + LANES:at + sticks] for at in starts]
    return jnp.concatenate(parts, axis=1)


def map_kernel(
    extent, sticks, in_row_hbm, in_col_hbm,
    even_ref, odd_ref, first_ref, src_ref, dst_ref, row_ref, col_ref,
    in_row_ref, in_col_ref, sems,
):
    for copy in fetch_all((in_row_hbm, in_col_hbm), (in_row_ref, in_col_ref), sems):
        copy.wait()
    windows = src_ref.shape[0]
    total = windows * LANES

    def signed(ref):
        value = ref[...]
        return window_row(jnp.where(value <= RADIUS, value, value - extent) + RADIUS, sticks)

    def dot(x, y, dims=((1,), (0,))):
        return lax.dot_general(x, y, (dims, ((), ())), preferred_element_type=F32)

    def bits(condition):
        return condition.astype(F32).astype(BF16)

    nt = ((1,), (1,))
    own_row, own_col = signed(in_row_ref), signed(in_col_ref)
    half = LANES // 2
    own_row = (own_row & 1) * row_blocks()[0] + (own_row >> 1)
    own_col = (own_col & 1) * half + (own_col >> 1)
    tall = lax.broadcasted_iota(jnp.int32, (LANES, total), 0)
    place = lax.broadcasted_iota(jnp.int32, (LANES, total), 1)
    in_col = tall == own_col
    row_hot, col_hot = bits(tall == own_row), bits(in_col)
    down = lax.broadcasted_iota(jnp.int32, (LANES, LANES), 0)
    across = lax.broadcasted_iota(jnp.int32, (LANES, LANES), 1)
    before = bits(down < across)
    after = bits(down > across)
    upto = bits(down >= across)
    ones = jnp.ones((LANES, LANES), BF16)
    taken = dot(row_hot, col_hot, nt)
    taken_t = dot(col_hot, row_hot, nt)
    taken_b, taken_tb = taken.astype(BF16), taken_t.astype(BF16)
    start = dot(dot(after, taken_b).astype(BF16), ones)
    end = start + dot(taken_b, ones)
    start_t = dot(ones, dot(taken_tb, before).astype(BF16))
    left = across < half
    standing = dot(taken_b, before) + start
    low_ones = bits(down < half)
    high_start = start + dot(taken_b, low_ones)
    ones_t = bits(across < half)
    high_start_t = start_t + dot(ones_t, taken_tb)
    limit = 2.0 * windows - 1.0

    def first_window(value):
        return jnp.minimum(jnp.floor(value * (1.0 / half)), limit)

    for ref, begin in ((even_ref, start), (odd_ref, high_start)):
        code = jnp.where(taken > 0.5, standing - half * first_window(begin), -1.0)
        turned = pltpu.roll(code, half, 1)
        both = jnp.where(left, code, turned) if ref is even_ref else jnp.where(left, turned, code)
        ref[...] = both.astype(jnp.int32)
    first_ref[...] = jnp.concatenate(
        [first_window(start_t[0:8]), first_window(high_start_t[0:8])], axis=0
    ).astype(jnp.int32)

    spot = place.astype(F32)
    in_range = (spot >= start[:, 0:1]) & (spot < end[:, 0:1])
    sorted_hot = bits(in_range)
    sorted_row = jnp.sum(jnp.where(in_range, tall, 0).astype(F32), axis=0, keepdims=True)
    sorted_rank = spot[0:1] - jnp.sum(jnp.where(in_range, start[:, 0:1], 0.0), axis=0, keepdims=True)
    counts = dot(dot(upto, taken_tb).astype(BF16), sorted_hot)
    sorted_col = jnp.sum((counts <= sorted_rank).astype(F32), axis=0, keepdims=True)
    names = place + 1
    name_hi = dot(jnp.where(in_col, names >> 6, 0).astype(F32).astype(BF16), row_hot, nt)
    name_lo = dot(jnp.where(in_col, names & 63, 0).astype(F32).astype(BF16), row_hot, nt)
    named = dot(name_hi.astype(BF16), sorted_hot) * 64.0 + dot(name_lo.astype(BF16), sorted_hot)
    source = jnp.sum(jnp.where(tall.astype(F32) == sorted_col, named, 0.0), axis=0, keepdims=True) - 1.0
    place_t = dot(after, taken_tb) + start_t
    place_hi = jnp.floor(place_t * (1.0 / 64.0))
    place_lo = place_t - 64.0 * place_hi
    placed = dot(place_hi.astype(BF16), row_hot) * 64.0 + dot(place_lo.astype(BF16), row_hot)
    target = jnp.sum(jnp.where(in_col, placed, 0.0), axis=0, keepdims=True)
    for values, ref in ((source, src_ref), (target, dst_ref)):
        values = values.astype(jnp.int32)
        for w in range(windows):
            ref[w:w + 1, :] = values[:, w * LANES:(w + 1) * LANES]
    is_left = left[0:8]
    shift = jnp.where(is_left, 0, half)
    sorted_col = sorted_col.astype(jnp.int32)
    sorted_key = sorted_row.astype(jnp.int32) * 2 + (sorted_col >> 6)
    sorted_col = sorted_col & (half - 1)
    for values, ref, add in ((sorted_key, row_ref, 0), (sorted_col, col_ref, shift)):
        for w in range(windows):
            line = jnp.broadcast_to(values[:, w * LANES:(w + 1) * LANES], (8, LANES))
            turned = pltpu.roll(line, half, 1)
            ref[2 * w:2 * w + 1, :] = (jnp.where(is_left, line, turned) + add)[0:1]
            ref[2 * w + 1:2 * w + 2, :] = (jnp.where(is_left, turned, line) + add)[0:1]
    row_ref[2 * windows:2 * windows + 1, :] = jnp.full((1, LANES), -1, jnp.int32)
    col_ref[2 * windows:2 * windows + 1, :] = jnp.zeros((1, LANES), jnp.int32)


def lane_take(x, index):
    return jnp.take_along_axis(x, index, axis=1, mode="promise_in_bounds")


def plane_kernel(
    planes, first_ref, even_ref, odd_ref, src_ref, dst_ref, row_ref, col_ref, recv_ref,
    *refs,
):
    table_hbm, pot_hbm, out_ref, x_ref, s_ref, t_ref, ge_ref, go_ref, table_ref, pot_ref, sems = refs
    devices = recv_ref.shape[0]
    padded_planes = recv_ref.shape[1] // 3
    windows = x_ref.shape[0]
    rows = ge_ref.shape[0] // padded_planes
    extent = pot_ref.shape[1]
    half = LANES // 2
    copies = fetch_all((table_hbm, pot_hbm), (table_ref, pot_ref), sems)

    low = lax.broadcasted_iota(jnp.int32, (padded_planes, LANES), 1) < half
    for d in range(devices):
        x_ref[d] = recv_ref[d, 0:2 * padded_planes, :]
    for e in range(devices // 2):
        first = recv_ref[2 * e, 2 * padded_planes:3 * padded_planes, :]
        second = recv_ref[2 * e + 1, 2 * padded_planes:3 * padded_planes, :]
        x_ref[devices + e, 0:padded_planes, :] = jnp.where(low, first, pltpu.roll(second, half, 1))
        x_ref[devices + e, padded_planes:2 * padded_planes, :] = jnp.where(
            low, pltpu.roll(first, half, 1), second
        )

    blocks = padded_planes // 8

    def reorder(order_ref, from_ref, to_ref):
        @pl.loop(0, windows, unroll=4)
        def _(v):
            order = jnp.broadcast_to(order_ref[pl.ds(v, 1), :], (8, LANES))
            index = order & (LANES - 1)
            window = order >> 7
            for j in range(2 * blocks):
                value = jnp.zeros((8, LANES), F32)
                for w in range(windows):
                    value = jnp.where(window == w, lane_take(from_ref[w, 8 * j:8 * j + 8, :], index), value)
                to_ref[v, 8 * j:8 * j + 8, :] = value

    reorder(src_ref, x_ref, s_ref)
    for w in range(windows):
        re, im = s_ref[w, 0:padded_planes, :], s_ref[w, padded_planes:2 * padded_planes, :]
        t_ref[2 * w] = jnp.where(low, re, pltpu.roll(im, half, 1))
        t_ref[2 * w + 1] = jnp.where(low, pltpu.roll(re, half, 1), im)

    left = low[0:8]
    upper_lanes = jnp.where(left, 0, half)
    sides = ((0, even_ref, ge_ref), (1, odd_ref, go_ref))

    @pl.loop(0, rows, unroll=8)
    def _(r):
        for side, code_ref, grid_ref in sides:
            first = first_ref[8 * side, r]
            code = jnp.broadcast_to(code_ref[pl.ds(r, 1), :], (8, LANES))
            index = (code & (half - 1)) + upper_lanes
            window = code >> 6
            for j in range(blocks):
                lead = lane_take(t_ref[first, 8 * j:8 * j + 8, :], index)
                trail = lane_take(t_ref[first + 1, 8 * j:8 * j + 8, :], index)
                value = jnp.where(window == 0, lead, jnp.where(window == 1, trail, 0.0))
                grid_ref[pl.ds(r + 8 * j * rows, 8, stride=rows), :] = value

    for copy in copies:
        copy.wait()
    even_rows, odd_rows = row_blocks()
    folded = extent // 2
    group = next(g for g in (8, 4, 2) if planes % g == 0)
    wide = 2 * LANES
    at_back = 3 * LANES
    at_y = at_back + 2 * wide
    at_even = at_y + 2 * folded
    at_odd = at_even + 2 * even_rows
    x_forward = (table_ref[0:at_back, :wide], table_ref[0:at_back, wide:])
    x_back = (table_ref[at_back:at_y, :wide], table_ref[at_back:at_y, wide:])
    y_even = table_ref[at_y:at_y + folded, :6 * even_rows]
    y_odd = table_ref[at_y + folded:at_even, :6 * odd_rows]
    back_even = table_ref[at_even:at_odd, :3 * folded]
    back_odd = table_ref[at_odd:at_odd + 2 * odd_rows, :3 * folded]

    def dot(x, y):
        return jnp.dot(x, y, preferred_element_type=F32)

    def stack(x, axis):
        hi, lo = split(x)
        return jnp.concatenate([hi, lo, hi], axis=axis)

    def turn(x):
        lane = lax.broadcasted_iota(jnp.int32, (x.shape[0], LANES), 1) < half
        parts = []
        for at in range(0, x.shape[1], LANES):
            rolled = pltpu.roll(x[:, at:at + LANES], half, 1)
            parts.append(jnp.where(lane, -rolled, rolled))
        return jnp.concatenate(parts, axis=1)

    @pl.loop(0, planes // group)
    def _(step):
        lines = []
        for t in range(group):
            base = pl.multiple_of((step * group + t) * rows, 16)
            parts = []
            for at, size, table in ((0, even_rows, y_even), (even_rows, odd_rows, y_odd)):
                pick = pl.ds(base + at, size)
                spectrum = jnp.concatenate([ge_ref[pick, :], go_ref[pick, :]], axis=1)
                both = jnp.concatenate([stack(spectrum, 0), stack(turn(spectrum), 0)], axis=0)
                parts.append(dot(table, both))
            lines.append(parts[0] + parts[1])
            lines.append(parts[0] - parts[1])
        lines = jnp.concatenate(lines, axis=0)
        field_even = dot(stack(lines[:, :LANES], 1), x_forward[0])
        field_odd = dot(stack(lines[:, LANES:], 1), x_forward[1])
        spare = jnp.zeros((extent, LANES - folded), F32)
        sums, differences = [], []
        for t in range(group):
            v = pot_ref[step * group + t]
            v_near = jnp.concatenate([v[:, :folded], spare], axis=1)
            v_far = jnp.concatenate([v[:, folded:], spare], axis=1)
            even = field_even[t * extent:(t + 1) * extent]
            odd = field_odd[t * extent:(t + 1) * extent]
            near = (even + odd) * jnp.concatenate([v_near, v_near], axis=1)
            far = (even - odd) * jnp.concatenate([v_far, v_far], axis=1)
            sums.append(near + far)
            differences.append(near - far)
        back = []
        for weighted, table in ((sums, x_back[0]), (differences, x_back[1])):
            both = dot(jnp.concatenate(split(jnp.concatenate(weighted, axis=0)), axis=1), table)
            back.append(both[:, :LANES] + both[:, LANES:])
        back = jnp.concatenate(back, axis=1)
        for t in range(group):
            base = pl.multiple_of((step * group + t) * rows, 16)
            upper = back[t * extent:t * extent + folded]
            lower = back[t * extent + folded:(t + 1) * extent]
            for at, size, table, value in (
                (0, even_rows, back_even, upper + lower), (even_rows, odd_rows, back_odd, upper - lower)
            ):
                both = dot(table, stack(value, 0))
                value = both[:size] - turn(both[size:])
                pick = pl.ds(base + at, size)
                ge_ref[pick, :] = value[:, :LANES]
                go_ref[pick, :] = value[:, LANES:]

    @pl.loop(0, rows, unroll=8)
    def _(r):
        for side, _, grid_ref in sides:
            first = first_ref[8 * side, r]
            values = [grid_ref[pl.ds(r + 8 * j * rows, 8, stride=rows), :] for j in range(blocks)]
            for t in range(2):
                index = jnp.broadcast_to(col_ref[pl.ds(first + t, 1), :], (8, LANES))
                hit = jnp.broadcast_to(row_ref[pl.ds(first + t, 1), :], (8, LANES)) == 2 * r + side
                for j in range(blocks):
                    pltpu.store(
                        t_ref.at[first + t, 8 * j:8 * j + 8, :], lane_take(values[j], index), mask=hit
                    )

    for w in range(windows):
        first, second = t_ref[2 * w], t_ref[2 * w + 1]
        s_ref[w, 0:padded_planes, :] = jnp.where(low, first, pltpu.roll(second, half, 1))
        s_ref[w, padded_planes:2 * padded_planes, :] = jnp.where(low, pltpu.roll(first, half, 1), second)
    reorder(dst_ref, s_ref, x_ref)
    for w in range(devices):
        out_ref[w, 0:2 * padded_planes, :] = x_ref[w]
    for e in range(devices // 2):
        re = x_ref[devices + e, 0:padded_planes, :]
        im = x_ref[devices + e, padded_planes:2 * padded_planes, :]
        out_ref[2 * e, 2 * padded_planes:3 * padded_planes, :] = jnp.where(
            low, re, pltpu.roll(im, half, 1)
        )
        out_ref[2 * e + 1, 2 * padded_planes:3 * padded_planes, :] = jnp.where(
            low, pltpu.roll(re, half, 1), im
        )
    for d in range(devices):
        out_ref[d, 3 * padded_planes:, :] = jnp.zeros((8, LANES), F32)


def inner_kernel(bands, volume, norm, place_ref, *refs):
    kc_ref = refs[0]
    coefs = refs[1:1 + bands]
    fields = refs[1 + bands:1 + 2 * bands]
    in_ref = refs[1 + 2 * bands]
    out_refs = refs[2 + 2 * bands:]
    devices = in_ref.shape[0]
    padded_planes = (in_ref.shape[1] - 8) // 3
    half = LANES // 2
    padded = coefs[0].shape[2]
    me, mine = place_ref[0], place_ref[1]
    low = lax.broadcasted_iota(jnp.int32, (padded_planes, LANES), 1) < half

    def fold(x):
        rows = x.shape[0]
        total = x[0:8]
        for at in range(8, rows, 8):
            total = total + x[at:at + 8]
        return total

    kc = kc_ref[...]
    kc_re, kc_im = kc[:, :padded], kc[:, padded:]
    sums = []
    for m in range(bands):
        c_re, c_im = coefs[m][:, 0, :], coefs[m][:, 1, :]
        sums.append([fold(c_re * kc_re + c_im * kc_im), fold(c_re * kc_im - c_im * kc_re)])
    local = [[jnp.zeros((8, LANES), F32), jnp.zeros((8, LANES), F32)] for _ in range(bands)]
    for d in range(devices):
        value = in_ref[d, 0:3 * padded_planes, :]
        re, im, rest = value[:padded_planes], value[padded_planes:2 * padded_planes], value[2 * padded_planes:]
        turned = pltpu.roll(rest, half, 1)
        other = jnp.concatenate([im, -re, jnp.where(low, turned, -turned)], axis=0)
        for m in range(bands):
            col = fields[m][d, 0:3 * padded_planes, :]
            local[m][0] = local[m][0] + fold(col * value)
            local[m][1] = local[m][1] + fold(col * other)
    lane = lax.broadcasted_iota(jnp.int32, (8, LANES), 1)
    row = lax.broadcasted_iota(jnp.int32, (8, LANES), 0)
    tile = jnp.zeros((8, LANES), F32)
    for m in range(bands):
        at = me ^ m
        for part, sign in ((0, 1.0), (1, -1.0)):
            partial = sums[m][part] + volume * local[m][part]
            scalar = jnp.sum(jnp.sum(partial, axis=1, keepdims=True), axis=0, keepdims=True)
            tile = jnp.where((lane == at) & (row == part), sign * norm * scalar, tile)
    for k in range(devices):
        out_refs[k][0:3 * padded_planes, :] = in_ref[lax.rem(mine + k, devices), 0:3 * padded_planes, :]
        out_refs[k][3 * padded_planes:, :] = tile


def final_kernel(volume, devices, me_ref, len_ref, *refs):
    ret_refs = refs[:devices]
    kc_ref, whi_ref, wlo_ref, sc_ref, ss_ref, out_ref, sub_ref, stack_ref = refs[devices:]
    padded_planes = (ret_refs[0].shape[0] - 8) // 3
    sticks, _, padded = out_ref.shape
    half = LANES // 2
    bands = sub_ref.shape[2]
    total = jnp.zeros((8, LANES), F32)
    me = me_ref[0]
    for k in range(devices):
        value = ret_refs[k][...]
        base = pl.multiple_of(lax.rem(me + devices - k, devices) * padded_planes, 8)
        total = total + value[3 * padded_planes:]
        rest = value[2 * padded_planes:3 * padded_planes]
        re = jnp.concatenate([value[:padded_planes], rest[:, :half]], axis=1)
        im = jnp.concatenate([value[padded_planes:2 * padded_planes], rest[:, half:]], axis=1)
        c = sc_ref[pl.ds(base, padded_planes), :]
        s = ss_ref[pl.ds(base, padded_planes), :]
        stack_ref[pl.ds(2 * base, padded_planes), :sticks] = re * c - im * s
        stack_ref[pl.ds(2 * base + padded_planes, padded_planes), :sticks] = re * s + im * c
    turned = jnp.transpose(stack_ref[...])[:sticks]
    local = dot3(split(turned), (whi_ref[...], wlo_ref[...])) * volume
    position = lax.broadcasted_iota(jnp.int32, (sticks, padded), 1).astype(F32)
    kept = position < len_ref[:, 0:1]
    kc = kc_ref[...]
    out_ref[:, 0, :] = jnp.where(kept, kc[:, :padded] + local[:, :padded], 0.0)
    out_ref[:, 1, :] = jnp.where(kept, kc[:, padded:] + local[:, padded:], 0.0)
    sub_ref[:, 0, :] = total[0:2, :bands]


def ring(count, k):
    return [(d, (d + k) % count) for d in range(count)]


def pairs(count, k):
    return [(d, d ^ k) for d in range(count)]


def shards(bands, devices, coefficients, stick_col, stick_row, stick_length, plane_of_slot, potential):
    extent = plane_of_slot.shape[0]
    sticks = coefficients.shape[1]
    padded = coefficients.shape[3]
    total_sticks = stick_col.shape[0]
    planes = potential.shape[0]
    padded_planes = up8(planes)
    powers = devices & (devices - 1) == 0 and bands & (bands - 1) == 0
    if sticks != LANES + LANES // 2 or not powers or planes % 2:
        raise ValueError("sizes")
    rows = sum(row_blocks())
    volume = 1.0 / (extent * extent * extent)
    me = lax.axis_index("tg").astype(jnp.int32)
    coef = coefficients.reshape(sticks, 2, padded)

    length, row, col = (v.reshape(-1, LANES) for v in (stick_length, stick_row, stick_col))
    slots = plane_of_slot.reshape(devices, planes)
    if padded_planes > planes:
        slots = jnp.pad(slots, ((0, 0), (0, padded_planes - planes)), constant_values=-1)
    slots = slots.reshape(1, devices * padded_planes)
    windows = total_sticks // LANES
    smem = pl.BlockSpec(memory_space=pltpu.SMEM)
    vmem = pl.BlockSpec(memory_space=pltpu.VMEM)
    hbm = pl.BlockSpec(memory_space=pltpu.HBM)

    block = 3 * padded_planes
    total_planes = devices * padded_planes
    *sent, kc, lengths, whi, wlo, shift_cos, shift_sin = pl.pallas_call(
        functools.partial(wave_kernel, extent, devices),
        out_shape=(
            *[jax.ShapeDtypeStruct((block, LANES), F32)] * devices,
            jax.ShapeDtypeStruct((sticks, 2 * padded), F32),
            jax.ShapeDtypeStruct((sticks, LANES), F32),
            jax.ShapeDtypeStruct((2 * total_planes, 2 * padded), BF16),
            jax.ShapeDtypeStruct((2 * total_planes, 2 * padded), BF16),
            jax.ShapeDtypeStruct((total_planes, sticks), F32),
            jax.ShapeDtypeStruct((total_planes, sticks), F32),
        ),
        in_specs=[smem] + [hbm] * 5,
        scratch_shapes=[
            pltpu.VMEM(length.shape, jnp.int32),
            pltpu.VMEM(row.shape, jnp.int32),
            pltpu.VMEM(col.shape, jnp.int32),
            pltpu.VMEM(slots.shape, jnp.int32),
            pltpu.VMEM(coef.shape, F32),
            pltpu.VMEM((devices, block, LANES), F32),
            pltpu.SemaphoreType.DMA((5,)),
        ],
        compiler_params=params(56),
        name="wave_to_planes",
    )(me.reshape(1), length, row, col, slots, coef)

    arrived = [sent[0]]
    for k in range(1, devices):
        arrived.append(lax.ppermute(sent[k], "tg", ring(devices, k)))
    received = pl.pallas_call(
        functools.partial(merge_kernel, devices),
        out_shape=jax.ShapeDtypeStruct((devices, block, LANES), F32),
        in_specs=[smem] + [vmem] * devices,
        compiler_params=params(4),
        name="merge",
    )(me.reshape(1), *arrived)

    window_list = jax.ShapeDtypeStruct((windows, LANES), jnp.int32)
    longer_list = jax.ShapeDtypeStruct((2 * windows + 1, LANES), jnp.int32)
    square = jax.ShapeDtypeStruct((LANES, LANES), jnp.int32)
    even_map, odd_map, first, source, target, row_w, col_w = pl.pallas_call(
        functools.partial(map_kernel, extent, sticks),
        out_shape=(
            square,
            square,
            jax.ShapeDtypeStruct((16, LANES), jnp.int32),
            window_list,
            window_list,
            longer_list,
            longer_list,
        ),
        in_specs=[hbm] * 2,
        scratch_shapes=[
            pltpu.VMEM(row.shape, jnp.int32),
            pltpu.VMEM(col.shape, jnp.int32),
            pltpu.SemaphoreType.DMA((2,)),
        ],
        compiler_params=params(14 * total_sticks / 1536),
        cost_estimate=cost(4e9, 1e5),
        name="stick_map",
    )(row, col)

    constants = jnp.asarray(tables(extent))
    weighted = pl.pallas_call(
        functools.partial(plane_kernel, planes),
        out_shape=jax.ShapeDtypeStruct((devices, block + 8, LANES), F32),
        in_specs=[smem] + [vmem] * 7 + [hbm] * 2,
        out_specs=vmem,
        scratch_shapes=[
            pltpu.VMEM((windows, 2 * padded_planes, LANES), F32),
            pltpu.VMEM((windows, 2 * padded_planes, LANES), F32),
            pltpu.VMEM((2 * windows + 1, padded_planes, LANES), F32),
            pltpu.VMEM((padded_planes * rows, LANES), F32),
            pltpu.VMEM((padded_planes * rows, LANES), F32),
            pltpu.VMEM(constants.shape, BF16),
            pltpu.VMEM(potential.shape, F32),
            pltpu.SemaphoreType.DMA((2,)),
        ],
        compiler_params=params(52),
        cost_estimate=cost(2e10, 1e7),
        name="planes",
    )(first, even_map, odd_map, source, target, row_w, col_w, received, constants, potential)

    coefs, fields = [coef], [received]
    for m in range(1, bands):
        coefs.append(lax.ppermute(coef, "band", pairs(bands, m)))
        fields.append(lax.ppermute(received, "band", pairs(bands, m)))
    band = lax.axis_index("band").astype(jnp.int32)
    norm = 1.0 / (total_sticks * padded)
    places = jnp.stack([band, me])
    outgoing = pl.pallas_call(
        functools.partial(inner_kernel, bands, volume, norm),
        out_shape=(jax.ShapeDtypeStruct((block + 8, LANES), F32),) * devices,
        in_specs=[smem] + [vmem] * (2 + 2 * bands),
        compiler_params=params(6 + 1.5 * bands),
        name="inner",
    )(places, kc, *coefs, *fields, weighted)

    returned = [outgoing[0]]
    for k in range(1, devices):
        returned.append(lax.ppermute(outgoing[k], "tg", ring(devices, k)))
    applied, subspace = pl.pallas_call(
        functools.partial(final_kernel, volume, devices),
        out_shape=(
            jax.ShapeDtypeStruct((sticks, 2, padded), F32),
            jax.ShapeDtypeStruct((2, 1, bands), F32),
        ),
        in_specs=[smem] + [vmem] * (6 + devices),
        scratch_shapes=[pltpu.VMEM((2 * total_planes, 2 * LANES), F32)],
        compiler_params=params(6 + 6 * total_planes / 192),
        name="planes_to_wave",
    )(me.reshape(1), lengths, *returned, kc, whi, wlo, shift_cos, shift_sin)
    return applied.reshape(1, sticks, 2, padded), subspace


def solution(mesh):
    in_specs = (P("band", "tg", None, None), P(), P(), P(), P(), P("tg", None, None))
    out_specs = (P("band", "tg", None, None), P(None, "band", None))
    body = functools.partial(shards, mesh.shape["band"], mesh.shape["tg"])
    return jax.shard_map(body, mesh=mesh, in_specs=in_specs, out_specs=out_specs, check_vma=False)
```

```python
import functools
import math

import jax
import jax.numpy as jnp
import ml_dtypes
import numpy as np
from jax import lax
from jax.experimental import pallas as pl
from jax.experimental.pallas import tpu as pltpu
from jax.sharding import PartitionSpec as P

RADIUS = 48
LANES = 128
F32 = jnp.float32
BF16 = jnp.bfloat16


def up8(n):
    return -(-n // 8) * 8


def split(x):
    hi = x.astype(BF16)
    return hi, (x - hi.astype(F32)).astype(BF16)


def dot3(a, b, dims=((1,), (0,))):
    def dot(x, y):
        return lax.dot_general(x, y, (dims, ((), ())), preferred_element_type=F32)

    return dot(a[0], b[0]) + (dot(a[0], b[1]) + dot(a[1], b[0]))


def trig(product, extent):
    n = product - extent * jnp.floor(product * (1.0 / extent) + 0.5)
    quarter = extent / 4.0
    unit = 2.0 * math.pi / extent

    def sine(m):
        u = m * unit
        v = u * u
        s = 1.0 / 6227020800.0
        for term in (-39916800.0, 362880.0, -5040.0, 120.0, -6.0, 1.0):
            s = s * v + 1.0 / term
        return u * s

    folded = jnp.where(
        jnp.abs(n) > quarter, jnp.where(n > 0, 2.0 * quarter, -2.0 * quarter) - n, n
    )
    return sine(quarter - jnp.abs(n)), sine(folded)


def pair(table):
    hi = table.astype(np.float32).astype(ml_dtypes.bfloat16)
    lo = (table - hi.astype(np.float64)).astype(ml_dtypes.bfloat16)
    return hi, lo


def row_blocks():
    even = -(-(RADIUS + 1) // 16) * 16
    odd = -(-RADIUS // 16) * 16
    return even, odd


@functools.cache
def tables(extent):
    half = extent // 2
    grid = np.arange(extent)
    freq = np.arange(2 * RADIUS + 1) - RADIUS

    def angles(f, g):
        a = 2.0 * np.pi * ((f[:, None] * g[None, :]) % extent) / extent
        return np.cos(a), np.sin(a)

    wide = 2 * LANES
    x_forward, x_back, forward, back = [], [], [], []
    for offset, rows in zip((0, 1), row_blocks()):
        cos, sin = angles(freq[offset::2], grid[:half])
        count = cos.shape[0]
        table = np.zeros((LANES, wide))
        table[:count, :half] = cos
        table[LANES // 2:LANES // 2 + count, :half] = -sin
        table[:count, LANES:LANES + half] = sin
        table[LANES // 2:LANES // 2 + count, LANES:LANES + half] = cos
        hi, lo = pair(table)
        x_forward.append(np.concatenate([hi, hi, lo], axis=0))
        hi, lo = pair(table.T.copy())
        x_back.append(
            np.concatenate(
                [np.concatenate([hi, lo], axis=1), np.concatenate([hi, np.zeros_like(lo)], axis=1)], axis=0
            )
        )
        parts = []
        for wave in (cos, sin):
            table = np.zeros((half, rows))
            table[:, :count] = wave.T
            hi, lo = pair(table)
            parts += [hi, hi, lo]
        forward.append(np.concatenate(parts, axis=1))
        table = np.zeros((2 * rows, half))
        table[:count] = cos
        table[rows:rows + count] = sin
        hi, lo = pair(table)
        back.append(np.concatenate([hi, hi, lo], axis=1))
    rows = [np.concatenate(x_forward, axis=1), np.concatenate(x_back, axis=1)]
    for table in forward + back:
        rows.append(np.pad(table, ((0, 0), (0, 2 * wide - table.shape[1]))))
    return np.concatenate(rows, axis=0)


def params(megabytes):
    return pltpu.CompilerParams(vmem_limit_bytes=int(min(megabytes, 56) * 2**20))


def fetch_all(sources, targets, sems):
    copies = [
        pltpu.make_async_copy(source, target, sems.at[i])
        for i, (source, target) in enumerate(zip(sources, targets))
    ]
    for copy in copies:
        copy.start()
    return copies


def cost(flops, nbytes):
    return pl.CostEstimate(flops=int(flops), bytes_accessed=int(nbytes), transcendentals=0)


def wave_kernel(
    extent, me_ref, length_hbm, row_hbm, col_hbm, plane_hbm, coef_hbm,
    out_ref, kc_ref, len_ref, whi_ref, wlo_ref, sc_ref, ss_ref,
    length_ref, row_ref, col_ref, plane_ref, coef_ref, sems,
):
    copies = fetch_all(
        (length_hbm, row_hbm, col_hbm, plane_hbm, coef_hbm),
        (length_ref, row_ref, col_ref, plane_ref, coef_ref),
        sems,
    )
    for copy in copies[:4]:
        copy.wait()
    devices = out_ref.shape[0]
    sticks, _, padded = coef_ref.shape
    padded_planes = plane_ref.shape[1] // devices
    me = me_ref[0]
    half = LANES // 2
    lead = (me * sticks) // LANES
    odd = (me * sticks) % LANES != 0

    def own(ref):
        first, second = ref[pl.ds(lead, 1), :], ref[pl.ds(lead + 1, 1), :]
        both = jnp.concatenate([first, second], axis=1)
        return jnp.where(odd, both[:, half:], both[:, :sticks])

    length_row = own(length_ref).astype(F32)
    at_row = own(row_ref)
    at_col = own(col_ref)
    at_row = jnp.where(at_row <= RADIUS, at_row, at_row - extent).astype(F32)
    at_col = jnp.where(at_col <= RADIUS, at_col, at_col - extent).astype(F32)
    square_row = at_row * at_row + at_col * at_col
    spare = jnp.ones((1, 2 * LANES - sticks), F32)
    aux = jnp.concatenate(
        [
            jnp.broadcast_to(jnp.concatenate([length_row, spare], axis=1), (LANES // 2, 2 * LANES)),
            jnp.broadcast_to(jnp.concatenate([square_row, spare], axis=1), (LANES // 2, 2 * LANES)),
        ],
        axis=0,
    )
    aux_col = jnp.transpose(aux)[:sticks]
    len_ref[...] = aux_col
    length = aux_col[:, 0:1]
    square = aux_col[:, LANES // 2:LANES // 2 + 1]
    middle = (length - 1.0) * 0.5
    position = lax.broadcasted_iota(jnp.int32, (sticks, padded), 1).astype(F32)
    total = plane_ref.shape[1]
    plane_row = jnp.broadcast_to(plane_ref[...].astype(F32), (LANES, total))
    plane_col = jnp.transpose(plane_row)[:, 0:1]
    real = (plane_col >= 0.0).astype(F32)
    plane_col = jnp.maximum(plane_col, 0.0)
    harmonic = lax.broadcasted_iota(jnp.int32, (total, padded), 1).astype(F32)
    cos, sin = trig(plane_col * harmonic, extent)
    cos, sin = cos * real, sin * real
    parts = []
    for d in range(devices):
        c = cos[d * padded_planes:(d + 1) * padded_planes]
        s = sin[d * padded_planes:(d + 1) * padded_planes]
        parts.append(jnp.concatenate([c, -s], axis=1))
        parts.append(jnp.concatenate([s, c], axis=1))
    table = split(jnp.concatenate(parts, axis=0))
    whi_ref[...] = table[0]
    wlo_ref[...] = table[1]
    shift_cos, shift_sin = trig(plane_col * ((length_row - 1.0) * 0.5), extent)
    sc_ref[...] = shift_cos
    ss_ref[...] = shift_sin
    copies[4].wait()
    kept = (position < length).astype(F32)
    kinetic = (square + (position - middle) * (position - middle)) * (1.0 / (RADIUS * RADIUS))
    wave = jnp.concatenate([coef_ref[:, 0, :] * kept, coef_ref[:, 1, :] * kept], axis=1)
    kc_ref[...] = wave * jnp.concatenate([kinetic, kinetic], axis=1)
    raw = dot3(table, split(wave), ((1,), (1,)))
    for d in range(devices):
        at = 2 * d * padded_planes
        re, im = raw[at:at + padded_planes], raw[at + padded_planes:at + 2 * padded_planes]
        c = shift_cos[d * padded_planes:(d + 1) * padded_planes]
        s = shift_sin[d * padded_planes:(d + 1) * padded_planes]
        along_re = re * c + im * s
        along_im = im * c - re * s
        out_ref[d, 0:padded_planes, :] = along_re[:, :LANES]
        out_ref[d, padded_planes:2 * padded_planes, :] = along_im[:, :LANES]
        out_ref[d, 2 * padded_planes:3 * padded_planes, :] = jnp.concatenate(
            [along_re[:, LANES:], along_im[:, LANES:]], axis=1
        )


def window_row(values, sticks):
    line = jnp.concatenate([values[i:i + 1] for i in range(values.shape[0])], axis=1)
    starts = range(0, line.shape[1], sticks)
    parts = [line[:, at:at + LANES] for at in starts]
    parts += [line[:, at + LANES:at + sticks] for at in starts]
    return jnp.concatenate(parts, axis=1)


def map_kernel(
    extent, sticks, in_row_hbm, in_col_hbm,
    even_ref, odd_ref, first_ref, src_ref, dst_ref, row_ref, col_ref,
    in_row_ref, in_col_ref, sems,
):
    for copy in fetch_all((in_row_hbm, in_col_hbm), (in_row_ref, in_col_ref), sems):
        copy.wait()
    windows = src_ref.shape[0]
    total = windows * LANES

    def signed(ref):
        value = ref[...]
        return window_row(jnp.where(value <= RADIUS, value, value - extent) + RADIUS, sticks)

    def dot(x, y, dims=((1,), (0,))):
        return lax.dot_general(x, y, (dims, ((), ())), preferred_element_type=F32)

    def bits(condition):
        return condition.astype(F32).astype(BF16)

    nt = ((1,), (1,))
    own_row, own_col = signed(in_row_ref), signed(in_col_ref)
    half = LANES // 2
    own_row = (own_row & 1) * row_blocks()[0] + (own_row >> 1)
    own_col = (own_col & 1) * half + (own_col >> 1)
    tall = lax.broadcasted_iota(jnp.int32, (LANES, total), 0)
    place = lax.broadcasted_iota(jnp.int32, (LANES, total), 1)
    in_col = tall == own_col
    row_hot, col_hot = bits(tall == own_row), bits(in_col)
    down = lax.broadcasted_iota(jnp.int32, (LANES, LANES), 0)
    across = lax.broadcasted_iota(jnp.int32, (LANES, LANES), 1)
    before = bits(down < across)
    after = bits(down > across)
    upto = bits(down >= across)
    ones = jnp.ones((LANES, LANES), BF16)
    taken = dot(row_hot, col_hot, nt)
    taken_t = dot(col_hot, row_hot, nt)
    taken_b, taken_tb = taken.astype(BF16), taken_t.astype(BF16)
    start = dot(dot(after, taken_b).astype(BF16), ones)
    end = start + dot(taken_b, ones)
    start_t = dot(ones, dot(taken_tb, before).astype(BF16))
    left = across < half
    standing = dot(taken_b, before) + start
    low_ones = bits(down < half)
    high_start = start + dot(taken_b, low_ones)
    ones_t = bits(across < half)
    high_start_t = start_t + dot(ones_t, taken_tb)
    limit = 2.0 * windows - 1.0

    def first_window(value):
        return jnp.minimum(jnp.floor(value * (1.0 / half)), limit)

    for ref, begin in ((even_ref, start), (odd_ref, high_start)):
        code = jnp.where(taken > 0.5, standing - half * first_window(begin), -1.0)
        turned = pltpu.roll(code, half, 1)
        both = jnp.where(left, code, turned) if ref is even_ref else jnp.where(left, turned, code)
        ref[...] = both.astype(jnp.int32)
    first_ref[...] = jnp.concatenate(
        [first_window(start_t[0:8]), first_window(high_start_t[0:8])], axis=0
    ).astype(jnp.int32)

    spot = place.astype(F32)
    in_range = (spot >= start[:, 0:1]) & (spot < end[:, 0:1])
    sorted_hot = bits(in_range)
    sorted_row = jnp.sum(jnp.where(in_range, tall, 0).astype(F32), axis=0, keepdims=True)
    sorted_rank = spot[0:1] - jnp.sum(jnp.where(in_range, start[:, 0:1], 0.0), axis=0, keepdims=True)
    counts = dot(dot(upto, taken_tb).astype(BF16), sorted_hot)
    sorted_col = jnp.sum((counts <= sorted_rank).astype(F32), axis=0, keepdims=True)
    names = place + 1
    name_hi = dot(jnp.where(in_col, names >> 6, 0).astype(F32).astype(BF16), row_hot, nt)
    name_lo = dot(jnp.where(in_col, names & 63, 0).astype(F32).astype(BF16), row_hot, nt)
    named = dot(name_hi.astype(BF16), sorted_hot) * 64.0 + dot(name_lo.astype(BF16), sorted_hot)
    source = jnp.sum(jnp.where(tall.astype(F32) == sorted_col, named, 0.0), axis=0, keepdims=True) - 1.0
    place_t = dot(after, taken_tb) + start_t
    place_hi = jnp.floor(place_t * (1.0 / 64.0))
    place_lo = place_t - 64.0 * place_hi
    placed = dot(place_hi.astype(BF16), row_hot) * 64.0 + dot(place_lo.astype(BF16), row_hot)
    target = jnp.sum(jnp.where(in_col, placed, 0.0), axis=0, keepdims=True)
    for values, ref in ((source, src_ref), (target, dst_ref)):
        values = values.astype(jnp.int32)
        for w in range(windows):
            ref[w:w + 1, :] = values[:, w * LANES:(w + 1) * LANES]
    is_left = left[0:8]
    shift = jnp.where(is_left, 0, half)
    sorted_col = sorted_col.astype(jnp.int32)
    sorted_key = sorted_row.astype(jnp.int32) * 2 + (sorted_col >> 6)
    sorted_col = sorted_col & (half - 1)
    for values, ref, add in ((sorted_key, row_ref, 0), (sorted_col, col_ref, shift)):
        for w in range(windows):
            line = jnp.broadcast_to(values[:, w * LANES:(w + 1) * LANES], (8, LANES))
            turned = pltpu.roll(line, half, 1)
            ref[2 * w:2 * w + 1, :] = (jnp.where(is_left, line, turned) + add)[0:1]
            ref[2 * w + 1:2 * w + 2, :] = (jnp.where(is_left, turned, line) + add)[0:1]
    row_ref[2 * windows:2 * windows + 1, :] = jnp.full((1, LANES), -1, jnp.int32)
    col_ref[2 * windows:2 * windows + 1, :] = jnp.zeros((1, LANES), jnp.int32)


def lane_take(x, index):
    return jnp.take_along_axis(x, index, axis=1, mode="promise_in_bounds")


def plane_kernel(
    planes, first_ref, even_ref, odd_ref, src_ref, dst_ref, row_ref, col_ref, recv_ref,
    *refs,
):
    table_hbm, pot_hbm, out_ref, x_ref, s_ref, t_ref, ge_ref, go_ref, table_ref, pot_ref, sems = refs
    devices = recv_ref.shape[0]
    padded_planes = recv_ref.shape[1] // 3
    windows = x_ref.shape[0]
    rows = ge_ref.shape[0] // padded_planes
    extent = pot_ref.shape[1]
    half = LANES // 2
    copies = fetch_all((table_hbm, pot_hbm), (table_ref, pot_ref), sems)

    low = lax.broadcasted_iota(jnp.int32, (padded_planes, LANES), 1) < half
    for d in range(devices):
        x_ref[d] = recv_ref[d, 0:2 * padded_planes, :]
    for e in range(devices // 2):
        first = recv_ref[2 * e, 2 * padded_planes:3 * padded_planes, :]
        second = recv_ref[2 * e + 1, 2 * padded_planes:3 * padded_planes, :]
        x_ref[devices + e, 0:padded_planes, :] = jnp.where(low, first, pltpu.roll(second, half, 1))
        x_ref[devices + e, padded_planes:2 * padded_planes, :] = jnp.where(
            low, pltpu.roll(first, half, 1), second
        )

    blocks = padded_planes // 8

    def reorder(order_ref, from_ref, to_ref):
        @pl.loop(0, windows, unroll=4)
        def _(v):
            order = jnp.broadcast_to(order_ref[pl.ds(v, 1), :], (8, LANES))
            index = order & (LANES - 1)
            window = order >> 7
            for j in range(2 * blocks):
                value = jnp.zeros((8, LANES), F32)
                for w in range(windows):
                    value = jnp.where(window == w, lane_take(from_ref[w, 8 * j:8 * j + 8, :], index), value)
                to_ref[v, 8 * j:8 * j + 8, :] = value

    reorder(src_ref, x_ref, s_ref)
    for w in range(windows):
        re, im = s_ref[w, 0:padded_planes, :], s_ref[w, padded_planes:2 * padded_planes, :]
        t_ref[2 * w] = jnp.where(low, re, pltpu.roll(im, half, 1))
        t_ref[2 * w + 1] = jnp.where(low, pltpu.roll(re, half, 1), im)

    left = low[0:8]
    upper_lanes = jnp.where(left, 0, half)
    sides = ((0, even_ref, ge_ref), (1, odd_ref, go_ref))

    @pl.loop(0, rows, unroll=8)
    def _(r):
        for side, code_ref, grid_ref in sides:
            first = first_ref[8 * side, r]
            code = jnp.broadcast_to(code_ref[pl.ds(r, 1), :], (8, LANES))
            index = (code & (half - 1)) + upper_lanes
            window = code >> 6
            for j in range(blocks):
                lead = lane_take(t_ref[first, 8 * j:8 * j + 8, :], index)
                trail = lane_take(t_ref[first + 1, 8 * j:8 * j + 8, :], index)
                value = jnp.where(window == 0, lead, jnp.where(window == 1, trail, 0.0))
                grid_ref[pl.ds(r + 8 * j * rows, 8, stride=rows), :] = value

    for copy in copies:
        copy.wait()
    even_rows, odd_rows = row_blocks()
    folded = extent // 2
    group = next(g for g in (12, 8, 6, 4, 2) if planes % g == 0)
    wide = 2 * LANES
    at_back = 3 * LANES
    at_y = at_back + 2 * wide
    at_even = at_y + 2 * folded
    at_odd = at_even + 2 * even_rows
    x_forward = (table_ref[0:at_back, :wide], table_ref[0:at_back, wide:])
    x_back = (table_ref[at_back:at_y, :wide], table_ref[at_back:at_y, wide:])
    y_even = table_ref[at_y:at_y + folded, :6 * even_rows]
    y_odd = table_ref[at_y + folded:at_even, :6 * odd_rows]
    back_even = table_ref[at_even:at_odd, :3 * folded]
    back_odd = table_ref[at_odd:at_odd + 2 * odd_rows, :3 * folded]

    def dot(x, y):
        return jnp.dot(x, y, preferred_element_type=F32)

    def stack(x, axis):
        hi, lo = split(x)
        return jnp.concatenate([hi, lo, hi], axis=axis)

    def turn(x):
        lane = lax.broadcasted_iota(jnp.int32, (x.shape[0], LANES), 1) < half
        parts = []
        for at in range(0, x.shape[1], LANES):
            rolled = pltpu.roll(x[:, at:at + LANES], half, 1)
            parts.append(jnp.where(lane, -rolled, rolled))
        return jnp.concatenate(parts, axis=1)

    @pl.loop(0, planes // group)
    def _(step):
        lines = []
        for t in range(group):
            base = pl.multiple_of((step * group + t) * rows, 16)
            parts = []
            for at, size, table in ((0, even_rows, y_even), (even_rows, odd_rows, y_odd)):
                pick = pl.ds(base + at, size)
                spectrum = jnp.concatenate([ge_ref[pick, :], go_ref[pick, :]], axis=1)
                both = jnp.concatenate([stack(spectrum, 0), stack(turn(spectrum), 0)], axis=0)
                parts.append(dot(table, both))
            lines.append(parts[0] + parts[1])
            lines.append(parts[0] - parts[1])
        lines = jnp.concatenate(lines, axis=0)
        field_even = dot(stack(lines[:, :LANES], 1), x_forward[0])
        field_odd = dot(stack(lines[:, LANES:], 1), x_forward[1])
        spare = jnp.zeros((extent, LANES - folded), F32)
        sums, differences = [], []
        for t in range(group):
            v = pot_ref[step * group + t]
            v_near = jnp.concatenate([v[:, :folded], spare], axis=1)
            v_far = jnp.concatenate([v[:, folded:], spare], axis=1)
            even = field_even[t * extent:(t + 1) * extent]
            odd = field_odd[t * extent:(t + 1) * extent]
            near = (even + odd) * jnp.concatenate([v_near, v_near], axis=1)
            far = (even - odd) * jnp.concatenate([v_far, v_far], axis=1)
            sums.append(near + far)
            differences.append(near - far)
        back = []
        for weighted, table in ((sums, x_back[0]), (differences, x_back[1])):
            both = dot(jnp.concatenate(split(jnp.concatenate(weighted, axis=0)), axis=1), table)
            back.append(both[:, :LANES] + both[:, LANES:])
        back = jnp.concatenate(back, axis=1)
        for t in range(group):
            base = pl.multiple_of((step * group + t) * rows, 16)
            upper = back[t * extent:t * extent + folded]
            lower = back[t * extent + folded:(t + 1) * extent]
            for at, size, table, value in (
                (0, even_rows, back_even, upper + lower), (even_rows, odd_rows, back_odd, upper - lower)
            ):
                both = dot(table, stack(value, 0))
                value = both[:size] - turn(both[size:])
                pick = pl.ds(base + at, size)
                ge_ref[pick, :] = value[:, :LANES]
                go_ref[pick, :] = value[:, LANES:]

    @pl.loop(0, rows, unroll=8)
    def _(r):
        for side, _, grid_ref in sides:
            first = first_ref[8 * side, r]
            values = [grid_ref[pl.ds(r + 8 * j * rows, 8, stride=rows), :] for j in range(blocks)]
            for t in range(2):
                index = jnp.broadcast_to(col_ref[pl.ds(first + t, 1), :], (8, LANES))
                hit = jnp.broadcast_to(row_ref[pl.ds(first + t, 1), :], (8, LANES)) == 2 * r + side
                for j in range(blocks):
                    pltpu.store(
                        t_ref.at[first + t, 8 * j:8 * j + 8, :], lane_take(values[j], index), mask=hit
                    )

    for w in range(windows):
        first, second = t_ref[2 * w], t_ref[2 * w + 1]
        s_ref[w, 0:padded_planes, :] = jnp.where(low, first, pltpu.roll(second, half, 1))
        s_ref[w, padded_planes:2 * padded_planes, :] = jnp.where(low, pltpu.roll(first, half, 1), second)
    reorder(dst_ref, s_ref, x_ref)
    for w in range(devices):
        out_ref[w, 0:2 * padded_planes, :] = x_ref[w]
    for e in range(devices // 2):
        re = x_ref[devices + e, 0:padded_planes, :]
        im = x_ref[devices + e, padded_planes:2 * padded_planes, :]
        out_ref[2 * e, 2 * padded_planes:3 * padded_planes, :] = jnp.where(
            low, re, pltpu.roll(im, half, 1)
        )
        out_ref[2 * e + 1, 2 * padded_planes:3 * padded_planes, :] = jnp.where(
            low, pltpu.roll(re, half, 1), im
        )
    for d in range(devices):
        out_ref[d, 3 * padded_planes:, :] = jnp.zeros((8, LANES), F32)


def inner_kernel(bands, volume, norm, place_ref, *refs):
    kc_ref = refs[0]
    coefs = refs[1:1 + bands]
    fields = refs[1 + bands:1 + 2 * bands]
    in_ref = refs[1 + 2 * bands]
    out_refs = refs[2 + 2 * bands:]
    devices = in_ref.shape[0]
    padded_planes = (in_ref.shape[1] - 8) // 3
    half = LANES // 2
    padded = coefs[0].shape[2]
    me, mine = place_ref[0], place_ref[1]
    low = lax.broadcasted_iota(jnp.int32, (padded_planes, LANES), 1) < half

    def fold(x):
        rows = x.shape[0]
        total = x[0:8]
        for at in range(8, rows, 8):
            total = total + x[at:at + 8]
        return total

    kc = kc_ref[...]
    kc_re, kc_im = kc[:, :padded], kc[:, padded:]
    sums = []
    for m in range(bands):
        c_re, c_im = coefs[m][:, 0, :], coefs[m][:, 1, :]
        sums.append([fold(c_re * kc_re + c_im * kc_im), fold(c_re * kc_im - c_im * kc_re)])
    local = [[jnp.zeros((8, LANES), F32), jnp.zeros((8, LANES), F32)] for _ in range(bands)]
    for d in range(devices):
        value = in_ref[d, 0:3 * padded_planes, :]
        re, im, rest = value[:padded_planes], value[padded_planes:2 * padded_planes], value[2 * padded_planes:]
        turned = pltpu.roll(rest, half, 1)
        other = jnp.concatenate([im, -re, jnp.where(low, turned, -turned)], axis=0)
        for m in range(bands):
            col = fields[m][d, 0:3 * padded_planes, :]
            local[m][0] = local[m][0] + fold(col * value)
            local[m][1] = local[m][1] + fold(col * other)
    lane = lax.broadcasted_iota(jnp.int32, (8, LANES), 1)
    row = lax.broadcasted_iota(jnp.int32, (8, LANES), 0)
    tile = jnp.zeros((8, LANES), F32)
    for m in range(bands):
        at = me ^ m
        for part, sign in ((0, 1.0), (1, -1.0)):
            partial = sums[m][part] + volume * local[m][part]
            scalar = jnp.sum(jnp.sum(partial, axis=1, keepdims=True), axis=0, keepdims=True)
            tile = jnp.where((lane == at) & (row == part), sign * norm * scalar, tile)
    for k in range(devices):
        out_refs[k][0:3 * padded_planes, :] = in_ref[lax.rem(mine + k, devices), 0:3 * padded_planes, :]
        out_refs[k][3 * padded_planes:, :] = tile


def final_kernel(volume, devices, me_ref, len_ref, *refs):
    ret_refs = refs[:devices]
    kc_ref, whi_ref, wlo_ref, sc_ref, ss_ref, out_ref, sub_ref, stack_ref = refs[devices:]
    padded_planes = (ret_refs[0].shape[0] - 8) // 3
    sticks, _, padded = out_ref.shape
    half = LANES // 2
    bands = sub_ref.shape[2]
    total = jnp.zeros((8, LANES), F32)
    me = me_ref[0]
    for k in range(devices):
        value = ret_refs[k][...]
        base = pl.multiple_of(lax.rem(me + devices - k, devices) * padded_planes, 8)
        total = total + value[3 * padded_planes:]
        rest = value[2 * padded_planes:3 * padded_planes]
        re = jnp.concatenate([value[:padded_planes], rest[:, :half]], axis=1)
        im = jnp.concatenate([value[padded_planes:2 * padded_planes], rest[:, half:]], axis=1)
        c = sc_ref[pl.ds(base, padded_planes), :]
        s = ss_ref[pl.ds(base, padded_planes), :]
        stack_ref[pl.ds(2 * base, padded_planes), :sticks] = re * c - im * s
        stack_ref[pl.ds(2 * base + padded_planes, padded_planes), :sticks] = re * s + im * c
    turned = jnp.transpose(stack_ref[...])[:sticks]
    local = dot3(split(turned), (whi_ref[...], wlo_ref[...])) * volume
    position = lax.broadcasted_iota(jnp.int32, (sticks, padded), 1).astype(F32)
    kept = position < len_ref[:, 0:1]
    kc = kc_ref[...]
    out_ref[:, 0, :] = jnp.where(kept, kc[:, :padded] + local[:, :padded], 0.0)
    out_ref[:, 1, :] = jnp.where(kept, kc[:, padded:] + local[:, padded:], 0.0)
    sub_ref[:, 0, :] = total[0:2, :bands]


def pairs(count, k):
    return [(d, d ^ k) for d in range(count)]


def shards(bands, devices, coefficients, stick_col, stick_row, stick_length, plane_of_slot, potential):
    extent = plane_of_slot.shape[0]
    sticks = coefficients.shape[1]
    padded = coefficients.shape[3]
    total_sticks = stick_col.shape[0]
    planes = potential.shape[0]
    padded_planes = up8(planes)
    if sticks != LANES + LANES // 2 or devices % 2 or planes % 2 or bands & (bands - 1):
        raise ValueError("sizes")
    rows = sum(row_blocks())
    volume = 1.0 / (extent * extent * extent)
    me = lax.axis_index("tg").astype(jnp.int32)
    coef = coefficients.reshape(sticks, 2, padded)

    length, row, col = (v.reshape(-1, LANES) for v in (stick_length, stick_row, stick_col))
    slots = plane_of_slot.reshape(devices, planes)
    if padded_planes > planes:
        slots = jnp.pad(slots, ((0, 0), (0, padded_planes - planes)), constant_values=-1)
    slots = slots.reshape(1, devices * padded_planes)
    windows = total_sticks // LANES
    smem = pl.BlockSpec(memory_space=pltpu.SMEM)
    vmem = pl.BlockSpec(memory_space=pltpu.VMEM)
    hbm = pl.BlockSpec(memory_space=pltpu.HBM)

    block = 3 * padded_planes
    total_planes = devices * padded_planes
    sent, kc, lengths, whi, wlo, shift_cos, shift_sin = pl.pallas_call(
        functools.partial(wave_kernel, extent),
        out_shape=(
            jax.ShapeDtypeStruct((devices, block, LANES), F32),
            jax.ShapeDtypeStruct((sticks, 2 * padded), F32),
            jax.ShapeDtypeStruct((sticks, LANES), F32),
            jax.ShapeDtypeStruct((2 * total_planes, 2 * padded), BF16),
            jax.ShapeDtypeStruct((2 * total_planes, 2 * padded), BF16),
            jax.ShapeDtypeStruct((total_planes, sticks), F32),
            jax.ShapeDtypeStruct((total_planes, sticks), F32),
        ),
        in_specs=[smem] + [hbm] * 5,
        scratch_shapes=[
            pltpu.VMEM(length.shape, jnp.int32),
            pltpu.VMEM(row.shape, jnp.int32),
            pltpu.VMEM(col.shape, jnp.int32),
            pltpu.VMEM(slots.shape, jnp.int32),
            pltpu.VMEM(coef.shape, F32),
            pltpu.SemaphoreType.DMA((5,)),
        ],
        compiler_params=params(56),
        name="wave_to_planes",
    )(me.reshape(1), length, row, col, slots, coef)

    received = lax.all_to_all(sent, "tg", split_axis=0, concat_axis=0, tiled=True)

    window_list = jax.ShapeDtypeStruct((windows, LANES), jnp.int32)
    longer_list = jax.ShapeDtypeStruct((2 * windows + 1, LANES), jnp.int32)
    square = jax.ShapeDtypeStruct((LANES, LANES), jnp.int32)
    even_map, odd_map, first, source, target, row_w, col_w = pl.pallas_call(
        functools.partial(map_kernel, extent, sticks),
        out_shape=(
            square,
            square,
            jax.ShapeDtypeStruct((16, LANES), jnp.int32),
            window_list,
            window_list,
            longer_list,
            longer_list,
        ),
        in_specs=[hbm] * 2,
        scratch_shapes=[
            pltpu.VMEM(row.shape, jnp.int32),
            pltpu.VMEM(col.shape, jnp.int32),
            pltpu.SemaphoreType.DMA((2,)),
        ],
        compiler_params=params(14 * total_sticks / 1536),
        cost_estimate=cost(4e9, 1e5),
        name="stick_map",
    )(row, col)

    constants = jnp.asarray(tables(extent))
    weighted = pl.pallas_call(
        functools.partial(plane_kernel, planes),
        out_shape=jax.ShapeDtypeStruct((devices, block + 8, LANES), F32),
        in_specs=[smem] + [vmem] * 7 + [hbm] * 2,
        out_specs=vmem,
        scratch_shapes=[
            pltpu.VMEM((windows, 2 * padded_planes, LANES), F32),
            pltpu.VMEM((windows, 2 * padded_planes, LANES), F32),
            pltpu.VMEM((2 * windows + 1, padded_planes, LANES), F32),
            pltpu.VMEM((padded_planes * rows, LANES), F32),
            pltpu.VMEM((padded_planes * rows, LANES), F32),
            pltpu.VMEM(constants.shape, BF16),
            pltpu.VMEM(potential.shape, F32),
            pltpu.SemaphoreType.DMA((2,)),
        ],
        compiler_params=params(52),
        cost_estimate=cost(2e10, 1e7),
        name="planes",
    )(first, even_map, odd_map, source, target, row_w, col_w, received, constants, potential)

    coefs, fields = [coef], [received]
    for m in range(1, bands):
        coefs.append(lax.ppermute(coef, "band", pairs(bands, m)))
        fields.append(lax.ppermute(received, "band", pairs(bands, m)))
    band = lax.axis_index("band").astype(jnp.int32)
    norm = 1.0 / (total_sticks * padded)
    places = jnp.stack([band, me])
    outgoing = pl.pallas_call(
        functools.partial(inner_kernel, bands, volume, norm),
        out_shape=(jax.ShapeDtypeStruct((block + 8, LANES), F32),) * devices,
        in_specs=[smem] + [vmem] * (2 + 2 * bands),
        compiler_params=params(6 + 1.5 * bands),
        name="inner",
    )(places, kc, *coefs, *fields, weighted)

    returned = [outgoing[0]]
    for k in range(1, devices):
        ring = [(d, (d + k) % devices) for d in range(devices)]
        returned.append(lax.ppermute(outgoing[k], "tg", ring))
    applied, subspace = pl.pallas_call(
        functools.partial(final_kernel, volume, devices),
        out_shape=(
            jax.ShapeDtypeStruct((sticks, 2, padded), F32),
            jax.ShapeDtypeStruct((2, 1, bands), F32),
        ),
        in_specs=[smem] + [vmem] * (6 + devices),
        scratch_shapes=[pltpu.VMEM((2 * total_planes, 2 * LANES), F32)],
        compiler_params=params(6 + 6 * total_planes / 192),
        name="planes_to_wave",
    )(me.reshape(1), lengths, *returned, kc, whi, wlo, shift_cos, shift_sin)
    return applied.reshape(1, sticks, 2, padded), subspace


def solution(mesh):
    in_specs = (P("band", "tg", None, None), P(), P(), P(), P(), P("tg", None, None))
    out_specs = (P("band", "tg", None, None), P(None, "band", None))
    body = functools.partial(shards, mesh.shape["band"], mesh.shape["tg"])
    return jax.shard_map(body, mesh=mesh, in_specs=in_specs, out_specs=out_specs, check_vma=False)
```

```python
import functools
import math

import jax
import jax.numpy as jnp
import ml_dtypes
import numpy as np
from jax import lax
from jax.experimental import pallas as pl
from jax.experimental.pallas import tpu as pltpu
from jax.sharding import PartitionSpec as P

RADIUS = 48
LANES = 128
F32 = jnp.float32
BF16 = jnp.bfloat16


def up8(n):
    return -(-n // 8) * 8


def split(x):
    hi = x.astype(BF16)
    return hi, (x - hi.astype(F32)).astype(BF16)


def dot3(a, b, dims=((1,), (0,))):
    def dot(x, y):
        return lax.dot_general(x, y, (dims, ((), ())), preferred_element_type=F32)

    return dot(a[0], b[0]) + (dot(a[0], b[1]) + dot(a[1], b[0]))


def trig(product, extent):
    n = product - extent * jnp.floor(product * (1.0 / extent) + 0.5)
    quarter = extent / 4.0
    unit = 2.0 * math.pi / extent

    def sine(m):
        u = m * unit
        v = u * u
        s = 1.0 / 6227020800.0
        for term in (-39916800.0, 362880.0, -5040.0, 120.0, -6.0, 1.0):
            s = s * v + 1.0 / term
        return u * s

    folded = jnp.where(
        jnp.abs(n) > quarter, jnp.where(n > 0, 2.0 * quarter, -2.0 * quarter) - n, n
    )
    return sine(quarter - jnp.abs(n)), sine(folded)


def pair(table):
    hi = table.astype(np.float32).astype(ml_dtypes.bfloat16)
    lo = (table - hi.astype(np.float64)).astype(ml_dtypes.bfloat16)
    return hi, lo


def row_blocks():
    even = -(-(RADIUS + 1) // 16) * 16
    odd = -(-RADIUS // 16) * 16
    return even, odd


@functools.cache
def tables(extent):
    half = extent // 2
    grid = np.arange(extent)
    freq = np.arange(2 * RADIUS + 1) - RADIUS

    def angles(f, g):
        a = 2.0 * np.pi * ((f[:, None] * g[None, :]) % extent) / extent
        return np.cos(a), np.sin(a)

    wide = 2 * LANES
    x_forward, x_back, forward, back = [], [], [], []
    for offset, rows in zip((0, 1), row_blocks()):
        cos, sin = angles(freq[offset::2], grid[:half])
        count = cos.shape[0]
        table = np.zeros((LANES, wide))
        table[:count, :half] = cos
        table[LANES // 2:LANES // 2 + count, :half] = -sin
        table[:count, LANES:LANES + half] = sin
        table[LANES // 2:LANES // 2 + count, LANES:LANES + half] = cos
        hi, lo = pair(table)
        x_forward.append(np.concatenate([hi, hi, lo], axis=0))
        hi, lo = pair(table.T.copy())
        x_back.append(
            np.concatenate(
                [np.concatenate([hi, lo], axis=1), np.concatenate([hi, np.zeros_like(lo)], axis=1)], axis=0
            )
        )
        parts = []
        for wave in (cos, sin):
            table = np.zeros((half, rows))
            table[:, :count] = wave.T
            hi, lo = pair(table)
            parts += [hi, hi, lo]
        forward.append(np.concatenate(parts, axis=1))
        table = np.zeros((2 * rows, half))
        table[:count] = cos
        table[rows:rows + count] = sin
        hi, lo = pair(table)
        back.append(np.concatenate([hi, hi, lo], axis=1))
    rows = [np.concatenate(x_forward, axis=1), np.concatenate(x_back, axis=1)]
    for table in forward + back:
        rows.append(np.pad(table, ((0, 0), (0, 2 * wide - table.shape[1]))))
    return np.concatenate(rows, axis=0)


def params(megabytes):
    return pltpu.CompilerParams(vmem_limit_bytes=int(min(megabytes, 56) * 2**20))


def fetch_all(sources, targets, sems):
    copies = [
        pltpu.make_async_copy(source, target, sems.at[i])
        for i, (source, target) in enumerate(zip(sources, targets))
    ]
    for copy in copies:
        copy.start()
    return copies


def cost(flops, nbytes):
    return pl.CostEstimate(flops=int(flops), bytes_accessed=int(nbytes), transcendentals=0)


def wave_kernel(
    extent, me_ref, length_hbm, row_hbm, col_hbm, plane_hbm, coef_hbm,
    out_ref, kc_ref, wave_ref, len_ref, whi_ref, wlo_ref, sc_ref, ss_ref,
    length_ref, row_ref, col_ref, plane_ref, coef_ref, sems,
):
    copies = fetch_all(
        (length_hbm, row_hbm, col_hbm, plane_hbm, coef_hbm),
        (length_ref, row_ref, col_ref, plane_ref, coef_ref),
        sems,
    )
    for copy in copies[:4]:
        copy.wait()
    devices = out_ref.shape[0]
    sticks, _, padded = coef_ref.shape
    padded_planes = plane_ref.shape[1] // devices
    me = me_ref[0]
    half = LANES // 2
    lead = (me * sticks) // LANES
    odd = (me * sticks) % LANES != 0

    def own(ref):
        first, second = ref[pl.ds(lead, 1), :], ref[pl.ds(lead + 1, 1), :]
        both = jnp.concatenate([first, second], axis=1)
        return jnp.where(odd, both[:, half:], both[:, :sticks])

    length_row = own(length_ref).astype(F32)
    at_row = own(row_ref)
    at_col = own(col_ref)
    at_row = jnp.where(at_row <= RADIUS, at_row, at_row - extent).astype(F32)
    at_col = jnp.where(at_col <= RADIUS, at_col, at_col - extent).astype(F32)
    square_row = at_row * at_row + at_col * at_col
    spare = jnp.ones((1, 2 * LANES - sticks), F32)
    aux = jnp.concatenate(
        [
            jnp.broadcast_to(jnp.concatenate([length_row, spare], axis=1), (LANES // 2, 2 * LANES)),
            jnp.broadcast_to(jnp.concatenate([square_row, spare], axis=1), (LANES // 2, 2 * LANES)),
        ],
        axis=0,
    )
    aux_col = jnp.transpose(aux)[:sticks]
    len_ref[...] = aux_col
    length = aux_col[:, 0:1]
    square = aux_col[:, LANES // 2:LANES // 2 + 1]
    middle = (length - 1.0) * 0.5
    position = lax.broadcasted_iota(jnp.int32, (sticks, padded), 1).astype(F32)
    total = plane_ref.shape[1]
    plane_row = jnp.broadcast_to(plane_ref[...].astype(F32), (LANES, total))
    plane_col = jnp.transpose(plane_row)[:, 0:1]
    real = (plane_col >= 0.0).astype(F32)
    plane_col = jnp.maximum(plane_col, 0.0)
    harmonic = lax.broadcasted_iota(jnp.int32, (total, padded), 1).astype(F32)
    cos, sin = trig(plane_col * harmonic, extent)
    cos, sin = cos * real, sin * real
    parts = []
    for d in range(devices):
        c = cos[d * padded_planes:(d + 1) * padded_planes]
        s = sin[d * padded_planes:(d + 1) * padded_planes]
        parts.append(jnp.concatenate([c, -s], axis=1))
        parts.append(jnp.concatenate([s, c], axis=1))
    table = split(jnp.concatenate(parts, axis=0))
    whi_ref[...] = table[0]
    wlo_ref[...] = table[1]
    shift_cos, shift_sin = trig(plane_col * ((length_row - 1.0) * 0.5), extent)
    sc_ref[...] = shift_cos
    ss_ref[...] = shift_sin
    copies[4].wait()
    kept = (position < length).astype(F32)
    kinetic = (square + (position - middle) * (position - middle)) * (1.0 / (RADIUS * RADIUS))
    wave = jnp.concatenate([coef_ref[:, 0, :] * kept, coef_ref[:, 1, :] * kept], axis=1)
    kc_ref[...] = wave * jnp.concatenate([kinetic, kinetic], axis=1)
    wave_ref[:sticks, :] = wave[:, :padded]
    wave_ref[sticks:, :] = wave[:, padded:]
    raw = dot3(table, split(wave), ((1,), (1,)))
    for d in range(devices):
        at = 2 * d * padded_planes
        re, im = raw[at:at + padded_planes], raw[at + padded_planes:at + 2 * padded_planes]
        c = shift_cos[d * padded_planes:(d + 1) * padded_planes]
        s = shift_sin[d * padded_planes:(d + 1) * padded_planes]
        along_re = re * c + im * s
        along_im = im * c - re * s
        out_ref[d, 0:padded_planes, :] = along_re[:, :LANES]
        out_ref[d, padded_planes:2 * padded_planes, :] = along_im[:, :LANES]
        out_ref[d, 2 * padded_planes:3 * padded_planes, :] = jnp.concatenate(
            [along_re[:, LANES:], along_im[:, LANES:]], axis=1
        )


def window_row(values, sticks):
    line = jnp.concatenate([values[i:i + 1] for i in range(values.shape[0])], axis=1)
    starts = range(0, line.shape[1], sticks)
    parts = [line[:, at:at + LANES] for at in starts]
    parts += [line[:, at + LANES:at + sticks] for at in starts]
    return jnp.concatenate(parts, axis=1)


def map_kernel(
    extent, sticks, in_row_hbm, in_col_hbm,
    even_ref, odd_ref, first_ref, src_ref, dst_ref, row_ref, col_ref,
    in_row_ref, in_col_ref, sems,
):
    for copy in fetch_all((in_row_hbm, in_col_hbm), (in_row_ref, in_col_ref), sems):
        copy.wait()
    windows = src_ref.shape[0]
    total = windows * LANES

    def signed(ref):
        value = ref[...]
        return window_row(jnp.where(value <= RADIUS, value, value - extent) + RADIUS, sticks)

    def dot(x, y, dims=((1,), (0,))):
        return lax.dot_general(x, y, (dims, ((), ())), preferred_element_type=F32)

    def bits(condition):
        return condition.astype(F32).astype(BF16)

    nt = ((1,), (1,))
    own_row, own_col = signed(in_row_ref), signed(in_col_ref)
    half = LANES // 2
    own_row = (own_row & 1) * row_blocks()[0] + (own_row >> 1)
    own_col = (own_col & 1) * half + (own_col >> 1)
    tall = lax.broadcasted_iota(jnp.int32, (LANES, total), 0)
    place = lax.broadcasted_iota(jnp.int32, (LANES, total), 1)
    in_col = tall == own_col
    row_hot, col_hot = bits(tall == own_row), bits(in_col)
    down = lax.broadcasted_iota(jnp.int32, (LANES, LANES), 0)
    across = lax.broadcasted_iota(jnp.int32, (LANES, LANES), 1)
    before = bits(down < across)
    after = bits(down > across)
    upto = bits(down >= across)
    ones = jnp.ones((LANES, LANES), BF16)
    taken = dot(row_hot, col_hot, nt)
    taken_t = dot(col_hot, row_hot, nt)
    taken_b, taken_tb = taken.astype(BF16), taken_t.astype(BF16)
    start = dot(dot(after, taken_b).astype(BF16), ones)
    end = start + dot(taken_b, ones)
    start_t = dot(ones, dot(taken_tb, before).astype(BF16))
    left = across < half
    standing = dot(taken_b, before) + start
    low_ones = bits(down < half)
    high_start = start + dot(taken_b, low_ones)
    ones_t = bits(across < half)
    high_start_t = start_t + dot(ones_t, taken_tb)
    limit = 2.0 * windows - 1.0

    def first_window(value):
        return jnp.minimum(jnp.floor(value * (1.0 / half)), limit)

    for ref, begin in ((even_ref, start), (odd_ref, high_start)):
        code = jnp.where(taken > 0.5, standing - half * first_window(begin), -1.0)
        turned = pltpu.roll(code, half, 1)
        both = jnp.where(left, code, turned) if ref is even_ref else jnp.where(left, turned, code)
        ref[...] = both.astype(jnp.int32)
    first_ref[...] = jnp.concatenate(
        [first_window(start_t[0:8]), first_window(high_start_t[0:8])], axis=0
    ).astype(jnp.int32)

    spot = place.astype(F32)
    in_range = (spot >= start[:, 0:1]) & (spot < end[:, 0:1])
    sorted_hot = bits(in_range)
    sorted_row = jnp.sum(jnp.where(in_range, tall, 0).astype(F32), axis=0, keepdims=True)
    sorted_rank = spot[0:1] - jnp.sum(jnp.where(in_range, start[:, 0:1], 0.0), axis=0, keepdims=True)
    counts = dot(dot(upto, taken_tb).astype(BF16), sorted_hot)
    sorted_col = jnp.sum((counts <= sorted_rank).astype(F32), axis=0, keepdims=True)
    names = place + 1
    name_hi = dot(jnp.where(in_col, names >> 6, 0).astype(F32).astype(BF16), row_hot, nt)
    name_lo = dot(jnp.where(in_col, names & 63, 0).astype(F32).astype(BF16), row_hot, nt)
    named = dot(name_hi.astype(BF16), sorted_hot) * 64.0 + dot(name_lo.astype(BF16), sorted_hot)
    source = jnp.sum(jnp.where(tall.astype(F32) == sorted_col, named, 0.0), axis=0, keepdims=True) - 1.0
    place_t = dot(after, taken_tb) + start_t
    place_hi = jnp.floor(place_t * (1.0 / 64.0))
    place_lo = place_t - 64.0 * place_hi
    placed = dot(place_hi.astype(BF16), row_hot) * 64.0 + dot(place_lo.astype(BF16), row_hot)
    target = jnp.sum(jnp.where(in_col, placed, 0.0), axis=0, keepdims=True)
    for values, ref in ((source, src_ref), (target, dst_ref)):
        values = values.astype(jnp.int32)
        for w in range(windows):
            ref[w:w + 1, :] = values[:, w * LANES:(w + 1) * LANES]
    is_left = left[0:8]
    shift = jnp.where(is_left, 0, half)
    sorted_col = sorted_col.astype(jnp.int32)
    sorted_key = sorted_row.astype(jnp.int32) * 2 + (sorted_col >> 6)
    sorted_col = sorted_col & (half - 1)
    for values, ref, add in ((sorted_key, row_ref, 0), (sorted_col, col_ref, shift)):
        for w in range(windows):
            line = jnp.broadcast_to(values[:, w * LANES:(w + 1) * LANES], (8, LANES))
            turned = pltpu.roll(line, half, 1)
            ref[2 * w:2 * w + 1, :] = (jnp.where(is_left, line, turned) + add)[0:1]
            ref[2 * w + 1:2 * w + 2, :] = (jnp.where(is_left, turned, line) + add)[0:1]
    row_ref[2 * windows:2 * windows + 1, :] = jnp.full((1, LANES), -1, jnp.int32)
    col_ref[2 * windows:2 * windows + 1, :] = jnp.zeros((1, LANES), jnp.int32)


def join_kernel(recv_ref, wave_ref, out_ref):
    devices, block, _ = recv_ref.shape
    for d in range(devices):
        out_ref[d * block:(d + 1) * block, :] = recv_ref[d]
    out_ref[devices * block:, :] = wave_ref[...]


def lane_take(x, index):
    return jnp.take_along_axis(x, index, axis=1, mode="promise_in_bounds")


def plane_kernel(
    planes, first_ref, even_ref, odd_ref, src_ref, dst_ref, row_ref, col_ref, recv_ref,
    *refs,
):
    table_hbm, pot_hbm, out_ref, x_ref, s_ref, t_ref, ge_ref, go_ref, table_ref, pot_ref, sems = refs
    devices = recv_ref.shape[0]
    padded_planes = recv_ref.shape[1] // 3
    windows = x_ref.shape[0]
    rows = ge_ref.shape[0] // padded_planes
    extent = pot_ref.shape[1]
    half = LANES // 2
    copies = fetch_all((table_hbm, pot_hbm), (table_ref, pot_ref), sems)

    low = lax.broadcasted_iota(jnp.int32, (padded_planes, LANES), 1) < half
    for d in range(devices):
        x_ref[d] = recv_ref[d, 0:2 * padded_planes, :]
    for e in range(devices // 2):
        first = recv_ref[2 * e, 2 * padded_planes:3 * padded_planes, :]
        second = recv_ref[2 * e + 1, 2 * padded_planes:3 * padded_planes, :]
        x_ref[devices + e, 0:padded_planes, :] = jnp.where(low, first, pltpu.roll(second, half, 1))
        x_ref[devices + e, padded_planes:2 * padded_planes, :] = jnp.where(
            low, pltpu.roll(first, half, 1), second
        )

    blocks = padded_planes // 8

    def reorder(order_ref, from_ref, to_ref):
        @pl.loop(0, windows, unroll=4)
        def _(v):
            order = jnp.broadcast_to(order_ref[pl.ds(v, 1), :], (8, LANES))
            index = order & (LANES - 1)
            window = order >> 7
            for j in range(2 * blocks):
                value = jnp.zeros((8, LANES), F32)
                for w in range(windows):
                    value = jnp.where(window == w, lane_take(from_ref[w, 8 * j:8 * j + 8, :], index), value)
                to_ref[v, 8 * j:8 * j + 8, :] = value

    reorder(src_ref, x_ref, s_ref)
    for w in range(windows):
        re, im = s_ref[w, 0:padded_planes, :], s_ref[w, padded_planes:2 * padded_planes, :]
        t_ref[2 * w] = jnp.where(low, re, pltpu.roll(im, half, 1))
        t_ref[2 * w + 1] = jnp.where(low, pltpu.roll(re, half, 1), im)

    left = low[0:8]
    upper_lanes = jnp.where(left, 0, half)
    sides = ((0, even_ref, ge_ref), (1, odd_ref, go_ref))

    @pl.loop(0, rows, unroll=8)
    def _(r):
        for side, code_ref, grid_ref in sides:
            first = first_ref[8 * side, r]
            code = jnp.broadcast_to(code_ref[pl.ds(r, 1), :], (8, LANES))
            index = (code & (half - 1)) + upper_lanes
            window = code >> 6
            for j in range(blocks):
                lead = lane_take(t_ref[first, 8 * j:8 * j + 8, :], index)
                trail = lane_take(t_ref[first + 1, 8 * j:8 * j + 8, :], index)
                value = jnp.where(window == 0, lead, jnp.where(window == 1, trail, 0.0))
                grid_ref[pl.ds(r + 8 * j * rows, 8, stride=rows), :] = value

    for copy in copies:
        copy.wait()
    even_rows, odd_rows = row_blocks()
    folded = extent // 2
    group = next(g for g in (12, 8, 6, 4, 2) if planes % g == 0)
    wide = 2 * LANES
    at_back = 3 * LANES
    at_y = at_back + 2 * wide
    at_even = at_y + 2 * folded
    at_odd = at_even + 2 * even_rows
    x_forward = (table_ref[0:at_back, :wide], table_ref[0:at_back, wide:])
    x_back = (table_ref[at_back:at_y, :wide], table_ref[at_back:at_y, wide:])
    y_even = table_ref[at_y:at_y + folded, :6 * even_rows]
    y_odd = table_ref[at_y + folded:at_even, :6 * odd_rows]
    back_even = table_ref[at_even:at_odd, :3 * folded]
    back_odd = table_ref[at_odd:at_odd + 2 * odd_rows, :3 * folded]

    def dot(x, y):
        return jnp.dot(x, y, preferred_element_type=F32)

    def stack(x, axis):
        hi, lo = split(x)
        return jnp.concatenate([hi, lo, hi], axis=axis)

    def turn(x):
        lane = lax.broadcasted_iota(jnp.int32, (x.shape[0], LANES), 1) < half
        parts = []
        for at in range(0, x.shape[1], LANES):
            rolled = pltpu.roll(x[:, at:at + LANES], half, 1)
            parts.append(jnp.where(lane, -rolled, rolled))
        return jnp.concatenate(parts, axis=1)

    @pl.loop(0, planes // group)
    def _(step):
        lines = []
        for t in range(group):
            base = pl.multiple_of((step * group + t) * rows, 16)
            parts = []
            for at, size, table in ((0, even_rows, y_even), (even_rows, odd_rows, y_odd)):
                pick = pl.ds(base + at, size)
                spectrum = jnp.concatenate([ge_ref[pick, :], go_ref[pick, :]], axis=1)
                both = jnp.concatenate([stack(spectrum, 0), stack(turn(spectrum), 0)], axis=0)
                parts.append(dot(table, both))
            lines.append(parts[0] + parts[1])
            lines.append(parts[0] - parts[1])
        lines = jnp.concatenate(lines, axis=0)
        field_even = dot(stack(lines[:, :LANES], 1), x_forward[0])
        field_odd = dot(stack(lines[:, LANES:], 1), x_forward[1])
        spare = jnp.zeros((extent, LANES - folded), F32)
        sums, differences = [], []
        for t in range(group):
            v = pot_ref[step * group + t]
            v_near = jnp.concatenate([v[:, :folded], spare], axis=1)
            v_far = jnp.concatenate([v[:, folded:], spare], axis=1)
            even = field_even[t * extent:(t + 1) * extent]
            odd = field_odd[t * extent:(t + 1) * extent]
            near = (even + odd) * jnp.concatenate([v_near, v_near], axis=1)
            far = (even - odd) * jnp.concatenate([v_far, v_far], axis=1)
            sums.append(near + far)
            differences.append(near - far)
        back = []
        for weighted, table in ((sums, x_back[0]), (differences, x_back[1])):
            both = dot(jnp.concatenate(split(jnp.concatenate(weighted, axis=0)), axis=1), table)
            back.append(both[:, :LANES] + both[:, LANES:])
        back = jnp.concatenate(back, axis=1)
        for t in range(group):
            base = pl.multiple_of((step * group + t) * rows, 16)
            upper = back[t * extent:t * extent + folded]
            lower = back[t * extent + folded:(t + 1) * extent]
            for at, size, table, value in (
                (0, even_rows, back_even, upper + lower), (even_rows, odd_rows, back_odd, upper - lower)
            ):
                both = dot(table, stack(value, 0))
                value = both[:size] - turn(both[size:])
                pick = pl.ds(base + at, size)
                ge_ref[pick, :] = value[:, :LANES]
                go_ref[pick, :] = value[:, LANES:]

    @pl.loop(0, rows, unroll=8)
    def _(r):
        for side, _, grid_ref in sides:
            first = first_ref[8 * side, r]
            values = [grid_ref[pl.ds(r + 8 * j * rows, 8, stride=rows), :] for j in range(blocks)]
            for t in range(2):
                index = jnp.broadcast_to(col_ref[pl.ds(first + t, 1), :], (8, LANES))
                hit = jnp.broadcast_to(row_ref[pl.ds(first + t, 1), :], (8, LANES)) == 2 * r + side
                for j in range(blocks):
                    pltpu.store(
                        t_ref.at[first + t, 8 * j:8 * j + 8, :], lane_take(values[j], index), mask=hit
                    )

    for w in range(windows):
        first, second = t_ref[2 * w], t_ref[2 * w + 1]
        s_ref[w, 0:padded_planes, :] = jnp.where(low, first, pltpu.roll(second, half, 1))
        s_ref[w, padded_planes:2 * padded_planes, :] = jnp.where(low, pltpu.roll(first, half, 1), second)
    reorder(dst_ref, s_ref, x_ref)
    for w in range(devices):
        out_ref[w, 0:2 * padded_planes, :] = x_ref[w]
    for e in range(devices // 2):
        re = x_ref[devices + e, 0:padded_planes, :]
        im = x_ref[devices + e, padded_planes:2 * padded_planes, :]
        out_ref[2 * e, 2 * padded_planes:3 * padded_planes, :] = jnp.where(
            low, re, pltpu.roll(im, half, 1)
        )
        out_ref[2 * e + 1, 2 * padded_planes:3 * padded_planes, :] = jnp.where(
            low, pltpu.roll(re, half, 1), im
        )
    for d in range(devices):
        out_ref[d, 3 * padded_planes:, :] = jnp.zeros((8, LANES), F32)


def inner_kernel(bands, volume, norm, place_ref, *refs):
    kc_ref = refs[0]
    joint = refs[1:1 + bands]
    in_ref = refs[1 + bands]
    out_refs = refs[2 + bands:]
    devices = in_ref.shape[0]
    padded_planes = (in_ref.shape[1] - 8) // 3
    half = LANES // 2
    sticks, padded = kc_ref.shape[0], kc_ref.shape[1] // 2
    block = 3 * padded_planes
    at = devices * block
    me, mine = place_ref[0], place_ref[1]
    low = lax.broadcasted_iota(jnp.int32, (padded_planes, LANES), 1) < half

    def fold(x):
        rows = x.shape[0]
        total = x[0:8]
        for at in range(8, rows, 8):
            total = total + x[at:at + 8]
        return total

    kc = kc_ref[...]
    kc_re, kc_im = kc[:, :padded], kc[:, padded:]
    sums = []
    for m in range(bands):
        c_re, c_im = joint[m][at:at + sticks, :], joint[m][at + sticks:, :]
        sums.append([fold(c_re * kc_re + c_im * kc_im), fold(c_re * kc_im - c_im * kc_re)])
    local = [[jnp.zeros((8, LANES), F32), jnp.zeros((8, LANES), F32)] for _ in range(bands)]
    for d in range(devices):
        value = in_ref[d, 0:3 * padded_planes, :]
        re, im, rest = value[:padded_planes], value[padded_planes:2 * padded_planes], value[2 * padded_planes:]
        turned = pltpu.roll(rest, half, 1)
        other = jnp.concatenate([im, -re, jnp.where(low, turned, -turned)], axis=0)
        for m in range(bands):
            col = joint[m][d * block:(d + 1) * block, :]
            local[m][0] = local[m][0] + fold(col * value)
            local[m][1] = local[m][1] + fold(col * other)
    lane = lax.broadcasted_iota(jnp.int32, (8, LANES), 1)
    row = lax.broadcasted_iota(jnp.int32, (8, LANES), 0)
    tile = jnp.zeros((8, LANES), F32)
    for m in range(bands):
        spot = me ^ m
        for part, sign in ((0, 1.0), (1, -1.0)):
            partial = sums[m][part] + volume * local[m][part]
            scalar = jnp.sum(jnp.sum(partial, axis=1, keepdims=True), axis=0, keepdims=True)
            tile = jnp.where((lane == spot) & (row == part), sign * norm * scalar, tile)
    for k in range(devices):
        out_refs[k][0:3 * padded_planes, :] = in_ref[lax.rem(mine + k, devices), 0:3 * padded_planes, :]
        out_refs[k][3 * padded_planes:, :] = tile


def final_kernel(volume, devices, me_ref, len_ref, *refs):
    ret_refs = refs[:devices]
    kc_ref, whi_ref, wlo_ref, sc_ref, ss_ref, out_ref, sub_ref, stack_ref = refs[devices:]
    padded_planes = (ret_refs[0].shape[0] - 8) // 3
    sticks, _, padded = out_ref.shape
    half = LANES // 2
    bands = sub_ref.shape[2]
    total = jnp.zeros((8, LANES), F32)
    me = me_ref[0]
    for k in range(devices):
        value = ret_refs[k][...]
        base = pl.multiple_of(lax.rem(me + devices - k, devices) * padded_planes, 8)
        total = total + value[3 * padded_planes:]
        rest = value[2 * padded_planes:3 * padded_planes]
        re = jnp.concatenate([value[:padded_planes], rest[:, :half]], axis=1)
        im = jnp.concatenate([value[padded_planes:2 * padded_planes], rest[:, half:]], axis=1)
        c = sc_ref[pl.ds(base, padded_planes), :]
        s = ss_ref[pl.ds(base, padded_planes), :]
        stack_ref[pl.ds(2 * base, padded_planes), :sticks] = re * c - im * s
        stack_ref[pl.ds(2 * base + padded_planes, padded_planes), :sticks] = re * s + im * c
    turned = jnp.transpose(stack_ref[...])[:sticks]
    local = dot3(split(turned), (whi_ref[...], wlo_ref[...])) * volume
    position = lax.broadcasted_iota(jnp.int32, (sticks, padded), 1).astype(F32)
    kept = position < len_ref[:, 0:1]
    kc = kc_ref[...]
    out_ref[:, 0, :] = jnp.where(kept, kc[:, :padded] + local[:, :padded], 0.0)
    out_ref[:, 1, :] = jnp.where(kept, kc[:, padded:] + local[:, padded:], 0.0)
    sub_ref[:, 0, :] = total[0:2, :bands]


def pairs(count, k):
    return [(d, d ^ k) for d in range(count)]


def shards(bands, devices, coefficients, stick_col, stick_row, stick_length, plane_of_slot, potential):
    extent = plane_of_slot.shape[0]
    sticks = coefficients.shape[1]
    padded = coefficients.shape[3]
    total_sticks = stick_col.shape[0]
    planes = potential.shape[0]
    padded_planes = up8(planes)
    if sticks != LANES + LANES // 2 or devices % 2 or planes % 2 or bands & (bands - 1):
        raise ValueError("sizes")
    rows = sum(row_blocks())
    volume = 1.0 / (extent * extent * extent)
    me = lax.axis_index("tg").astype(jnp.int32)
    coef = coefficients.reshape(sticks, 2, padded)

    length, row, col = (v.reshape(-1, LANES) for v in (stick_length, stick_row, stick_col))
    slots = plane_of_slot.reshape(devices, planes)
    if padded_planes > planes:
        slots = jnp.pad(slots, ((0, 0), (0, padded_planes - planes)), constant_values=-1)
    slots = slots.reshape(1, devices * padded_planes)
    windows = total_sticks // LANES
    smem = pl.BlockSpec(memory_space=pltpu.SMEM)
    vmem = pl.BlockSpec(memory_space=pltpu.VMEM)
    hbm = pl.BlockSpec(memory_space=pltpu.HBM)

    block = 3 * padded_planes
    total_planes = devices * padded_planes
    sent, kc, wave, lengths, whi, wlo, shift_cos, shift_sin = pl.pallas_call(
        functools.partial(wave_kernel, extent),
        out_shape=(
            jax.ShapeDtypeStruct((devices, block, LANES), F32),
            jax.ShapeDtypeStruct((sticks, 2 * padded), F32),
            jax.ShapeDtypeStruct((2 * sticks, padded), F32),
            jax.ShapeDtypeStruct((sticks, LANES), F32),
            jax.ShapeDtypeStruct((2 * total_planes, 2 * padded), BF16),
            jax.ShapeDtypeStruct((2 * total_planes, 2 * padded), BF16),
            jax.ShapeDtypeStruct((total_planes, sticks), F32),
            jax.ShapeDtypeStruct((total_planes, sticks), F32),
        ),
        in_specs=[smem] + [hbm] * 5,
        scratch_shapes=[
            pltpu.VMEM(length.shape, jnp.int32),
            pltpu.VMEM(row.shape, jnp.int32),
            pltpu.VMEM(col.shape, jnp.int32),
            pltpu.VMEM(slots.shape, jnp.int32),
            pltpu.VMEM(coef.shape, F32),
            pltpu.SemaphoreType.DMA((5,)),
        ],
        compiler_params=params(56),
        name="wave_to_planes",
    )(me.reshape(1), length, row, col, slots, coef)

    received = lax.all_to_all(sent, "tg", split_axis=0, concat_axis=0, tiled=True)

    window_list = jax.ShapeDtypeStruct((windows, LANES), jnp.int32)
    longer_list = jax.ShapeDtypeStruct((2 * windows + 1, LANES), jnp.int32)
    square = jax.ShapeDtypeStruct((LANES, LANES), jnp.int32)
    even_map, odd_map, first, source, target, row_w, col_w = pl.pallas_call(
        functools.partial(map_kernel, extent, sticks),
        out_shape=(
            square,
            square,
            jax.ShapeDtypeStruct((16, LANES), jnp.int32),
            window_list,
            window_list,
            longer_list,
            longer_list,
        ),
        in_specs=[hbm] * 2,
        scratch_shapes=[
            pltpu.VMEM(row.shape, jnp.int32),
            pltpu.VMEM(col.shape, jnp.int32),
            pltpu.SemaphoreType.DMA((2,)),
        ],
        compiler_params=params(14 * total_sticks / 1536),
        cost_estimate=cost(4e9, 1e5),
        name="stick_map",
    )(row, col)

    constants = jnp.asarray(tables(extent))
    weighted = pl.pallas_call(
        functools.partial(plane_kernel, planes),
        out_shape=jax.ShapeDtypeStruct((devices, block + 8, LANES), F32),
        in_specs=[smem] + [vmem] * 7 + [hbm] * 2,
        out_specs=vmem,
        scratch_shapes=[
            pltpu.VMEM((windows, 2 * padded_planes, LANES), F32),
            pltpu.VMEM((windows, 2 * padded_planes, LANES), F32),
            pltpu.VMEM((2 * windows + 1, padded_planes, LANES), F32),
            pltpu.VMEM((padded_planes * rows, LANES), F32),
            pltpu.VMEM((padded_planes * rows, LANES), F32),
            pltpu.VMEM(constants.shape, BF16),
            pltpu.VMEM(potential.shape, F32),
            pltpu.SemaphoreType.DMA((2,)),
        ],
        compiler_params=params(52),
        cost_estimate=cost(2e10, 1e7),
        name="planes",
    )(first, even_map, odd_map, source, target, row_w, col_w, received, constants, potential)

    own = pl.pallas_call(
        join_kernel,
        out_shape=jax.ShapeDtypeStruct((devices * block + 2 * sticks, LANES), F32),
        in_specs=[vmem] * 2,
        compiler_params=params(4),
        name="join",
    )(received, wave)
    joint = [own] + [lax.ppermute(own, "band", pairs(bands, m)) for m in range(1, bands)]
    band = lax.axis_index("band").astype(jnp.int32)
    norm = 1.0 / (total_sticks * padded)
    places = jnp.stack([band, me])
    outgoing = pl.pallas_call(
        functools.partial(inner_kernel, bands, volume, norm),
        out_shape=(jax.ShapeDtypeStruct((block + 8, LANES), F32),) * devices,
        in_specs=[smem] + [vmem] * (2 + bands),
        compiler_params=params(6 + 1.5 * bands),
        name="inner",
    )(places, kc, *joint, weighted)

    returned = [outgoing[0]]
    for k in range(1, devices):
        ring = [(d, (d + k) % devices) for d in range(devices)]
        returned.append(lax.ppermute(outgoing[k], "tg", ring))
    applied, subspace = pl.pallas_call(
        functools.partial(final_kernel, volume, devices),
        out_shape=(
            jax.ShapeDtypeStruct((sticks, 2, padded), F32),
            jax.ShapeDtypeStruct((2, 1, bands), F32),
        ),
        in_specs=[smem] + [vmem] * (6 + devices),
        scratch_shapes=[pltpu.VMEM((2 * total_planes, 2 * LANES), F32)],
        compiler_params=params(6 + 6 * total_planes / 192),
        name="planes_to_wave",
    )(me.reshape(1), lengths, *returned, kc, whi, wlo, shift_cos, shift_sin)
    return applied.reshape(1, sticks, 2, padded), subspace


def solution(mesh):
    in_specs = (P("band", "tg", None, None), P(), P(), P(), P(), P("tg", None, None))
    out_specs = (P("band", "tg", None, None), P(None, "band", None))
    body = functools.partial(shards, mesh.shape["band"], mesh.shape["tg"])
    return jax.shard_map(body, mesh=mesh, in_specs=in_specs, out_specs=out_specs, check_vma=False)
```

```python
import functools
import math

import jax
import jax.numpy as jnp
import ml_dtypes
import numpy as np
from jax import lax
from jax.experimental import pallas as pl
from jax.experimental.pallas import tpu as pltpu
from jax.sharding import PartitionSpec as P

RADIUS = 48
LANES = 128
F32 = jnp.float32
BF16 = jnp.bfloat16


def up8(n):
    return -(-n // 8) * 8


def split(x):
    hi = x.astype(BF16)
    return hi, (x - hi.astype(F32)).astype(BF16)


def dot3(a, b, dims=((1,), (0,))):
    def dot(x, y):
        return lax.dot_general(x, y, (dims, ((), ())), preferred_element_type=F32)

    return dot(a[0], b[0]) + (dot(a[0], b[1]) + dot(a[1], b[0]))


def trig(product, extent):
    n = product - extent * jnp.floor(product * (1.0 / extent) + 0.5)
    quarter = extent / 4.0
    unit = 2.0 * math.pi / extent

    def sine(m):
        u = m * unit
        v = u * u
        s = 1.0 / 6227020800.0
        for term in (-39916800.0, 362880.0, -5040.0, 120.0, -6.0, 1.0):
            s = s * v + 1.0 / term
        return u * s

    folded = jnp.where(
        jnp.abs(n) > quarter, jnp.where(n > 0, 2.0 * quarter, -2.0 * quarter) - n, n
    )
    return sine(quarter - jnp.abs(n)), sine(folded)


def pair(table):
    hi = table.astype(np.float32).astype(ml_dtypes.bfloat16)
    lo = (table - hi.astype(np.float64)).astype(ml_dtypes.bfloat16)
    return hi, lo


def row_blocks():
    even = -(-(RADIUS + 1) // 16) * 16
    odd = -(-RADIUS // 16) * 16
    return even, odd


@functools.cache
def tables(extent):
    half = extent // 2
    grid = np.arange(extent)
    freq = np.arange(2 * RADIUS + 1) - RADIUS

    def angles(f, g):
        a = 2.0 * np.pi * ((f[:, None] * g[None, :]) % extent) / extent
        return np.cos(a), np.sin(a)

    wide = 2 * LANES
    x_forward, x_back, forward, back = [], [], [], []
    for offset, rows in zip((0, 1), row_blocks()):
        cos, sin = angles(freq[offset::2], grid[:half])
        count = cos.shape[0]
        table = np.zeros((LANES, wide))
        table[:count, :half] = cos
        table[LANES // 2:LANES // 2 + count, :half] = -sin
        table[:count, LANES:LANES + half] = sin
        table[LANES // 2:LANES // 2 + count, LANES:LANES + half] = cos
        hi, lo = pair(table)
        x_forward.append(np.concatenate([hi, hi, lo], axis=0))
        hi, lo = pair(table.T.copy())
        x_back.append(
            np.concatenate(
                [np.concatenate([hi, lo], axis=1), np.concatenate([hi, np.zeros_like(lo)], axis=1)], axis=0
            )
        )
        parts = []
        for wave in (cos, sin):
            table = np.zeros((half, rows))
            table[:, :count] = wave.T
            hi, lo = pair(table)
            parts += [hi, hi, lo]
        forward.append(np.concatenate(parts, axis=1))
        table = np.zeros((2 * rows, half))
        table[:count] = cos
        table[rows:rows + count] = sin
        hi, lo = pair(table)
        back.append(np.concatenate([hi, hi, lo], axis=1))
    rows = [np.concatenate(x_forward, axis=1), np.concatenate(x_back, axis=1)]
    for table in forward + back:
        rows.append(np.pad(table, ((0, 0), (0, 2 * wide - table.shape[1]))))
    return np.concatenate(rows, axis=0)


def params(megabytes):
    return pltpu.CompilerParams(vmem_limit_bytes=int(min(megabytes, 56) * 2**20))


def fetch_all(sources, targets, sems):
    copies = [
        pltpu.make_async_copy(source, target, sems.at[i])
        for i, (source, target) in enumerate(zip(sources, targets))
    ]
    for copy in copies:
        copy.start()
    return copies


def cost(flops, nbytes):
    return pl.CostEstimate(flops=int(flops), bytes_accessed=int(nbytes), transcendentals=0)


def wave_kernel(
    extent, me_ref, length_hbm, row_hbm, col_hbm, plane_hbm, coef_hbm,
    out_ref, kc_ref, wave_ref, len_ref, whi_ref, wlo_ref, sc_ref, ss_ref,
    length_ref, row_ref, col_ref, plane_ref, coef_ref, sems,
):
    copies = fetch_all(
        (length_hbm, row_hbm, col_hbm, plane_hbm, coef_hbm),
        (length_ref, row_ref, col_ref, plane_ref, coef_ref),
        sems,
    )
    for copy in copies[:4]:
        copy.wait()
    devices = out_ref.shape[0]
    sticks, _, padded = coef_ref.shape
    padded_planes = plane_ref.shape[1] // devices
    me = me_ref[0]
    half = LANES // 2
    lead = (me * sticks) // LANES
    odd = (me * sticks) % LANES != 0

    def own(ref):
        first, second = ref[pl.ds(lead, 1), :], ref[pl.ds(lead + 1, 1), :]
        both = jnp.concatenate([first, second], axis=1)
        return jnp.where(odd, both[:, half:], both[:, :sticks])

    length_row = own(length_ref).astype(F32)
    at_row = own(row_ref)
    at_col = own(col_ref)
    at_row = jnp.where(at_row <= RADIUS, at_row, at_row - extent).astype(F32)
    at_col = jnp.where(at_col <= RADIUS, at_col, at_col - extent).astype(F32)
    square_row = at_row * at_row + at_col * at_col
    spare = jnp.ones((1, 2 * LANES - sticks), F32)
    aux = jnp.concatenate(
        [
            jnp.broadcast_to(jnp.concatenate([length_row, spare], axis=1), (LANES // 2, 2 * LANES)),
            jnp.broadcast_to(jnp.concatenate([square_row, spare], axis=1), (LANES // 2, 2 * LANES)),
        ],
        axis=0,
    )
    aux_col = jnp.transpose(aux)[:sticks]
    len_ref[...] = aux_col
    length = aux_col[:, 0:1]
    square = aux_col[:, LANES // 2:LANES // 2 + 1]
    middle = (length - 1.0) * 0.5
    position = lax.broadcasted_iota(jnp.int32, (sticks, padded), 1).astype(F32)
    total = plane_ref.shape[1]
    plane_row = jnp.broadcast_to(plane_ref[...].astype(F32), (LANES, total))
    plane_col = jnp.transpose(plane_row)[:, 0:1]
    real = (plane_col >= 0.0).astype(F32)
    plane_col = jnp.maximum(plane_col, 0.0)
    harmonic = lax.broadcasted_iota(jnp.int32, (total, padded), 1).astype(F32)
    cos, sin = trig(plane_col * harmonic, extent)
    cos, sin = cos * real, sin * real
    parts = []
    for d in range(devices):
        c = cos[d * padded_planes:(d + 1) * padded_planes]
        s = sin[d * padded_planes:(d + 1) * padded_planes]
        parts.append(jnp.concatenate([c, -s], axis=1))
        parts.append(jnp.concatenate([s, c], axis=1))
    table = split(jnp.concatenate(parts, axis=0))
    whi_ref[...] = table[0]
    wlo_ref[...] = table[1]
    shift_cos, shift_sin = trig(plane_col * ((length_row - 1.0) * 0.5), extent)
    sc_ref[...] = shift_cos
    ss_ref[...] = shift_sin
    copies[4].wait()
    kept = (position < length).astype(F32)
    kinetic = (square + (position - middle) * (position - middle)) * (1.0 / (RADIUS * RADIUS))
    wave = jnp.concatenate([coef_ref[:, 0, :] * kept, coef_ref[:, 1, :] * kept], axis=1)
    kc_ref[...] = wave * jnp.concatenate([kinetic, kinetic], axis=1)
    wave_ref[:sticks, :] = wave[:, :padded]
    wave_ref[sticks:, :] = wave[:, padded:]
    raw = dot3(table, split(wave), ((1,), (1,)))
    for d in range(devices):
        at = 2 * d * padded_planes
        re, im = raw[at:at + padded_planes], raw[at + padded_planes:at + 2 * padded_planes]
        c = shift_cos[d * padded_planes:(d + 1) * padded_planes]
        s = shift_sin[d * padded_planes:(d + 1) * padded_planes]
        along_re = re * c + im * s
        along_im = im * c - re * s
        out_ref[d, 0:padded_planes, :] = along_re[:, :LANES]
        out_ref[d, padded_planes:2 * padded_planes, :] = along_im[:, :LANES]
        out_ref[d, 2 * padded_planes:3 * padded_planes, :] = jnp.concatenate(
            [along_re[:, LANES:], along_im[:, LANES:]], axis=1
        )


def window_row(values, sticks):
    line = jnp.concatenate([values[i:i + 1] for i in range(values.shape[0])], axis=1)
    starts = range(0, line.shape[1], sticks)
    parts = [line[:, at:at + LANES] for at in starts]
    parts += [line[:, at + LANES:at + sticks] for at in starts]
    return jnp.concatenate(parts, axis=1)


def map_kernel(
    extent, sticks, in_row_hbm, in_col_hbm,
    even_ref, odd_ref, first_ref, src_ref, dst_ref, row_ref, col_ref,
    in_row_ref, in_col_ref, sems,
):
    for copy in fetch_all((in_row_hbm, in_col_hbm), (in_row_ref, in_col_ref), sems):
        copy.wait()
    windows = src_ref.shape[0]
    total = windows * LANES

    def signed(ref):
        value = ref[...]
        return window_row(jnp.where(value <= RADIUS, value, value - extent) + RADIUS, sticks)

    def dot(x, y, dims=((1,), (0,))):
        return lax.dot_general(x, y, (dims, ((), ())), preferred_element_type=F32)

    def bits(condition):
        return condition.astype(F32).astype(BF16)

    nt = ((1,), (1,))
    own_row, own_col = signed(in_row_ref), signed(in_col_ref)
    half = LANES // 2
    own_row = (own_row & 1) * row_blocks()[0] + (own_row >> 1)
    own_col = (own_col & 1) * half + (own_col >> 1)
    tall = lax.broadcasted_iota(jnp.int32, (LANES, total), 0)
    place = lax.broadcasted_iota(jnp.int32, (LANES, total), 1)
    in_col = tall == own_col
    row_hot, col_hot = bits(tall == own_row), bits(in_col)
    down = lax.broadcasted_iota(jnp.int32, (LANES, LANES), 0)
    across = lax.broadcasted_iota(jnp.int32, (LANES, LANES), 1)
    before = bits(down < across)
    after = bits(down > across)
    upto = bits(down >= across)
    ones = jnp.ones((LANES, LANES), BF16)
    taken = dot(row_hot, col_hot, nt)
    taken_t = dot(col_hot, row_hot, nt)
    taken_b, taken_tb = taken.astype(BF16), taken_t.astype(BF16)
    start = dot(dot(after, taken_b).astype(BF16), ones)
    end = start + dot(taken_b, ones)
    start_t = dot(ones, dot(taken_tb, before).astype(BF16))
    left = across < half
    standing = dot(taken_b, before) + start
    low_ones = bits(down < half)
    high_start = start + dot(taken_b, low_ones)
    ones_t = bits(across < half)
    high_start_t = start_t + dot(ones_t, taken_tb)
    limit = 2.0 * windows - 1.0

    def first_window(value):
        return jnp.minimum(jnp.floor(value * (1.0 / half)), limit)

    for ref, begin in ((even_ref, start), (odd_ref, high_start)):
        code = jnp.where(taken > 0.5, standing - half * first_window(begin), -1.0)
        turned = pltpu.roll(code, half, 1)
        both = jnp.where(left, code, turned) if ref is even_ref else jnp.where(left, turned, code)
        ref[...] = both.astype(jnp.int32)
    first_ref[...] = jnp.concatenate(
        [first_window(start_t[0:8]), first_window(high_start_t[0:8])], axis=0
    ).astype(jnp.int32)

    spot = place.astype(F32)
    in_range = (spot >= start[:, 0:1]) & (spot < end[:, 0:1])
    sorted_hot = bits(in_range)
    sorted_row = jnp.sum(jnp.where(in_range, tall, 0).astype(F32), axis=0, keepdims=True)
    sorted_rank = spot[0:1] - jnp.sum(jnp.where(in_range, start[:, 0:1], 0.0), axis=0, keepdims=True)
    counts = dot(dot(upto, taken_tb).astype(BF16), sorted_hot)
    sorted_col = jnp.sum((counts <= sorted_rank).astype(F32), axis=0, keepdims=True)
    names = place + 1
    name_hi = dot(jnp.where(in_col, names >> 6, 0).astype(F32).astype(BF16), row_hot, nt)
    name_lo = dot(jnp.where(in_col, names & 63, 0).astype(F32).astype(BF16), row_hot, nt)
    named = dot(name_hi.astype(BF16), sorted_hot) * 64.0 + dot(name_lo.astype(BF16), sorted_hot)
    source = jnp.sum(jnp.where(tall.astype(F32) == sorted_col, named, 0.0), axis=0, keepdims=True) - 1.0
    place_t = dot(after, taken_tb) + start_t
    place_hi = jnp.floor(place_t * (1.0 / 64.0))
    place_lo = place_t - 64.0 * place_hi
    placed = dot(place_hi.astype(BF16), row_hot) * 64.0 + dot(place_lo.astype(BF16), row_hot)
    target = jnp.sum(jnp.where(in_col, placed, 0.0), axis=0, keepdims=True)
    for values, ref in ((source, src_ref), (target, dst_ref)):
        values = values.astype(jnp.int32)
        for w in range(windows):
            ref[w:w + 1, :] = values[:, w * LANES:(w + 1) * LANES]
    is_left = left[0:8]
    shift = jnp.where(is_left, 0, half)
    sorted_col = sorted_col.astype(jnp.int32)
    sorted_key = sorted_row.astype(jnp.int32) * 2 + (sorted_col >> 6)
    sorted_col = sorted_col & (half - 1)
    for values, ref, add in ((sorted_key, row_ref, 0), (sorted_col, col_ref, shift)):
        for w in range(windows):
            line = jnp.broadcast_to(values[:, w * LANES:(w + 1) * LANES], (8, LANES))
            turned = pltpu.roll(line, half, 1)
            ref[2 * w:2 * w + 1, :] = (jnp.where(is_left, line, turned) + add)[0:1]
            ref[2 * w + 1:2 * w + 2, :] = (jnp.where(is_left, turned, line) + add)[0:1]
    row_ref[2 * windows:2 * windows + 1, :] = jnp.full((1, LANES), -1, jnp.int32)
    col_ref[2 * windows:2 * windows + 1, :] = jnp.zeros((1, LANES), jnp.int32)


def lane_take(x, index):
    return jnp.take_along_axis(x, index, axis=1, mode="promise_in_bounds")


def plane_kernel(
    planes, first_ref, even_ref, odd_ref, src_ref, dst_ref, row_ref, col_ref, recv_ref,
    *refs,
):
    table_hbm, pot_hbm, out_ref, x_ref, s_ref, t_ref, ge_ref, go_ref, table_ref, pot_ref, sems = refs
    devices = recv_ref.shape[0]
    padded_planes = recv_ref.shape[1] // 3
    windows = x_ref.shape[0]
    rows = ge_ref.shape[0] // padded_planes
    extent = pot_ref.shape[1]
    half = LANES // 2
    copies = fetch_all((table_hbm, pot_hbm), (table_ref, pot_ref), sems)

    low = lax.broadcasted_iota(jnp.int32, (padded_planes, LANES), 1) < half
    for d in range(devices):
        x_ref[d] = recv_ref[d, 0:2 * padded_planes, :]
    for e in range(devices // 2):
        first = recv_ref[2 * e, 2 * padded_planes:3 * padded_planes, :]
        second = recv_ref[2 * e + 1, 2 * padded_planes:3 * padded_planes, :]
        x_ref[devices + e, 0:padded_planes, :] = jnp.where(low, first, pltpu.roll(second, half, 1))
        x_ref[devices + e, padded_planes:2 * padded_planes, :] = jnp.where(
            low, pltpu.roll(first, half, 1), second
        )

    blocks = padded_planes // 8

    def reorder(order_ref, from_ref, to_ref):
        @pl.loop(0, windows, unroll=4)
        def _(v):
            order = jnp.broadcast_to(order_ref[pl.ds(v, 1), :], (8, LANES))
            index = order & (LANES - 1)
            window = order >> 7
            for j in range(2 * blocks):
                value = jnp.zeros((8, LANES), F32)
                for w in range(windows):
                    value = jnp.where(window == w, lane_take(from_ref[w, 8 * j:8 * j + 8, :], index), value)
                to_ref[v, 8 * j:8 * j + 8, :] = value

    reorder(src_ref, x_ref, s_ref)
    for w in range(windows):
        re, im = s_ref[w, 0:padded_planes, :], s_ref[w, padded_planes:2 * padded_planes, :]
        t_ref[2 * w] = jnp.where(low, re, pltpu.roll(im, half, 1))
        t_ref[2 * w + 1] = jnp.where(low, pltpu.roll(re, half, 1), im)

    left = low[0:8]
    upper_lanes = jnp.where(left, 0, half)
    sides = ((0, even_ref, ge_ref), (1, odd_ref, go_ref))
    even_rows, odd_rows = row_blocks()
    used = up8(RADIUS + 1)
    for p in range(planes):
        for at in range(p * rows + used, p * rows + even_rows, 8):
            ge_ref[at:at + 8, :] = jnp.zeros((8, LANES), F32)
            go_ref[at:at + 8, :] = jnp.zeros((8, LANES), F32)

    def each_row(body):
        pl.loop(0, used, unroll=8)(body)
        pl.loop(even_rows, rows, unroll=8)(body)

    @each_row
    def _(r):
        for side, code_ref, grid_ref in sides:
            first = first_ref[8 * side, r]
            code = jnp.broadcast_to(code_ref[pl.ds(r, 1), :], (8, LANES))
            index = (code & (half - 1)) + upper_lanes
            window = code >> 6
            for j in range(blocks):
                lead = lane_take(t_ref[first, 8 * j:8 * j + 8, :], index)
                trail = lane_take(t_ref[first + 1, 8 * j:8 * j + 8, :], index)
                value = jnp.where(window == 0, lead, jnp.where(window == 1, trail, 0.0))
                grid_ref[pl.ds(r + 8 * j * rows, 8, stride=rows), :] = value

    for copy in copies:
        copy.wait()
    folded = extent // 2
    group = next(g for g in (12, 8, 6, 4, 2) if planes % g == 0)
    wide = 2 * LANES
    at_back = 3 * LANES
    at_y = at_back + 2 * wide
    at_even = at_y + 2 * folded
    at_odd = at_even + 2 * even_rows
    x_forward = (table_ref[0:at_back, :wide], table_ref[0:at_back, wide:])
    x_back = (table_ref[at_back:at_y, :wide], table_ref[at_back:at_y, wide:])
    y_even = table_ref[at_y:at_y + folded, :6 * even_rows]
    y_odd = table_ref[at_y + folded:at_even, :6 * odd_rows]
    back_even = table_ref[at_even:at_odd, :3 * folded]
    back_odd = table_ref[at_odd:at_odd + 2 * odd_rows, :3 * folded]

    def dot(x, y):
        return jnp.dot(x, y, preferred_element_type=F32)

    def stack(x, axis):
        hi, lo = split(x)
        return jnp.concatenate([hi, lo, hi], axis=axis)

    def turn(x):
        lane = lax.broadcasted_iota(jnp.int32, (x.shape[0], LANES), 1) < half
        parts = []
        for at in range(0, x.shape[1], LANES):
            rolled = pltpu.roll(x[:, at:at + LANES], half, 1)
            parts.append(jnp.where(lane, -rolled, rolled))
        return jnp.concatenate(parts, axis=1)

    @pl.loop(0, planes // group)
    def _(step):
        lines = []
        for t in range(group):
            base = pl.multiple_of((step * group + t) * rows, 16)
            parts = []
            for at, size, table in ((0, even_rows, y_even), (even_rows, odd_rows, y_odd)):
                pick = pl.ds(base + at, size)
                spectrum = jnp.concatenate([ge_ref[pick, :], go_ref[pick, :]], axis=1)
                both = jnp.concatenate([stack(spectrum, 0), stack(turn(spectrum), 0)], axis=0)
                parts.append(dot(table, both))
            lines.append(parts[0] + parts[1])
            lines.append(parts[0] - parts[1])
        lines = jnp.concatenate(lines, axis=0)
        field_even = dot(stack(lines[:, :LANES], 1), x_forward[0])
        field_odd = dot(stack(lines[:, LANES:], 1), x_forward[1])
        spare = jnp.zeros((extent, LANES - folded), F32)
        sums, differences = [], []
        for t in range(group):
            v = pot_ref[step * group + t]
            v_near = jnp.concatenate([v[:, :folded], spare], axis=1)
            v_far = jnp.concatenate([v[:, folded:], spare], axis=1)
            even = field_even[t * extent:(t + 1) * extent]
            odd = field_odd[t * extent:(t + 1) * extent]
            near = (even + odd) * jnp.concatenate([v_near, v_near], axis=1)
            far = (even - odd) * jnp.concatenate([v_far, v_far], axis=1)
            sums.append(near + far)
            differences.append(near - far)
        back = []
        for weighted, table in ((sums, x_back[0]), (differences, x_back[1])):
            both = dot(jnp.concatenate(split(jnp.concatenate(weighted, axis=0)), axis=1), table)
            back.append(both[:, :LANES] + both[:, LANES:])
        back = jnp.concatenate(back, axis=1)
        for t in range(group):
            base = pl.multiple_of((step * group + t) * rows, 16)
            upper = back[t * extent:t * extent + folded]
            lower = back[t * extent + folded:(t + 1) * extent]
            for at, size, table, value in (
                (0, even_rows, back_even, upper + lower), (even_rows, odd_rows, back_odd, upper - lower)
            ):
                both = dot(table, stack(value, 0))
                value = both[:size] - turn(both[size:])
                pick = pl.ds(base + at, size)
                ge_ref[pick, :] = value[:, :LANES]
                go_ref[pick, :] = value[:, LANES:]

    @each_row
    def _(r):
        for side, _, grid_ref in sides:
            first = first_ref[8 * side, r]
            values = [grid_ref[pl.ds(r + 8 * j * rows, 8, stride=rows), :] for j in range(blocks)]
            for t in range(2):
                index = jnp.broadcast_to(col_ref[pl.ds(first + t, 1), :], (8, LANES))
                hit = jnp.broadcast_to(row_ref[pl.ds(first + t, 1), :], (8, LANES)) == 2 * r + side
                for j in range(blocks):
                    pltpu.store(
                        t_ref.at[first + t, 8 * j:8 * j + 8, :], lane_take(values[j], index), mask=hit
                    )

    for w in range(windows):
        first, second = t_ref[2 * w], t_ref[2 * w + 1]
        s_ref[w, 0:padded_planes, :] = jnp.where(low, first, pltpu.roll(second, half, 1))
        s_ref[w, padded_planes:2 * padded_planes, :] = jnp.where(low, pltpu.roll(first, half, 1), second)
    reorder(dst_ref, s_ref, x_ref)
    for w in range(devices):
        out_ref[w, 0:2 * padded_planes, :] = x_ref[w]
    for e in range(devices // 2):
        re = x_ref[devices + e, 0:padded_planes, :]
        im = x_ref[devices + e, padded_planes:2 * padded_planes, :]
        out_ref[2 * e, 2 * padded_planes:3 * padded_planes, :] = jnp.where(
            low, re, pltpu.roll(im, half, 1)
        )
        out_ref[2 * e + 1, 2 * padded_planes:3 * padded_planes, :] = jnp.where(
            low, pltpu.roll(re, half, 1), im
        )
    for d in range(devices):
        out_ref[d, 3 * padded_planes:, :] = jnp.zeros((8, LANES), F32)


def inner_kernel(bands, volume, norm, place_ref, *refs):
    kc_ref = refs[0]
    waves = refs[1:1 + bands]
    fields = refs[1 + bands:1 + 2 * bands]
    in_ref = refs[1 + 2 * bands]
    out_refs = refs[2 + 2 * bands:]
    devices = in_ref.shape[0]
    padded_planes = (in_ref.shape[1] - 8) // 3
    half = LANES // 2
    sticks, padded = kc_ref.shape[0], kc_ref.shape[1] // 2
    me, mine = place_ref[0], place_ref[1]
    low = lax.broadcasted_iota(jnp.int32, (padded_planes, LANES), 1) < half

    def fold(x):
        rows = x.shape[0]
        total = x[0:8]
        for at in range(8, rows, 8):
            total = total + x[at:at + 8]
        return total

    kc = kc_ref[...]
    kc_re, kc_im = kc[:, :padded], kc[:, padded:]
    sums = []
    for m in range(bands):
        c_re, c_im = waves[m][:sticks, :], waves[m][sticks:, :]
        sums.append([fold(c_re * kc_re + c_im * kc_im), fold(c_re * kc_im - c_im * kc_re)])
    local = [[jnp.zeros((8, LANES), F32), jnp.zeros((8, LANES), F32)] for _ in range(bands)]
    for d in range(devices):
        value = in_ref[d, 0:3 * padded_planes, :]
        re, im, rest = value[:padded_planes], value[padded_planes:2 * padded_planes], value[2 * padded_planes:]
        turned = pltpu.roll(rest, half, 1)
        other = jnp.concatenate([im, -re, jnp.where(low, turned, -turned)], axis=0)
        for m in range(bands):
            col = fields[m][d, 0:3 * padded_planes, :]
            local[m][0] = local[m][0] + fold(col * value)
            local[m][1] = local[m][1] + fold(col * other)
    lane = lax.broadcasted_iota(jnp.int32, (8, LANES), 1)
    row = lax.broadcasted_iota(jnp.int32, (8, LANES), 0)
    tile = jnp.zeros((8, LANES), F32)
    for m in range(bands):
        spot = me ^ m
        for part, sign in ((0, 1.0), (1, -1.0)):
            partial = sums[m][part] + volume * local[m][part]
            scalar = jnp.sum(jnp.sum(partial, axis=1, keepdims=True), axis=0, keepdims=True)
            tile = jnp.where((lane == spot) & (row == part), sign * norm * scalar, tile)
    for k in range(devices):
        out_refs[k][0:3 * padded_planes, :] = in_ref[lax.rem(mine + k, devices), 0:3 * padded_planes, :]
        out_refs[k][3 * padded_planes:, :] = tile


def final_kernel(volume, devices, me_ref, len_ref, *refs):
    ret_refs = refs[:devices]
    kc_ref, whi_ref, wlo_ref, sc_ref, ss_ref, out_ref, sub_ref, stack_ref = refs[devices:]
    padded_planes = (ret_refs[0].shape[0] - 8) // 3
    sticks, _, padded = out_ref.shape
    half = LANES // 2
    bands = sub_ref.shape[2]
    total = jnp.zeros((8, LANES), F32)
    me = me_ref[0]
    for k in range(devices):
        value = ret_refs[k][...]
        base = pl.multiple_of(lax.rem(me + devices - k, devices) * padded_planes, 8)
        total = total + value[3 * padded_planes:]
        rest = value[2 * padded_planes:3 * padded_planes]
        re = jnp.concatenate([value[:padded_planes], rest[:, :half]], axis=1)
        im = jnp.concatenate([value[padded_planes:2 * padded_planes], rest[:, half:]], axis=1)
        c = sc_ref[pl.ds(base, padded_planes), :]
        s = ss_ref[pl.ds(base, padded_planes), :]
        stack_ref[pl.ds(2 * base, padded_planes), :sticks] = re * c - im * s
        stack_ref[pl.ds(2 * base + padded_planes, padded_planes), :sticks] = re * s + im * c
    turned = jnp.transpose(stack_ref[...])[:sticks]
    local = dot3(split(turned), (whi_ref[...], wlo_ref[...])) * volume
    position = lax.broadcasted_iota(jnp.int32, (sticks, padded), 1).astype(F32)
    kept = position < len_ref[:, 0:1]
    kc = kc_ref[...]
    out_ref[:, 0, :] = jnp.where(kept, kc[:, :padded] + local[:, :padded], 0.0)
    out_ref[:, 1, :] = jnp.where(kept, kc[:, padded:] + local[:, padded:], 0.0)
    sub_ref[:, 0, :] = total[0:2, :bands]


def pairs(count, k):
    return [(d, d ^ k) for d in range(count)]


def shards(bands, devices, coefficients, stick_col, stick_row, stick_length, plane_of_slot, potential):
    extent = plane_of_slot.shape[0]
    sticks = coefficients.shape[1]
    padded = coefficients.shape[3]
    total_sticks = stick_col.shape[0]
    planes = potential.shape[0]
    padded_planes = up8(planes)
    if sticks != LANES + LANES // 2 or devices % 2 or planes % 2 or bands & (bands - 1):
        raise ValueError("sizes")
    rows = sum(row_blocks())
    volume = 1.0 / (extent * extent * extent)
    me = lax.axis_index("tg").astype(jnp.int32)
    coef = coefficients.reshape(sticks, 2, padded)

    length, row, col = (v.reshape(-1, LANES) for v in (stick_length, stick_row, stick_col))
    slots = plane_of_slot.reshape(devices, planes)
    if padded_planes > planes:
        slots = jnp.pad(slots, ((0, 0), (0, padded_planes - planes)), constant_values=-1)
    slots = slots.reshape(1, devices * padded_planes)
    windows = total_sticks // LANES
    smem = pl.BlockSpec(memory_space=pltpu.SMEM)
    vmem = pl.BlockSpec(memory_space=pltpu.VMEM)
    hbm = pl.BlockSpec(memory_space=pltpu.HBM)

    block = 3 * padded_planes
    total_planes = devices * padded_planes
    sent, kc, wave, lengths, whi, wlo, shift_cos, shift_sin = pl.pallas_call(
        functools.partial(wave_kernel, extent),
        out_shape=(
            jax.ShapeDtypeStruct((devices, block, LANES), F32),
            jax.ShapeDtypeStruct((sticks, 2 * padded), F32),
            jax.ShapeDtypeStruct((2 * sticks, padded), F32),
            jax.ShapeDtypeStruct((sticks, LANES), F32),
            jax.ShapeDtypeStruct((2 * total_planes, 2 * padded), BF16),
            jax.ShapeDtypeStruct((2 * total_planes, 2 * padded), BF16),
            jax.ShapeDtypeStruct((total_planes, sticks), F32),
            jax.ShapeDtypeStruct((total_planes, sticks), F32),
        ),
        in_specs=[smem] + [hbm] * 5,
        scratch_shapes=[
            pltpu.VMEM(length.shape, jnp.int32),
            pltpu.VMEM(row.shape, jnp.int32),
            pltpu.VMEM(col.shape, jnp.int32),
            pltpu.VMEM(slots.shape, jnp.int32),
            pltpu.VMEM(coef.shape, F32),
            pltpu.SemaphoreType.DMA((5,)),
        ],
        compiler_params=params(56),
        name="wave_to_planes",
    )(me.reshape(1), length, row, col, slots, coef)

    received = lax.all_to_all(sent, "tg", split_axis=0, concat_axis=0, tiled=True)

    window_list = jax.ShapeDtypeStruct((windows, LANES), jnp.int32)
    longer_list = jax.ShapeDtypeStruct((2 * windows + 1, LANES), jnp.int32)
    square = jax.ShapeDtypeStruct((LANES, LANES), jnp.int32)
    even_map, odd_map, first, source, target, row_w, col_w = pl.pallas_call(
        functools.partial(map_kernel, extent, sticks),
        out_shape=(
            square,
            square,
            jax.ShapeDtypeStruct((16, LANES), jnp.int32),
            window_list,
            window_list,
            longer_list,
            longer_list,
        ),
        in_specs=[hbm] * 2,
        scratch_shapes=[
            pltpu.VMEM(row.shape, jnp.int32),
            pltpu.VMEM(col.shape, jnp.int32),
            pltpu.SemaphoreType.DMA((2,)),
        ],
        compiler_params=params(14 * total_sticks / 1536),
        cost_estimate=cost(4e9, 1e5),
        name="stick_map",
    )(row, col)

    constants = jnp.asarray(tables(extent))
    weighted = pl.pallas_call(
        functools.partial(plane_kernel, planes),
        out_shape=jax.ShapeDtypeStruct((devices, block + 8, LANES), F32),
        in_specs=[smem] + [vmem] * 7 + [hbm] * 2,
        out_specs=vmem,
        scratch_shapes=[
            pltpu.VMEM((windows, 2 * padded_planes, LANES), F32),
            pltpu.VMEM((windows, 2 * padded_planes, LANES), F32),
            pltpu.VMEM((2 * windows + 1, padded_planes, LANES), F32),
            pltpu.VMEM((padded_planes * rows, LANES), F32),
            pltpu.VMEM((padded_planes * rows, LANES), F32),
            pltpu.VMEM(constants.shape, BF16),
            pltpu.VMEM(potential.shape, F32),
            pltpu.SemaphoreType.DMA((2,)),
        ],
        compiler_params=params(52),
        cost_estimate=cost(2e10, 1e7),
        name="planes",
    )(first, even_map, odd_map, source, target, row_w, col_w, received, constants, potential)

    waves, fields = [wave], [received]
    for m in range(1, bands):
        waves.append(lax.ppermute(wave, "band", pairs(bands, m)))
        fields.append(lax.ppermute(received, "band", pairs(bands, m)))
    band = lax.axis_index("band").astype(jnp.int32)
    norm = 1.0 / (total_sticks * padded)
    places = jnp.stack([band, me])
    outgoing = pl.pallas_call(
        functools.partial(inner_kernel, bands, volume, norm),
        out_shape=(jax.ShapeDtypeStruct((block + 8, LANES), F32),) * devices,
        in_specs=[smem] + [vmem] * (2 + 2 * bands),
        compiler_params=params(6 + 1.5 * bands),
        name="inner",
    )(places, kc, *waves, *fields, weighted)

    returned = [outgoing[0]]
    for k in range(1, devices):
        ring = [(d, (d + k) % devices) for d in range(devices)]
        returned.append(lax.ppermute(outgoing[k], "tg", ring))
    applied, subspace = pl.pallas_call(
        functools.partial(final_kernel, volume, devices),
        out_shape=(
            jax.ShapeDtypeStruct((sticks, 2, padded), F32),
            jax.ShapeDtypeStruct((2, 1, bands), F32),
        ),
        in_specs=[smem] + [vmem] * (6 + devices),
        scratch_shapes=[pltpu.VMEM((2 * total_planes, 2 * LANES), F32)],
        compiler_params=params(6 + 6 * total_planes / 192),
        name="planes_to_wave",
    )(me.reshape(1), lengths, *returned, kc, whi, wlo, shift_cos, shift_sin)
    return applied.reshape(1, sticks, 2, padded), subspace


def solution(mesh):
    in_specs = (P("band", "tg", None, None), P(), P(), P(), P(), P("tg", None, None))
    out_specs = (P("band", "tg", None, None), P(None, "band", None))
    body = functools.partial(shards, mesh.shape["band"], mesh.shape["tg"])
    return jax.shard_map(body, mesh=mesh, in_specs=in_specs, out_specs=out_specs, check_vma=False)
```

```python
import functools
import math

import jax
import jax.numpy as jnp
import ml_dtypes
import numpy as np
from jax import lax
from jax.experimental import pallas as pl
from jax.experimental.pallas import tpu as pltpu
from jax.sharding import PartitionSpec as P

RADIUS = 48
LANES = 128
F32 = jnp.float32
BF16 = jnp.bfloat16


def up8(n):
    return -(-n // 8) * 8


def split(x):
    hi = x.astype(BF16)
    return hi, (x - hi.astype(F32)).astype(BF16)


def dot3(a, b, dims=((1,), (0,))):
    def dot(x, y):
        return lax.dot_general(x, y, (dims, ((), ())), preferred_element_type=F32)

    return dot(a[0], b[0]) + (dot(a[0], b[1]) + dot(a[1], b[0]))


def trig(product, extent):
    n = product - extent * jnp.floor(product * (1.0 / extent) + 0.5)
    quarter = extent / 4.0
    unit = 2.0 * math.pi / extent

    def sine(m):
        u = m * unit
        v = u * u
        s = 1.0 / 6227020800.0
        for term in (-39916800.0, 362880.0, -5040.0, 120.0, -6.0, 1.0):
            s = s * v + 1.0 / term
        return u * s

    folded = jnp.where(
        jnp.abs(n) > quarter, jnp.where(n > 0, 2.0 * quarter, -2.0 * quarter) - n, n
    )
    return sine(quarter - jnp.abs(n)), sine(folded)


def pair(table):
    hi = table.astype(np.float32).astype(ml_dtypes.bfloat16)
    lo = (table - hi.astype(np.float64)).astype(ml_dtypes.bfloat16)
    return hi, lo


def row_blocks():
    even = -(-(RADIUS + 1) // 16) * 16
    odd = -(-RADIUS // 16) * 16
    return even, odd


@functools.cache
def tables(extent):
    half = extent // 2
    grid = np.arange(extent)
    freq = np.arange(2 * RADIUS + 1) - RADIUS

    def angles(f, g):
        a = 2.0 * np.pi * ((f[:, None] * g[None, :]) % extent) / extent
        return np.cos(a), np.sin(a)

    wide = 2 * LANES
    x_forward, x_back, forward, back = [], [], [], []
    for offset, rows in zip((0, 1), row_blocks()):
        cos, sin = angles(freq[offset::2], grid[:half])
        count = cos.shape[0]
        table = np.zeros((LANES, wide))
        table[:count, :half] = cos
        table[LANES // 2:LANES // 2 + count, :half] = -sin
        table[:count, LANES:LANES + half] = sin
        table[LANES // 2:LANES // 2 + count, LANES:LANES + half] = cos
        hi, lo = pair(table)
        x_forward.append(np.concatenate([hi, hi, lo], axis=0))
        hi, lo = pair(table.T.copy())
        x_back.append(
            np.concatenate(
                [np.concatenate([hi, lo], axis=1), np.concatenate([hi, np.zeros_like(lo)], axis=1)], axis=0
            )
        )
        parts = []
        for wave in (cos, sin):
            table = np.zeros((half, rows))
            table[:, :count] = wave.T
            hi, lo = pair(table)
            parts += [hi, hi, lo]
        forward.append(np.concatenate(parts, axis=1))
        table = np.zeros((2 * rows, half))
        table[:count] = cos
        table[rows:rows + count] = sin
        hi, lo = pair(table)
        back.append(np.concatenate([hi, hi, lo], axis=1))
    rows = [np.concatenate(x_forward, axis=1), np.concatenate(x_back, axis=1)]
    for table in forward + back:
        rows.append(np.pad(table, ((0, 0), (0, 2 * wide - table.shape[1]))))
    return np.concatenate(rows, axis=0)


def params(megabytes):
    return pltpu.CompilerParams(vmem_limit_bytes=int(min(megabytes, 56) * 2**20))


def fetch_all(sources, targets, sems):
    copies = [
        pltpu.make_async_copy(source, target, sems.at[i])
        for i, (source, target) in enumerate(zip(sources, targets))
    ]
    for copy in copies:
        copy.start()
    return copies


def cost(flops, nbytes):
    return pl.CostEstimate(flops=int(flops), bytes_accessed=int(nbytes), transcendentals=0)


def wave_kernel(
    extent, me_ref, length_hbm, row_hbm, col_hbm, plane_hbm, coef_hbm,
    out_ref, kc_ref, wave_ref, len_ref, whi_ref, wlo_ref, sc_ref, ss_ref,
    length_ref, row_ref, col_ref, plane_ref, coef_ref, sems,
):
    copies = fetch_all(
        (length_hbm, row_hbm, col_hbm, plane_hbm, coef_hbm),
        (length_ref, row_ref, col_ref, plane_ref, coef_ref),
        sems,
    )
    for copy in copies[:4]:
        copy.wait()
    devices = out_ref.shape[0]
    sticks, _, padded = coef_ref.shape
    padded_planes = plane_ref.shape[1] // devices
    me = me_ref[0]
    half = LANES // 2
    lead = (me * sticks) // LANES
    odd = (me * sticks) % LANES != 0

    def own(ref):
        first, second = ref[pl.ds(lead, 1), :], ref[pl.ds(lead + 1, 1), :]
        both = jnp.concatenate([first, second], axis=1)
        return jnp.where(odd, both[:, half:], both[:, :sticks])

    length_row = own(length_ref).astype(F32)
    at_row = own(row_ref)
    at_col = own(col_ref)
    at_row = jnp.where(at_row <= RADIUS, at_row, at_row - extent).astype(F32)
    at_col = jnp.where(at_col <= RADIUS, at_col, at_col - extent).astype(F32)
    square_row = at_row * at_row + at_col * at_col
    spare = jnp.ones((1, 2 * LANES - sticks), F32)
    aux = jnp.concatenate(
        [
            jnp.broadcast_to(jnp.concatenate([length_row, spare], axis=1), (LANES // 2, 2 * LANES)),
            jnp.broadcast_to(jnp.concatenate([square_row, spare], axis=1), (LANES // 2, 2 * LANES)),
        ],
        axis=0,
    )
    aux_col = jnp.transpose(aux)[:sticks]
    len_ref[...] = aux_col
    length = aux_col[:, 0:1]
    square = aux_col[:, LANES // 2:LANES // 2 + 1]
    middle = (length - 1.0) * 0.5
    position = lax.broadcasted_iota(jnp.int32, (sticks, padded), 1).astype(F32)
    total = plane_ref.shape[1]
    plane_row = jnp.broadcast_to(plane_ref[...].astype(F32), (LANES, total))
    plane_col = jnp.transpose(plane_row)[:, 0:1]
    real = (plane_col >= 0.0).astype(F32)
    plane_col = jnp.maximum(plane_col, 0.0)
    harmonic = lax.broadcasted_iota(jnp.int32, (total, padded), 1).astype(F32)
    cos, sin = trig(plane_col * harmonic, extent)
    cos, sin = cos * real, sin * real
    parts = []
    for d in range(devices):
        c = cos[d * padded_planes:(d + 1) * padded_planes]
        s = sin[d * padded_planes:(d + 1) * padded_planes]
        parts.append(jnp.concatenate([c, -s], axis=1))
        parts.append(jnp.concatenate([s, c], axis=1))
    table = split(jnp.concatenate(parts, axis=0))
    whi_ref[...] = table[0]
    wlo_ref[...] = table[1]
    shift_cos, shift_sin = trig(plane_col * ((length_row - 1.0) * 0.5), extent)
    sc_ref[...] = shift_cos
    ss_ref[...] = shift_sin
    copies[4].wait()
    kept = (position < length).astype(F32)
    kinetic = (square + (position - middle) * (position - middle)) * (1.0 / (RADIUS * RADIUS))
    wave = jnp.concatenate([coef_ref[:, 0, :] * kept, coef_ref[:, 1, :] * kept], axis=1)
    kc_ref[...] = wave * jnp.concatenate([kinetic, kinetic], axis=1)
    wave_ref[:sticks, :] = wave[:, :padded]
    wave_ref[sticks:, :] = wave[:, padded:]
    raw = dot3(table, split(wave), ((1,), (1,)))
    for d in range(devices):
        at = 2 * d * padded_planes
        re, im = raw[at:at + padded_planes], raw[at + padded_planes:at + 2 * padded_planes]
        c = shift_cos[d * padded_planes:(d + 1) * padded_planes]
        s = shift_sin[d * padded_planes:(d + 1) * padded_planes]
        along_re = re * c + im * s
        along_im = im * c - re * s
        out_ref[d, 0:padded_planes, :] = along_re[:, :LANES]
        out_ref[d, padded_planes:2 * padded_planes, :] = along_im[:, :LANES]
        out_ref[d, 2 * padded_planes:3 * padded_planes, :] = jnp.concatenate(
            [along_re[:, LANES:], along_im[:, LANES:]], axis=1
        )


def window_row(values, sticks):
    line = jnp.concatenate([values[i:i + 1] for i in range(values.shape[0])], axis=1)
    starts = range(0, line.shape[1], sticks)
    parts = [line[:, at:at + LANES] for at in starts]
    parts += [line[:, at + LANES:at + sticks] for at in starts]
    return jnp.concatenate(parts, axis=1)


def map_kernel(
    extent, sticks, in_row_hbm, in_col_hbm,
    even_ref, odd_ref, first_ref, src_ref, dst_ref, row_ref, col_ref,
    in_row_ref, in_col_ref, sems,
):
    for copy in fetch_all((in_row_hbm, in_col_hbm), (in_row_ref, in_col_ref), sems):
        copy.wait()
    windows = src_ref.shape[0]
    total = windows * LANES

    def signed(ref):
        value = ref[...]
        return window_row(jnp.where(value <= RADIUS, value, value - extent) + RADIUS, sticks)

    def dot(x, y, dims=((1,), (0,))):
        return lax.dot_general(x, y, (dims, ((), ())), preferred_element_type=F32)

    def bits(condition):
        return condition.astype(F32).astype(BF16)

    nt = ((1,), (1,))
    own_row, own_col = signed(in_row_ref), signed(in_col_ref)
    half = LANES // 2
    own_row = (own_row & 1) * row_blocks()[0] + (own_row >> 1)
    own_col = (own_col & 1) * half + (own_col >> 1)
    tall = lax.broadcasted_iota(jnp.int32, (LANES, total), 0)
    place = lax.broadcasted_iota(jnp.int32, (LANES, total), 1)
    in_col = tall == own_col
    row_hot, col_hot = bits(tall == own_row), bits(in_col)
    down = lax.broadcasted_iota(jnp.int32, (LANES, LANES), 0)
    across = lax.broadcasted_iota(jnp.int32, (LANES, LANES), 1)
    before = bits(down < across)
    after = bits(down > across)
    upto = bits(down >= across)
    ones = jnp.ones((LANES, LANES), BF16)
    taken = dot(row_hot, col_hot, nt)
    taken_t = dot(col_hot, row_hot, nt)
    taken_b, taken_tb = taken.astype(BF16), taken_t.astype(BF16)
    start = dot(dot(after, taken_b).astype(BF16), ones)
    end = start + dot(taken_b, ones)
    start_t = dot(ones, dot(taken_tb, before).astype(BF16))
    left = across < half
    standing = dot(taken_b, before) + start
    low_ones = bits(down < half)
    high_start = start + dot(taken_b, low_ones)
    ones_t = bits(across < half)
    high_start_t = start_t + dot(ones_t, taken_tb)
    limit = 2.0 * windows - 1.0

    def first_window(value):
        return jnp.minimum(jnp.floor(value * (1.0 / half)), limit)

    for ref, begin in ((even_ref, start), (odd_ref, high_start)):
        code = jnp.where(taken > 0.5, standing - half * first_window(begin), -1.0)
        turned = pltpu.roll(code, half, 1)
        both = jnp.where(left, code, turned) if ref is even_ref else jnp.where(left, turned, code)
        ref[...] = both.astype(jnp.int32)
    first_ref[...] = jnp.concatenate(
        [first_window(start_t[0:8]), first_window(high_start_t[0:8])], axis=0
    ).astype(jnp.int32)

    spot = place.astype(F32)
    in_range = (spot >= start[:, 0:1]) & (spot < end[:, 0:1])
    sorted_hot = bits(in_range)
    sorted_row = jnp.sum(jnp.where(in_range, tall, 0).astype(F32), axis=0, keepdims=True)
    sorted_rank = spot[0:1] - jnp.sum(jnp.where(in_range, start[:, 0:1], 0.0), axis=0, keepdims=True)
    counts = dot(dot(upto, taken_tb).astype(BF16), sorted_hot)
    sorted_col = jnp.sum((counts <= sorted_rank).astype(F32), axis=0, keepdims=True)
    names = place + 1
    name_hi = dot(jnp.where(in_col, names >> 6, 0).astype(F32).astype(BF16), row_hot, nt)
    name_lo = dot(jnp.where(in_col, names & 63, 0).astype(F32).astype(BF16), row_hot, nt)
    named = dot(name_hi.astype(BF16), sorted_hot) * 64.0 + dot(name_lo.astype(BF16), sorted_hot)
    source = jnp.sum(jnp.where(tall.astype(F32) == sorted_col, named, 0.0), axis=0, keepdims=True) - 1.0
    place_t = dot(after, taken_tb) + start_t
    place_hi = jnp.floor(place_t * (1.0 / 64.0))
    place_lo = place_t - 64.0 * place_hi
    placed = dot(place_hi.astype(BF16), row_hot) * 64.0 + dot(place_lo.astype(BF16), row_hot)
    target = jnp.sum(jnp.where(in_col, placed, 0.0), axis=0, keepdims=True)
    for values, ref in ((source, src_ref), (target, dst_ref)):
        values = values.astype(jnp.int32)
        for w in range(windows):
            ref[w:w + 1, :] = values[:, w * LANES:(w + 1) * LANES]
    is_left = left[0:8]
    shift = jnp.where(is_left, 0, half)
    sorted_col = sorted_col.astype(jnp.int32)
    sorted_key = sorted_row.astype(jnp.int32) * 2 + (sorted_col >> 6)
    sorted_col = sorted_col & (half - 1)
    for values, ref, add in ((sorted_key, row_ref, 0), (sorted_col, col_ref, shift)):
        for w in range(windows):
            line = jnp.broadcast_to(values[:, w * LANES:(w + 1) * LANES], (8, LANES))
            turned = pltpu.roll(line, half, 1)
            ref[2 * w:2 * w + 1, :] = (jnp.where(is_left, line, turned) + add)[0:1]
            ref[2 * w + 1:2 * w + 2, :] = (jnp.where(is_left, turned, line) + add)[0:1]
    row_ref[2 * windows:2 * windows + 1, :] = jnp.full((1, LANES), -1, jnp.int32)
    col_ref[2 * windows:2 * windows + 1, :] = jnp.zeros((1, LANES), jnp.int32)


def lane_take(x, index):
    return jnp.take_along_axis(x, index, axis=1, mode="promise_in_bounds")


def plane_kernel(
    planes, first_ref, even_ref, odd_ref, src_ref, dst_ref, row_ref, col_ref, recv_ref,
    *refs,
):
    table_hbm, pot_hbm, out_ref, x_ref, s_ref, t_ref, ge_ref, go_ref, table_ref, pot_ref, sems = refs
    devices = recv_ref.shape[0]
    padded_planes = recv_ref.shape[1] // 3
    windows = x_ref.shape[0]
    rows = ge_ref.shape[0] // padded_planes
    extent = pot_ref.shape[1]
    half = LANES // 2
    copies = fetch_all((table_hbm, pot_hbm), (table_ref, pot_ref), sems)

    low = lax.broadcasted_iota(jnp.int32, (padded_planes, LANES), 1) < half
    for d in range(devices):
        x_ref[d] = recv_ref[d, 0:2 * padded_planes, :]
    for e in range(devices // 2):
        first = recv_ref[2 * e, 2 * padded_planes:3 * padded_planes, :]
        second = recv_ref[2 * e + 1, 2 * padded_planes:3 * padded_planes, :]
        x_ref[devices + e, 0:padded_planes, :] = jnp.where(low, first, pltpu.roll(second, half, 1))
        x_ref[devices + e, padded_planes:2 * padded_planes, :] = jnp.where(
            low, pltpu.roll(first, half, 1), second
        )

    blocks = padded_planes // 8

    def reorder(order_ref, from_ref, to_ref):
        @pl.loop(0, windows, unroll=4)
        def _(v):
            order = jnp.broadcast_to(order_ref[pl.ds(v, 1), :], (8, LANES))
            index = order & (LANES - 1)
            window = order >> 7
            for j in range(2 * blocks):
                value = jnp.zeros((8, LANES), F32)
                for w in range(windows):
                    value = jnp.where(window == w, lane_take(from_ref[w, 8 * j:8 * j + 8, :], index), value)
                to_ref[v, 8 * j:8 * j + 8, :] = value

    reorder(src_ref, x_ref, s_ref)
    for w in range(windows):
        re, im = s_ref[w, 0:padded_planes, :], s_ref[w, padded_planes:2 * padded_planes, :]
        t_ref[2 * w] = jnp.where(low, re, pltpu.roll(im, half, 1))
        t_ref[2 * w + 1] = jnp.where(low, pltpu.roll(re, half, 1), im)

    left = low[0:8]
    upper_lanes = jnp.where(left, 0, half)
    sides = ((0, even_ref, ge_ref), (1, odd_ref, go_ref))
    even_rows, odd_rows = row_blocks()
    used = up8(RADIUS + 1)
    for p in range(planes):
        for at in range(p * rows + used, p * rows + even_rows, 8):
            ge_ref[at:at + 8, :] = jnp.zeros((8, LANES), F32)
            go_ref[at:at + 8, :] = jnp.zeros((8, LANES), F32)

    def each_row(body):
        pl.loop(0, used, unroll=8)(body)
        pl.loop(even_rows, rows, unroll=8)(body)

    @each_row
    def _(r):
        for side, code_ref, grid_ref in sides:
            first = first_ref[8 * side, r]
            code = jnp.broadcast_to(code_ref[pl.ds(r, 1), :], (8, LANES))
            index = (code & (half - 1)) + upper_lanes
            window = code >> 6
            for j in range(blocks):
                lead = lane_take(t_ref[first, 8 * j:8 * j + 8, :], index)
                trail = lane_take(t_ref[first + 1, 8 * j:8 * j + 8, :], index)
                value = jnp.where(window == 0, lead, jnp.where(window == 1, trail, 0.0))
                grid_ref[pl.ds(r + 8 * j * rows, 8, stride=rows), :] = value

    for copy in copies:
        copy.wait()
    folded = extent // 2
    group = next(g for g in (24, 12, 8, 6, 4, 2) if planes % g == 0)
    wide = 2 * LANES
    at_back = 3 * LANES
    at_y = at_back + 2 * wide
    at_even = at_y + 2 * folded
    at_odd = at_even + 2 * even_rows
    x_forward = (table_ref[0:at_back, :wide], table_ref[0:at_back, wide:])
    x_back = (table_ref[at_back:at_y, :wide], table_ref[at_back:at_y, wide:])
    y_even = table_ref[at_y:at_y + folded, :6 * even_rows]
    y_odd = table_ref[at_y + folded:at_even, :6 * odd_rows]
    back_even = table_ref[at_even:at_odd, :3 * folded]
    back_odd = table_ref[at_odd:at_odd + 2 * odd_rows, :3 * folded]

    def dot(x, y):
        return jnp.dot(x, y, preferred_element_type=F32)

    def stack(x, axis):
        hi, lo = split(x)
        return jnp.concatenate([hi, lo, hi], axis=axis)

    def turn(x):
        lane = lax.broadcasted_iota(jnp.int32, (x.shape[0], LANES), 1) < half
        parts = []
        for at in range(0, x.shape[1], LANES):
            rolled = pltpu.roll(x[:, at:at + LANES], half, 1)
            parts.append(jnp.where(lane, -rolled, rolled))
        return jnp.concatenate(parts, axis=1)

    @pl.loop(0, planes // group)
    def _(step):
        lines = []
        for t in range(group):
            base = pl.multiple_of((step * group + t) * rows, 16)
            parts = []
            for at, size, table in ((0, even_rows, y_even), (even_rows, odd_rows, y_odd)):
                pick = pl.ds(base + at, size)
                spectrum = jnp.concatenate([ge_ref[pick, :], go_ref[pick, :]], axis=1)
                both = jnp.concatenate([stack(spectrum, 0), stack(turn(spectrum), 0)], axis=0)
                parts.append(dot(table, both))
            lines.append(parts[0] + parts[1])
            lines.append(parts[0] - parts[1])
        lines = jnp.concatenate(lines, axis=0)
        field_even = dot(stack(lines[:, :LANES], 1), x_forward[0])
        field_odd = dot(stack(lines[:, LANES:], 1), x_forward[1])
        spare = jnp.zeros((extent, LANES - folded), F32)
        sums, differences = [], []
        for t in range(group):
            v = pot_ref[step * group + t]
            v_near = jnp.concatenate([v[:, :folded], spare], axis=1)
            v_far = jnp.concatenate([v[:, folded:], spare], axis=1)
            even = field_even[t * extent:(t + 1) * extent]
            odd = field_odd[t * extent:(t + 1) * extent]
            near = (even + odd) * jnp.concatenate([v_near, v_near], axis=1)
            far = (even - odd) * jnp.concatenate([v_far, v_far], axis=1)
            sums.append(near + far)
            differences.append(near - far)
        back = []
        for weighted, table in ((sums, x_back[0]), (differences, x_back[1])):
            both = dot(jnp.concatenate(split(jnp.concatenate(weighted, axis=0)), axis=1), table)
            back.append(both[:, :LANES] + both[:, LANES:])
        back = jnp.concatenate(back, axis=1)
        for t in range(group):
            base = pl.multiple_of((step * group + t) * rows, 16)
            upper = back[t * extent:t * extent + folded]
            lower = back[t * extent + folded:(t + 1) * extent]
            for at, size, table, value in (
                (0, even_rows, back_even, upper + lower), (even_rows, odd_rows, back_odd, upper - lower)
            ):
                both = dot(table, stack(value, 0))
                value = both[:size] - turn(both[size:])
                pick = pl.ds(base + at, size)
                ge_ref[pick, :] = value[:, :LANES]
                go_ref[pick, :] = value[:, LANES:]

    @each_row
    def _(r):
        for side, _, grid_ref in sides:
            first = first_ref[8 * side, r]
            values = [grid_ref[pl.ds(r + 8 * j * rows, 8, stride=rows), :] for j in range(blocks)]
            for t in range(2):
                index = jnp.broadcast_to(col_ref[pl.ds(first + t, 1), :], (8, LANES))
                hit = jnp.broadcast_to(row_ref[pl.ds(first + t, 1), :], (8, LANES)) == 2 * r + side
                for j in range(blocks):
                    pltpu.store(
                        t_ref.at[first + t, 8 * j:8 * j + 8, :], lane_take(values[j], index), mask=hit
                    )

    for w in range(windows):
        first, second = t_ref[2 * w], t_ref[2 * w + 1]
        s_ref[w, 0:padded_planes, :] = jnp.where(low, first, pltpu.roll(second, half, 1))
        s_ref[w, padded_planes:2 * padded_planes, :] = jnp.where(low, pltpu.roll(first, half, 1), second)
    reorder(dst_ref, s_ref, x_ref)
    for w in range(devices):
        out_ref[w, 0:2 * padded_planes, :] = x_ref[w]
    for e in range(devices // 2):
        re = x_ref[devices + e, 0:padded_planes, :]
        im = x_ref[devices + e, padded_planes:2 * padded_planes, :]
        out_ref[2 * e, 2 * padded_planes:3 * padded_planes, :] = jnp.where(
            low, re, pltpu.roll(im, half, 1)
        )
        out_ref[2 * e + 1, 2 * padded_planes:3 * padded_planes, :] = jnp.where(
            low, pltpu.roll(re, half, 1), im
        )
    for d in range(devices):
        out_ref[d, 3 * padded_planes:, :] = jnp.zeros((8, LANES), F32)


def inner_kernel(bands, volume, norm, place_ref, *refs):
    kc_ref = refs[0]
    waves = refs[1:1 + bands]
    fields = refs[1 + bands:1 + 2 * bands]
    in_ref = refs[1 + 2 * bands]
    out_refs = refs[2 + 2 * bands:]
    devices = in_ref.shape[0]
    padded_planes = (in_ref.shape[1] - 8) // 3
    half = LANES // 2
    sticks, padded = kc_ref.shape[0], kc_ref.shape[1] // 2
    me, mine = place_ref[0], place_ref[1]
    low = lax.broadcasted_iota(jnp.int32, (padded_planes, LANES), 1) < half

    def fold(x):
        rows = x.shape[0]
        total = x[0:8]
        for at in range(8, rows, 8):
            total = total + x[at:at + 8]
        return total

    kc = kc_ref[...]
    kc_re, kc_im = kc[:, :padded], kc[:, padded:]
    sums = []
    for m in range(bands):
        c_re, c_im = waves[m][:sticks, :], waves[m][sticks:, :]
        sums.append([fold(c_re * kc_re + c_im * kc_im), fold(c_re * kc_im - c_im * kc_re)])
    local = [[jnp.zeros((8, LANES), F32), jnp.zeros((8, LANES), F32)] for _ in range(bands)]
    for d in range(devices):
        value = in_ref[d, 0:3 * padded_planes, :]
        re, im, rest = value[:padded_planes], value[padded_planes:2 * padded_planes], value[2 * padded_planes:]
        turned = pltpu.roll(rest, half, 1)
        other = jnp.concatenate([im, -re, jnp.where(low, turned, -turned)], axis=0)
        for m in range(bands):
            col = fields[m][d, 0:3 * padded_planes, :]
            local[m][0] = local[m][0] + fold(col * value)
            local[m][1] = local[m][1] + fold(col * other)
    lane = lax.broadcasted_iota(jnp.int32, (8, LANES), 1)
    row = lax.broadcasted_iota(jnp.int32, (8, LANES), 0)
    tile = jnp.zeros((8, LANES), F32)
    for m in range(bands):
        spot = me ^ m
        for part, sign in ((0, 1.0), (1, -1.0)):
            partial = sums[m][part] + volume * local[m][part]
            scalar = jnp.sum(jnp.sum(partial, axis=1, keepdims=True), axis=0, keepdims=True)
            tile = jnp.where((lane == spot) & (row == part), sign * norm * scalar, tile)
    for k in range(devices):
        out_refs[k][0:3 * padded_planes, :] = in_ref[partner(mine, k, devices, 1), 0:3 * padded_planes, :]
        out_refs[k][3 * padded_planes:, :] = tile


def final_kernel(volume, devices, me_ref, len_ref, *refs):
    ret_refs = refs[:devices]
    kc_ref, whi_ref, wlo_ref, sc_ref, ss_ref, out_ref, sub_ref, stack_ref = refs[devices:]
    padded_planes = (ret_refs[0].shape[0] - 8) // 3
    sticks, _, padded = out_ref.shape
    half = LANES // 2
    bands = sub_ref.shape[2]
    total = jnp.zeros((8, LANES), F32)
    me = me_ref[0]
    for k in range(devices):
        value = ret_refs[k][...]
        base = pl.multiple_of(partner(me, k, devices, -1) * padded_planes, 8)
        total = total + value[3 * padded_planes:]
        rest = value[2 * padded_planes:3 * padded_planes]
        re = jnp.concatenate([value[:padded_planes], rest[:, :half]], axis=1)
        im = jnp.concatenate([value[padded_planes:2 * padded_planes], rest[:, half:]], axis=1)
        c = sc_ref[pl.ds(base, padded_planes), :]
        s = ss_ref[pl.ds(base, padded_planes), :]
        stack_ref[pl.ds(2 * base, padded_planes), :sticks] = re * c - im * s
        stack_ref[pl.ds(2 * base + padded_planes, padded_planes), :sticks] = re * s + im * c
    turned = jnp.transpose(stack_ref[...])[:sticks]
    local = dot3(split(turned), (whi_ref[...], wlo_ref[...])) * volume
    position = lax.broadcasted_iota(jnp.int32, (sticks, padded), 1).astype(F32)
    kept = position < len_ref[:, 0:1]
    kc = kc_ref[...]
    out_ref[:, 0, :] = jnp.where(kept, kc[:, :padded] + local[:, :padded], 0.0)
    out_ref[:, 1, :] = jnp.where(kept, kc[:, padded:] + local[:, padded:], 0.0)
    sub_ref[:, 0, :] = total[0:2, :bands]


def partner(device, k, count, sign):
    half = count // 2
    return ((device >> 1) + half + sign * (k >> 1)) % half * 2 + ((device & 1) ^ (k & 1))


def pairs(count, k):
    return [(d, d ^ k) for d in range(count)]


def shards(bands, devices, coefficients, stick_col, stick_row, stick_length, plane_of_slot, potential):
    extent = plane_of_slot.shape[0]
    sticks = coefficients.shape[1]
    padded = coefficients.shape[3]
    total_sticks = stick_col.shape[0]
    planes = potential.shape[0]
    padded_planes = up8(planes)
    if sticks != LANES + LANES // 2 or devices % 2 or planes % 2 or bands & (bands - 1):
        raise ValueError("sizes")
    rows = sum(row_blocks())
    volume = 1.0 / (extent * extent * extent)
    me = lax.axis_index("tg").astype(jnp.int32)
    coef = coefficients.reshape(sticks, 2, padded)

    length, row, col = (v.reshape(-1, LANES) for v in (stick_length, stick_row, stick_col))
    slots = plane_of_slot.reshape(devices, planes)
    if padded_planes > planes:
        slots = jnp.pad(slots, ((0, 0), (0, padded_planes - planes)), constant_values=-1)
    slots = slots.reshape(1, devices * padded_planes)
    windows = total_sticks // LANES
    smem = pl.BlockSpec(memory_space=pltpu.SMEM)
    vmem = pl.BlockSpec(memory_space=pltpu.VMEM)
    hbm = pl.BlockSpec(memory_space=pltpu.HBM)

    block = 3 * padded_planes
    total_planes = devices * padded_planes
    sent, kc, wave, lengths, whi, wlo, shift_cos, shift_sin = pl.pallas_call(
        functools.partial(wave_kernel, extent),
        out_shape=(
            jax.ShapeDtypeStruct((devices, block, LANES), F32),
            jax.ShapeDtypeStruct((sticks, 2 * padded), F32),
            jax.ShapeDtypeStruct((2 * sticks, padded), F32),
            jax.ShapeDtypeStruct((sticks, LANES), F32),
            jax.ShapeDtypeStruct((2 * total_planes, 2 * padded), BF16),
            jax.ShapeDtypeStruct((2 * total_planes, 2 * padded), BF16),
            jax.ShapeDtypeStruct((total_planes, sticks), F32),
            jax.ShapeDtypeStruct((total_planes, sticks), F32),
        ),
        in_specs=[smem] + [hbm] * 5,
        scratch_shapes=[
            pltpu.VMEM(length.shape, jnp.int32),
            pltpu.VMEM(row.shape, jnp.int32),
            pltpu.VMEM(col.shape, jnp.int32),
            pltpu.VMEM(slots.shape, jnp.int32),
            pltpu.VMEM(coef.shape, F32),
            pltpu.SemaphoreType.DMA((5,)),
        ],
        compiler_params=params(56),
        name="wave_to_planes",
    )(me.reshape(1), length, row, col, slots, coef)

    received = lax.all_to_all(sent, "tg", split_axis=0, concat_axis=0, tiled=True)

    window_list = jax.ShapeDtypeStruct((windows, LANES), jnp.int32)
    longer_list = jax.ShapeDtypeStruct((2 * windows + 1, LANES), jnp.int32)
    square = jax.ShapeDtypeStruct((LANES, LANES), jnp.int32)
    even_map, odd_map, first, source, target, row_w, col_w = pl.pallas_call(
        functools.partial(map_kernel, extent, sticks),
        out_shape=(
            square,
            square,
            jax.ShapeDtypeStruct((16, LANES), jnp.int32),
            window_list,
            window_list,
            longer_list,
            longer_list,
        ),
        in_specs=[hbm] * 2,
        scratch_shapes=[
            pltpu.VMEM(row.shape, jnp.int32),
            pltpu.VMEM(col.shape, jnp.int32),
            pltpu.SemaphoreType.DMA((2,)),
        ],
        compiler_params=params(14 * total_sticks / 1536),
        cost_estimate=cost(4e9, 1e5),
        name="stick_map",
    )(row, col)

    constants = jnp.asarray(tables(extent))
    weighted = pl.pallas_call(
        functools.partial(plane_kernel, planes),
        out_shape=jax.ShapeDtypeStruct((devices, block + 8, LANES), F32),
        in_specs=[smem] + [vmem] * 7 + [hbm] * 2,
        out_specs=vmem,
        scratch_shapes=[
            pltpu.VMEM((windows, 2 * padded_planes, LANES), F32),
            pltpu.VMEM((windows, 2 * padded_planes, LANES), F32),
            pltpu.VMEM((2 * windows + 1, padded_planes, LANES), F32),
            pltpu.VMEM((padded_planes * rows, LANES), F32),
            pltpu.VMEM((padded_planes * rows, LANES), F32),
            pltpu.VMEM(constants.shape, BF16),
            pltpu.VMEM(potential.shape, F32),
            pltpu.SemaphoreType.DMA((2,)),
        ],
        compiler_params=params(52),
        cost_estimate=cost(2e10, 1e7),
        name="planes",
    )(first, even_map, odd_map, source, target, row_w, col_w, received, constants, potential)

    waves, fields = [wave], [received]
    for m in range(1, bands):
        waves.append(lax.ppermute(wave, "band", pairs(bands, m)))
        fields.append(lax.ppermute(received, "band", pairs(bands, m)))
    band = lax.axis_index("band").astype(jnp.int32)
    norm = 1.0 / (total_sticks * padded)
    places = jnp.stack([band, me])
    outgoing = pl.pallas_call(
        functools.partial(inner_kernel, bands, volume, norm),
        out_shape=(jax.ShapeDtypeStruct((block + 8, LANES), F32),) * devices,
        in_specs=[smem] + [vmem] * (2 + 2 * bands),
        compiler_params=params(6 + 1.5 * bands),
        name="inner",
    )(places, kc, *waves, *fields, weighted)

    returned = [outgoing[0]]
    for k in range(1, devices):
        steps = [(d, partner(d, k, devices, 1)) for d in range(devices)]
        returned.append(lax.ppermute(outgoing[k], "tg", steps))
    applied, subspace = pl.pallas_call(
        functools.partial(final_kernel, volume, devices),
        out_shape=(
            jax.ShapeDtypeStruct((sticks, 2, padded), F32),
            jax.ShapeDtypeStruct((2, 1, bands), F32),
        ),
        in_specs=[smem] + [vmem] * (6 + devices),
        scratch_shapes=[pltpu.VMEM((2 * total_planes, 2 * LANES), F32)],
        compiler_params=params(6 + 6 * total_planes / 192),
        name="planes_to_wave",
    )(me.reshape(1), lengths, *returned, kc, whi, wlo, shift_cos, shift_sin)
    return applied.reshape(1, sticks, 2, padded), subspace


def solution(mesh):
    in_specs = (P("band", "tg", None, None), P(), P(), P(), P(), P("tg", None, None))
    out_specs = (P("band", "tg", None, None), P(None, "band", None))
    body = functools.partial(shards, mesh.shape["band"], mesh.shape["tg"])
    return jax.shard_map(body, mesh=mesh, in_specs=in_specs, out_specs=out_specs, check_vma=False)
```

```python
import functools
import math

import jax
import jax.numpy as jnp
import ml_dtypes
import numpy as np
from jax import lax
from jax.experimental import pallas as pl
from jax.experimental.pallas import tpu as pltpu
from jax.sharding import PartitionSpec as P

RADIUS = 48
LANES = 128
F32 = jnp.float32
BF16 = jnp.bfloat16


def up8(n):
    return -(-n // 8) * 8


def split(x):
    hi = x.astype(BF16)
    return hi, (x - hi.astype(F32)).astype(BF16)


def dot3(a, b, dims=((1,), (0,))):
    def dot(x, y):
        return lax.dot_general(x, y, (dims, ((), ())), preferred_element_type=F32)

    return dot(a[0], b[0]) + (dot(a[0], b[1]) + dot(a[1], b[0]))


def trig(product, extent):
    n = product - extent * jnp.floor(product * (1.0 / extent) + 0.5)
    quarter = extent / 4.0
    unit = 2.0 * math.pi / extent

    def sine(m):
        u = m * unit
        v = u * u
        s = 1.0 / 6227020800.0
        for term in (-39916800.0, 362880.0, -5040.0, 120.0, -6.0, 1.0):
            s = s * v + 1.0 / term
        return u * s

    folded = jnp.where(
        jnp.abs(n) > quarter, jnp.where(n > 0, 2.0 * quarter, -2.0 * quarter) - n, n
    )
    return sine(quarter - jnp.abs(n)), sine(folded)


def pair(table):
    hi = table.astype(np.float32).astype(ml_dtypes.bfloat16)
    lo = (table - hi.astype(np.float64)).astype(ml_dtypes.bfloat16)
    return hi, lo


def row_blocks():
    even = -(-(RADIUS + 1) // 16) * 16
    odd = -(-RADIUS // 16) * 16
    return even, odd


@functools.cache
def tables(extent):
    half = extent // 2
    grid = np.arange(extent)
    freq = np.arange(2 * RADIUS + 1) - RADIUS

    def angles(f, g):
        a = 2.0 * np.pi * ((f[:, None] * g[None, :]) % extent) / extent
        return np.cos(a), np.sin(a)

    wide = 2 * LANES
    x_forward, x_back, forward, back = [], [], [], []
    for offset, rows in zip((0, 1), row_blocks()):
        cos, sin = angles(freq[offset::2], grid[:half])
        count = cos.shape[0]
        table = np.zeros((LANES, wide))
        table[:count, :half] = cos
        table[LANES // 2:LANES // 2 + count, :half] = -sin
        table[:count, LANES:LANES + half] = sin
        table[LANES // 2:LANES // 2 + count, LANES:LANES + half] = cos
        hi, lo = pair(table)
        x_forward.append(np.concatenate([hi, hi, lo], axis=0))
        hi, lo = pair(table.T.copy())
        x_back.append(
            np.concatenate(
                [np.concatenate([hi, lo], axis=1), np.concatenate([hi, np.zeros_like(lo)], axis=1)], axis=0
            )
        )
        parts = []
        for wave in (cos, sin):
            table = np.zeros((half, rows))
            table[:, :count] = wave.T
            hi, lo = pair(table)
            parts += [hi, hi, lo]
        forward.append(np.concatenate(parts, axis=1))
        table = np.zeros((2 * rows, half))
        table[:count] = cos
        table[rows:rows + count] = sin
        hi, lo = pair(table)
        back.append(np.concatenate([hi, hi, lo], axis=1))
    rows = [np.concatenate(x_forward, axis=1), np.concatenate(x_back, axis=1)]
    for table in forward + back:
        rows.append(np.pad(table, ((0, 0), (0, 2 * wide - table.shape[1]))))
    return np.concatenate(rows, axis=0)


def params(megabytes):
    return pltpu.CompilerParams(vmem_limit_bytes=int(min(megabytes, 56) * 2**20))


def fetch_all(sources, targets, sems):
    copies = [
        pltpu.make_async_copy(source, target, sems.at[i])
        for i, (source, target) in enumerate(zip(sources, targets))
    ]
    for copy in copies:
        copy.start()
    return copies


def cost(flops, nbytes):
    return pl.CostEstimate(flops=int(flops), bytes_accessed=int(nbytes), transcendentals=0)


def wave_kernel(
    extent, me_ref, length_hbm, row_hbm, col_hbm, plane_hbm, coef_hbm,
    out_ref, kc_ref, wave_ref, len_ref, whi_ref, wlo_ref, sc_ref, ss_ref,
    length_ref, row_ref, col_ref, plane_ref, coef_ref, sems,
):
    copies = fetch_all(
        (length_hbm, row_hbm, col_hbm, plane_hbm, coef_hbm),
        (length_ref, row_ref, col_ref, plane_ref, coef_ref),
        sems,
    )
    for copy in copies[:4]:
        copy.wait()
    devices = out_ref.shape[0]
    sticks, _, padded = coef_ref.shape
    padded_planes = plane_ref.shape[1] // devices
    me = me_ref[0]
    half = LANES // 2
    lead = (me * sticks) // LANES
    odd = (me * sticks) % LANES != 0

    def own(ref):
        first, second = ref[pl.ds(lead, 1), :], ref[pl.ds(lead + 1, 1), :]
        both = jnp.concatenate([first, second], axis=1)
        return jnp.where(odd, both[:, half:], both[:, :sticks])

    length_row = own(length_ref).astype(F32)
    at_row = own(row_ref)
    at_col = own(col_ref)
    at_row = jnp.where(at_row <= RADIUS, at_row, at_row - extent).astype(F32)
    at_col = jnp.where(at_col <= RADIUS, at_col, at_col - extent).astype(F32)
    square_row = at_row * at_row + at_col * at_col
    spare = jnp.ones((1, 2 * LANES - sticks), F32)
    aux = jnp.concatenate(
        [
            jnp.broadcast_to(jnp.concatenate([length_row, spare], axis=1), (LANES // 2, 2 * LANES)),
            jnp.broadcast_to(jnp.concatenate([square_row, spare], axis=1), (LANES // 2, 2 * LANES)),
        ],
        axis=0,
    )
    aux_col = jnp.transpose(aux)[:sticks]
    len_ref[...] = aux_col
    length = aux_col[:, 0:1]
    square = aux_col[:, LANES // 2:LANES // 2 + 1]
    middle = (length - 1.0) * 0.5
    position = lax.broadcasted_iota(jnp.int32, (sticks, padded), 1).astype(F32)
    total = plane_ref.shape[1]
    plane_row = jnp.broadcast_to(plane_ref[...].astype(F32), (LANES, total))
    plane_col = jnp.transpose(plane_row)[:, 0:1]
    real = (plane_col >= 0.0).astype(F32)
    plane_col = jnp.maximum(plane_col, 0.0)
    harmonic = lax.broadcasted_iota(jnp.int32, (total, padded), 1).astype(F32)
    cos, sin = trig(plane_col * harmonic, extent)
    cos, sin = cos * real, sin * real
    parts = []
    for d in range(devices):
        c = cos[d * padded_planes:(d + 1) * padded_planes]
        s = sin[d * padded_planes:(d + 1) * padded_planes]
        parts.append(jnp.concatenate([c, -s], axis=1))
        parts.append(jnp.concatenate([s, c], axis=1))
    table = split(jnp.concatenate(parts, axis=0))
    whi_ref[...] = table[0]
    wlo_ref[...] = table[1]
    shift_cos, shift_sin = trig(plane_col * ((length_row - 1.0) * 0.5), extent)
    sc_ref[...] = shift_cos
    ss_ref[...] = shift_sin
    copies[4].wait()
    kept = (position < length).astype(F32)
    kinetic = (square + (position - middle) * (position - middle)) * (1.0 / (RADIUS * RADIUS))
    wave = jnp.concatenate([coef_ref[:, 0, :] * kept, coef_ref[:, 1, :] * kept], axis=1)
    kc_ref[...] = wave * jnp.concatenate([kinetic, kinetic], axis=1)
    wave_ref[:sticks, :] = wave[:, :padded]
    wave_ref[sticks:, :] = wave[:, padded:]
    raw = dot3(table, split(wave), ((1,), (1,)))
    for d in range(devices):
        at = 2 * d * padded_planes
        re, im = raw[at:at + padded_planes], raw[at + padded_planes:at + 2 * padded_planes]
        c = shift_cos[d * padded_planes:(d + 1) * padded_planes]
        s = shift_sin[d * padded_planes:(d + 1) * padded_planes]
        along_re = re * c + im * s
        along_im = im * c - re * s
        out_ref[d, 0:padded_planes, :] = along_re[:, :LANES]
        out_ref[d, padded_planes:2 * padded_planes, :] = along_im[:, :LANES]
        out_ref[d, 2 * padded_planes:3 * padded_planes, :] = jnp.concatenate(
            [along_re[:, LANES:], along_im[:, LANES:]], axis=1
        )


def window_row(values, sticks):
    line = jnp.concatenate([values[i:i + 1] for i in range(values.shape[0])], axis=1)
    starts = range(0, line.shape[1], sticks)
    parts = [line[:, at:at + LANES] for at in starts]
    parts += [line[:, at + LANES:at + sticks] for at in starts]
    return jnp.concatenate(parts, axis=1)


def map_kernel(
    extent, sticks, in_row_hbm, in_col_hbm,
    even_ref, odd_ref, first_ref, src_ref, dst_ref, row_ref, col_ref,
    in_row_ref, in_col_ref, sems,
):
    for copy in fetch_all((in_row_hbm, in_col_hbm), (in_row_ref, in_col_ref), sems):
        copy.wait()
    windows = src_ref.shape[0]
    total = windows * LANES

    def signed(ref):
        value = ref[...]
        return window_row(jnp.where(value <= RADIUS, value, value - extent) + RADIUS, sticks)

    def dot(x, y, dims=((1,), (0,))):
        return lax.dot_general(x, y, (dims, ((), ())), preferred_element_type=F32)

    def bits(condition):
        return condition.astype(F32).astype(BF16)

    nt = ((1,), (1,))
    own_row, own_col = signed(in_row_ref), signed(in_col_ref)
    half = LANES // 2
    own_row = (own_row & 1) * row_blocks()[0] + (own_row >> 1)
    own_col = (own_col & 1) * half + (own_col >> 1)
    tall = lax.broadcasted_iota(jnp.int32, (LANES, total), 0)
    place = lax.broadcasted_iota(jnp.int32, (LANES, total), 1)
    in_col = tall == own_col
    row_hot, col_hot = bits(tall == own_row), bits(in_col)
    down = lax.broadcasted_iota(jnp.int32, (LANES, LANES), 0)
    across = lax.broadcasted_iota(jnp.int32, (LANES, LANES), 1)
    before = bits(down < across)
    after = bits(down > across)
    upto = bits(down >= across)
    ones = jnp.ones((LANES, LANES), BF16)
    taken = dot(row_hot, col_hot, nt)
    taken_t = dot(col_hot, row_hot, nt)
    taken_b, taken_tb = taken.astype(BF16), taken_t.astype(BF16)
    start = dot(dot(after, taken_b).astype(BF16), ones)
    end = start + dot(taken_b, ones)
    start_t = dot(ones, dot(taken_tb, before).astype(BF16))
    left = across < half
    standing = dot(taken_b, before) + start
    low_ones = bits(down < half)
    high_start = start + dot(taken_b, low_ones)
    ones_t = bits(across < half)
    high_start_t = start_t + dot(ones_t, taken_tb)
    limit = 2.0 * windows - 1.0

    def first_window(value):
        return jnp.minimum(jnp.floor(value * (1.0 / half)), limit)

    for ref, begin in ((even_ref, start), (odd_ref, high_start)):
        code = jnp.where(taken > 0.5, standing - half * first_window(begin), -1.0)
        turned = pltpu.roll(code, half, 1)
        both = jnp.where(left, code, turned) if ref is even_ref else jnp.where(left, turned, code)
        ref[...] = both.astype(jnp.int32)
    first_ref[...] = jnp.concatenate(
        [first_window(start_t[0:8]), first_window(high_start_t[0:8])], axis=0
    ).astype(jnp.int32)

    spot = place.astype(F32)
    in_range = (spot >= start[:, 0:1]) & (spot < end[:, 0:1])
    sorted_hot = bits(in_range)
    sorted_row = jnp.sum(jnp.where(in_range, tall, 0).astype(F32), axis=0, keepdims=True)
    sorted_rank = spot[0:1] - jnp.sum(jnp.where(in_range, start[:, 0:1], 0.0), axis=0, keepdims=True)
    counts = dot(dot(upto, taken_tb).astype(BF16), sorted_hot)
    sorted_col = jnp.sum((counts <= sorted_rank).astype(F32), axis=0, keepdims=True)
    names = place + 1
    name_hi = dot(jnp.where(in_col, names >> 6, 0).astype(F32).astype(BF16), row_hot, nt)
    name_lo = dot(jnp.where(in_col, names & 63, 0).astype(F32).astype(BF16), row_hot, nt)
    named = dot(name_hi.astype(BF16), sorted_hot) * 64.0 + dot(name_lo.astype(BF16), sorted_hot)
    source = jnp.sum(jnp.where(tall.astype(F32) == sorted_col, named, 0.0), axis=0, keepdims=True) - 1.0
    place_t = dot(after, taken_tb) + start_t
    place_hi = jnp.floor(place_t * (1.0 / 64.0))
    place_lo = place_t - 64.0 * place_hi
    placed = dot(place_hi.astype(BF16), row_hot) * 64.0 + dot(place_lo.astype(BF16), row_hot)
    target = jnp.sum(jnp.where(in_col, placed, 0.0), axis=0, keepdims=True)
    for values, ref in ((source, src_ref), (target, dst_ref)):
        values = values.astype(jnp.int32)
        for w in range(windows):
            ref[w:w + 1, :] = values[:, w * LANES:(w + 1) * LANES]
    is_left = left[0:8]
    shift = jnp.where(is_left, 0, half)
    sorted_col = sorted_col.astype(jnp.int32)
    sorted_key = sorted_row.astype(jnp.int32) * 2 + (sorted_col >> 6)
    sorted_col = sorted_col & (half - 1)
    for values, ref, add in ((sorted_key, row_ref, 0), (sorted_col, col_ref, shift)):
        for w in range(windows):
            line = jnp.broadcast_to(values[:, w * LANES:(w + 1) * LANES], (8, LANES))
            turned = pltpu.roll(line, half, 1)
            ref[2 * w:2 * w + 1, :] = (jnp.where(is_left, line, turned) + add)[0:1]
            ref[2 * w + 1:2 * w + 2, :] = (jnp.where(is_left, turned, line) + add)[0:1]
    row_ref[2 * windows:2 * windows + 1, :] = jnp.full((1, LANES), -1, jnp.int32)
    col_ref[2 * windows:2 * windows + 1, :] = jnp.zeros((1, LANES), jnp.int32)


def lane_take(x, index):
    return jnp.take_along_axis(x, index, axis=1, mode="promise_in_bounds")


def plane_kernel(
    planes, first_ref, even_ref, odd_ref, src_ref, dst_ref, row_ref, col_ref, recv_ref,
    *refs,
):
    table_hbm, pot_hbm, out_ref, x_ref, s_ref, t_ref, ge_ref, go_ref, table_ref, pot_ref, sems = refs
    devices = recv_ref.shape[0]
    padded_planes = recv_ref.shape[1] // 3
    windows = x_ref.shape[0]
    rows = ge_ref.shape[0] // padded_planes
    extent = pot_ref.shape[1]
    half = LANES // 2
    copies = fetch_all((table_hbm, pot_hbm), (table_ref, pot_ref), sems)

    low = lax.broadcasted_iota(jnp.int32, (padded_planes, LANES), 1) < half
    for d in range(devices):
        x_ref[d] = recv_ref[d, 0:2 * padded_planes, :]
    for e in range(devices // 2):
        first = recv_ref[2 * e, 2 * padded_planes:3 * padded_planes, :]
        second = recv_ref[2 * e + 1, 2 * padded_planes:3 * padded_planes, :]
        x_ref[devices + e, 0:padded_planes, :] = jnp.where(low, first, pltpu.roll(second, half, 1))
        x_ref[devices + e, padded_planes:2 * padded_planes, :] = jnp.where(
            low, pltpu.roll(first, half, 1), second
        )

    blocks = padded_planes // 8

    def reorder(order_ref, from_ref, to_ref):
        @pl.loop(0, windows, unroll=4)
        def _(v):
            order = jnp.broadcast_to(order_ref[pl.ds(v, 1), :], (8, LANES))
            index = order & (LANES - 1)
            window = order >> 7
            for j in range(2 * blocks):
                value = jnp.zeros((8, LANES), F32)
                for w in range(windows):
                    value = jnp.where(window == w, lane_take(from_ref[w, 8 * j:8 * j + 8, :], index), value)
                to_ref[v, 8 * j:8 * j + 8, :] = value

    reorder(src_ref, x_ref, s_ref)
    for w in range(windows):
        re, im = s_ref[w, 0:padded_planes, :], s_ref[w, padded_planes:2 * padded_planes, :]
        t_ref[2 * w] = jnp.where(low, re, pltpu.roll(im, half, 1))
        t_ref[2 * w + 1] = jnp.where(low, pltpu.roll(re, half, 1), im)

    left = low[0:8]
    upper_lanes = jnp.where(left, 0, half)
    sides = ((0, even_ref, ge_ref), (1, odd_ref, go_ref))
    even_rows, odd_rows = row_blocks()
    used = up8(RADIUS + 1)
    for p in range(planes):
        for at in range(p * rows + used, p * rows + even_rows, 8):
            ge_ref[at:at + 8, :] = jnp.zeros((8, LANES), F32)
            go_ref[at:at + 8, :] = jnp.zeros((8, LANES), F32)

    def each_row(body):
        pl.loop(0, used, unroll=8)(body)
        pl.loop(even_rows, rows, unroll=8)(body)

    @each_row
    def _(r):
        for side, code_ref, grid_ref in sides:
            first = first_ref[8 * side, r]
            code = jnp.broadcast_to(code_ref[pl.ds(r, 1), :], (8, LANES))
            index = (code & (half - 1)) + upper_lanes
            window = code >> 6
            for j in range(blocks):
                lead = lane_take(t_ref[first, 8 * j:8 * j + 8, :], index)
                trail = lane_take(t_ref[first + 1, 8 * j:8 * j + 8, :], index)
                value = jnp.where(window == 0, lead, jnp.where(window == 1, trail, 0.0))
                grid_ref[pl.ds(r + 8 * j * rows, 8, stride=rows), :] = value

    for copy in copies:
        copy.wait()
    folded = extent // 2
    group = next(g for g in (24, 12, 8, 6, 4, 2) if planes % g == 0)
    wide = 2 * LANES
    at_back = 3 * LANES
    at_y = at_back + 2 * wide
    at_even = at_y + 2 * folded
    at_odd = at_even + 2 * even_rows
    x_forward = (table_ref[0:at_back, :wide], table_ref[0:at_back, wide:])
    x_back = (table_ref[at_back:at_y, :wide], table_ref[at_back:at_y, wide:])
    y_even = table_ref[at_y:at_y + folded, :6 * even_rows]
    y_odd = table_ref[at_y + folded:at_even, :6 * odd_rows]
    back_even = table_ref[at_even:at_odd, :3 * folded]
    back_odd = table_ref[at_odd:at_odd + 2 * odd_rows, :3 * folded]

    def dot(x, y):
        return jnp.dot(x, y, preferred_element_type=F32)

    def stack(x, axis):
        hi, lo = split(x)
        return jnp.concatenate([hi, lo, hi], axis=axis)

    def turn(x):
        lane = lax.broadcasted_iota(jnp.int32, (x.shape[0], LANES), 1) < half
        parts = []
        for at in range(0, x.shape[1], LANES):
            rolled = pltpu.roll(x[:, at:at + LANES], half, 1)
            parts.append(jnp.where(lane, -rolled, rolled))
        return jnp.concatenate(parts, axis=1)

    @pl.loop(0, planes // group)
    def _(step):
        lines = []
        for t in range(group):
            base = pl.multiple_of((step * group + t) * rows, 16)
            parts = []
            for at, size, table in ((0, even_rows, y_even), (even_rows, odd_rows, y_odd)):
                pick = pl.ds(base + at, size)
                spectrum = jnp.concatenate([ge_ref[pick, :], go_ref[pick, :]], axis=1)
                both = jnp.concatenate([stack(spectrum, 0), stack(turn(spectrum), 0)], axis=0)
                parts.append(dot(table, both))
            lines.append(parts[0] + parts[1])
            lines.append(parts[0] - parts[1])
        lines = jnp.concatenate(lines, axis=0)
        field_even = dot(stack(lines[:, :LANES], 1), x_forward[0])
        field_odd = dot(stack(lines[:, LANES:], 1), x_forward[1])
        spare = jnp.zeros((extent, LANES - folded), F32)
        sums, differences = [], []
        for t in range(group):
            v = pot_ref[step * group + t]
            v_near = jnp.concatenate([v[:, :folded], spare], axis=1)
            v_far = jnp.concatenate([v[:, folded:], spare], axis=1)
            even = field_even[t * extent:(t + 1) * extent]
            odd = field_odd[t * extent:(t + 1) * extent]
            near = (even + odd) * jnp.concatenate([v_near, v_near], axis=1)
            far = (even - odd) * jnp.concatenate([v_far, v_far], axis=1)
            sums.append(near + far)
            differences.append(near - far)
        back = []
        for weighted, table in ((sums, x_back[0]), (differences, x_back[1])):
            both = dot(jnp.concatenate(split(jnp.concatenate(weighted, axis=0)), axis=1), table)
            back.append(both[:, :LANES] + both[:, LANES:])
        back = jnp.concatenate(back, axis=1)
        for t in range(group):
            base = pl.multiple_of((step * group + t) * rows, 16)
            upper = back[t * extent:t * extent + folded]
            lower = back[t * extent + folded:(t + 1) * extent]
            for at, size, table, value in (
                (0, even_rows, back_even, upper + lower), (even_rows, odd_rows, back_odd, upper - lower)
            ):
                both = dot(table, stack(value, 0))
                value = both[:size] - turn(both[size:])
                pick = pl.ds(base + at, size)
                ge_ref[pick, :] = value[:, :LANES]
                go_ref[pick, :] = value[:, LANES:]

    @each_row
    def _(r):
        for side, _, grid_ref in sides:
            first = first_ref[8 * side, r]
            values = [grid_ref[pl.ds(r + 8 * j * rows, 8, stride=rows), :] for j in range(blocks)]
            for t in range(2):
                index = jnp.broadcast_to(col_ref[pl.ds(first + t, 1), :], (8, LANES))
                hit = jnp.broadcast_to(row_ref[pl.ds(first + t, 1), :], (8, LANES)) == 2 * r + side
                for j in range(blocks):
                    pltpu.store(
                        t_ref.at[first + t, 8 * j:8 * j + 8, :], lane_take(values[j], index), mask=hit
                    )

    for w in range(windows):
        first, second = t_ref[2 * w], t_ref[2 * w + 1]
        s_ref[w, 0:padded_planes, :] = jnp.where(low, first, pltpu.roll(second, half, 1))
        s_ref[w, padded_planes:2 * padded_planes, :] = jnp.where(low, pltpu.roll(first, half, 1), second)
    reorder(dst_ref, s_ref, x_ref)
    for w in range(devices):
        out_ref[w, 0:2 * padded_planes, :] = x_ref[w]
    for e in range(devices // 2):
        re = x_ref[devices + e, 0:padded_planes, :]
        im = x_ref[devices + e, padded_planes:2 * padded_planes, :]
        out_ref[2 * e, 2 * padded_planes:3 * padded_planes, :] = jnp.where(
            low, re, pltpu.roll(im, half, 1)
        )
        out_ref[2 * e + 1, 2 * padded_planes:3 * padded_planes, :] = jnp.where(
            low, pltpu.roll(re, half, 1), im
        )
    for d in range(devices):
        out_ref[d, 3 * padded_planes:, :] = jnp.zeros((8, LANES), F32)


def inner_kernel(bands, volume, norm, place_ref, *refs):
    kc_ref = refs[0]
    waves = refs[1:1 + bands]
    fields = refs[1 + bands:1 + 2 * bands]
    in_ref = refs[1 + 2 * bands]
    out_refs = refs[2 + 2 * bands:]
    devices = in_ref.shape[0]
    padded_planes = (in_ref.shape[1] - 8) // 3
    half = LANES // 2
    sticks, padded = kc_ref.shape[0], kc_ref.shape[1] // 2
    me, mine = place_ref[0], place_ref[1]
    low = lax.broadcasted_iota(jnp.int32, (padded_planes, LANES), 1) < half

    def fold(x):
        rows = x.shape[0]
        total = x[0:8]
        for at in range(8, rows, 8):
            total = total + x[at:at + 8]
        return total

    kc = kc_ref[...]
    kc_re, kc_im = kc[:, :padded], kc[:, padded:]
    sums = []
    for m in range(bands):
        c_re, c_im = waves[m][:sticks, :], waves[m][sticks:, :]
        sums.append([fold(c_re * kc_re + c_im * kc_im), fold(c_re * kc_im - c_im * kc_re)])
    local = [[jnp.zeros((8, LANES), F32), jnp.zeros((8, LANES), F32)] for _ in range(bands)]
    for d in range(devices):
        value = in_ref[d, 0:3 * padded_planes, :]
        re, im, rest = value[:padded_planes], value[padded_planes:2 * padded_planes], value[2 * padded_planes:]
        turned = pltpu.roll(rest, half, 1)
        other = jnp.concatenate([im, -re, jnp.where(low, turned, -turned)], axis=0)
        for m in range(bands):
            col = fields[m][d, 0:3 * padded_planes, :]
            local[m][0] = local[m][0] + fold(col * value)
            local[m][1] = local[m][1] + fold(col * other)
    lane = lax.broadcasted_iota(jnp.int32, (8, LANES), 1)
    row = lax.broadcasted_iota(jnp.int32, (8, LANES), 0)
    tile = jnp.zeros((8, LANES), F32)
    for m in range(bands):
        spot = me ^ m
        for part, sign in ((0, 1.0), (1, -1.0)):
            partial = sums[m][part] + volume * local[m][part]
            scalar = jnp.sum(jnp.sum(partial, axis=1, keepdims=True), axis=0, keepdims=True)
            tile = jnp.where((lane == spot) & (row == part), sign * norm * scalar, tile)
    for k in range(devices):
        out_refs[k][0:3 * padded_planes, :] = in_ref[lax.rem(mine + k, devices), 0:3 * padded_planes, :]
        out_refs[k][3 * padded_planes:, :] = tile


def final_kernel(volume, devices, me_ref, len_ref, *refs):
    ret_refs = refs[:devices]
    kc_ref, whi_ref, wlo_ref, sc_ref, ss_ref, out_ref, sub_ref, stack_ref = refs[devices:]
    padded_planes = (ret_refs[0].shape[0] - 8) // 3
    sticks, _, padded = out_ref.shape
    half = LANES // 2
    bands = sub_ref.shape[2]
    total = jnp.zeros((8, LANES), F32)
    me = me_ref[0]
    for k in range(devices):
        value = ret_refs[k][...]
        base = pl.multiple_of(lax.rem(me + devices - k, devices) * padded_planes, 8)
        total = total + value[3 * padded_planes:]
        rest = value[2 * padded_planes:3 * padded_planes]
        re = jnp.concatenate([value[:padded_planes], rest[:, :half]], axis=1)
        im = jnp.concatenate([value[padded_planes:2 * padded_planes], rest[:, half:]], axis=1)
        c = sc_ref[pl.ds(base, padded_planes), :]
        s = ss_ref[pl.ds(base, padded_planes), :]
        stack_ref[pl.ds(2 * base, padded_planes), :sticks] = re * c - im * s
        stack_ref[pl.ds(2 * base + padded_planes, padded_planes), :sticks] = re * s + im * c
    turned = jnp.transpose(stack_ref[...])[:sticks]
    local = dot3(split(turned), (whi_ref[...], wlo_ref[...])) * volume
    position = lax.broadcasted_iota(jnp.int32, (sticks, padded), 1).astype(F32)
    kept = position < len_ref[:, 0:1]
    kc = kc_ref[...]
    out_ref[:, 0, :] = jnp.where(kept, kc[:, :padded] + local[:, :padded], 0.0)
    out_ref[:, 1, :] = jnp.where(kept, kc[:, padded:] + local[:, padded:], 0.0)
    sub_ref[:, 0, :] = total[0:2, :bands]


def pairs(count, k):
    return [(d, d ^ k) for d in range(count)]


def shards(bands, devices, coefficients, stick_col, stick_row, stick_length, plane_of_slot, potential):
    extent = plane_of_slot.shape[0]
    sticks = coefficients.shape[1]
    padded = coefficients.shape[3]
    total_sticks = stick_col.shape[0]
    planes = potential.shape[0]
    padded_planes = up8(planes)
    if sticks != LANES + LANES // 2 or devices % 2 or planes % 2 or bands & (bands - 1):
        raise ValueError("sizes")
    rows = sum(row_blocks())
    volume = 1.0 / (extent * extent * extent)
    me = lax.axis_index("tg").astype(jnp.int32)
    coef = coefficients.reshape(sticks, 2, padded)

    length, row, col = (v.reshape(-1, LANES) for v in (stick_length, stick_row, stick_col))
    slots = plane_of_slot.reshape(devices, planes)
    if padded_planes > planes:
        slots = jnp.pad(slots, ((0, 0), (0, padded_planes - planes)), constant_values=-1)
    slots = slots.reshape(1, devices * padded_planes)
    windows = total_sticks // LANES
    smem = pl.BlockSpec(memory_space=pltpu.SMEM)
    vmem = pl.BlockSpec(memory_space=pltpu.VMEM)
    hbm = pl.BlockSpec(memory_space=pltpu.HBM)

    block = 3 * padded_planes
    total_planes = devices * padded_planes
    sent, kc, wave, lengths, whi, wlo, shift_cos, shift_sin = pl.pallas_call(
        functools.partial(wave_kernel, extent),
        out_shape=(
            jax.ShapeDtypeStruct((devices, block, LANES), F32),
            jax.ShapeDtypeStruct((sticks, 2 * padded), F32),
            jax.ShapeDtypeStruct((2 * sticks, padded), F32),
            jax.ShapeDtypeStruct((sticks, LANES), F32),
            jax.ShapeDtypeStruct((2 * total_planes, 2 * padded), BF16),
            jax.ShapeDtypeStruct((2 * total_planes, 2 * padded), BF16),
            jax.ShapeDtypeStruct((total_planes, sticks), F32),
            jax.ShapeDtypeStruct((total_planes, sticks), F32),
        ),
        in_specs=[smem] + [hbm] * 5,
        scratch_shapes=[
            pltpu.VMEM(length.shape, jnp.int32),
            pltpu.VMEM(row.shape, jnp.int32),
            pltpu.VMEM(col.shape, jnp.int32),
            pltpu.VMEM(slots.shape, jnp.int32),
            pltpu.VMEM(coef.shape, F32),
            pltpu.SemaphoreType.DMA((5,)),
        ],
        compiler_params=params(56),
        name="wave_to_planes",
    )(me.reshape(1), length, row, col, slots, coef)

    received = lax.all_to_all(sent, "tg", split_axis=0, concat_axis=0, tiled=True)

    window_list = jax.ShapeDtypeStruct((windows, LANES), jnp.int32)
    longer_list = jax.ShapeDtypeStruct((2 * windows + 1, LANES), jnp.int32)
    square = jax.ShapeDtypeStruct((LANES, LANES), jnp.int32)
    even_map, odd_map, first, source, target, row_w, col_w = pl.pallas_call(
        functools.partial(map_kernel, extent, sticks),
        out_shape=(
            square,
            square,
            jax.ShapeDtypeStruct((16, LANES), jnp.int32),
            window_list,
            window_list,
            longer_list,
            longer_list,
        ),
        in_specs=[hbm] * 2,
        scratch_shapes=[
            pltpu.VMEM(row.shape, jnp.int32),
            pltpu.VMEM(col.shape, jnp.int32),
            pltpu.SemaphoreType.DMA((2,)),
        ],
        compiler_params=params(14 * total_sticks / 1536),
        cost_estimate=cost(4e9, 1e5),
        name="stick_map",
    )(row, col)

    constants = jnp.asarray(tables(extent))
    weighted = pl.pallas_call(
        functools.partial(plane_kernel, planes),
        out_shape=jax.ShapeDtypeStruct((devices, block + 8, LANES), F32),
        in_specs=[smem] + [vmem] * 7 + [hbm] * 2,
        out_specs=vmem,
        scratch_shapes=[
            pltpu.VMEM((windows, 2 * padded_planes, LANES), F32),
            pltpu.VMEM((windows, 2 * padded_planes, LANES), F32),
            pltpu.VMEM((2 * windows + 1, padded_planes, LANES), F32),
            pltpu.VMEM((padded_planes * rows, LANES), F32),
            pltpu.VMEM((padded_planes * rows, LANES), F32),
            pltpu.VMEM(constants.shape, BF16),
            pltpu.VMEM(potential.shape, F32),
            pltpu.SemaphoreType.DMA((2,)),
        ],
        compiler_params=params(52),
        cost_estimate=cost(2e10, 1e7),
        name="planes",
    )(first, even_map, odd_map, source, target, row_w, col_w, received, constants, potential)

    waves, fields = [wave], [received]
    for m in range(1, bands):
        waves.append(lax.ppermute(wave, "band", pairs(bands, m)))
        fields.append(lax.ppermute(received, "band", pairs(bands, m)))
    band = lax.axis_index("band").astype(jnp.int32)
    norm = 1.0 / (total_sticks * padded)
    places = jnp.stack([band, me])
    outgoing = pl.pallas_call(
        functools.partial(inner_kernel, bands, volume, norm),
        out_shape=(jax.ShapeDtypeStruct((block + 8, LANES), F32),) * devices,
        in_specs=[smem] + [vmem] * (2 + 2 * bands),
        compiler_params=params(6 + 1.5 * bands),
        name="inner",
    )(places, kc, *waves, *fields, weighted)

    returned = list(outgoing)
    for k in sorted(range(1, devices), key=lambda k: abs(k - devices // 2)):
        ring = [(d, (d + k) % devices) for d in range(devices)]
        returned[k] = lax.ppermute(outgoing[k], "tg", ring)
    applied, subspace = pl.pallas_call(
        functools.partial(final_kernel, volume, devices),
        out_shape=(
            jax.ShapeDtypeStruct((sticks, 2, padded), F32),
            jax.ShapeDtypeStruct((2, 1, bands), F32),
        ),
        in_specs=[smem] + [vmem] * (6 + devices),
        scratch_shapes=[pltpu.VMEM((2 * total_planes, 2 * LANES), F32)],
        compiler_params=params(6 + 6 * total_planes / 192),
        name="planes_to_wave",
    )(me.reshape(1), lengths, *returned, kc, whi, wlo, shift_cos, shift_sin)
    return applied.reshape(1, sticks, 2, padded), subspace


def solution(mesh):
    in_specs = (P("band", "tg", None, None), P(), P(), P(), P(), P("tg", None, None))
    out_specs = (P("band", "tg", None, None), P(None, "band", None))
    body = functools.partial(shards, mesh.shape["band"], mesh.shape["tg"])
    return jax.shard_map(body, mesh=mesh, in_specs=in_specs, out_specs=out_specs, check_vma=False)
```

```python
import functools
import math

import jax
import jax.numpy as jnp
import ml_dtypes
import numpy as np
from jax import lax
from jax.experimental import pallas as pl
from jax.experimental.pallas import tpu as pltpu
from jax.sharding import PartitionSpec as P

RADIUS = 48
LANES = 128
F32 = jnp.float32
BF16 = jnp.bfloat16


def up8(n):
    return -(-n // 8) * 8


def split(x):
    hi = x.astype(BF16)
    return hi, (x - hi.astype(F32)).astype(BF16)


def dot3(a, b, dims=((1,), (0,))):
    def dot(x, y):
        return lax.dot_general(x, y, (dims, ((), ())), preferred_element_type=F32)

    return dot(a[0], b[0]) + (dot(a[0], b[1]) + dot(a[1], b[0]))


def trig(product, extent):
    n = product - extent * jnp.floor(product * (1.0 / extent) + 0.5)
    quarter = extent / 4.0
    unit = 2.0 * math.pi / extent

    def sine(m):
        u = m * unit
        v = u * u
        s = 1.0 / 6227020800.0
        for term in (-39916800.0, 362880.0, -5040.0, 120.0, -6.0, 1.0):
            s = s * v + 1.0 / term
        return u * s

    folded = jnp.where(
        jnp.abs(n) > quarter, jnp.where(n > 0, 2.0 * quarter, -2.0 * quarter) - n, n
    )
    return sine(quarter - jnp.abs(n)), sine(folded)


def pair(table):
    hi = table.astype(np.float32).astype(ml_dtypes.bfloat16)
    lo = (table - hi.astype(np.float64)).astype(ml_dtypes.bfloat16)
    return hi, lo


def row_blocks():
    even = -(-(RADIUS + 1) // 16) * 16
    odd = -(-RADIUS // 16) * 16
    return even, odd


@functools.cache
def tables(extent):
    half = extent // 2
    grid = np.arange(extent)
    freq = np.arange(2 * RADIUS + 1) - RADIUS

    def angles(f, g):
        a = 2.0 * np.pi * ((f[:, None] * g[None, :]) % extent) / extent
        return np.cos(a), np.sin(a)

    wide = 2 * LANES
    x_forward, x_back, forward, back = [], [], [], []
    for offset, rows in zip((0, 1), row_blocks()):
        cos, sin = angles(freq[offset::2], grid[:half])
        count = cos.shape[0]
        table = np.zeros((LANES, wide))
        table[:count, :half] = cos
        table[LANES // 2:LANES // 2 + count, :half] = -sin
        table[:count, LANES:LANES + half] = sin
        table[LANES // 2:LANES // 2 + count, LANES:LANES + half] = cos
        hi, lo = pair(table)
        x_forward.append(np.concatenate([hi, hi, lo], axis=0))
        hi, lo = pair(table.T.copy())
        x_back.append(
            np.concatenate(
                [np.concatenate([hi, lo], axis=1), np.concatenate([hi, np.zeros_like(lo)], axis=1)], axis=0
            )
        )
        parts = []
        for wave in (cos, sin):
            table = np.zeros((half, rows))
            table[:, :count] = wave.T
            hi, lo = pair(table)
            parts += [hi, hi, lo]
        forward.append(np.concatenate(parts, axis=1))
        table = np.zeros((2 * rows, half))
        table[:count] = cos
        table[rows:rows + count] = sin
        hi, lo = pair(table)
        back.append(np.concatenate([hi, hi, lo], axis=1))
    rows = [np.concatenate(x_forward, axis=1), np.concatenate(x_back, axis=1)]
    for table in forward + back:
        rows.append(np.pad(table, ((0, 0), (0, 2 * wide - table.shape[1]))))
    return np.concatenate(rows, axis=0)


def params(megabytes):
    return pltpu.CompilerParams(vmem_limit_bytes=int(min(megabytes, 56) * 2**20))


def fetch_all(sources, targets, sems):
    copies = [
        pltpu.make_async_copy(source, target, sems.at[i])
        for i, (source, target) in enumerate(zip(sources, targets))
    ]
    for copy in copies:
        copy.start()
    return copies


def cost(flops, nbytes):
    return pl.CostEstimate(flops=int(flops), bytes_accessed=int(nbytes), transcendentals=0)


def wave_kernel(
    extent, me_ref, length_hbm, row_hbm, col_hbm, plane_hbm, coef_hbm,
    out_ref, kc_ref, wave_ref, len_ref, whi_ref, wlo_ref, sc_ref, ss_ref,
    length_ref, row_ref, col_ref, plane_ref, coef_ref, sems,
):
    copies = fetch_all(
        (length_hbm, row_hbm, col_hbm, plane_hbm, coef_hbm),
        (length_ref, row_ref, col_ref, plane_ref, coef_ref),
        sems,
    )
    for copy in copies[:4]:
        copy.wait()
    devices = out_ref.shape[0]
    sticks, _, padded = coef_ref.shape
    padded_planes = plane_ref.shape[1] // devices
    me = me_ref[0]
    half = LANES // 2
    lead = (me * sticks) // LANES
    odd = (me * sticks) % LANES != 0

    def own(ref):
        first, second = ref[pl.ds(lead, 1), :], ref[pl.ds(lead + 1, 1), :]
        both = jnp.concatenate([first, second], axis=1)
        return jnp.where(odd, both[:, half:], both[:, :sticks])

    length_row = own(length_ref).astype(F32)
    at_row = own(row_ref)
    at_col = own(col_ref)
    at_row = jnp.where(at_row <= RADIUS, at_row, at_row - extent).astype(F32)
    at_col = jnp.where(at_col <= RADIUS, at_col, at_col - extent).astype(F32)
    square_row = at_row * at_row + at_col * at_col
    spare = jnp.ones((1, 2 * LANES - sticks), F32)
    aux = jnp.concatenate(
        [
            jnp.broadcast_to(jnp.concatenate([length_row, spare], axis=1), (LANES // 2, 2 * LANES)),
            jnp.broadcast_to(jnp.concatenate([square_row, spare], axis=1), (LANES // 2, 2 * LANES)),
        ],
        axis=0,
    )
    aux_col = jnp.transpose(aux)[:sticks]
    len_ref[...] = aux_col
    length = aux_col[:, 0:1]
    square = aux_col[:, LANES // 2:LANES // 2 + 1]
    middle = (length - 1.0) * 0.5
    position = lax.broadcasted_iota(jnp.int32, (sticks, padded), 1).astype(F32)
    total = plane_ref.shape[1]
    plane_row = jnp.broadcast_to(plane_ref[...].astype(F32), (LANES, total))
    plane_col = jnp.transpose(plane_row)[:, 0:1]
    real = (plane_col >= 0.0).astype(F32)
    plane_col = jnp.maximum(plane_col, 0.0)
    harmonic = lax.broadcasted_iota(jnp.int32, (total, padded), 1).astype(F32)
    cos, sin = trig(plane_col * harmonic, extent)
    cos, sin = cos * real, sin * real
    parts = []
    for d in range(devices):
        c = cos[d * padded_planes:(d + 1) * padded_planes]
        s = sin[d * padded_planes:(d + 1) * padded_planes]
        parts.append(jnp.concatenate([c, -s], axis=1))
        parts.append(jnp.concatenate([s, c], axis=1))
    table = split(jnp.concatenate(parts, axis=0))
    whi_ref[...] = table[0]
    wlo_ref[...] = table[1]
    shift_cos, shift_sin = trig(plane_col * ((length_row - 1.0) * 0.5), extent)
    sc_ref[...] = shift_cos
    ss_ref[...] = shift_sin
    copies[4].wait()
    kept = (position < length).astype(F32)
    kinetic = (square + (position - middle) * (position - middle)) * (1.0 / (RADIUS * RADIUS))
    wave = jnp.concatenate([coef_ref[:, 0, :] * kept, coef_ref[:, 1, :] * kept], axis=1)
    kc_ref[...] = wave * jnp.concatenate([kinetic, kinetic], axis=1)
    wave_ref[:sticks, :] = wave[:, :padded]
    wave_ref[sticks:, :] = wave[:, padded:]
    raw = dot3(table, split(wave), ((1,), (1,)))
    for d in range(devices):
        at = 2 * d * padded_planes
        re, im = raw[at:at + padded_planes], raw[at + padded_planes:at + 2 * padded_planes]
        c = shift_cos[d * padded_planes:(d + 1) * padded_planes]
        s = shift_sin[d * padded_planes:(d + 1) * padded_planes]
        along_re = re * c + im * s
        along_im = im * c - re * s
        out_ref[d, 0:padded_planes, :] = along_re[:, :LANES]
        out_ref[d, padded_planes:2 * padded_planes, :] = along_im[:, :LANES]
        out_ref[d, 2 * padded_planes:3 * padded_planes, :] = jnp.concatenate(
            [along_re[:, LANES:], along_im[:, LANES:]], axis=1
        )


def window_row(values, sticks):
    line = jnp.concatenate([values[i:i + 1] for i in range(values.shape[0])], axis=1)
    starts = range(0, line.shape[1], sticks)
    parts = [line[:, at:at + LANES] for at in starts]
    parts += [line[:, at + LANES:at + sticks] for at in starts]
    return jnp.concatenate(parts, axis=1)


def map_kernel(
    extent, sticks, in_row_hbm, in_col_hbm,
    even_ref, odd_ref, first_ref, src_ref, dst_ref, row_ref, col_ref,
    in_row_ref, in_col_ref, sems,
):
    for copy in fetch_all((in_row_hbm, in_col_hbm), (in_row_ref, in_col_ref), sems):
        copy.wait()
    windows = src_ref.shape[0]
    total = windows * LANES

    def signed(ref):
        value = ref[...]
        return window_row(jnp.where(value <= RADIUS, value, value - extent) + RADIUS, sticks)

    def dot(x, y, dims=((1,), (0,))):
        return lax.dot_general(x, y, (dims, ((), ())), preferred_element_type=F32)

    def bits(condition):
        return condition.astype(F32).astype(BF16)

    nt = ((1,), (1,))
    own_row, own_col = signed(in_row_ref), signed(in_col_ref)
    half = LANES // 2
    own_row = (own_row & 1) * row_blocks()[0] + (own_row >> 1)
    own_col = (own_col & 1) * half + (own_col >> 1)
    tall = lax.broadcasted_iota(jnp.int32, (LANES, total), 0)
    place = lax.broadcasted_iota(jnp.int32, (LANES, total), 1)
    in_col = tall == own_col
    row_hot, col_hot = bits(tall == own_row), bits(in_col)
    down = lax.broadcasted_iota(jnp.int32, (LANES, LANES), 0)
    across = lax.broadcasted_iota(jnp.int32, (LANES, LANES), 1)
    before = bits(down < across)
    after = bits(down > across)
    upto = bits(down >= across)
    ones = jnp.ones((LANES, LANES), BF16)
    taken = dot(row_hot, col_hot, nt)
    taken_t = dot(col_hot, row_hot, nt)
    taken_b, taken_tb = taken.astype(BF16), taken_t.astype(BF16)
    start = dot(dot(after, taken_b).astype(BF16), ones)
    end = start + dot(taken_b, ones)
    start_t = dot(ones, dot(taken_tb, before).astype(BF16))
    left = across < half
    standing = dot(taken_b, before) + start
    low_ones = bits(down < half)
    high_start = start + dot(taken_b, low_ones)
    ones_t = bits(across < half)
    high_start_t = start_t + dot(ones_t, taken_tb)
    limit = 2.0 * windows - 1.0

    def first_window(value):
        return jnp.minimum(jnp.floor(value * (1.0 / half)), limit)

    for ref, begin in ((even_ref, start), (odd_ref, high_start)):
        code = jnp.where(taken > 0.5, standing - half * first_window(begin), -1.0)
        turned = pltpu.roll(code, half, 1)
        both = jnp.where(left, code, turned) if ref is even_ref else jnp.where(left, turned, code)
        ref[...] = both.astype(jnp.int32)
    first_ref[...] = jnp.concatenate(
        [first_window(start_t[0:8]), first_window(high_start_t[0:8])], axis=0
    ).astype(jnp.int32)

    spot = place.astype(F32)
    in_range = (spot >= start[:, 0:1]) & (spot < end[:, 0:1])
    sorted_hot = bits(in_range)
    sorted_row = jnp.sum(jnp.where(in_range, tall, 0).astype(F32), axis=0, keepdims=True)
    sorted_rank = spot[0:1] - jnp.sum(jnp.where(in_range, start[:, 0:1], 0.0), axis=0, keepdims=True)
    counts = dot(dot(upto, taken_tb).astype(BF16), sorted_hot)
    sorted_col = jnp.sum((counts <= sorted_rank).astype(F32), axis=0, keepdims=True)
    names = place + 1
    name_hi = dot(jnp.where(in_col, names >> 6, 0).astype(F32).astype(BF16), row_hot, nt)
    name_lo = dot(jnp.where(in_col, names & 63, 0).astype(F32).astype(BF16), row_hot, nt)
    named = dot(name_hi.astype(BF16), sorted_hot) * 64.0 + dot(name_lo.astype(BF16), sorted_hot)
    source = jnp.sum(jnp.where(tall.astype(F32) == sorted_col, named, 0.0), axis=0, keepdims=True) - 1.0
    place_t = dot(after, taken_tb) + start_t
    place_hi = jnp.floor(place_t * (1.0 / 64.0))
    place_lo = place_t - 64.0 * place_hi
    placed = dot(place_hi.astype(BF16), row_hot) * 64.0 + dot(place_lo.astype(BF16), row_hot)
    target = jnp.sum(jnp.where(in_col, placed, 0.0), axis=0, keepdims=True)
    for values, ref in ((source, src_ref), (target, dst_ref)):
        values = values.astype(jnp.int32)
        for w in range(windows):
            ref[w:w + 1, :] = values[:, w * LANES:(w + 1) * LANES]
    is_left = left[0:8]
    shift = jnp.where(is_left, 0, half)
    sorted_col = sorted_col.astype(jnp.int32)
    sorted_key = sorted_row.astype(jnp.int32) * 2 + (sorted_col >> 6)
    sorted_col = sorted_col & (half - 1)
    for values, ref, add in ((sorted_key, row_ref, 0), (sorted_col, col_ref, shift)):
        for w in range(windows):
            line = jnp.broadcast_to(values[:, w * LANES:(w + 1) * LANES], (8, LANES))
            turned = pltpu.roll(line, half, 1)
            ref[2 * w:2 * w + 1, :] = (jnp.where(is_left, line, turned) + add)[0:1]
            ref[2 * w + 1:2 * w + 2, :] = (jnp.where(is_left, turned, line) + add)[0:1]
    row_ref[2 * windows:2 * windows + 1, :] = jnp.full((1, LANES), -1, jnp.int32)
    col_ref[2 * windows:2 * windows + 1, :] = jnp.zeros((1, LANES), jnp.int32)


def lane_take(x, index):
    return jnp.take_along_axis(x, index, axis=1, mode="promise_in_bounds")


def plane_kernel(
    planes, first_ref, even_ref, odd_ref, src_ref, dst_ref, row_ref, col_ref, recv_ref,
    *refs,
):
    table_hbm, pot_hbm, out_ref, x_ref, s_ref, t_ref, ge_ref, go_ref, table_ref, pot_ref, sems = refs
    devices = recv_ref.shape[0]
    padded_planes = recv_ref.shape[1] // 3
    windows = x_ref.shape[0]
    rows = ge_ref.shape[0] // padded_planes
    extent = pot_ref.shape[1]
    half = LANES // 2
    copies = fetch_all((table_hbm, pot_hbm), (table_ref, pot_ref), sems)

    low = lax.broadcasted_iota(jnp.int32, (padded_planes, LANES), 1) < half
    for d in range(devices):
        x_ref[d] = recv_ref[d, 0:2 * padded_planes, :]
    for e in range(devices // 2):
        first = recv_ref[2 * e, 2 * padded_planes:3 * padded_planes, :]
        second = recv_ref[2 * e + 1, 2 * padded_planes:3 * padded_planes, :]
        x_ref[devices + e, 0:padded_planes, :] = jnp.where(low, first, pltpu.roll(second, half, 1))
        x_ref[devices + e, padded_planes:2 * padded_planes, :] = jnp.where(
            low, pltpu.roll(first, half, 1), second
        )

    blocks = padded_planes // 8

    def reorder(order_ref, from_ref, to_ref):
        @pl.loop(0, windows, unroll=4)
        def _(v):
            order = jnp.broadcast_to(order_ref[pl.ds(v, 1), :], (8, LANES))
            index = order & (LANES - 1)
            window = order >> 7
            for j in range(2 * blocks):
                value = jnp.zeros((8, LANES), F32)
                for w in range(windows):
                    value = jnp.where(window == w, lane_take(from_ref[w, 8 * j:8 * j + 8, :], index), value)
                to_ref[v, 8 * j:8 * j + 8, :] = value

    reorder(src_ref, x_ref, s_ref)
    for w in range(windows):
        re, im = s_ref[w, 0:padded_planes, :], s_ref[w, padded_planes:2 * padded_planes, :]
        t_ref[2 * w] = jnp.where(low, re, pltpu.roll(im, half, 1))
        t_ref[2 * w + 1] = jnp.where(low, pltpu.roll(re, half, 1), im)

    left = low[0:8]
    upper_lanes = jnp.where(left, 0, half)
    sides = ((0, even_ref, ge_ref), (1, odd_ref, go_ref))
    even_rows, odd_rows = row_blocks()
    used = up8(RADIUS + 1)
    for p in range(planes):
        for at in range(p * rows + used, p * rows + even_rows, 8):
            ge_ref[at:at + 8, :] = jnp.zeros((8, LANES), F32)
            go_ref[at:at + 8, :] = jnp.zeros((8, LANES), F32)

    def each_row(body):
        pl.loop(0, used, unroll=8)(body)
        pl.loop(even_rows, rows, unroll=8)(body)

    @each_row
    def _(r):
        for side, code_ref, grid_ref in sides:
            first = first_ref[8 * side, r]
            code = jnp.broadcast_to(code_ref[pl.ds(r, 1), :], (8, LANES))
            index = (code & (half - 1)) + upper_lanes
            window = code >> 6
            for j in range(blocks):
                lead = lane_take(t_ref[first, 8 * j:8 * j + 8, :], index)
                trail = lane_take(t_ref[first + 1, 8 * j:8 * j + 8, :], index)
                value = jnp.where(window == 0, lead, jnp.where(window == 1, trail, 0.0))
                grid_ref[pl.ds(r + 8 * j * rows, 8, stride=rows), :] = value

    for copy in copies:
        copy.wait()
    folded = extent // 2
    group = next(g for g in (24, 12, 8, 6, 4, 2) if planes % g == 0)
    wide = 2 * LANES
    at_back = 3 * LANES
    at_y = at_back + 2 * wide
    at_even = at_y + 2 * folded
    at_odd = at_even + 2 * even_rows
    x_forward = (table_ref[0:at_back, :wide], table_ref[0:at_back, wide:])
    x_back = (table_ref[at_back:at_y, :wide], table_ref[at_back:at_y, wide:])
    y_even = table_ref[at_y:at_y + folded, :6 * even_rows]
    y_odd = table_ref[at_y + folded:at_even, :6 * odd_rows]
    back_even = table_ref[at_even:at_odd, :3 * folded]
    back_odd = table_ref[at_odd:at_odd + 2 * odd_rows, :3 * folded]

    def dot(x, y):
        return jnp.dot(x, y, preferred_element_type=F32)

    def stack(x, axis):
        hi, lo = split(x)
        return jnp.concatenate([hi, lo, hi], axis=axis)

    def turn(x):
        lane = lax.broadcasted_iota(jnp.int32, (x.shape[0], LANES), 1) < half
        parts = []
        for at in range(0, x.shape[1], LANES):
            rolled = pltpu.roll(x[:, at:at + LANES], half, 1)
            parts.append(jnp.where(lane, -rolled, rolled))
        return jnp.concatenate(parts, axis=1)

    @pl.loop(0, planes // group)
    def _(step):
        lines = []
        for t in range(group):
            base = pl.multiple_of((step * group + t) * rows, 16)
            parts = []
            for at, size, table in ((0, even_rows, y_even), (even_rows, odd_rows, y_odd)):
                pick = pl.ds(base + at, size)
                spectrum = jnp.concatenate([ge_ref[pick, :], go_ref[pick, :]], axis=1)
                both = jnp.concatenate([stack(spectrum, 0), stack(turn(spectrum), 0)], axis=0)
                parts.append(dot(table, both))
            lines.append(parts[0] + parts[1])
            lines.append(parts[0] - parts[1])
        lines = jnp.concatenate(lines, axis=0)
        field_even = dot(stack(lines[:, :LANES], 1), x_forward[0])
        field_odd = dot(stack(lines[:, LANES:], 1), x_forward[1])
        spare = jnp.zeros((extent, LANES - folded), F32)
        sums, differences = [], []
        for t in range(group):
            v = pot_ref[step * group + t]
            v_near = jnp.concatenate([v[:, :folded], spare], axis=1)
            v_far = jnp.concatenate([v[:, folded:], spare], axis=1)
            even = field_even[t * extent:(t + 1) * extent]
            odd = field_odd[t * extent:(t + 1) * extent]
            near = (even + odd) * jnp.concatenate([v_near, v_near], axis=1)
            far = (even - odd) * jnp.concatenate([v_far, v_far], axis=1)
            sums.append(near + far)
            differences.append(near - far)
        back = []
        for weighted, table in ((sums, x_back[0]), (differences, x_back[1])):
            both = dot(jnp.concatenate(split(jnp.concatenate(weighted, axis=0)), axis=1), table)
            back.append(both[:, :LANES] + both[:, LANES:])
        back = jnp.concatenate(back, axis=1)
        for t in range(group):
            base = pl.multiple_of((step * group + t) * rows, 16)
            upper = back[t * extent:t * extent + folded]
            lower = back[t * extent + folded:(t + 1) * extent]
            for at, size, table, value in (
                (0, even_rows, back_even, upper + lower), (even_rows, odd_rows, back_odd, upper - lower)
            ):
                both = dot(table, stack(value, 0))
                value = both[:size] - turn(both[size:])
                pick = pl.ds(base + at, size)
                ge_ref[pick, :] = value[:, :LANES]
                go_ref[pick, :] = value[:, LANES:]

    @each_row
    def _(r):
        for side, _, grid_ref in sides:
            first = first_ref[8 * side, r]
            values = [grid_ref[pl.ds(r + 8 * j * rows, 8, stride=rows), :] for j in range(blocks)]
            for t in range(2):
                index = jnp.broadcast_to(col_ref[pl.ds(first + t, 1), :], (8, LANES))
                hit = jnp.broadcast_to(row_ref[pl.ds(first + t, 1), :], (8, LANES)) == 2 * r + side
                for j in range(blocks):
                    pltpu.store(
                        t_ref.at[first + t, 8 * j:8 * j + 8, :], lane_take(values[j], index), mask=hit
                    )

    for w in range(windows):
        first, second = t_ref[2 * w], t_ref[2 * w + 1]
        s_ref[w, 0:padded_planes, :] = jnp.where(low, first, pltpu.roll(second, half, 1))
        s_ref[w, padded_planes:2 * padded_planes, :] = jnp.where(low, pltpu.roll(first, half, 1), second)
    reorder(dst_ref, s_ref, x_ref)
    for w in range(devices):
        out_ref[w, 0:2 * padded_planes, :] = x_ref[w]
    for e in range(devices // 2):
        re = x_ref[devices + e, 0:padded_planes, :]
        im = x_ref[devices + e, padded_planes:2 * padded_planes, :]
        out_ref[2 * e, 2 * padded_planes:3 * padded_planes, :] = jnp.where(
            low, re, pltpu.roll(im, half, 1)
        )
        out_ref[2 * e + 1, 2 * padded_planes:3 * padded_planes, :] = jnp.where(
            low, pltpu.roll(re, half, 1), im
        )
    for d in range(devices):
        out_ref[d, 3 * padded_planes:, :] = jnp.zeros((8, LANES), F32)


def inner_kernel(bands, volume, norm, place_ref, *refs):
    kc_ref = refs[0]
    waves = refs[1:1 + bands]
    fields = refs[1 + bands:1 + 2 * bands]
    in_ref = refs[1 + 2 * bands]
    out_refs = refs[2 + 2 * bands:]
    devices = in_ref.shape[0]
    padded_planes = (in_ref.shape[1] - 8) // 3
    half = LANES // 2
    sticks, padded = kc_ref.shape[0], kc_ref.shape[1] // 2
    me, mine = place_ref[0], place_ref[1]
    low = lax.broadcasted_iota(jnp.int32, (padded_planes, LANES), 1) < half

    def fold(x):
        rows = x.shape[0]
        total = x[0:8]
        for at in range(8, rows, 8):
            total = total + x[at:at + 8]
        return total

    kc = kc_ref[...]
    kc_re, kc_im = kc[:, :padded], kc[:, padded:]
    sums = []
    for m in range(bands):
        c_re, c_im = waves[m][:sticks, :], waves[m][sticks:, :]
        sums.append([fold(c_re * kc_re + c_im * kc_im), fold(c_re * kc_im - c_im * kc_re)])
    local = [[jnp.zeros((8, LANES), F32), jnp.zeros((8, LANES), F32)] for _ in range(bands)]
    for d in range(devices):
        value = in_ref[d, 0:3 * padded_planes, :]
        re, im, rest = value[:padded_planes], value[padded_planes:2 * padded_planes], value[2 * padded_planes:]
        turned = pltpu.roll(rest, half, 1)
        other = jnp.concatenate([im, -re, jnp.where(low, turned, -turned)], axis=0)
        for m in range(bands):
            col = fields[m][d, 0:3 * padded_planes, :]
            local[m][0] = local[m][0] + fold(col * value)
            local[m][1] = local[m][1] + fold(col * other)
    lane = lax.broadcasted_iota(jnp.int32, (8, LANES), 1)
    row = lax.broadcasted_iota(jnp.int32, (8, LANES), 0)
    tile = jnp.zeros((8, LANES), F32)
    for m in range(bands):
        spot = me ^ m
        for part, sign in ((0, 1.0), (1, -1.0)):
            partial = sums[m][part] + volume * local[m][part]
            scalar = jnp.sum(jnp.sum(partial, axis=1, keepdims=True), axis=0, keepdims=True)
            tile = jnp.where((lane == spot) & (row == part), sign * norm * scalar, tile)
    for k in range(devices):
        out_refs[k][0:3 * padded_planes, :] = in_ref[lax.rem(mine + k, devices), 0:3 * padded_planes, :]
        out_refs[k][3 * padded_planes:, :] = tile


def final_kernel(volume, devices, me_ref, len_ref, *refs):
    ret_refs = refs[:devices]
    kc_ref, whi_ref, wlo_ref, sc_ref, ss_ref, out_ref, sub_ref, stack_ref = refs[devices:]
    padded_planes = (ret_refs[0].shape[0] - 8) // 3
    sticks, _, padded = out_ref.shape
    half = LANES // 2
    bands = sub_ref.shape[2]
    total = jnp.zeros((8, LANES), F32)
    me = me_ref[0]
    for i, k in enumerate(far_first(devices)):
        value = ret_refs[i][...]
        base = pl.multiple_of(lax.rem(me + devices - k, devices) * padded_planes, 8)
        total = total + value[3 * padded_planes:]
        rest = value[2 * padded_planes:3 * padded_planes]
        re = jnp.concatenate([value[:padded_planes], rest[:, :half]], axis=1)
        im = jnp.concatenate([value[padded_planes:2 * padded_planes], rest[:, half:]], axis=1)
        c = sc_ref[pl.ds(base, padded_planes), :]
        s = ss_ref[pl.ds(base, padded_planes), :]
        stack_ref[pl.ds(2 * base, padded_planes), :sticks] = re * c - im * s
        stack_ref[pl.ds(2 * base + padded_planes, padded_planes), :sticks] = re * s + im * c
    turned = jnp.transpose(stack_ref[...])[:sticks]
    local = dot3(split(turned), (whi_ref[...], wlo_ref[...])) * volume
    position = lax.broadcasted_iota(jnp.int32, (sticks, padded), 1).astype(F32)
    kept = position < len_ref[:, 0:1]
    kc = kc_ref[...]
    out_ref[:, 0, :] = jnp.where(kept, kc[:, :padded] + local[:, :padded], 0.0)
    out_ref[:, 1, :] = jnp.where(kept, kc[:, padded:] + local[:, padded:], 0.0)
    sub_ref[:, 0, :] = total[0:2, :bands]


def far_first(count):
    return [0] + sorted(range(1, count), key=lambda k: abs(k - count // 2))


def pairs(count, k):
    return [(d, d ^ k) for d in range(count)]


def shards(bands, devices, coefficients, stick_col, stick_row, stick_length, plane_of_slot, potential):
    extent = plane_of_slot.shape[0]
    sticks = coefficients.shape[1]
    padded = coefficients.shape[3]
    total_sticks = stick_col.shape[0]
    planes = potential.shape[0]
    padded_planes = up8(planes)
    if sticks != LANES + LANES // 2 or devices % 2 or planes % 2 or bands & (bands - 1):
        raise ValueError("sizes")
    rows = sum(row_blocks())
    volume = 1.0 / (extent * extent * extent)
    me = lax.axis_index("tg").astype(jnp.int32)
    coef = coefficients.reshape(sticks, 2, padded)

    length, row, col = (v.reshape(-1, LANES) for v in (stick_length, stick_row, stick_col))
    slots = plane_of_slot.reshape(devices, planes)
    if padded_planes > planes:
        slots = jnp.pad(slots, ((0, 0), (0, padded_planes - planes)), constant_values=-1)
    slots = slots.reshape(1, devices * padded_planes)
    windows = total_sticks // LANES
    smem = pl.BlockSpec(memory_space=pltpu.SMEM)
    vmem = pl.BlockSpec(memory_space=pltpu.VMEM)
    hbm = pl.BlockSpec(memory_space=pltpu.HBM)

    block = 3 * padded_planes
    total_planes = devices * padded_planes
    sent, kc, wave, lengths, whi, wlo, shift_cos, shift_sin = pl.pallas_call(
        functools.partial(wave_kernel, extent),
        out_shape=(
            jax.ShapeDtypeStruct((devices, block, LANES), F32),
            jax.ShapeDtypeStruct((sticks, 2 * padded), F32),
            jax.ShapeDtypeStruct((2 * sticks, padded), F32),
            jax.ShapeDtypeStruct((sticks, LANES), F32),
            jax.ShapeDtypeStruct((2 * total_planes, 2 * padded), BF16),
            jax.ShapeDtypeStruct((2 * total_planes, 2 * padded), BF16),
            jax.ShapeDtypeStruct((total_planes, sticks), F32),
            jax.ShapeDtypeStruct((total_planes, sticks), F32),
        ),
        in_specs=[smem] + [hbm] * 5,
        scratch_shapes=[
            pltpu.VMEM(length.shape, jnp.int32),
            pltpu.VMEM(row.shape, jnp.int32),
            pltpu.VMEM(col.shape, jnp.int32),
            pltpu.VMEM(slots.shape, jnp.int32),
            pltpu.VMEM(coef.shape, F32),
            pltpu.SemaphoreType.DMA((5,)),
        ],
        compiler_params=params(56),
        name="wave_to_planes",
    )(me.reshape(1), length, row, col, slots, coef)

    received = lax.all_to_all(sent, "tg", split_axis=0, concat_axis=0, tiled=True)

    window_list = jax.ShapeDtypeStruct((windows, LANES), jnp.int32)
    longer_list = jax.ShapeDtypeStruct((2 * windows + 1, LANES), jnp.int32)
    square = jax.ShapeDtypeStruct((LANES, LANES), jnp.int32)
    even_map, odd_map, first, source, target, row_w, col_w = pl.pallas_call(
        functools.partial(map_kernel, extent, sticks),
        out_shape=(
            square,
            square,
            jax.ShapeDtypeStruct((16, LANES), jnp.int32),
            window_list,
            window_list,
            longer_list,
            longer_list,
        ),
        in_specs=[hbm] * 2,
        scratch_shapes=[
            pltpu.VMEM(row.shape, jnp.int32),
            pltpu.VMEM(col.shape, jnp.int32),
            pltpu.SemaphoreType.DMA((2,)),
        ],
        compiler_params=params(14 * total_sticks / 1536),
        cost_estimate=cost(4e9, 1e5),
        name="stick_map",
    )(row, col)

    constants = jnp.asarray(tables(extent))
    weighted = pl.pallas_call(
        functools.partial(plane_kernel, planes),
        out_shape=jax.ShapeDtypeStruct((devices, block + 8, LANES), F32),
        in_specs=[smem] + [vmem] * 7 + [hbm] * 2,
        out_specs=vmem,
        scratch_shapes=[
            pltpu.VMEM((windows, 2 * padded_planes, LANES), F32),
            pltpu.VMEM((windows, 2 * padded_planes, LANES), F32),
            pltpu.VMEM((2 * windows + 1, padded_planes, LANES), F32),
            pltpu.VMEM((padded_planes * rows, LANES), F32),
            pltpu.VMEM((padded_planes * rows, LANES), F32),
            pltpu.VMEM(constants.shape, BF16),
            pltpu.VMEM(potential.shape, F32),
            pltpu.SemaphoreType.DMA((2,)),
        ],
        compiler_params=params(52),
        cost_estimate=cost(2e10, 1e7),
        name="planes",
    )(first, even_map, odd_map, source, target, row_w, col_w, received, constants, potential)

    waves, fields = [wave], [received]
    for m in range(1, bands):
        waves.append(lax.ppermute(wave, "band", pairs(bands, m)))
        fields.append(lax.ppermute(received, "band", pairs(bands, m)))
    band = lax.axis_index("band").astype(jnp.int32)
    norm = 1.0 / (total_sticks * padded)
    places = jnp.stack([band, me])
    outgoing = pl.pallas_call(
        functools.partial(inner_kernel, bands, volume, norm),
        out_shape=(jax.ShapeDtypeStruct((block + 8, LANES), F32),) * devices,
        in_specs=[smem] + [vmem] * (2 + 2 * bands),
        compiler_params=params(6 + 1.5 * bands),
        name="inner",
    )(places, kc, *waves, *fields, weighted)

    returned = list(outgoing)
    for k in far_first(devices)[1:]:
        ring = [(d, (d + k) % devices) for d in range(devices)]
        returned[k] = lax.ppermute(outgoing[k], "tg", ring)
    applied, subspace = pl.pallas_call(
        functools.partial(final_kernel, volume, devices),
        out_shape=(
            jax.ShapeDtypeStruct((sticks, 2, padded), F32),
            jax.ShapeDtypeStruct((2, 1, bands), F32),
        ),
        in_specs=[smem] + [vmem] * (6 + devices),
        scratch_shapes=[pltpu.VMEM((2 * total_planes, 2 * LANES), F32)],
        compiler_params=params(6 + 6 * total_planes / 192),
        name="planes_to_wave",
    )(me.reshape(1), lengths, *[returned[k] for k in far_first(devices)], kc, whi, wlo, shift_cos, shift_sin)
    return applied.reshape(1, sticks, 2, padded), subspace


def solution(mesh):
    in_specs = (P("band", "tg", None, None), P(), P(), P(), P(), P("tg", None, None))
    out_specs = (P("band", "tg", None, None), P(None, "band", None))
    body = functools.partial(shards, mesh.shape["band"], mesh.shape["tg"])
    return jax.shard_map(body, mesh=mesh, in_specs=in_specs, out_specs=out_specs, check_vma=False)
```
